32 devices in a mesh: dp: 8 (over z, x), chan: 4 (over y, core).
Axes of the slice: x: 2, y: 2, z: 4, core: 2. Of those that a mesh axis runs over, the one named last changes fastest.
Arguments:
- tokens: bfloat16 [75264, 1024], P(('dp', 'chan')), may hold values from -6 to 6
- frame_counts: int32 [8], P('dp'), may hold values from 2 to 12, as said below
- cotangent: bfloat16 [75264, 1024], P(('dp', 'chan')), may hold values from -6 to 6
- w_reduce: float32 [2, 1024, 256], P(None, None, 'chan'), may hold values from -0.1875 to 0.1875
- w_mix: float32 [2, 256, 256], P(None, None, 'chan'), may hold values from -0.375 to 0.375
- w_depth: float32 [2, 27, 256], P(None, None, 'chan'), may hold values from -1.25 to 1.25
- w_expand: float32 [2, 256, 1024], P(None, 'chan'), may hold values from -0.375 to 0.375
- norm_mid: float32 [2, 3, 2, 256], P(None, None, None, 'chan'), may hold values from -1.2 to 1.4
- norm_out: float32 [2, 2, 1024], replicated, may hold values from -1.2 to 1.4
- moment_reduce: float32 [2, 1024, 256], P(None, None, 'chan'), may hold values from -2352 to 2352
- moment_mix: float32 [2, 256, 256], P(None, None, 'chan'), may hold values from -2352 to 2352
- moment_depth: float32 [2, 27, 256], P(None, None, 'chan'), may hold values from -2352 to 2352
- moment_expand: float32 [2, 256, 1024], P(None, 'chan'), may hold values from -2352 to 2352
- moment_mid: float32 [2, 3, 2, 256], P(None, None, None, 'chan'), may hold values from -2352 to 2352
- moment_out: float32 [2, 2, 1024], replicated, may hold values from -2352 to 2352
Outputs:
- output: bfloat16 [75264, 1024], P(('dp', 'chan'))
- grad_tokens: bfloat16 [75264, 1024], P(('dp', 'chan'))
- grad_reduce: float32 [2, 1024, 256], P(None, None, 'chan')
- grad_mix: float32 [2, 256, 256], P(None, None, 'chan')
- grad_depth: float32 [2, 27, 256], P(None, None, 'chan')
- grad_expand: float32 [2, 256, 1024], P(None, 'chan')
- grad_mid: float32 [2, 3, 2, 256], P(None, None, None, 'chan')
- grad_out: float32 [2, 2, 1024], replicated
- new_reduce: float32 [2, 1024, 256], P(None, None, 'chan')
- new_mix: float32 [2, 256, 256], P(None, None, 'chan')
- new_depth: float32 [2, 27, 256], P(None, None, 'chan')
- new_expand: float32 [2, 256, 1024], P(None, 'chan')
- new_mid: float32 [2, 3, 2, 256], P(None, None, None, 'chan')
- new_out: float32 [2, 2, 1024], replicated
- new_moment_reduce: float32 [2, 1024, 256], P(None, None, 'chan')
- new_moment_mix: float32 [2, 256, 256], P(None, None, 'chan')
- new_moment_depth: float32 [2, 27, 256], P(None, None, 'chan')
- new_moment_expand: float32 [2, 256, 1024], P(None, 'chan')
- new_moment_mid: float32 [2, 3, 2, 256], P(None, None, None, 'chan')
- new_moment_out: float32 [2, 2, 1024], replicated
The draws below stay inside these ranges and needn't reach their ends.
Inputs may be any that keep to these rules, and one draw needn't show every extreme that they name: `frame_counts`: each clip has 2 to 12 real frames; some clip has exactly 12 and some exactly 2.
All inputs are finite; a program needn't handle non-finite values.
Results may differ from the reference program's by a relative error of at most 0.018.
Values may be sent and summed in bfloat16 or wider, within the bound.
A program may use at most 384 MiB of HBM per device.

```python
import functools
import jax
import jax.numpy as jnp
from jax import lax

D = 1024
C = 256
KVOL = 27
FRAMES = 12
HH = 28
WW = 28
BLOCKS = 2
CLIPS = 8
VOX = 75264


def gain_shift(key, lead, width):
    gain_key, shift_key = jax.random.split(key)
    gains = jax.random.uniform(gain_key, lead + (1, width), jnp.float32, 0.6, 1.4)
    shifts = jnp.clip(0.3 * jax.random.normal(shift_key, lead + (1, width), jnp.float32), -1.2, 1.2)
    return jnp.concatenate([gains, shifts], axis=len(lead))


def draw_frame_counts(key, part):
    key = jax.random.fold_in(key, 11)
    first_key, order_key = jax.random.split(key)
    counts = jax.random.randint(first_key, (CLIPS,), 2, FRAMES + 1)
    order = jax.random.permutation(order_key, CLIPS)
    counts = jnp.where(order == 0, FRAMES, counts)
    counts = jnp.where(order == 1, 2, counts)
    return counts.astype(jnp.int32)


def draw_norm_mid(key, part):
    key = jax.random.fold_in(key, 23)
    return gain_shift(key, (BLOCKS, 3), C)


def draw_norm_out(key, part):
    key = jax.random.fold_in(key, 37)
    return gain_shift(key, (BLOCKS,), D)


def level_of(rng, dims, cuts, least, top_value):
    factor_of, own = 1.0, jax.random.fold_in(rng, 6)
    for dim, shards_of in cuts:
        heights = jnp.exp(jax.random.uniform(jax.random.fold_in(own, dim), (shards_of,), jnp.float32, least / len(cuts), top_value / len(cuts)))
        factor_of = factor_of * jnp.repeat(heights, dims[dim] // shards_of).reshape([-1 if axis == dim else 1 for axis in range(len(dims))])
    return factor_of


def bell_draw(rng, extent, scale, bound, cuts=(), held_as=jnp.bfloat16):
    values = scale * jax.random.normal(rng, extent, jnp.float32)
    if cuts:
        values = values * level_of(rng, extent, cuts, -0.22, 0.18)
    return jnp.clip(values, -bound, bound).astype(held_as)


def setup_inputs(seed: int = 0) -> dict:
    streams_of = jax.random.split(jax.random.key(seed), 16)
    return {
        "tokens": bell_draw(streams_of[0], (VOX, D), 1.0, 6.0, ((0, 32),)),
        "frame_counts": draw_frame_counts(jax.random.fold_in(streams_of[15], 71), 0),
        "cotangent": bell_draw(streams_of[2], (VOX, D), 1.0, 6.0, ((0, 32),)),
        "w_reduce": bell_draw(streams_of[3], (BLOCKS, D, C), D ** -0.5, 0.1875, ((2, 4),), jnp.float32),
        "w_mix": bell_draw(streams_of[4], (BLOCKS, C, C), C ** -0.5, 0.375, ((2, 4),), jnp.float32),
        "w_depth": bell_draw(streams_of[5], (BLOCKS, KVOL, C), KVOL ** -0.5, 1.25, ((2, 4),), jnp.float32),
        "w_expand": bell_draw(streams_of[6], (BLOCKS, C, D), C ** -0.5, 0.375, ((1, 4),), jnp.float32),
        "norm_mid": draw_norm_mid(jax.random.fold_in(streams_of[15], 71), 0),
        "norm_out": draw_norm_out(jax.random.fold_in(streams_of[15], 71), 0),
        "moment_reduce": bell_draw(streams_of[9], (BLOCKS, D, C), (HH * WW // 2), 2352.0, ((2, 4),), jnp.float32),
        "moment_mix": bell_draw(streams_of[10], (BLOCKS, C, C), (HH * WW // 2), 2352.0, ((2, 4),), jnp.float32),
        "moment_depth": bell_draw(streams_of[11], (BLOCKS, KVOL, C), (HH * WW // 2), 2352.0, ((2, 4),), jnp.float32),
        "moment_expand": bell_draw(streams_of[12], (BLOCKS, C, D), (HH * WW // 2), 2352.0, ((1, 4),), jnp.float32),
        "moment_mid": bell_draw(streams_of[13], (BLOCKS, 3, 2, C), (HH * WW // 2), 2352.0, ((3, 4),), jnp.float32),
        "moment_out": bell_draw(streams_of[14], (BLOCKS, 2, D), (HH * WW // 2), 2352.0, (), jnp.float32),
    }


EPS = 1e-05
LEARN_RATE = 0.001
MOMENTUM = 0.9
DECAY = 0.0001

@jax.custom_vjp
def low(v):
    return lax.optimization_barrier(v.astype(jnp.bfloat16)).astype(jnp.float32)

@jax.custom_vjp
def low_back(v):
    return v

def low_keep(v):
    return (low(v), None)

def low_pass(kept, grad):
    return (grad,)

def back_keep(v):
    return (v, None)

def back_low(kept, grad):
    return (low(grad),)
low.defvjp(low_keep, low_pass)
low_back.defvjp(back_keep, back_low)

def gelu_soft(value):
    return jax.nn.gelu(value, approximate=True)

def matmul(left, right):
    return jnp.dot(left, right, precision=lax.Precision.HIGHEST, preferred_element_type=jnp.float32)

def masked_norm(field, mask, count, gain, shift):
    mean = lax.optimization_barrier(jnp.sum(field * mask, axis=0)) / count
    var = lax.optimization_barrier(jnp.sum(field * field * mask, axis=0)) / count - mean * mean
    return mask * ((field - mean) * lax.rsqrt(var + EPS) * gain + shift)

def depthwise(field, kern):
    volume = field.reshape(CLIPS, FRAMES, HH, WW, C)
    padded = jnp.pad(volume, ((0, 0), (1, 1), (1, 1), (1, 1), (0, 0)))
    total = jnp.zeros_like(volume)
    for step in range(3):
        for row in range(3):
            for column in range(3):
                tap = kern[step * 9 + row * 3 + column]
                total = total + tap * padded[:, step:step + FRAMES, row:row + HH, column:column + WW]
    return total.reshape(-1, C)

def block(inputs, mask, count, w_reduce, w_mix, w_depth, w_expand, norm_mid, norm_out):
    first = low_back(matmul(inputs, low(w_reduce)))
    act_one = low(mask * gelu_soft(masked_norm(first, mask, count, norm_mid[0, 0], norm_mid[0, 1])))
    second = low_back(matmul(act_one, low(w_mix)))
    act_two = masked_norm(second, mask, count, norm_mid[1, 0], norm_mid[1, 1])
    third = depthwise(act_two, w_depth)
    act_three = low(mask * gelu_soft(masked_norm(third, mask, count, norm_mid[2, 0], norm_mid[2, 1])))
    fourth = low_back(matmul(act_three, low(w_expand)))
    return low(mask * gelu_soft(masked_norm(fourth, mask, count, norm_out[0], norm_out[1]) + inputs))

def forward(tokens, w_reduce, w_mix, w_depth, w_expand, norm_mid, norm_out, mask, count):
    hidden = low(tokens)
    for index in range(BLOCKS):
        hidden = block(hidden, mask, count, w_reduce[index], w_mix[index], w_depth[index], w_expand[index], norm_mid[index], norm_out[index])
    return hidden

def descend(weight, moment, grad):
    moment_new = MOMENTUM * moment + grad + DECAY * weight
    return (weight - LEARN_RATE * moment_new, moment_new)

def reference(tokens, frame_counts, cotangent, w_reduce, w_mix, w_depth, w_expand, norm_mid, norm_out, moment_reduce, moment_mix, moment_depth, moment_expand, moment_mid, moment_out):
    alive = (jnp.arange(FRAMES)[None, :] < frame_counts[:, None]).astype(jnp.float32)
    mask = jnp.broadcast_to(alive[:, :, None], (CLIPS, FRAMES, HH * WW)).reshape(-1, 1)
    count = jnp.sum(mask)
    params = (w_reduce, w_mix, w_depth, w_expand, norm_mid, norm_out)
    moments = (moment_reduce, moment_mix, moment_depth, moment_expand, moment_mid, moment_out)
    func = functools.partial(forward, mask=mask, count=count)
    output, pull = jax.vjp(func, tokens.astype(jnp.float32), *params)
    grads = pull(cotangent.astype(jnp.float32))
    updated = [descend(w, m, g) for w, m, g in zip(params, moments, grads[1:])]
    return (output.astype(jnp.bfloat16), grads[0].astype(jnp.bfloat16), grads[1], grads[2], grads[3], grads[4], grads[5], grads[6], updated[0][0], updated[1][0], updated[2][0], updated[3][0], updated[4][0], updated[5][0], updated[0][1], updated[1][1], updated[2][1], updated[3][1], updated[4][1], updated[5][1])
```

```python
import functools

import jax
import jax.numpy as jnp
from jax import lax
from jax.experimental import pallas as pl
from jax.experimental.pallas import tpu as pltpu
from jax.sharding import PartitionSpec as P

FRAMES = 12
HH = 28
WW = 28
BLOCKS = 2

EPS = 1e-05
LEARN_RATE = 0.001
MOMENTUM = 0.9
DECAY = 0.0001
MESH = pl.DeviceIdType.MESH


def gelu_soft(value):
    return jax.nn.gelu(value, approximate=True)


def gelu_back(value, grad):
    return jax.vjp(gelu_soft, value)[1](grad)[0]


def dot(left, right, over_left, over_right):
    return lax.dot_general(
        left, right, (((over_left,), (over_right,)), ((), ())), preferred_element_type=jnp.float32
    )


def sum_kernel(sizes, x_ref, o_ref, near, far, near_send, near_recv, far_send, far_recv):
    lanes, groups = sizes
    row = lax.axis_index("dp")
    lane = lax.axis_index("chan")
    barrier = pltpu.get_barrier_semaphore()
    near_peers = [(lax.rem(lane + o, lanes)) for o in range(1, lanes)]
    far_peers = [(lax.rem(row + o, groups)) for o in range(1, groups)]
    for peer in near_peers:
        pl.semaphore_signal(barrier, inc=1, device_id=(row, peer), device_id_type=MESH)
    for peer in far_peers:
        pl.semaphore_signal(barrier, inc=1, device_id=(peer, lane), device_id_type=MESH)
    pl.semaphore_wait(barrier, lanes + groups - 2)

    def stage(slots, send, recv, me, peers, place):
        copies = []
        for step, peer in enumerate(peers):
            copy = pltpu.make_async_remote_copy(
                src_ref=slots.at[me],
                dst_ref=slots.at[me],
                send_sem=send.at[step],
                recv_sem=recv.at[me],
                device_id=place(peer),
                device_id_type=MESH,
            )
            copy.start()
            copies.append(copy)
        for step, peer in enumerate(peers):
            pltpu.make_async_remote_copy(
                src_ref=slots.at[peer],
                dst_ref=slots.at[peer],
                send_sem=send.at[step],
                recv_sem=recv.at[peer],
                device_id=place(peer),
                device_id_type=MESH,
            ).wait_recv()
        for copy in copies:
            copy.wait_send()
        total = slots[0]
        for index in range(1, slots.shape[0]):
            total = total + slots[index]
        return total

    near[lane] = x_ref[...]
    far[row] = stage(near, near_send, near_recv, lane, near_peers, lambda p: (row, p))
    o_ref[...] = stage(far, far_send, far_recv, row, far_peers, lambda p: (p, lane))


def all_sum(sizes, rows):
    flat = jnp.concatenate([r.reshape(-1, 128) for r in rows], axis=0)
    pad = -flat.shape[0] % 8
    flat = jnp.pad(flat, ((0, pad), (0, 0)))
    lanes, groups = sizes
    shape = flat.shape
    total = pl.pallas_call(
        functools.partial(sum_kernel, sizes),
        out_shape=jax.ShapeDtypeStruct(shape, jnp.float32),
        in_specs=[pl.BlockSpec(memory_space=pltpu.VMEM)],
        out_specs=pl.BlockSpec(memory_space=pltpu.VMEM),
        scratch_shapes=[
            pltpu.VMEM((lanes,) + shape, jnp.float32),
            pltpu.VMEM((groups,) + shape, jnp.float32),
            pltpu.SemaphoreType.DMA((lanes,)),
            pltpu.SemaphoreType.DMA((lanes,)),
            pltpu.SemaphoreType.DMA((groups,)),
            pltpu.SemaphoreType.DMA((groups,)),
        ],
        compiler_params=pltpu.CompilerParams(collective_id=shape[0], has_side_effects=True),
    )(flat)
    out, at = [], 0
    for r in rows:
        n = r.size // 128
        out.append(total[at : at + n].reshape(r.shape))
        at += n
    return out


def halo(field, lanes):
    before = lax.ppermute(field[-1:], "chan", [(i, i + 1) for i in range(lanes - 1)])
    after = lax.ppermute(field[:1], "chan", [(i + 1, i) for i in range(lanes - 1)])
    return jnp.concatenate([before, field, after], axis=0)


def depthwise(deep, kern, frames):
    padded = jnp.pad(deep, ((0, 0), (1, 1), (1, 1), (0, 0)))
    total = 0.0
    for step in range(3):
        for row in range(3):
            for column in range(3):
                tap = kern[step * 9 + row * 3 + column]
                total = total + tap * padded[step : step + frames, row : row + HH, column : column + WW]
    return total


def kernel_grad(field, deep, frames):
    padded = jnp.pad(deep, ((0, 0), (1, 1), (1, 1), (0, 0)))
    taps = []
    for step in range(3):
        for row in range(3):
            for column in range(3):
                part = padded[2 - step : 2 - step + frames, 2 - row : 2 - row + HH, 2 - column : 2 - column + WW]
                taps.append(jnp.sum(field * part, axis=(0, 1, 2)))
    return jnp.stack(taps)


def descend(weight, moment, grad):
    moment_new = MOMENTUM * moment + grad + DECAY * weight
    return (weight - LEARN_RATE * moment_new, moment_new)


def column_sum(value):
    return jnp.sum(value, axis=0)


def affine_of(totals, squares, count, gain, shift):
    mean = totals / count
    var = squares / count - mean * mean
    scale = lax.rsqrt(var + EPS)
    return (mean, scale, gain * scale, shift - mean * gain * scale)


def shards(
    tokens,
    frame_counts,
    cotangent,
    w_reduce,
    w_mix,
    w_depth,
    w_expand,
    norm_mid,
    norm_out,
    moment_reduce,
    moment_mix,
    moment_depth,
    moment_expand,
    moment_mid,
    moment_out,
):
    row = lax.axis_index("dp")
    lane = lax.axis_index("chan")
    lanes = lax.axis_size("chan")
    sizes = (lanes, lax.axis_size("dp"))
    frames = tokens.shape[0] // (HH * WW)
    narrow = w_reduce.shape[2]
    gather = lambda v, axis: lax.all_gather(v, "chan", axis=axis, tiled=True)
    reduce_all = gather(w_reduce.astype(jnp.bfloat16), 2)
    mix_all = gather(w_mix.astype(jnp.bfloat16), 2)
    expand_all = gather(w_expand.astype(jnp.bfloat16), 1)
    depth_all = gather(w_depth, 2)
    mid_all = gather(norm_mid, 3)
    alive = (lane * frames - 1 + jnp.arange(frames + 2) < frame_counts[0]) & (
        lane * frames - 1 + jnp.arange(frames + 2) >= 0
    )
    alive = alive.astype(jnp.float32)
    mask = jnp.repeat(alive[1:-1], HH * WW)[:, None]
    wide = mix_all.shape[1]
    flat = lambda v: v.reshape(-1, wide)
    deepen = lambda v: v.reshape(-1, HH, WW, wide)

    hidden = tokens
    stored = []
    count = None
    for b in range(BLOCKS):
        mid = mid_all[b]
        first = dot(hidden, reduce_all[b], 1, 0)
        sums = [column_sum(first * mask), column_sum(first * first * mask)]
        if count is None:
            sums.append(jnp.full((128,), jnp.sum(mask)))
            t, q, n = all_sum(sizes, sums)
            count = n[0]
        else:
            t, q = all_sum(sizes, sums)
        mean1, scale1, a1, b1 = affine_of(t, q, count, mid[0, 0], mid[0, 1])
        act1 = (mask * gelu_soft(first * a1 + b1)).astype(jnp.bfloat16)
        second = dot(act1, mix_all[b], 1, 0)
        masked2 = second * mask
        conv = flat(depthwise(halo(deepen(masked2), lanes), depth_all[b], frames))
        ones = jnp.broadcast_to(alive[:, None, None, None], (frames + 2, HH, WW, 1))
        edge = flat(depthwise(ones, depth_all[b], frames))
        t, q, sc, scc, sce, se, see = all_sum(
            sizes,
            [
                column_sum(masked2),
                column_sum(masked2 * masked2),
                column_sum(conv * mask),
                column_sum(conv * conv * mask),
                column_sum(conv * edge * mask),
                column_sum(edge * mask),
                column_sum(edge * edge * mask),
            ],
        )
        mean2, scale2, a2, b2 = affine_of(t, q, count, mid[1, 0], mid[1, 1])
        t3 = a2 * sc + b2 * se
        q3 = a2 * a2 * scc + 2.0 * a2 * b2 * sce + b2 * b2 * see
        mean3, scale3, a3, b3 = affine_of(t3, q3, count, mid[2, 0], mid[2, 1])
        third = a2 * conv + b2 * edge
        norm3 = third * a3 + b3
        act3 = (mask * gelu_soft(norm3)).astype(jnp.bfloat16)
        fourth = dot(act3, expand_all[b], 1, 0)
        t, q = all_sum(sizes, [column_sum(fourth * mask), column_sum(fourth * fourth * mask)])
        mean4, scale4, a4, b4 = affine_of(t, q, count, norm_out[b, 0], norm_out[b, 1])
        pre = mask * (fourth * a4 + b4) + hidden.astype(jnp.float32)
        result = (mask * gelu_soft(pre)).astype(jnp.bfloat16)
        stored.append(
            (hidden, first, act1, second, conv, edge, third, norm3, act3, fourth, pre)
            + ((mean1, scale1, a1, b1), (mean2, scale2, a2, b2), (mean3, scale3, a3, b3), (mean4, scale4, a4, b4))
            + ((sc, scc, sce, se, see),)
        )
        hidden = result

    gradient = cotangent.astype(jnp.float32)
    collected = [None] * BLOCKS
    for b in reversed(range(BLOCKS)):
        (x, first, act1, second, conv, edge, third, norm3, act3, fourth, pre) = stored[b][:11]
        ((mean1, scale1, a1, b1), (mean2, scale2, a2, b2), (mean3, scale3, a3, b3), (mean4, scale4, a4, b4)) = stored[b][11:15]
        sc, scc, sce, se, see = stored[b][15]
        residual = gelu_back(pre, mask * gradient)
        unit4 = (fourth - mean4) * scale4
        shift4, gain4 = all_sum(sizes, [column_sum(residual), column_sum(residual * unit4)])
        fourth_grad = (mask * a4 * (residual - shift4 / count - unit4 * gain4 / count)).astype(jnp.bfloat16)
        grad_expand = dot(act3, fourth_grad, 0, 0)
        e3 = mask * gelu_back(norm3, dot(fourth_grad, expand_all[b], 1, 1))
        e3_sum, e3_conv, e3_edge = all_sum(sizes, [column_sum(e3), column_sum(e3 * conv), column_sum(e3 * edge)])
        shift3 = e3_sum
        gain3 = scale3 * (a2 * e3_conv + b2 * e3_edge - mean3 * e3_sum)
        r = -a3 * scale3 * gain3 / count
        q = -a3 * shift3 / count - r * mean3
        p = a3
        third_conv = a2 * scc + b2 * sce
        third_edge = a2 * sce + b2 * see
        d3_conv = p * e3_conv + q * sc + r * third_conv
        d3_edge = p * e3_edge + q * se + r * third_edge
        shift2 = d3_edge
        gain2 = scale2 * (d3_conv - mean2 * d3_edge)
        third_grad = mask * (p * e3 + q + r * third)
        deep = halo(deepen(third_grad), lanes)
        act2 = mask * (second * a2 + b2)
        grad_depth = kernel_grad(deepen(act2), deep, frames)
        act2_grad = flat(depthwise(deep, depth_all[b][::-1], frames))
        unit2 = (second - mean2) * scale2
        second_grad = (mask * a2 * (act2_grad - shift2 / count - unit2 * gain2 / count)).astype(jnp.bfloat16)
        grad_mix = dot(act1, second_grad, 0, 0)
        e1 = mask * gelu_back(first * a1 + b1, dot(second_grad, mix_all[b], 1, 1))
        unit1 = (first - mean1) * scale1
        shift1, gain1 = all_sum(sizes, [column_sum(e1), column_sum(e1 * unit1)])
        first_grad = (mask * a1 * (e1 - shift1 / count - unit1 * gain1 / count)).astype(jnp.bfloat16)
        grad_reduce = dot(x, first_grad, 0, 0)
        gradient = dot(first_grad, reduce_all[b], 1, 1) + residual
        grad_mid = jnp.stack(
            [jnp.stack([gain1, shift1]), jnp.stack([gain2, shift2]), jnp.stack([gain3, shift3])]
        )
        collected[b] = (grad_reduce, grad_mix, grad_depth, grad_expand, grad_mid, jnp.stack([gain4, shift4]))
    stacked = [jnp.stack([pieces[slot] for pieces in collected]) for slot in range(6)]
    scatter = lambda v, axis: lax.psum_scatter(v, "chan", scatter_dimension=axis, tiled=True)
    grad_reduce, grad_mix, grad_depth, grad_expand = lax.psum(
        (scatter(stacked[0], 2), scatter(stacked[1], 2), scatter(stacked[2], 2), scatter(stacked[3], 1)), "dp"
    )
    grad_mid = lax.dynamic_slice_in_dim(stacked[4], lane * narrow, narrow, 3)
    grad_out = stacked[5]
    grads = (grad_reduce, grad_mix, grad_depth, grad_expand, grad_mid, grad_out)
    params = (w_reduce, w_mix, w_depth, w_expand, norm_mid, norm_out)
    moments = (moment_reduce, moment_mix, moment_depth, moment_expand, moment_mid, moment_out)
    updated = [descend(w, m, g) for w, m, g in zip(params, moments, grads)]
    return (
        (hidden, gradient.astype(jnp.bfloat16)) + grads + tuple(u[0] for u in updated) + tuple(u[1] for u in updated)
    )


def solution(mesh):
    rows = P(("dp", "chan"), None)
    weights = (
        P(None, None, "chan"),
        P(None, None, "chan"),
        P(None, None, "chan"),
        P(None, "chan", None),
        P(None, None, None, "chan"),
        P(),
    )
    return jax.shard_map(
        shards,
        mesh=mesh,
        in_specs=(rows, P("dp"), rows) + weights + weights,
        out_specs=(rows, rows) + weights + weights + weights,
        check_vma=False,
    )
```

```python
import functools

import jax
import jax.numpy as jnp
from jax import lax
from jax.experimental import pallas as pl
from jax.experimental.pallas import tpu as pltpu
from jax.sharding import PartitionSpec as P

FRAMES = 12
HH = 28
WW = 28
WP = 32
KVOL = 27
BLOCKS = 2
GROUP = 4
QUADS = HH // GROUP
FLAT = GROUP * WW
WIDE = GROUP * WP

EPS = 1e-05
LEARN_RATE = 0.001
MOMENTUM = 0.9
DECAY = 0.0001
MESH = pl.DeviceIdType.MESH
F32 = jnp.float32
BF16 = jnp.bfloat16
ROOT = 0.7978845608028654
CUBE = 0.044715


def gelu_fwd(v):
    t = jnp.tanh(v * (ROOT + (ROOT * CUBE) * (v * v)))
    h = 0.5 * v
    return h * t + h


def gelu_slope(v):
    s = v * v
    t = jnp.tanh(v * (ROOT + (ROOT * CUBE) * s))
    return 0.5 * (1.0 + t) + (0.5 * v) * (1.0 - t * t) * (ROOT + (3.0 * ROOT * CUBE) * s)


def dot(left, right):
    return jnp.dot(left, right, preferred_element_type=F32)


def fold(v):
    return jnp.sum(v.reshape(v.shape[0] // 8, 8, v.shape[1]), axis=0)


def spread(v):
    gap = jnp.zeros((WP - WW, v.shape[1]), v.dtype)
    parts = []
    for h in range(GROUP):
        parts += [v[WW * h : WW * (h + 1)], gap]
    return jnp.concatenate(parts, axis=0)


def squeeze(v):
    return jnp.concatenate([v[WP * h : WP * h + WW] for h in range(GROUP)], axis=0)


def rows_of(*vectors):
    parts = []
    for v in vectors:
        parts += [v[:, 256 * i : 256 * (i + 1)] for i in range(v.shape[1] // 256)]
    if len(parts) < 8:
        parts.append(jnp.zeros((8 - len(parts), 256), F32))
    return jnp.concatenate(parts, axis=0)


def flat_sum(v):
    return jnp.sum(v, axis=0, keepdims=True)


def wide_row(v, first):
    return jnp.concatenate([v[first + i : first + i + 1] for i in range(4)], axis=1)


class Net:
    def __init__(self, groups, lanes):
        self.groups, self.lanes = groups, lanes
        self.row = lax.axis_index("dp")
        self.lane = lax.axis_index("chan")
        self.core = lax.rem(self.lane, 2)
        self.side = lax.div(self.lane, 2)
        self.half = lanes // 2

    def near(self):
        return [(1 - self.core, (self.row, self.side * 2 + 1 - self.core))]

    def far(self):
        out = []
        for o in range(self.groups):
            for p in range(self.half):
                if o or p:
                    row = lax.rem(self.row + o, self.groups)
                    side = lax.rem(self.side + p, self.half)
                    out.append((row * self.half + side, (row, side * 2 + self.core)))
        return out

    def far_slot(self):
        return self.row * self.half + self.side

    def chan_peers(self):
        return [
            (lax.rem(self.lane + o, self.lanes), (self.row, lax.rem(self.lane + o, self.lanes)))
            for o in range(1, self.lanes)
        ]


def push(src, dst, send, recv, device):
    copy = pltpu.make_async_remote_copy(
        src_ref=src, dst_ref=dst, send_sem=send, recv_sem=recv, device_id=device, device_id_type=MESH
    )
    return copy


def forward_kernel(
    groups,
    lanes,
    counts,
    tokens,
    reduce_loc,
    mix_loc,
    expand_loc,
    small_loc,
    norm_out,
    out_hbm,
    x1_hbm,
    z1_out,
    z2_out,
    c_out,
    sums_out,
    x0,
    x1,
    red_t,
    red,
    mix_t,
    mix,
    exp,
    small,
    z1,
    a1s,
    z2,
    conv,
    a3s,
    edge,
    halo_send,
    halo_recv,
    near,
    far,
    near_send,
    near_recv,
    far_send,
    far_recv,
    gather_send,
    gather_recv,
    halo_ssem,
    halo_rsem,
    load_sem,
    store_sem,
):
    net = Net(groups, lanes)
    lane = net.lane
    frames = tokens.shape[0] // (HH * WW)
    frame_rows = HH * WW
    count_here = counts[0]

    def live(frame):
        position = lane * frames + frame
        return jnp.where((position >= 0) & (position < count_here), 1.0, 0.0)

    loads = []
    for f in range(frames):
        rows = pl.ds(f * frame_rows, frame_rows)
        copy = pltpu.make_async_copy(tokens.at[rows], x0.at[rows], load_sem.at[f])
        copy.start()
        loads.append(copy)

    barrier = pltpu.get_barrier_semaphore()
    friends = [d for _, d in net.near()] + [d for _, d in net.far()] + [d for _, d in net.chan_peers()]
    for device in friends:
        pl.semaphore_signal(barrier, inc=1, device_id=device, device_id_type=MESH)
    pl.semaphore_wait(barrier, len(friends))

    own = net.lane
    share = red_t.shape[1] // lanes
    late = []

    def gather(slot, src, dst_of):
        for step, (_, device) in enumerate(net.chan_peers()):
            copy = push(src, dst_of(own), gather_send.at[slot, step], gather_recv.at[slot, own], device)
            copy.start()
            late.append(copy)
        dst_of(own)[...] = src[...]

    def gather_wait(slot, src, dst_of):
        for step, (peer, device) in enumerate(net.chan_peers()):
            push(src, dst_of(peer), gather_send.at[slot, step], gather_recv.at[slot, peer], device).wait_recv()

    def block_rows(ref, b):
        return lambda who: ref.at[b, pl.ds(pl.multiple_of(who * share, share), share)]

    plan = {
        ("red", 0): (0, reduce_loc.at[0], block_rows(red_t, 0)),
        ("mix", 0): (1, mix_loc.at[0], block_rows(mix_t, 0)),
        ("small", 0): (2, small_loc, lambda who: small.at[who]),
        ("exp", 0): (3, expand_loc.at[0], block_rows(exp, 0)),
        ("red", 1): (4, reduce_loc.at[1], block_rows(red_t, 1)),
        ("mix", 1): (5, mix_loc.at[1], block_rows(mix_t, 1)),
        ("exp", 1): (6, expand_loc.at[1], block_rows(exp, 1)),
    }
    for slot, src, dst_of in plan.values():
        gather(slot, src, dst_of)

    def total_start(i, value):
        near[i, net.core] = value
        for who, device in net.near():
            copy = push(
                near.at[i, net.core], near.at[i, net.core], near_send.at[i], near_recv.at[i], device
            )
            copy.start()
            late.append(copy)
            copy.wait_recv()
        far[i, net.far_slot()] = near[i, 0] + near[i, 1]
        for step, (who, device) in enumerate(net.far()):
            copy = push(
                far.at[i, net.far_slot()],
                far.at[i, net.far_slot()],
                far_send.at[i, step],
                far_recv.at[i, net.far_slot()],
                device,
            )
            copy.start()
            late.append(copy)

    def total_finish(i):
        for step, (who, device) in enumerate(net.far()):
            push(
                far.at[i, who], far.at[i, who], far_send.at[i, step], far_recv.at[i, who], device
            ).wait_recv()
        total = far[i, 0]
        for j in range(1, groups * net.half):
            total = total + far[i, j]
        return total

    column = lax.broadcasted_iota(jnp.int32, (WIDE, 256), 0) % WP
    pad_mask = (column < WW).astype(F32)

    def affine(total, square, count, gain, shift):
        mean = total / count
        var = square / count - mean * mean
        scale = lax.rsqrt(var + EPS)
        return mean, scale, gain * scale, shift - mean * (gain * scale)

    def zero8(n=256):
        return jnp.zeros((8, n), F32)

    for ref in (z2,):
        for b in range(BLOCKS):
            for f in range(frames + 2):
                ref[b, f, 0] = jnp.zeros((WP, 256), F32)
                ref[b, f, HH + 1] = jnp.zeros((WP, 256), F32)

    gather_wait(*plan["red", 0])
    red[0] = red_t[0].T

    carry = (zero8(), zero8())
    for f in range(frames):
        loads[f].wait()
        alive = live(f)

        def project(j, carry):
            q = f * QUADS + j
            x = x0[pl.ds(pl.multiple_of(q * FLAT, FLAT), FLAT)]
            z = dot(x, red[0])
            z1[0, pl.ds(q * GROUP, GROUP)] = spread(z).reshape(GROUP, WP, 256)
            z = z * alive
            return (carry[0] + fold(z), carry[1] + fold(z * z))

        carry = lax.fori_loop(0, QUADS, project, carry)

    gather_wait(*plan["small", 0])
    taps = small[0]
    for who in range(1, lanes):
        taps = taps + small[who]
    small[0] = taps

    def mid(b, norm, which):
        r = BLOCKS * KVOL + (b * 3 + norm) * 2 + which
        return small[0, r : r + 1]

    edge_sums = []
    pattern_col = lax.broadcasted_iota(jnp.int32, (WP, 256), 0)
    for b in range(BLOCKS):
        taps_b = [[small[0, b * KVOL + dt * 9 + k : b * KVOL + dt * 9 + k + 1] for k in range(9)] for dt in range(3)]
        se = jnp.zeros((1, 256), F32)
        see = jnp.zeros((1, 256), F32)
        for f in range(-1, frames + 1):
            here = live(f)
            t = [
                here * (live(f - 1) * taps_b[0][k] + here * taps_b[1][k] + live(f + 1) * taps_b[2][k])
                for k in range(9)
            ]
            for cls in range(3):
                use = [dh for dh in range(3) if not (cls == 0 and dh == 0) and not (cls == 2 and dh == 2)]
                col = []
                for dw in range(3):
                    v = t[use[0] * 3 + dw]
                    for dh in use[1:]:
                        v = v + t[dh * 3 + dw]
                    col.append(v)
                middle = col[0] + col[1] + col[2]
                first, last = col[1] + col[2], col[0] + col[1]
                edge[b, f + 1, cls] = jnp.where(
                    pattern_col == 0,
                    first,
                    jnp.where(pattern_col == WW - 1, last, jnp.where(pattern_col < WW - 1, middle, 0.0)),
                )
                if 0 <= f < frames:
                    times = 1.0 if cls != 1 else HH - 2.0
                    se = se + times * (first + last + (WW - 2.0) * middle)
                    see = see + times * (first * first + last * last + (WW - 2.0) * (middle * middle))
        edge_sums += [se, see]

    alive_all = sum(live(f) for f in range(frames)) * (HH * WW)
    here_count = jnp.full((1, 256), 1.0, F32) * alive_all
    total_start(0, rows_of(flat_sum(carry[0]), flat_sum(carry[1]), here_count, *edge_sums))

    for slot in (("mix", 0), ("exp", 0), ("red", 1), ("mix", 1), ("exp", 1)):
        gather_wait(*plan[slot])
    for b in range(BLOCKS):
        mix[b] = mix_t[b].T
    red[1] = red_t[1].T

    got = total_finish(0)
    sums_out[0] = got
    count = got[2:3]
    global_edge = [(got[3:4], got[4:5]), (got[5:6], got[6:7])]
    first_sums = (got[0:1], got[1:2])

    def edge_rows(b, f, j):
        top = jnp.where(j == 0, 0, 1)
        bottom = jnp.where(j == QUADS - 1, 2, 1)
        middle = edge[b, f + 1, 1]
        return jnp.concatenate([edge[b, f + 1, top], middle, middle, edge[b, f + 1, bottom]], axis=0)

    for b in range(BLOCKS):
        mean1, scale1, a1, b1 = affine(first_sums[0], first_sums[1], count, mid(b, 0, 0), mid(b, 0, 1))
        carry = (zero8(), zero8())
        for f in (0, frames - 1) + tuple(range(1, frames - 1)):
            alive = live(f)

            def mixing(j, carry):
                q = f * QUADS + j
                z = z1[b, pl.ds(q * GROUP, GROUP)].reshape(WIDE, 256)
                act = (gelu_fwd(z * a1 + b1) * (pad_mask * alive)).astype(BF16)
                a1s[b, pl.ds(q * GROUP, GROUP)] = act.reshape(GROUP, WP, 256)
                m = dot(act, mix[b])
                z2[b, f + 1, pl.ds(1 + j * GROUP, GROUP)] = m.reshape(GROUP, WP, 256)
                if f in (0, frames - 1):
                    halo_send[b, 0 if f == 0 else 1, pl.ds(j * GROUP, GROUP)] = m.astype(BF16).reshape(GROUP, WP, 256)
                return (carry[0] + fold(m), carry[1] + fold(m * m))

            carry = lax.fori_loop(0, QUADS, mixing, carry)

            if f == 0:

                @pl.when(lane > 0)
                def _():
                    push(
                        halo_send.at[b, 0], halo_recv.at[b, 1], halo_ssem.at[b, 0], halo_rsem.at[b, 1], (net.row, lane - 1)
                    ).start()

            if f == frames - 1:

                @pl.when(lane < lanes - 1)
                def _():
                    push(
                        halo_send.at[b, 1], halo_recv.at[b, 0], halo_ssem.at[b, 1], halo_rsem.at[b, 0], (net.row, lane + 1)
                    ).start()

        def taps_of(b, half):
            cols = slice(128 * half, 128 * (half + 1))
            return [small[0, b * KVOL + k : b * KVOL + k + 1, cols] for k in range(KVOL)]

        def convolve(b, f, acc):
            alive = live(f)
            parts = []
            for half in range(2):
                lanes_here = slice(128 * half, 128 * (half + 1))
                kern = taps_of(b, half)
                pad = pad_mask[:WP, :128] * alive

                def two_rows(i, carry):
                    s0, s1, s2 = carry
                    h = 2 * i
                    part = [[None] * 3 for _ in range(2)]
                    for dt in range(3):
                        for rr in range(4):
                            v = z2[b, f + dt, h + rr, :, lanes_here]
                            for o in range(2):
                                dh = rr - o
                                if 0 <= dh < 3:
                                    for dw in range(3):
                                        term = kern[dt * 9 + dh * 3 + dw] * v
                                        part[o][dw] = term if part[o][dw] is None else part[o][dw] + term
                    for o in range(2):
                        p = part[o]
                        c = p[1] + pltpu.roll(p[0], 1, 0) + pltpu.roll(p[2], WP - 1, 0)
                        c = c * pad
                        conv[b, f * HH + h + o, :, lanes_here] = c
                        cls = jnp.where(h + o == 0, 0, jnp.where(h + o == HH - 1, 2, 1))
                        e = edge[b, f + 1, cls, :, lanes_here]
                        s0 = s0 + fold(c)
                        s1 = s1 + fold(c * c)
                        s2 = s2 + fold(c * e)
                    return (s0, s1, s2)

                parts.append(lax.fori_loop(0, HH // 2, two_rows, tuple(a[half] for a in acc)))
            return [[parts[0][k], parts[1][k]] for k in range(3)]

        acc = [[zero8(128), zero8(128)] for _ in range(3)]
        for f in range(1, frames - 1):
            acc = convolve(b, f, acc)

        def fill(side, frame, present):
            @pl.when(present)
            def _():
                push(
                    halo_send.at[b, 1 - side],
                    halo_recv.at[b, side],
                    halo_ssem.at[b, 1 - side],
                    halo_rsem.at[b, side],
                    (net.row, jnp.where(side == 0, jnp.maximum(lane - 1, 0), jnp.minimum(lane + 1, lanes - 1))),
                ).wait_recv()

                def widen(j, _):
                    z2[b, frame, pl.ds(1 + j * GROUP, GROUP)] = halo_recv[b, side, pl.ds(j * GROUP, GROUP)].astype(F32)
                    return 0

                lax.fori_loop(0, QUADS, widen, 0)

            @pl.when(jnp.logical_not(present))
            def _():
                def clear(j, _):
                    z2[b, frame, pl.ds(1 + j * GROUP, GROUP)] = jnp.zeros((GROUP, WP, 256), F32)
                    return 0

                lax.fori_loop(0, QUADS, clear, 0)

        fill(0, 0, lane > 0)
        acc = convolve(b, 0, acc)
        fill(1, frames + 1, lane < lanes - 1)
        acc = convolve(b, frames - 1, acc)
        joined = [jnp.concatenate([flat_sum(a[0]), flat_sum(a[1])], axis=1) for a in acc]
        total_start(3 * b + 1, rows_of(flat_sum(carry[0]), flat_sum(carry[1]), *joined))
        got = total_finish(3 * b + 1)
        sums_out[3 * b + 1] = got
        mean2, scale2, a2, b2 = affine(got[0:1], got[1:2], count, mid(b, 1, 0), mid(b, 1, 1))
        sc, scc, sce = got[2:3], got[3:4], got[4:5]
        se, see = global_edge[b]
        total3 = a2 * sc + b2 * se
        square3 = a2 * a2 * scc + 2.0 * a2 * b2 * sce + b2 * b2 * see
        mean3, scale3, a3, b3 = affine(total3, square3, count, mid(b, 2, 0), mid(b, 2, 1))

        pc, pe = a3 * a2, a3 * b2

        def expanding(q, carry):
            f = lax.div(q, QUADS)
            j = lax.rem(q, QUADS)
            alive = live(f)
            c = conv[b, pl.ds(q * GROUP, GROUP)].reshape(WIDE, 256)
            n3 = c * pc + (edge_rows(b, f, j) * pe + b3)
            act = squeeze(gelu_fwd(n3) * alive).astype(BF16)
            a3s[b, pl.ds(pl.multiple_of(q * FLAT, FLAT), FLAT)] = act
            z = dot(act, exp[b])
            return (carry[0] + fold(z), carry[1] + fold(z * z))

        carry = lax.fori_loop(0, frames * QUADS, expanding, (zero8(1024), zero8(1024)))
        total_start(3 * b + 2, rows_of(flat_sum(carry[0]), flat_sum(carry[1])))
        got = total_finish(3 * b + 2)
        sums_out[3 * b + 2] = got
        gain4, shift4 = norm_out[b, 0:1], norm_out[b, 1:2]
        mean4, scale4, a4, b4 = affine(
            wide_row(got, 0), wide_row(got, 4), jnp.concatenate([count] * 4, axis=1), gain4, shift4
        )

        source = x0 if b == 0 else x1

        def closing(q, carry):
            f = lax.div(q, QUADS)
            alive = live(f)
            rows = pl.ds(pl.multiple_of(q * FLAT, FLAT), FLAT)
            z = dot(a3s[b, rows], exp[b])
            pre = (z * a4 + b4) * alive + source[rows].astype(F32)
            result = (gelu_fwd(pre) * alive).astype(BF16)
            if b == 0:
                x1[rows] = result
                z = dot(result, red[1])
                z1[1, pl.ds(q * GROUP, GROUP)] = spread(z).reshape(GROUP, WP, 256)
                return (carry[0] + fold(z), carry[1] + fold(z * z))
            x0[rows] = result
            return carry

        carry = lax.fori_loop(0, frames * QUADS, closing, (zero8(), zero8()))
        if b == 0:
            total_start(3, rows_of(flat_sum(carry[0]), flat_sum(carry[1])))
            got = total_finish(3)
            sums_out[3] = got
            first_sums = (got[0:1], got[1:2])

    stores = []
    for k, (src, dst) in enumerate(((x0, out_hbm), (x1, x1_hbm), (z1, z1_out), (conv, c_out))):
        copy = pltpu.make_async_copy(src, dst, store_sem.at[k])
        copy.start()
        stores.append(copy)
    for b in range(BLOCKS):
        copy = pltpu.make_async_copy(z2.at[b, pl.ds(1, frames), pl.ds(1, HH)], z2_out.at[b], store_sem.at[4 + b])
        copy.start()
        stores.append(copy)
    for copy in stores:
        copy.wait()
    for copy in late:
        copy.wait_send()
    for b in range(BLOCKS):

        @pl.when(lane > 0)
        def _():
            push(
                halo_send.at[b, 0], halo_recv.at[b, 1], halo_ssem.at[b, 0], halo_rsem.at[b, 1], (net.row, jnp.maximum(lane - 1, 0))
            ).wait_send()

        @pl.when(lane < lanes - 1)
        def _():
            push(
                halo_send.at[b, 1], halo_recv.at[b, 0], halo_ssem.at[b, 1], halo_rsem.at[b, 0], (net.row, jnp.minimum(lane + 1, lanes - 1))
            ).wait_send()


def forward_call(groups, lanes, counts, tokens, reduce_loc, mix_loc, expand_loc, small_loc, norm_out):
    rows = tokens.shape[0]
    frames = rows // (HH * WW)
    whole = pl.BlockSpec(memory_space=pltpu.VMEM)
    hbm = pl.BlockSpec(memory_space=pl.ANY)
    dma = pltpu.SemaphoreType.DMA
    far = groups * (lanes // 2)
    lines = frames * HH
    return pl.pallas_call(
        functools.partial(forward_kernel, groups, lanes),
        out_shape=(
            jax.ShapeDtypeStruct((rows, 1024), BF16),
            jax.ShapeDtypeStruct((rows, 1024), BF16),
            jax.ShapeDtypeStruct((BLOCKS, lines, WP, 256), F32),
            jax.ShapeDtypeStruct((BLOCKS, frames, HH, WP, 256), F32),
            jax.ShapeDtypeStruct((BLOCKS, lines, WP, 256), F32),
            jax.ShapeDtypeStruct((6, 8, 256), F32),
        ),
        in_specs=[pl.BlockSpec(memory_space=pltpu.SMEM), hbm] + [whole] * 5,
        out_specs=[hbm] * 5 + [whole],
        scratch_shapes=[
            pltpu.VMEM((rows, 1024), BF16),
            pltpu.VMEM((rows, 1024), BF16),
            pltpu.VMEM((BLOCKS, 256, 1024), BF16),
            pltpu.VMEM((BLOCKS, 1024, 256), BF16),
            pltpu.VMEM((BLOCKS, 256, 256), BF16),
            pltpu.VMEM((BLOCKS, 256, 256), BF16),
            pltpu.VMEM((BLOCKS, 256, 1024), BF16),
            pltpu.VMEM((lanes,) + small_loc.shape, F32),
            pltpu.VMEM((BLOCKS, lines, WP, 256), F32),
            pltpu.VMEM((BLOCKS, lines, WP, 256), BF16),
            pltpu.VMEM((BLOCKS, frames + 2, HH + 2, WP, 256), F32),
            pltpu.VMEM((BLOCKS, lines, WP, 256), F32),
            pltpu.VMEM((BLOCKS, rows, 256), BF16),
            pltpu.VMEM((BLOCKS, frames + 2, 3, WP, 256), F32),
            pltpu.VMEM((BLOCKS, 2, HH, WP, 256), BF16),
            pltpu.VMEM((BLOCKS, 2, HH, WP, 256), BF16),
            pltpu.VMEM((6, 2, 8, 256), F32),
            pltpu.VMEM((6, far, 8, 256), F32),
            dma((6,)),
            dma((6,)),
            dma((6, far)),
            dma((6, far)),
            dma((7, lanes)),
            dma((7, lanes)),
            dma((BLOCKS, 2)),
            dma((BLOCKS, 2)),
            dma((frames,)),
            dma((6,)),
        ],
        compiler_params=pltpu.CompilerParams(
            collective_id=1, has_side_effects=True, vmem_limit_bytes=60 * 2**20
        ),
    )(counts, tokens, reduce_loc, mix_loc, expand_loc, small_loc, norm_out)


def gelu_soft(value):
    return jax.nn.gelu(value, approximate=True)


def gelu_back(value, grad):
    return jax.vjp(gelu_soft, value)[1](grad)[0]


def dot_over(left, right, over_left, over_right):
    return lax.dot_general(
        left, right, (((over_left,), (over_right,)), ((), ())), preferred_element_type=jnp.float32
    )


def sum_kernel(sizes, x_ref, o_ref, near, far, near_send, near_recv, far_send, far_recv):
    lanes, groups = sizes
    row = lax.axis_index("dp")
    lane = lax.axis_index("chan")
    barrier = pltpu.get_barrier_semaphore()
    near_peers = [(lax.rem(lane + o, lanes)) for o in range(1, lanes)]
    far_peers = [(lax.rem(row + o, groups)) for o in range(1, groups)]
    for peer in near_peers:
        pl.semaphore_signal(barrier, inc=1, device_id=(row, peer), device_id_type=MESH)
    for peer in far_peers:
        pl.semaphore_signal(barrier, inc=1, device_id=(peer, lane), device_id_type=MESH)
    pl.semaphore_wait(barrier, lanes + groups - 2)

    def stage(slots, send, recv, me, peers, place):
        copies = []
        for step, peer in enumerate(peers):
            copy = pltpu.make_async_remote_copy(
                src_ref=slots.at[me],
                dst_ref=slots.at[me],
                send_sem=send.at[step],
                recv_sem=recv.at[me],
                device_id=place(peer),
                device_id_type=MESH,
            )
            copy.start()
            copies.append(copy)
        for step, peer in enumerate(peers):
            pltpu.make_async_remote_copy(
                src_ref=slots.at[peer],
                dst_ref=slots.at[peer],
                send_sem=send.at[step],
                recv_sem=recv.at[peer],
                device_id=place(peer),
                device_id_type=MESH,
            ).wait_recv()
        for copy in copies:
            copy.wait_send()
        total = slots[0]
        for index in range(1, slots.shape[0]):
            total = total + slots[index]
        return total

    near[lane] = x_ref[...]
    far[row] = stage(near, near_send, near_recv, lane, near_peers, lambda p: (row, p))
    o_ref[...] = stage(far, far_send, far_recv, row, far_peers, lambda p: (p, lane))


def all_sum(sizes, rows):
    flat = jnp.concatenate([r.reshape(-1, 128) for r in rows], axis=0)
    pad = -flat.shape[0] % 8
    flat = jnp.pad(flat, ((0, pad), (0, 0)))
    lanes, groups = sizes
    shape = flat.shape
    total = pl.pallas_call(
        functools.partial(sum_kernel, sizes),
        out_shape=jax.ShapeDtypeStruct(shape, jnp.float32),
        in_specs=[pl.BlockSpec(memory_space=pltpu.VMEM)],
        out_specs=pl.BlockSpec(memory_space=pltpu.VMEM),
        scratch_shapes=[
            pltpu.VMEM((lanes,) + shape, jnp.float32),
            pltpu.VMEM((groups,) + shape, jnp.float32),
            pltpu.SemaphoreType.DMA((lanes,)),
            pltpu.SemaphoreType.DMA((lanes,)),
            pltpu.SemaphoreType.DMA((groups,)),
            pltpu.SemaphoreType.DMA((groups,)),
        ],
        compiler_params=pltpu.CompilerParams(collective_id=shape[0], has_side_effects=True),
    )(flat)
    out, at = [], 0
    for r in rows:
        n = r.size // 128
        out.append(total[at : at + n].reshape(r.shape))
        at += n
    return out


def halo(field, lanes):
    before = lax.ppermute(field[-1:], "chan", [(i, i + 1) for i in range(lanes - 1)])
    after = lax.ppermute(field[:1], "chan", [(i + 1, i) for i in range(lanes - 1)])
    return jnp.concatenate([before, field, after], axis=0)


def depthwise(deep, kern, frames):
    padded = jnp.pad(deep, ((0, 0), (1, 1), (1, 1), (0, 0)))
    total = 0.0
    for step in range(3):
        for row in range(3):
            for column in range(3):
                tap = kern[step * 9 + row * 3 + column]
                total = total + tap * padded[step : step + frames, row : row + HH, column : column + WW]
    return total


def kernel_grad(field, deep, frames):
    padded = jnp.pad(deep, ((0, 0), (1, 1), (1, 1), (0, 0)))
    taps = []
    for step in range(3):
        for row in range(3):
            for column in range(3):
                part = padded[2 - step : 2 - step + frames, 2 - row : 2 - row + HH, 2 - column : 2 - column + WW]
                taps.append(jnp.sum(field * part, axis=(0, 1, 2)))
    return jnp.stack(taps)


def descend(weight, moment, grad):
    moment_new = MOMENTUM * moment + grad + DECAY * weight
    return (weight - LEARN_RATE * moment_new, moment_new)


def column_sum(value):
    return jnp.sum(value, axis=0)


def affine_of(totals, squares, count, gain, shift):
    mean = totals / count
    var = squares / count - mean * mean
    scale = lax.rsqrt(var + EPS)
    return (mean, scale, gain * scale, shift - mean * gain * scale)


def shards(
    tokens,
    frame_counts,
    cotangent,
    w_reduce,
    w_mix,
    w_depth,
    w_expand,
    norm_mid,
    norm_out,
    moment_reduce,
    moment_mix,
    moment_depth,
    moment_expand,
    moment_mid,
    moment_out,
):
    row = lax.axis_index("dp")
    lane = lax.axis_index("chan")
    lanes = lax.axis_size("chan")
    sizes = (lanes, lax.axis_size("dp"))
    frames = tokens.shape[0] // (HH * WW)
    narrow = w_reduce.shape[2]
    gather = lambda v, axis: lax.all_gather(v, "chan", axis=axis, tiled=True)
    reduce_all = gather(w_reduce.astype(jnp.bfloat16), 2)
    mix_all = gather(w_mix.astype(jnp.bfloat16), 2)
    expand_all = gather(w_expand.astype(jnp.bfloat16), 1)
    depth_all = gather(w_depth, 2)
    mid_all = gather(norm_mid, 3)
    alive = (lane * frames - 1 + jnp.arange(frames + 2) < frame_counts[0]) & (
        lane * frames - 1 + jnp.arange(frames + 2) >= 0
    )
    alive = alive.astype(jnp.float32)
    mask = jnp.repeat(alive[1:-1], HH * WW)[:, None]
    wide = mix_all.shape[1]
    flat = lambda v: v.reshape(-1, wide)
    deepen = lambda v: v.reshape(-1, HH, WW, wide)

    small = jnp.concatenate([w_depth.reshape(-1, narrow), norm_mid.reshape(-1, narrow)], axis=0)
    small = jnp.pad(small, ((0, -small.shape[0] % 8), (0, 0)))
    small = lax.dynamic_update_slice(jnp.zeros((small.shape[0], mix_all.shape[1]), F32), small, (0, lane * narrow))
    hidden, x1, z1, z2, c, sums = forward_call(
        sizes[1],
        lanes,
        frame_counts,
        tokens,
        jnp.swapaxes(w_reduce, 1, 2).astype(BF16),
        jnp.swapaxes(w_mix, 1, 2).astype(BF16),
        w_expand.astype(BF16),
        small,
        norm_out,
    )
    unpad = lambda v: v.reshape(-1, HH, WP, wide)[:, :, :WW].reshape(-1, wide)
    count = sums[0, 2, 0]
    stored = []
    for b in range(BLOCKS):
        mid = mid_all[b]
        x = tokens if b == 0 else x1
        first, second, conv = unpad(z1[b]), unpad(z2[b]), unpad(c[b])
        got = sums[0] if b == 0 else sums[3]
        mean1, scale1, a1, b1 = affine_of(got[0], got[1], count, mid[0, 0], mid[0, 1])
        act1 = (mask * gelu_soft(first * a1 + b1)).astype(jnp.bfloat16)
        ones = jnp.broadcast_to(alive[:, None, None, None], (frames + 2, HH, WW, 1))
        edge = flat(depthwise(ones, depth_all[b], frames))
        t, q, sc, scc, sce = [sums[3 * b + 1, i] for i in range(5)]
        se, see = sums[0, 3 + 2 * b], sums[0, 4 + 2 * b]
        mean2, scale2, a2, b2 = affine_of(t, q, count, mid[1, 0], mid[1, 1])
        t3 = a2 * sc + b2 * se
        q3 = a2 * a2 * scc + 2.0 * a2 * b2 * sce + b2 * b2 * see
        mean3, scale3, a3, b3 = affine_of(t3, q3, count, mid[2, 0], mid[2, 1])
        third = a2 * conv + b2 * edge
        norm3 = third * a3 + b3
        act3 = (mask * gelu_soft(norm3)).astype(jnp.bfloat16)
        fourth = dot_over(act3, expand_all[b], 1, 0)
        t, q = sums[3 * b + 2, :4].reshape(-1), sums[3 * b + 2, 4:].reshape(-1)
        mean4, scale4, a4, b4 = affine_of(t, q, count, norm_out[b, 0], norm_out[b, 1])
        pre = mask * (fourth * a4 + b4) + x.astype(jnp.float32)
        stored.append(
            (x, first, act1, second, conv, edge, third, norm3, act3, fourth, pre)
            + ((mean1, scale1, a1, b1), (mean2, scale2, a2, b2), (mean3, scale3, a3, b3), (mean4, scale4, a4, b4))
            + ((sc, scc, sce, se, see),)
        )

    gradient = cotangent.astype(jnp.float32)
    collected = [None] * BLOCKS
    for b in reversed(range(BLOCKS)):
        (x, first, act1, second, conv, edge, third, norm3, act3, fourth, pre) = stored[b][:11]
        ((mean1, scale1, a1, b1), (mean2, scale2, a2, b2), (mean3, scale3, a3, b3), (mean4, scale4, a4, b4)) = stored[b][11:15]
        sc, scc, sce, se, see = stored[b][15]
        residual = gelu_back(pre, mask * gradient)
        unit4 = (fourth - mean4) * scale4
        shift4, gain4 = all_sum(sizes, [column_sum(residual), column_sum(residual * unit4)])
        fourth_grad = (mask * a4 * (residual - shift4 / count - unit4 * gain4 / count)).astype(jnp.bfloat16)
        grad_expand = dot_over(act3, fourth_grad, 0, 0)
        e3 = mask * gelu_back(norm3, dot_over(fourth_grad, expand_all[b], 1, 1))
        e3_sum, e3_conv, e3_edge = all_sum(sizes, [column_sum(e3), column_sum(e3 * conv), column_sum(e3 * edge)])
        shift3 = e3_sum
        gain3 = scale3 * (a2 * e3_conv + b2 * e3_edge - mean3 * e3_sum)
        r = -a3 * scale3 * gain3 / count
        q = -a3 * shift3 / count - r * mean3
        p = a3
        third_conv = a2 * scc + b2 * sce
        third_edge = a2 * sce + b2 * see
        d3_conv = p * e3_conv + q * sc + r * third_conv
        d3_edge = p * e3_edge + q * se + r * third_edge
        shift2 = d3_edge
        gain2 = scale2 * (d3_conv - mean2 * d3_edge)
        third_grad = mask * (p * e3 + q + r * third)
        deep = halo(deepen(third_grad), lanes)
        act2 = mask * (second * a2 + b2)
        grad_depth = kernel_grad(deepen(act2), deep, frames)
        act2_grad = flat(depthwise(deep, depth_all[b][::-1], frames))
        unit2 = (second - mean2) * scale2
        second_grad = (mask * a2 * (act2_grad - shift2 / count - unit2 * gain2 / count)).astype(jnp.bfloat16)
        grad_mix = dot_over(act1, second_grad, 0, 0)
        e1 = mask * gelu_back(first * a1 + b1, dot_over(second_grad, mix_all[b], 1, 1))
        unit1 = (first - mean1) * scale1
        shift1, gain1 = all_sum(sizes, [column_sum(e1), column_sum(e1 * unit1)])
        first_grad = (mask * a1 * (e1 - shift1 / count - unit1 * gain1 / count)).astype(jnp.bfloat16)
        grad_reduce = dot_over(x, first_grad, 0, 0)
        gradient = dot_over(first_grad, reduce_all[b], 1, 1) + residual
        grad_mid = jnp.stack(
            [jnp.stack([gain1, shift1]), jnp.stack([gain2, shift2]), jnp.stack([gain3, shift3])]
        )
        collected[b] = (grad_reduce, grad_mix, grad_depth, grad_expand, grad_mid, jnp.stack([gain4, shift4]))
    stacked = [jnp.stack([pieces[slot] for pieces in collected]) for slot in range(6)]
    scatter = lambda v, axis: lax.psum_scatter(v, "chan", scatter_dimension=axis, tiled=True)
    grad_reduce, grad_mix, grad_depth, grad_expand = lax.psum(
        (scatter(stacked[0], 2), scatter(stacked[1], 2), scatter(stacked[2], 2), scatter(stacked[3], 1)), "dp"
    )
    grad_mid = lax.dynamic_slice_in_dim(stacked[4], lane * narrow, narrow, 3)
    grad_out = stacked[5]
    grads = (grad_reduce, grad_mix, grad_depth, grad_expand, grad_mid, grad_out)
    params = (w_reduce, w_mix, w_depth, w_expand, norm_mid, norm_out)
    moments = (moment_reduce, moment_mix, moment_depth, moment_expand, moment_mid, moment_out)
    updated = [descend(w, m, g) for w, m, g in zip(params, moments, grads)]
    return (
        (hidden, gradient.astype(jnp.bfloat16)) + grads + tuple(u[0] for u in updated) + tuple(u[1] for u in updated)
    )


def solution(mesh):
    rows = P(("dp", "chan"), None)
    weights = (
        P(None, None, "chan"),
        P(None, None, "chan"),
        P(None, None, "chan"),
        P(None, "chan", None),
        P(None, None, None, "chan"),
        P(),
    )
    return jax.shard_map(
        shards,
        mesh=mesh,
        in_specs=(rows, P("dp"), rows) + weights + weights,
        out_specs=(rows, rows) + weights + weights + weights,
        check_vma=False,
    )
```

```python
import functools

import jax
import jax.numpy as jnp
from jax import lax
from jax.experimental import pallas as pl
from jax.experimental.pallas import tpu as pltpu
from jax.sharding import PartitionSpec as P

FRAMES = 12
HH = 28
WW = 28
WP = 32
KVOL = 27
BLOCKS = 2
GROUP = 4
QUADS = HH // GROUP
FLAT = GROUP * WW
WIDE = GROUP * WP

EPS = 1e-05
LEARN_RATE = 0.001
MOMENTUM = 0.9
DECAY = 0.0001
MESH = pl.DeviceIdType.MESH
F32 = jnp.float32
BF16 = jnp.bfloat16
ROOT = 0.7978845608028654
CUBE = 0.044715


def gelu_fwd(v):
    t = jnp.tanh(v * (ROOT + (ROOT * CUBE) * (v * v)))
    h = 0.5 * v
    return h * t + h


def gelu_slope(v):
    s = v * v
    t = jnp.tanh(v * (ROOT + (ROOT * CUBE) * s))
    return 0.5 * (1.0 + t) + (0.5 * v) * (1.0 - t * t) * (ROOT + (3.0 * ROOT * CUBE) * s)


def dot_rows(left, right):
    return lax.dot_general(left, right, (((0,), (0,)), ((), ())), preferred_element_type=F32)


def dot(left, right):
    return jnp.dot(left, right, preferred_element_type=F32)


def fold(v):
    return jnp.sum(v.reshape(v.shape[0] // 8, 8, v.shape[1]), axis=0)


def spread(v):
    gap = jnp.zeros((WP - WW, v.shape[1]), v.dtype)
    parts = []
    for h in range(GROUP):
        parts += [v[WW * h : WW * (h + 1)], gap]
    return jnp.concatenate(parts, axis=0)


def squeeze(v):
    return jnp.concatenate([v[WP * h : WP * h + WW] for h in range(GROUP)], axis=0)


def rows_of(*vectors):
    parts = []
    for v in vectors:
        parts += [v[:, 256 * i : 256 * (i + 1)] for i in range(v.shape[1] // 256)]
    if len(parts) < 8:
        parts.append(jnp.zeros((8 - len(parts), 256), F32))
    return jnp.concatenate(parts, axis=0)


def flat_sum(v):
    return jnp.sum(v, axis=0, keepdims=True)


def wide_row(v, first):
    return jnp.concatenate([v[first + i : first + i + 1] for i in range(4)], axis=1)


class Net:
    def __init__(self, groups, lanes):
        self.lanes = lanes
        self.low, self.high = stages(groups)
        self.row = lax.axis_index("dp")
        self.lane = lax.axis_index("chan")
        self.core = lax.rem(self.lane, 2)
        self.side = lax.div(self.lane, 2)
        self.half = lanes // 2
        self.row_low = lax.rem(self.row, self.low)
        self.row_high = lax.div(self.row, self.low)

    def near(self):
        return [(1 - self.core, (self.row, self.side * 2 + 1 - self.core))]

    def far(self):
        out = []
        for o in range(self.low):
            for p in range(self.half):
                if o or p:
                    row = lax.rem(self.row_low + o, self.low)
                    side = lax.rem(self.side + p, self.half)
                    out.append((row * self.half + side, (self.row_high * self.low + row, side * 2 + self.core)))
        return out

    def far_slot(self):
        return self.row_low * self.half + self.side

    def top(self):
        rows = [lax.rem(self.row_high + o, self.high) for o in range(1, self.high)]
        return [(row, (row * self.low + self.row_low, self.lane)) for row in rows]

    def chan_peers(self):
        lanes = [lax.rem(self.lane + o, self.lanes) for o in range(1, self.lanes)]
        return [(lane, (self.row, lane)) for lane in lanes]


def stages(groups):
    low = min(groups, 8)
    return low, groups // low


def push(src, dst, send, recv, device):
    copy = pltpu.make_async_remote_copy(
        src_ref=src, dst_ref=dst, send_sem=send, recv_sem=recv, device_id=device, device_id_type=MESH
    )
    return copy


def whole_kernel(
    groups,
    lanes,
    counts,
    tokens,
    cotangent,
    reduce_loc,
    mix_loc,
    expand_loc,
    small_loc,
    norm_out,
    out_hbm,
    gtok_hbm,
    gred_hbm,
    gexp_hbm,
    gmix_hbm,
    gdep_out,
    gmid_out,
    gout_out,
    x0,
    x1,
    yb,
    sb,
    red_t,
    exp,
    tbuf,
    mix_t,
    mix,
    small,
    z1,
    a1s,
    z2,
    dz,
    hz,
    conv,
    a3s,
    edge,
    pat,
    d2s,
    halo_send,
    halo_recv,
    gbig,
    gmix,
    near,
    far,
    top,
    near_send,
    near_recv,
    far_send,
    far_recv,
    top_send,
    top_recv,
    gather_send,
    gather_recv,
    halo_ssem,
    halo_rsem,
    load_sem,
    store_sem,
):
    net = Net(groups, lanes)
    lane = net.lane
    frames = tokens.shape[0] // (HH * WW)
    frame_rows = HH * WW
    last = frames - 1
    count_here = counts[0]
    xs = (x0, x1)

    def live(frame):
        position = lane * frames + frame
        return jnp.where((position >= 0) & (position < count_here), 1.0, 0.0)

    def frame_copy(src, dst, f, sem):
        rows = pl.ds(f * frame_rows, frame_rows)
        return pltpu.make_async_copy(src.at[rows], dst.at[rows], sem)

    loads = [frame_copy(tokens, x0, f, load_sem.at[f]) for f in range(frames)]
    cot_load = pltpu.make_async_copy(cotangent, sb, load_sem.at[frames])
    for copy in loads:
        copy.start()
    cot_load.start()

    barrier = pltpu.get_barrier_semaphore()
    friends = [d for peers in (net.near(), net.far(), net.top(), net.chan_peers()) for _, d in peers]
    for device in friends:
        pl.semaphore_signal(barrier, inc=1, device_id=device, device_id_type=MESH)
    pl.semaphore_wait(barrier, len(friends))

    own = net.lane
    share = red_t.shape[1] // lanes
    late = []

    def gather(slot, src, dst_of):
        for step, (_, device) in enumerate(net.chan_peers()):
            copy = push(src, dst_of(own), gather_send.at[slot, step], gather_recv.at[slot, own], device)
            copy.start()
            late.append(copy)
        dst_of(own)[...] = src[...]

    def gather_wait(slot, src, dst_of):
        for step, (peer, device) in enumerate(net.chan_peers()):
            push(src, dst_of(peer), gather_send.at[slot, step], gather_recv.at[slot, peer], device).wait_recv()

    def block_rows(ref, b):
        return lambda who: ref.at[b, pl.ds(pl.multiple_of(who * share, share), share)]

    plan = {
        ("red", 0): (0, reduce_loc.at[0], block_rows(red_t, 0)),
        ("mix", 0): (1, mix_loc.at[0], block_rows(mix_t, 0)),
        ("small", 0): (2, small_loc, lambda who: small.at[who]),
        ("exp", 0): (3, expand_loc.at[0], block_rows(exp, 0)),
        ("red", 1): (4, reduce_loc.at[1], block_rows(red_t, 1)),
        ("mix", 1): (5, mix_loc.at[1], block_rows(mix_t, 1)),
        ("exp", 1): (6, expand_loc.at[1], block_rows(exp, 1)),
    }
    for slot, src, dst_of in plan.values():
        gather(slot, src, dst_of)

    def total_start(i, value):
        near[i, net.core] = value
        for who, device in net.near():
            copy = push(near.at[i, net.core], near.at[i, net.core], near_send.at[i], near_recv.at[i], device)
            copy.start()
            late.append(copy)
            copy.wait_recv()
        far[i, net.far_slot()] = near[i, 0] + near[i, 1]
        for step, (who, device) in enumerate(net.far()):
            mine = far.at[i, net.far_slot()]
            copy = push(mine, mine, far_send.at[i, step], far_recv.at[i, net.far_slot()], device)
            copy.start()
            late.append(copy)

    def total_finish(i):
        for step, (who, device) in enumerate(net.far()):
            push(far.at[i, who], far.at[i, who], far_send.at[i, step], far_recv.at[i, who], device).wait_recv()
        total = far[i, 0]
        for j in range(1, net.low * net.half):
            total = total + far[i, j]
        if net.high > 1:
            mine = top.at[i, net.row_high]
            top[i, net.row_high] = total
            for step, (who, device) in enumerate(net.top()):
                copy = push(mine, mine, top_send.at[i, step], top_recv.at[i, net.row_high], device)
                copy.start()
                late.append(copy)
            for step, (who, device) in enumerate(net.top()):
                push(top.at[i, who], top.at[i, who], top_send.at[i, step], top_recv.at[i, who], device).wait_recv()
            total = top[i, 0]
            for j in range(1, net.high):
                total = total + top[i, j]
        return total

    def halo_copy(kind, slot, side):
        step = -1 if side == 0 else 1
        return push(
            halo_send.at[side],
            halo_recv.at[slot, 1 - side],
            halo_ssem.at[kind, side],
            halo_rsem.at[kind, 1 - side],
            (net.row, lane + step),
        )

    def sends_to(side):
        return lane > 0 if side == 0 else lane < lanes - 1

    def halo_start(kind, slot, side):
        @pl.when(sends_to(side))
        def _():
            halo_copy(kind, slot, side).start()

    def halo_sent(kind, slot, side):
        @pl.when(sends_to(side))
        def _():
            halo_copy(kind, slot, side).wait_send()

    def halo_wait(kind, slot, side):
        step = -1 if side == 0 else 1
        push(
            halo_send.at[1 - side],
            halo_recv.at[slot, side],
            halo_ssem.at[kind, 1 - side],
            halo_rsem.at[kind, side],
            (net.row, lane + step),
        ).wait_recv()

    column = lax.broadcasted_iota(jnp.int32, (WIDE, 256), 0) % WP
    pad_mask = (column < WW).astype(F32)

    def affine(total, square, count, gain, shift):
        mean = total / count
        var = square / count - mean * mean
        scale = lax.rsqrt(var + EPS)
        return mean, scale, gain * scale, shift - mean * (gain * scale)

    def back_affine(e_sum, ez_sum, count, norm):
        mean, scale, a, _ = norm
        gain_grad = scale * (ez_sum - mean * e_sum)
        slope = -a * scale * gain_grad / count
        bias = -a * e_sum / count - slope * mean
        return slope, bias, gain_grad, e_sum

    def zero8(n=256):
        return jnp.zeros((8, n), F32)

    blank = jnp.zeros((WP, 256), F32)
    for f in range(frames):
        for b in range(BLOCKS):
            z2[b, f, 0] = blank
            z2[b, f, HH + 1] = blank
        dz[f, 0] = blank
        dz[f, HH + 1] = blank
    for side in range(2):
        hz[side, 0] = blank
        hz[side, HH + 1] = blank

    gather_wait(*plan["red", 0])
    tbuf[...] = red_t[0].T

    carry = (zero8(), zero8())
    for f in range(frames):
        loads[f].wait()
        alive = live(f)

        def project(j, carry):
            q = f * QUADS + j
            x = x0[pl.ds(pl.multiple_of(q * FLAT, FLAT), FLAT)]
            z = dot(x, tbuf[...])
            z1[0, pl.ds(q * GROUP, GROUP)] = spread(z).reshape(GROUP, WP, 256)
            z = z * alive
            return (carry[0] + fold(z), carry[1] + fold(z * z))

        carry = lax.fori_loop(0, QUADS, project, carry)

    alive_all = sum(live(f) for f in range(frames)) * (HH * WW)
    here_count = jnp.full((1, 256), 1.0, F32) * alive_all
    total_start(0, rows_of(flat_sum(carry[0]), flat_sum(carry[1]), here_count))

    gather_wait(*plan["small", 0])
    taps = small[0]
    for who in range(1, lanes):
        taps = taps + small[who]
    small[0] = taps

    def mid(b, norm, which):
        r = BLOCKS * KVOL + (b * 3 + norm) * 2 + which
        return small[0, r : r + 1]

    edge_sums = []
    pattern_col = lax.broadcasted_iota(jnp.int32, (WP, 256), 0)
    for b in range(BLOCKS):
        taps_b = [[small[0, b * KVOL + dt * 9 + k : b * KVOL + dt * 9 + k + 1] for k in range(9)] for dt in range(3)]
        se = jnp.zeros((1, 256), F32)
        see = jnp.zeros((1, 256), F32)
        for f in range(-1, frames + 1):
            here = live(f)
            t = [
                here * (live(f - 1) * taps_b[0][k] + here * taps_b[1][k] + live(f + 1) * taps_b[2][k])
                for k in range(9)
            ]
            for cls in range(3):
                use = [dh for dh in range(3) if not (cls == 0 and dh == 0) and not (cls == 2 and dh == 2)]
                col = []
                for dw in range(3):
                    v = t[use[0] * 3 + dw]
                    for dh in use[1:]:
                        v = v + t[dh * 3 + dw]
                    col.append(v)
                inner = col[0] + col[1] + col[2]
                left, right = col[1] + col[2], col[0] + col[1]
                edge[b, f + 1, cls] = jnp.where(
                    pattern_col == 0,
                    left,
                    jnp.where(pattern_col == WW - 1, right, jnp.where(pattern_col < WW - 1, inner, 0.0)),
                )
                if 0 <= f < frames:
                    times = 1.0 if cls != 1 else HH - 2.0
                    se = se + times * (left + right + (WW - 2.0) * inner)
                    see = see + times * (left * left + right * right + (WW - 2.0) * (inner * inner))
        edge_sums.append((se, see))

    for slot in (("mix", 0), ("exp", 0), ("red", 1), ("mix", 1), ("exp", 1)):
        gather_wait(*plan[slot])
    for b in range(BLOCKS):
        mix[b] = mix_t[b].T
    tbuf[...] = red_t[1].T

    got = total_finish(0)
    count = got[2:3]
    count4 = jnp.concatenate([count] * 4, axis=1)
    first_sums = (got[0:1], got[1:2])

    def edge_rows(ref, j):
        top = jnp.where(j == 0, 0, 1)
        bottom = jnp.where(j == QUADS - 1, 2, 1)
        middle = ref[1]
        return jnp.concatenate([ref[top], middle, middle, ref[bottom]], axis=0)

    def row_class(h):
        return jnp.where(h == 0, 0, jnp.where(h == HH - 1, 2, 1))

    def convolve(local, f, b, flip, emit, acc):
        done = []
        for half in range(2):
            cols = slice(128 * half, 128 * (half + 1))
            kern = [small[0, b * KVOL + k : b * KVOL + k + 1, cols] for k in range(KVOL)]
            if flip:
                kern = kern[::-1]
            planes = []
            for dt in range(3):
                g = f + dt - 1
                planes.append(hz.at[0] if g < 0 else hz.at[1] if g > last else local.at[g])

            def two_rows(i, carry):
                h = 2 * i
                part = [[None] * 3 for _ in range(2)]
                for dt in range(3):
                    for rr in range(4):
                        v = planes[dt][h + rr, :, cols]
                        for o in range(2):
                            dh = rr - o
                            if 0 <= dh < 3:
                                for dw in range(3):
                                    term = kern[dt * 9 + dh * 3 + dw] * v
                                    part[o][dw] = term if part[o][dw] is None else part[o][dw] + term
                for o in range(2):
                    p = part[o]
                    c = p[1] + pltpu.roll(p[0], 1, 0) + pltpu.roll(p[2], WP - 1, 0)
                    carry = emit(h + o, half, cols, c, carry)
                return carry

            done.append(lax.fori_loop(0, HH // 2, two_rows, tuple(a[half] for a in acc)))
        return [[done[0][k], done[1][k]] for k in range(len(acc))]

    order = (0, last) + tuple(range(1, last))
    norms = []
    mid_grads = {}
    out_grads = {}

    def open_block(b, q, f, rows):
        z = dot(a3s[b, rows], exp[b])
        a4, b4 = norms[b][3][2], norms[b][3][3]
        return z, (z * a4 + b4) * live(f) + xs[b][rows].astype(F32)

    out_store = [frame_copy(yb, out_hbm, f, store_sem.at[f]) for f in range(frames)]

    for b in range(BLOCKS):
        norm1 = affine(first_sums[0], first_sums[1], count, mid(b, 0, 0), mid(b, 0, 1))
        _, _, a1, b1 = norm1
        carry = (zero8(), zero8())
        if b > 0:
            for side in range(2):
                halo_sent(2 * (b - 1) + 1, 2 + b - 1, side)
        for f in order:
            alive = live(f)

            def mixing(j, carry):
                q = f * QUADS + j
                z = z1[b, pl.ds(q * GROUP, GROUP)].reshape(WIDE, 256)
                act = (gelu_fwd(z * a1 + b1) * (pad_mask * alive)).astype(BF16)
                m = dot(act, mix[b])
                z2[b, f, pl.ds(1 + j * GROUP, GROUP)] = m.reshape(GROUP, WP, 256)
                if f in (0, last):
                    halo_send[0 if f == 0 else 1, pl.ds(j * GROUP, GROUP)] = m.astype(BF16).reshape(GROUP, WP, 256)
                return (carry[0] + fold(m), carry[1] + fold(m * m))

            carry = lax.fori_loop(0, QUADS, mixing, carry)
            if f in (0, last):
                halo_start(2 * b, b, 0 if f == 0 else 1)

        def emit_conv(f):
            pad = pad_mask[:WP, :128] * live(f)

            def emit(row, half, cols, c, carry):
                c = c * pad
                conv[b, f * HH + row, :, cols] = c
                if f in (0, last):
                    halo_send[0 if f == 0 else 1, row, :, cols] = c.astype(BF16)
                e = edge[b, f + 1, row_class(row), :, cols]
                s0, s1, s2 = carry
                return (s0 + fold(c), s1 + fold(c * c), s2 + fold(c * e))

            return emit

        def fill(side):
            present = lane > 0 if side == 0 else lane < lanes - 1

            @pl.when(present)
            def _():
                halo_wait(2 * b, b, side)

                def widen(j, _):
                    hz[side, pl.ds(1 + j * GROUP, GROUP)] = halo_recv[b, side, pl.ds(j * GROUP, GROUP)].astype(F32)
                    return 0

                lax.fori_loop(0, QUADS, widen, 0)

            @pl.when(jnp.logical_not(present))
            def _():
                def clear(j, _):
                    hz[side, pl.ds(1 + j * GROUP, GROUP)] = jnp.zeros((GROUP, WP, 256), F32)
                    return 0

                lax.fori_loop(0, QUADS, clear, 0)

        acc = [[zero8(128), zero8(128)] for _ in range(3)]
        for f in range(1, last):
            acc = convolve(z2.at[b], f, b, False, emit_conv(f), acc)
        for side in range(2):
            fill(side)
            halo_sent(2 * b, b, side)
            f = 0 if side == 0 else last
            acc = convolve(z2.at[b], f, b, False, emit_conv(f), acc)
            halo_start(2 * b + 1, 2 + b, side)
        joined = [jnp.concatenate([flat_sum(a[0]), flat_sum(a[1])], axis=1) for a in acc]
        total_start(3 * b + 1, rows_of(flat_sum(carry[0]), flat_sum(carry[1]), *joined, *edge_sums[b]))
        got = total_finish(3 * b + 1)
        norm2 = affine(got[0:1], got[1:2], count, mid(b, 1, 0), mid(b, 1, 1))
        _, _, a2, b2 = norm2
        sc, scc, sce, se, see = [got[i : i + 1] for i in range(2, 7)]
        total3 = a2 * sc + b2 * se
        square3 = a2 * a2 * scc + 2.0 * a2 * b2 * sce + b2 * b2 * see
        norm3 = affine(total3, square3, count, mid(b, 2, 0), mid(b, 2, 1))
        _, _, a3, b3 = norm3

        def expanding(q, carry):
            f = lax.div(q, QUADS)
            j = lax.rem(q, QUADS)
            c = conv[b, pl.ds(q * GROUP, GROUP)].reshape(WIDE, 256)
            n3 = c * (a3 * a2) + (edge_rows(edge.at[b, f + 1], j) * (a3 * b2) + b3)
            act = squeeze(gelu_fwd(n3) * live(f)).astype(BF16)
            a3s[b, pl.ds(pl.multiple_of(q * FLAT, FLAT), FLAT)] = act
            z = dot(act, exp[b])
            return (carry[0] + fold(z), carry[1] + fold(z * z))

        carry = lax.fori_loop(0, frames * QUADS, expanding, (zero8(1024), zero8(1024)))
        total_start(3 * b + 2, rows_of(flat_sum(carry[0]), flat_sum(carry[1])))
        got = total_finish(3 * b + 2)
        norm4 = affine(wide_row(got, 0), wide_row(got, 4), count4, norm_out[b, 0:1], norm_out[b, 1:2])
        norms.append((norm1, norm2, norm3, norm4, (sc, scc, sce, se, see)))

        if b == 0:
            def closing(q, carry):
                f = lax.div(q, QUADS)
                rows = pl.ds(pl.multiple_of(q * FLAT, FLAT), FLAT)
                _, pre = open_block(0, q, f, rows)
                result = (gelu_fwd(pre) * live(f)).astype(BF16)
                x1[rows] = result
                z = dot(result, tbuf[...])
                z1[1, pl.ds(q * GROUP, GROUP)] = spread(z).reshape(GROUP, WP, 256)
                return (carry[0] + fold(z), carry[1] + fold(z * z))

            carry = lax.fori_loop(0, frames * QUADS, closing, (zero8(), zero8()))
            total_start(3, rows_of(flat_sum(carry[0]), flat_sum(carry[1])))
            tbuf[...] = exp[1].T
            got = total_finish(3)
            first_sums = (got[0:1], got[1:2])

    cot_load.wait()

    def ending(q, carry):
        f = lax.div(q, QUADS)
        alive = live(f)
        rows = pl.ds(pl.multiple_of(q * FLAT, FLAT), FLAT)
        z, pre = open_block(1, q, f, rows)
        yb[rows] = (gelu_fwd(pre) * alive).astype(BF16)
        s = gelu_slope(pre) * (sb[rows].astype(F32) * alive)
        sb[rows] = s.astype(BF16)
        return (carry[0] + fold(s), carry[1] + fold(s * z))

    carry = lax.fori_loop(0, frames * QUADS, ending, (zero8(1024), zero8(1024)))
    total_start(6, rows_of(flat_sum(carry[0]), flat_sum(carry[1])))
    for copy in out_store:
        copy.start()

    grad_stores = []
    for b in reversed(range(BLOCKS)):
        turn = BLOCKS - 1 - b
        base = 6 + 3 * turn
        norm1, norm2, norm3, norm4, (sc, scc, sce, se, see) = norms[b]
        _, _, a1, b1 = norm1
        mean2, scale2, a2, b2 = norm2
        mean3, scale3, a3, b3 = norm3
        a4 = norm4[2]

        got = total_finish(base)
        slope4, bias4, gain_grad, shift_grad = back_affine(wide_row(got, 0), wide_row(got, 4), count4, norm4)
        out_grads[b] = (gain_grad, shift_grad)
        if turn == 0:
            for copy in out_store:
                copy.wait()
        for side in range(2):
            if turn == 0:
                halo_sent(2 * (BLOCKS - 1) + 1, 2 + BLOCKS - 1, side)
            else:
                halo_sent(2 * BLOCKS + turn - 1, b + 1, side)

        kind = 2 * BLOCKS + turn
        acc = (zero8(), zero8(), zero8())
        for f in order:
            alive = live(f)

            def shrinking(j, acc):
                q = f * QUADS + j
                rows = pl.ds(pl.multiple_of(q * FLAT, FLAT), FLAT)
                z = dot(a3s[b, rows], exp[b])
                d4 = (sb[rows].astype(F32) * a4 + (z * slope4 + bias4) * alive).astype(BF16)
                yb[rows] = d4
                c = conv[b, pl.ds(q * GROUP, GROUP)].reshape(WIDE, 256)
                e = edge_rows(edge.at[b, f + 1], j)
                n3 = c * (a3 * a2) + (e * (a3 * b2) + b3)
                e3 = spread(dot(d4, tbuf[...])) * gelu_slope(n3)
                dz[f, pl.ds(1 + j * GROUP, GROUP)] = e3.reshape(GROUP, WP, 256)
                if f in (0, last):
                    halo_send[0 if f == 0 else 1, pl.ds(j * GROUP, GROUP)] = e3.astype(BF16).reshape(GROUP, WP, 256)
                return (acc[0] + fold(e3), acc[1] + fold(e3 * c), acc[2] + fold(e3 * e))

            acc = lax.fori_loop(0, QUADS, shrinking, acc)
            if f in (0, last):
                halo_start(kind, b, 0 if f == 0 else 1)
        total_start(base + 1, rows_of(*[flat_sum(a) for a in acc]))

        if turn > 0:
            for copy in grad_stores:
                copy.wait()

        def expand_grad(i, _):
            cols = pl.ds(pl.multiple_of(i * 256, 256), 256)
            gbig[0, :, cols] = dot_rows(a3s[b], yb[:, cols])
            return 0

        lax.fori_loop(0, 4, expand_grad, 0)
        if b > 0:
            tbuf[...] = exp[b - 1].T

        got = total_finish(base + 1)
        e3_sum, e3_conv, e3_edge = got[0:1], got[1:2], got[2:3]
        e3_third = a2 * e3_conv + b2 * e3_edge
        slope3, bias3, gain3, shift3 = back_affine(e3_sum, e3_third, count, norm3)
        third_conv = a2 * scc + b2 * sce
        third_edge = a2 * sce + b2 * see
        d3_conv = a3 * e3_conv + bias3 * sc + slope3 * third_conv
        d3_edge = a3 * e3_edge + bias3 * se + slope3 * third_edge
        slope2, bias2, gain2, shift2 = back_affine(d3_edge, d3_conv, count, norm2)

        for f in range(-1, frames + 1):
            live_pad = pad_mask[:WP] * live(f)
            for cls in range(3):
                pat[f + 1, cls] = bias3 * live_pad + (slope3 * b2) * edge[b, f + 1, cls]
        slope_c = slope3 * a2

        def to_d3(q, _):
            f = lax.div(q, QUADS)
            j = lax.rem(q, QUADS)
            rows = pl.ds(1 + j * GROUP, GROUP)
            c = conv[b, pl.ds(q * GROUP, GROUP)].reshape(WIDE, 256)
            e3 = dz[f, rows].reshape(WIDE, 256)
            d3 = e3 * a3 + c * slope_c + edge_rows(pat.at[f + 1], j)
            dz[f, rows] = d3.reshape(GROUP, WP, 256)
            return 0

        lax.fori_loop(0, frames * QUADS, to_d3, 0)

        def fill_back(side):
            present = lane > 0 if side == 0 else lane < lanes - 1
            f = -1 if side == 0 else frames

            @pl.when(present)
            def _():
                halo_wait(2 * b + 1, 2 + b, side)
                halo_wait(kind, b, side)

                def widen(j, _):
                    rows = pl.ds(j * GROUP, GROUP)
                    c = halo_recv[2 + b, side, rows].astype(F32).reshape(WIDE, 256)
                    e3 = halo_recv[b, side, rows].astype(F32).reshape(WIDE, 256)
                    d3 = e3 * a3 + c * slope_c + edge_rows(pat.at[f + 1], j)
                    hz[side, pl.ds(1 + j * GROUP, GROUP)] = d3.reshape(GROUP, WP, 256)
                    return 0

                lax.fori_loop(0, QUADS, widen, 0)

            @pl.when(jnp.logical_not(present))
            def _():
                def clear(j, _):
                    hz[side, pl.ds(1 + j * GROUP, GROUP)] = jnp.zeros((GROUP, WP, 256), F32)
                    return 0

                lax.fori_loop(0, QUADS, clear, 0)

        for side in range(2):
            fill_back(side)

        def emit_back(f):
            pad = pad_mask[:WP, :128] * live(f)

            def emit(row, half, cols, e2, carry):
                z = z2[b, f, row + 1, :, cols]
                d2 = (e2 * a2[:, cols] + (z * slope2[:, cols] + bias2[:, cols])) * pad
                d2s[f * HH + row, :, cols] = d2.astype(BF16)
                return carry

            return emit

        for f in range(frames):
            convolve(dz, f, b, True, emit_back(f), [])

        def unmixing(q, acc):
            rows = pl.ds(q * GROUP, GROUP)
            e = dot(d2s[rows].reshape(WIDE, 256), mix_t[b])
            z = z1[b, rows].reshape(WIDE, 256)
            n1 = z * a1 + b1
            a1s[rows] = (gelu_fwd(n1) * (pad_mask * live(lax.div(q, QUADS)))).astype(BF16).reshape(GROUP, WP, 256)
            e1 = e * gelu_slope(n1)
            conv[b, rows] = e1.reshape(GROUP, WP, 256)
            return (acc[0] + fold(e1), acc[1] + fold(e1 * z))

        acc = lax.fori_loop(0, frames * QUADS, unmixing, (zero8(), zero8()))
        total_start(base + 2, rows_of(*[flat_sum(a) for a in acc]))

        for half in range(2):
            cols = slice(128 * half, 128 * (half + 1))
            taps_grad = tuple(zero8(128) for _ in range(KVOL))
            for f in range(frames):
                planes = []
                for dt in range(3):
                    g = f - (dt - 1)
                    planes.append(hz.at[0] if g < 0 else hz.at[1] if g > last else dz.at[g])
                shift_rows = b2[:, cols] * (pad_mask[:WP, :128] * live(f))

                def tap_rows(h, taps_grad):
                    a = z2[b, f, h + 1, :, cols] * a2[:, cols] + shift_rows
                    moved = [pltpu.roll(a, 1, 0), a, pltpu.roll(a, WP - 1, 0)]
                    new = list(taps_grad)
                    for dt in range(3):
                        for dh in range(3):
                            d = planes[dt][h + 1 - (dh - 1), :, cols]
                            for dw in range(3):
                                k = dt * 9 + dh * 3 + dw
                                new[k] = new[k] + fold(d * moved[dw])
                    return tuple(new)

                taps_grad = lax.fori_loop(0, HH, tap_rows, taps_grad)
            for k in range(KVOL):
                gdep_out[b, k : k + 1, cols] = flat_sum(taps_grad[k])
        gmix[b] = dot_rows(d2s[...].reshape(frames * HH * WP, 256), a1s[...].reshape(frames * HH * WP, 256))

        got = total_finish(base + 2)
        slope1, bias1, gain1, shift1 = back_affine(got[0:1], got[1:2], count, norm1)
        mid_grads[b] = ((gain1, shift1), (gain2, shift2), (gain3, shift3))

        def input_grad(q):
            f = lax.div(q, QUADS)
            rows = pl.ds(pl.multiple_of(q * FLAT, FLAT), FLAT)
            wide = pl.ds(q * GROUP, GROUP)
            e1 = conv[b, wide].reshape(WIDE, 256)
            z = z1[b, wide].reshape(WIDE, 256)
            d1 = squeeze((e1 * a1 + (z * slope1 + bias1)) * live(f)).astype(BF16)
            a3s[b, rows] = d1
            return f, rows, dot(d1, red_t[b]) + sb[rows].astype(F32)

        if b > 0:

            def passing(q, carry):
                f, rows, g = input_grad(q)
                z, pre = open_block(b - 1, q, f, rows)
                s = gelu_slope(pre) * (g * live(f))
                sb[rows] = s.astype(BF16)
                return (carry[0] + fold(s), carry[1] + fold(s * z))

            carry = lax.fori_loop(0, frames * QUADS, passing, (zero8(1024), zero8(1024)))
            total_start(base + 3, rows_of(flat_sum(carry[0]), flat_sum(carry[1])))
        else:

            def final(q, _):
                f, rows, g = input_grad(q)
                yb[rows] = g.astype(BF16)
                return 0

            lax.fori_loop(0, frames * QUADS, final, 0)
            gtok_store = [frame_copy(yb, gtok_hbm, f, store_sem.at[f]) for f in range(frames)]
            for copy in gtok_store:
                copy.start()

        def reduce_grad(i, _):
            cols = pl.ds(pl.multiple_of(i * 256, 256), 256)
            gbig[1, :, cols] = dot_rows(a3s[b], xs[b][:, cols])
            return 0

        lax.fori_loop(0, 4, reduce_grad, 0)
        grad_stores = [
            pltpu.make_async_copy(gbig.at[0], gexp_hbm.at[b], store_sem.at[frames]),
            pltpu.make_async_copy(gbig.at[1], gred_hbm.at[b], store_sem.at[frames + 1]),
            pltpu.make_async_copy(gmix.at[b], gmix_hbm.at[b], store_sem.at[frames + 2]),
        ]
        for copy in grad_stores:
            copy.start()

    for b in range(BLOCKS):
        for k in range(3):
            for w in range(2):
                r = (b * 3 + k) * 2 + w
                gmid_out[r : r + 1] = mid_grads[b][k][w]
        for w in range(2):
            gout_out[2 * b + w : 2 * b + w + 1] = out_grads[b][w]

    for copy in grad_stores + gtok_store:
        copy.wait()
    for copy in late:
        copy.wait_send()
    for side in range(2):
        halo_sent(2 * BLOCKS + BLOCKS - 1, 0, side)


def whole_call(groups, lanes, counts, tokens, cotangent, reduce_loc, mix_loc, expand_loc, small_loc, norm_out):
    rows = tokens.shape[0]
    frames = rows // (HH * WW)
    whole = pl.BlockSpec(memory_space=pltpu.VMEM)
    hbm = pl.BlockSpec(memory_space=pl.ANY)
    dma = pltpu.SemaphoreType.DMA
    low, high = stages(groups)
    far = low * (lanes // 2)
    lines = frames * HH
    sums = 6 * BLOCKS
    kinds = 3 * BLOCKS
    shape = jax.ShapeDtypeStruct
    return pl.pallas_call(
        functools.partial(whole_kernel, groups, lanes),
        out_shape=(
            shape((rows, 1024), BF16),
            shape((rows, 1024), BF16),
            shape((BLOCKS, 256, 1024), F32),
            shape((BLOCKS, 256, 1024), F32),
            shape((BLOCKS, 256, 256), F32),
            shape((BLOCKS, KVOL, 256), F32),
            shape((BLOCKS * 6, 256), F32),
            shape((BLOCKS * 2, 1024), F32),
        ),
        in_specs=[pl.BlockSpec(memory_space=pltpu.SMEM), hbm, hbm] + [whole] * 5,
        out_specs=[hbm] * 5 + [whole] * 3,
        scratch_shapes=[
            pltpu.VMEM((rows, 1024), BF16),
            pltpu.VMEM((rows, 1024), BF16),
            pltpu.VMEM((rows, 1024), BF16),
            pltpu.VMEM((rows, 1024), BF16),
            pltpu.VMEM((BLOCKS, 256, 1024), BF16),
            pltpu.VMEM((BLOCKS, 256, 1024), BF16),
            pltpu.VMEM((1024, 256), BF16),
            pltpu.VMEM((BLOCKS, 256, 256), BF16),
            pltpu.VMEM((BLOCKS, 256, 256), BF16),
            pltpu.VMEM((lanes,) + small_loc.shape, F32),
            pltpu.VMEM((BLOCKS, lines, WP, 256), F32),
            pltpu.VMEM((lines, WP, 256), BF16),
            pltpu.VMEM((BLOCKS, frames, HH + 2, WP, 256), F32),
            pltpu.VMEM((frames, HH + 2, WP, 256), F32),
            pltpu.VMEM((2, HH + 2, WP, 256), F32),
            pltpu.VMEM((BLOCKS, lines, WP, 256), F32),
            pltpu.VMEM((BLOCKS, rows, 256), BF16),
            pltpu.VMEM((BLOCKS, frames + 2, 3, WP, 256), F32),
            pltpu.VMEM((frames + 2, 3, WP, 256), F32),
            pltpu.VMEM((lines, WP, 256), BF16),
            pltpu.VMEM((2, HH, WP, 256), BF16),
            pltpu.VMEM((2 * BLOCKS, 2, HH, WP, 256), BF16),
            pltpu.VMEM((2, 256, 1024), F32),
            pltpu.VMEM((BLOCKS, 256, 256), F32),
            pltpu.VMEM((sums, 2, 8, 256), F32),
            pltpu.VMEM((sums, far, 8, 256), F32),
            pltpu.VMEM((sums, high, 8, 256), F32),
            dma((sums,)),
            dma((sums,)),
            dma((sums, far)),
            dma((sums, far)),
            dma((sums, high)),
            dma((sums, high)),
            dma((7, lanes)),
            dma((7, lanes)),
            dma((kinds, 2)),
            dma((kinds, 2)),
            dma((frames + 1,)),
            dma((frames + 3,)),
        ],
        compiler_params=pltpu.CompilerParams(
            collective_id=1, has_side_effects=True, vmem_limit_bytes=63 * 2**20
        ),
    )(counts, tokens, cotangent, reduce_loc, mix_loc, expand_loc, small_loc, norm_out)


def descend(weight, moment, grad):
    moment_new = MOMENTUM * moment + grad + DECAY * weight
    return (weight - LEARN_RATE * moment_new, moment_new)


def shards(
    tokens,
    frame_counts,
    cotangent,
    w_reduce,
    w_mix,
    w_depth,
    w_expand,
    norm_mid,
    norm_out,
    moment_reduce,
    moment_mix,
    moment_depth,
    moment_expand,
    moment_mid,
    moment_out,
):
    lane = lax.axis_index("chan")
    lanes = lax.axis_size("chan")
    narrow = w_reduce.shape[2]
    small = jnp.concatenate([w_depth.reshape(-1, narrow), norm_mid.reshape(-1, narrow)], axis=0)
    small = jnp.pad(small, ((0, -small.shape[0] % 8), (0, 0)))
    small = lax.dynamic_update_slice(jnp.zeros((small.shape[0], narrow * lanes), F32), small, (0, lane * narrow))
    output, grad_tokens, gred, gexp, gmix, gdep, gmid, gout = whole_call(
        lax.axis_size("dp"),
        lanes,
        frame_counts,
        tokens,
        cotangent,
        jnp.swapaxes(w_reduce, 1, 2).astype(BF16),
        jnp.swapaxes(w_mix, 1, 2).astype(BF16),
        w_expand.astype(BF16),
        small,
        norm_out,
    )
    scatter = lambda v, axis: lax.psum_scatter(v, "chan", scatter_dimension=axis, tiled=True)
    gred, gmix, gdep, gexp = lax.psum((scatter(gred, 1), scatter(gmix, 1), scatter(gdep, 2), scatter(gexp, 1)), "dp")
    grads = (
        jnp.swapaxes(gred, 1, 2),
        jnp.swapaxes(gmix, 1, 2),
        gdep,
        gexp,
        lax.dynamic_slice_in_dim(gmid.reshape(BLOCKS, 3, 2, -1), lane * narrow, narrow, 3),
        gout.reshape(BLOCKS, 2, -1),
    )
    params = (w_reduce, w_mix, w_depth, w_expand, norm_mid, norm_out)
    moments = (moment_reduce, moment_mix, moment_depth, moment_expand, moment_mid, moment_out)
    updated = [descend(w, m, g) for w, m, g in zip(params, moments, grads)]
    return (output, grad_tokens) + grads + tuple(u[0] for u in updated) + tuple(u[1] for u in updated)


def solution(mesh):
    rows = P(("dp", "chan"), None)
    weights = (
        P(None, None, "chan"),
        P(None, None, "chan"),
        P(None, None, "chan"),
        P(None, "chan", None),
        P(None, None, None, "chan"),
        P(),
    )
    return jax.shard_map(
        shards,
        mesh=mesh,
        in_specs=(rows, P("dp"), rows) + weights + weights,
        out_specs=(rows, rows) + weights + weights + weights,
        check_vma=False,
    )
```

```python
import functools

import jax
import jax.numpy as jnp
from jax import lax
from jax.experimental import pallas as pl
from jax.experimental.pallas import tpu as pltpu
from jax.sharding import PartitionSpec as P

FRAMES = 12
HH = 28
WW = 28
WP = 32
KVOL = 27
BLOCKS = 2
GROUP = 4
QUADS = HH // GROUP
FLAT = GROUP * WW
WIDE = GROUP * WP
PIECES = 8

EPS = 1e-05
LEARN_RATE = 0.001
MOMENTUM = 0.9
DECAY = 0.0001
MESH = pl.DeviceIdType.MESH
F32 = jnp.float32
BF16 = jnp.bfloat16
ROOT = 0.7978845608028654
CUBE = 0.044715


def gelu_fwd(v):
    t = jnp.tanh(v * (ROOT + (ROOT * CUBE) * (v * v)))
    h = 0.5 * v
    return h * t + h


def gelu_slope(v):
    s = v * v
    t = jnp.tanh(v * (ROOT + (ROOT * CUBE) * s))
    return 0.5 * (1.0 + t) + (0.5 * v) * (1.0 - t * t) * (ROOT + (3.0 * ROOT * CUBE) * s)


def dot_rows(left, right):
    return lax.dot_general(left, right, (((0,), (0,)), ((), ())), preferred_element_type=F32)


def dot(left, right):
    return jnp.dot(left, right, preferred_element_type=F32)


def fold(v):
    return jnp.sum(v.reshape(v.shape[0] // 8, 8, v.shape[1]), axis=0)


def spread(v):
    gap = jnp.zeros((WP - WW, v.shape[1]), v.dtype)
    parts = []
    for h in range(GROUP):
        parts += [v[WW * h : WW * (h + 1)], gap]
    return jnp.concatenate(parts, axis=0)


def squeeze(v):
    return jnp.concatenate([v[WP * h : WP * h + WW] for h in range(GROUP)], axis=0)


def rows_of(*vectors):
    parts = []
    for v in vectors:
        parts += [v[:, 256 * i : 256 * (i + 1)] for i in range(v.shape[1] // 256)]
    if len(parts) < 8:
        parts.append(jnp.zeros((8 - len(parts), 256), F32))
    return jnp.concatenate(parts, axis=0)


def flat_sum(v):
    return jnp.sum(v, axis=0, keepdims=True)


def wide_row(v, first):
    return jnp.concatenate([v[first + i : first + i + 1] for i in range(4)], axis=1)


class Net:
    def __init__(self, groups, lanes):
        self.lanes = lanes
        self.low, self.high = stages(groups)
        self.row = lax.axis_index("dp")
        self.lane = lax.axis_index("chan")
        self.core = lax.rem(self.lane, 2)
        self.side = lax.div(self.lane, 2)
        self.half = lanes // 2
        self.row_low = lax.rem(self.row, self.low)
        self.row_high = lax.div(self.row, self.low)

    def near(self):
        return [(1 - self.core, (self.row, self.side * 2 + 1 - self.core))]

    def far(self):
        out = []
        for o in range(self.low):
            for p in range(self.half):
                if o or p:
                    row = lax.rem(self.row_low + o, self.low)
                    side = lax.rem(self.side + p, self.half)
                    out.append((row * self.half + side, (self.row_high * self.low + row, side * 2 + self.core)))
        return out

    def far_slot(self):
        return self.row_low * self.half + self.side

    def top(self):
        rows = [lax.rem(self.row_high + o, self.high) for o in range(1, self.high)]
        return [(row, (row * self.low + self.row_low, self.lane)) for row in rows]

    def chan_peers(self):
        lanes = [lax.rem(self.lane + o, self.lanes) for o in range(1, self.lanes)]
        return [(lane, (self.row, lane)) for lane in lanes]


def stages(groups):
    low = min(groups, 8)
    return low, groups // low


def push(src, dst, send, recv, device):
    copy = pltpu.make_async_remote_copy(
        src_ref=src, dst_ref=dst, send_sem=send, recv_sem=recv, device_id=device, device_id_type=MESH
    )
    return copy


def whole_kernel(
    groups,
    lanes,
    counts,
    tokens,
    cotangent,
    reduce_loc,
    mix_loc,
    expand_loc,
    small_loc,
    norm_out,
    out_hbm,
    gtok_hbm,
    grads_out,
    gmid_out,
    gout_out,
    x0,
    x1,
    yb,
    sb,
    red_t,
    exp,
    tbuf,
    mix_t,
    mix,
    small,
    z1,
    a1s,
    z2,
    dz,
    hz,
    conv,
    a3s,
    edge,
    pat,
    d2s,
    halo_send,
    halo_recv,
    grad_a,
    grad_ra,
    grad_b,
    grad_rb,
    grad_all,
    grad_top,
    near,
    far,
    top,
    near_send,
    near_recv,
    far_send,
    far_recv,
    top_send,
    top_recv,
    gather_send,
    gather_recv,
    halo_ssem,
    halo_rsem,
    load_sem,
    store_sem,
    grad_sa,
    grad_qa,
    grad_sb,
    grad_qb,
    grad_sc,
    grad_qc,
    grad_st,
    grad_qt,
):
    net = Net(groups, lanes)
    lane = net.lane
    frames = tokens.shape[0] // (HH * WW)
    frame_rows = HH * WW
    last = frames - 1
    count_here = counts[0]
    xs = (x0, x1)

    def live(frame):
        position = lane * frames + frame
        return jnp.where((position >= 0) & (position < count_here), 1.0, 0.0)

    def frame_copy(src, dst, f, sem):
        rows = pl.ds(f * frame_rows, frame_rows)
        return pltpu.make_async_copy(src.at[rows], dst.at[rows], sem)

    loads = [frame_copy(tokens, x0, f, load_sem.at[f]) for f in range(frames)]
    cot_load = pltpu.make_async_copy(cotangent, sb, load_sem.at[frames])
    for copy in loads:
        copy.start()
    cot_load.start()

    barrier = pltpu.get_barrier_semaphore()
    friends = [d for peers in (net.near(), net.far(), net.top(), net.chan_peers()) for _, d in peers]
    for device in friends:
        pl.semaphore_signal(barrier, inc=1, device_id=device, device_id_type=MESH)
    pl.semaphore_wait(barrier, len(friends))

    own = net.lane
    share = red_t.shape[1] // lanes
    late = []

    def gather(slot, src, dst_of):
        for step, (_, device) in enumerate(net.chan_peers()):
            copy = push(src, dst_of(own), gather_send.at[slot, step], gather_recv.at[slot, own], device)
            copy.start()
            late.append(copy)
        dst_of(own)[...] = src[...]

    def gather_wait(slot, src, dst_of):
        for step, (peer, device) in enumerate(net.chan_peers()):
            push(src, dst_of(peer), gather_send.at[slot, step], gather_recv.at[slot, peer], device).wait_recv()

    def block_rows(ref, b):
        return lambda who: ref.at[b, pl.ds(pl.multiple_of(who * share, share), share)]

    plan = {
        ("red", 0): (0, reduce_loc.at[0], block_rows(red_t, 0)),
        ("mix", 0): (1, mix_loc.at[0], block_rows(mix_t, 0)),
        ("small", 0): (2, small_loc, lambda who: small.at[who]),
        ("exp", 0): (3, expand_loc.at[0], block_rows(exp, 0)),
        ("red", 1): (4, reduce_loc.at[1], block_rows(red_t, 1)),
        ("mix", 1): (5, mix_loc.at[1], block_rows(mix_t, 1)),
        ("exp", 1): (6, expand_loc.at[1], block_rows(exp, 1)),
    }
    for slot, src, dst_of in plan.values():
        gather(slot, src, dst_of)

    def total_start(i, value):
        near[i, net.core] = value
        for who, device in net.near():
            copy = push(near.at[i, net.core], near.at[i, net.core], near_send.at[i], near_recv.at[i], device)
            copy.start()
            late.append(copy)
            copy.wait_recv()
        far[i, net.far_slot()] = near[i, 0] + near[i, 1]
        for step, (who, device) in enumerate(net.far()):
            mine = far.at[i, net.far_slot()]
            copy = push(mine, mine, far_send.at[i, step], far_recv.at[i, net.far_slot()], device)
            copy.start()
            late.append(copy)

    def total_finish(i):
        for step, (who, device) in enumerate(net.far()):
            push(far.at[i, who], far.at[i, who], far_send.at[i, step], far_recv.at[i, who], device).wait_recv()
        total = far[i, 0]
        for j in range(1, net.low * net.half):
            total = total + far[i, j]
        if net.high > 1:
            mine = top.at[i, net.row_high]
            top[i, net.row_high] = total
            for step, (who, device) in enumerate(net.top()):
                copy = push(mine, mine, top_send.at[i, step], top_recv.at[i, net.row_high], device)
                copy.start()
                late.append(copy)
            for step, (who, device) in enumerate(net.top()):
                push(top.at[i, who], top.at[i, who], top_send.at[i, step], top_recv.at[i, who], device).wait_recv()
            total = top[i, 0]
            for j in range(1, net.high):
                total = total + top[i, j]
        return total

    def halo_copy(kind, slot, side):
        step = -1 if side == 0 else 1
        return push(
            halo_send.at[side],
            halo_recv.at[slot, 1 - side],
            halo_ssem.at[kind, side],
            halo_rsem.at[kind, 1 - side],
            (net.row, lane + step),
        )

    def sends_to(side):
        return lane > 0 if side == 0 else lane < lanes - 1

    def halo_start(kind, slot, side):
        @pl.when(sends_to(side))
        def _():
            halo_copy(kind, slot, side).start()

    def halo_sent(kind, slot, side):
        @pl.when(sends_to(side))
        def _():
            halo_copy(kind, slot, side).wait_send()

    def halo_wait(kind, slot, side):
        step = -1 if side == 0 else 1
        push(
            halo_send.at[1 - side],
            halo_recv.at[slot, side],
            halo_ssem.at[kind, 1 - side],
            halo_rsem.at[kind, side],
            (net.row, lane + step),
        ).wait_recv()

    column = lax.broadcasted_iota(jnp.int32, (WIDE, 256), 0) % WP
    pad_mask = (column < WW).astype(F32)

    def affine(total, square, count, gain, shift):
        mean = total / count
        var = square / count - mean * mean
        scale = lax.rsqrt(var + EPS)
        return mean, scale, gain * scale, shift - mean * (gain * scale)

    def back_affine(e_sum, ez_sum, count, norm):
        mean, scale, a, _ = norm
        gain_grad = scale * (ez_sum - mean * e_sum)
        slope = -a * scale * gain_grad / count
        bias = -a * e_sum / count - slope * mean
        return slope, bias, gain_grad, e_sum

    def zero8(n=256):
        return jnp.zeros((8, n), F32)

    blank = jnp.zeros((WP, 256), F32)
    for f in range(frames):
        for b in range(BLOCKS):
            z2[b, f, 0] = blank
            z2[b, f, HH + 1] = blank
        dz[f, 0] = blank
        dz[f, HH + 1] = blank
    for side in range(2):
        hz[side, 0] = blank
        hz[side, HH + 1] = blank

    gather_wait(*plan["red", 0])
    tbuf[...] = red_t[0].T

    carry = (zero8(), zero8())
    for f in range(frames):
        loads[f].wait()
        alive = live(f)

        def project(j, carry):
            q = f * QUADS + j
            x = x0[pl.ds(pl.multiple_of(q * FLAT, FLAT), FLAT)]
            z = dot(x, tbuf[...])
            z1[0, pl.ds(q * GROUP, GROUP)] = spread(z).reshape(GROUP, WP, 256)
            z = z * alive
            return (carry[0] + fold(z), carry[1] + fold(z * z))

        carry = lax.fori_loop(0, QUADS, project, carry)

    alive_all = sum(live(f) for f in range(frames)) * (HH * WW)
    here_count = jnp.full((1, 256), 1.0, F32) * alive_all
    total_start(0, rows_of(flat_sum(carry[0]), flat_sum(carry[1]), here_count))

    gather_wait(*plan["small", 0])
    taps = small[0]
    for who in range(1, lanes):
        taps = taps + small[who]
    small[0] = taps

    def mid(b, norm, which):
        r = BLOCKS * KVOL + (b * 3 + norm) * 2 + which
        return small[0, r : r + 1]

    edge_sums = []
    pattern_col = lax.broadcasted_iota(jnp.int32, (WP, 256), 0)
    for b in range(BLOCKS):
        taps_b = [[small[0, b * KVOL + dt * 9 + k : b * KVOL + dt * 9 + k + 1] for k in range(9)] for dt in range(3)]
        se = jnp.zeros((1, 256), F32)
        see = jnp.zeros((1, 256), F32)
        for f in range(-1, frames + 1):
            here = live(f)
            t = [
                here * (live(f - 1) * taps_b[0][k] + here * taps_b[1][k] + live(f + 1) * taps_b[2][k])
                for k in range(9)
            ]
            for cls in range(3):
                use = [dh for dh in range(3) if not (cls == 0 and dh == 0) and not (cls == 2 and dh == 2)]
                col = []
                for dw in range(3):
                    v = t[use[0] * 3 + dw]
                    for dh in use[1:]:
                        v = v + t[dh * 3 + dw]
                    col.append(v)
                inner = col[0] + col[1] + col[2]
                left, right = col[1] + col[2], col[0] + col[1]
                edge[b, f + 1, cls] = jnp.where(
                    pattern_col == 0,
                    left,
                    jnp.where(pattern_col == WW - 1, right, jnp.where(pattern_col < WW - 1, inner, 0.0)),
                )
                if 0 <= f < frames:
                    times = 1.0 if cls != 1 else HH - 2.0
                    se = se + times * (left + right + (WW - 2.0) * inner)
                    see = see + times * (left * left + right * right + (WW - 2.0) * (inner * inner))
        edge_sums.append((se, see))

    for slot in (("mix", 0), ("exp", 0), ("red", 1), ("mix", 1), ("exp", 1)):
        gather_wait(*plan[slot])
    for b in range(BLOCKS):
        mix[b] = mix_t[b].T
    tbuf[...] = red_t[1].T

    got = total_finish(0)
    count = got[2:3]
    count4 = jnp.concatenate([count] * 4, axis=1)
    first_sums = (got[0:1], got[1:2])

    def edge_rows(ref, j):
        top = jnp.where(j == 0, 0, 1)
        bottom = jnp.where(j == QUADS - 1, 2, 1)
        middle = ref[1]
        return jnp.concatenate([ref[top], middle, middle, ref[bottom]], axis=0)

    def row_class(h):
        return jnp.where(h == 0, 0, jnp.where(h == HH - 1, 2, 1))

    def convolve(local, f, b, flip, emit, acc):
        done = []
        for half in range(2):
            cols = slice(128 * half, 128 * (half + 1))
            kern = [small[0, b * KVOL + k : b * KVOL + k + 1, cols] for k in range(KVOL)]
            if flip:
                kern = kern[::-1]
            planes = []
            for dt in range(3):
                g = f + dt - 1
                planes.append(hz.at[0] if g < 0 else hz.at[1] if g > last else local.at[g])

            def two_rows(i, carry):
                h = 2 * i
                part = [[None] * 3 for _ in range(2)]
                for dt in range(3):
                    for rr in range(4):
                        v = planes[dt][h + rr, :, cols]
                        for o in range(2):
                            dh = rr - o
                            if 0 <= dh < 3:
                                for dw in range(3):
                                    term = kern[dt * 9 + dh * 3 + dw] * v
                                    part[o][dw] = term if part[o][dw] is None else part[o][dw] + term
                for o in range(2):
                    p = part[o]
                    c = p[1] + pltpu.roll(p[0], 1, 0) + pltpu.roll(p[2], WP - 1, 0)
                    carry = emit(h + o, half, cols, c, carry)
                return carry

            done.append(lax.fori_loop(0, HH // 2, two_rows, tuple(a[half] for a in acc)))
        return [[done[0][k], done[1][k]] for k in range(len(acc))]

    class Reduction:
        def __init__(self, first, size, out_row):
            self.lines = pl.ds(first, size)
            self.size, self.out_row = size, out_row
            self.which = 0 if first == 0 else 1
            self.open = []

        def put(self, who, piece, first, value):
            grad_a[who, piece, pl.ds(self.lines.start + first, value.shape[0])] = value.astype(BF16)

        def clear(self):
            for copy in self.open:
                copy.wait_send()
            self.open = []

        def move(self, copy):
            copy.start()
            self.open.append(copy)

        def to_chan(self, b):
            i = 2 * b + self.which
            for step, (who, device) in enumerate(net.chan_peers()):
                src, dst = grad_a.at[who, :, self.lines], grad_ra.at[own, :, self.lines]
                self.move(push(src, dst, grad_sa.at[i, step], grad_qa.at[i, own], device))

        def low_peers(self):
            rows = [lax.rem(net.row_low + o, net.low) for o in range(1, net.low)]
            return [(row, (net.row_high * net.low + row, lane)) for row in rows]

        def to_rows(self, b):
            i = 2 * b + self.which
            for step, (who, device) in enumerate(net.chan_peers()):
                src, dst = grad_a.at[who, :, self.lines], grad_ra.at[who, :, self.lines]
                push(src, dst, grad_sa.at[i, step], grad_qa.at[i, who], device).wait_recv()

            def add(piece, _):
                total = grad_a[own, piece, self.lines].astype(F32)
                for who, _device in net.chan_peers():
                    total = total + grad_ra[who, piece, self.lines].astype(F32)
                grad_b[piece, self.lines] = total.astype(BF16)
                return 0

            lax.fori_loop(0, PIECES, add, 0)
            each = PIECES // net.low
            for step, (who, device) in enumerate(self.low_peers()):
                src = grad_b.at[pl.ds(who * each, each), self.lines]
                dst = grad_rb.at[net.row_low, :, self.lines]
                self.move(push(src, dst, grad_sb.at[i, step], grad_qb.at[i, net.row_low], device))

        def to_all(self, b):
            i = 2 * b + self.which
            each = PIECES // net.low
            mine = pl.ds(net.row_low * each, each)
            for step, (who, device) in enumerate(self.low_peers()):
                src, dst = grad_b.at[mine, self.lines], grad_rb.at[who, :, self.lines]
                push(src, dst, grad_sb.at[i, step], grad_qb.at[i, who], device).wait_recv()
            total = grad_b[mine, self.lines].astype(F32)
            for who, _device in self.low_peers():
                total = total + grad_rb[who, :, self.lines].astype(F32)
            if net.high > 1:
                grad_top[b, net.row_high, :, self.lines] = total.astype(BF16)
                for step, (who, device) in enumerate(net.top()):
                    here = grad_top.at[b, net.row_high, :, self.lines]
                    self.move(push(here, here, grad_st.at[i, step], grad_qt.at[i, net.row_high], device))
                for step, (who, device) in enumerate(net.top()):
                    there = grad_top.at[b, who, :, self.lines]
                    push(there, there, grad_st.at[i, step], grad_qt.at[i, who], device).wait_recv()
                total = grad_top[b, 0, :, self.lines].astype(F32)
                for j in range(1, net.high):
                    total = total + grad_top[b, j, :, self.lines].astype(F32)
            grad_all[mine, self.lines] = total.astype(BF16)
            for step, (who, device) in enumerate(self.low_peers()):
                here = grad_all.at[mine, self.lines]
                self.move(push(here, here, grad_sc.at[i, step], grad_qc.at[i, net.row_low], device))

        def finish(self, b):
            i = 2 * b + self.which
            each = PIECES // net.low
            for step, (who, device) in enumerate(self.low_peers()):
                there = grad_all.at[pl.ds(who * each, each), self.lines]
                push(there, there, grad_sc.at[i, step], grad_qc.at[i, who], device).wait_recv()
            for piece in range(PIECES):
                cols = slice(128 * piece, 128 * (piece + 1))
                grads_out[b, self.out_row : self.out_row + self.size, cols] = grad_all[piece, self.lines].astype(F32)

    early = Reduction(0, 96, 0)
    final = Reduction(96, 64, 96)

    order = (0, last) + tuple(range(1, last))
    norms = []
    mid_grads = {}
    out_grads = {}

    def open_block(b, q, f, rows):
        z = dot(a3s[b, rows], exp[b])
        a4, b4 = norms[b][3][2], norms[b][3][3]
        return z, (z * a4 + b4) * live(f) + xs[b][rows].astype(F32)

    out_store = [frame_copy(yb, out_hbm, f, store_sem.at[f]) for f in range(frames)]

    for b in range(BLOCKS):
        norm1 = affine(first_sums[0], first_sums[1], count, mid(b, 0, 0), mid(b, 0, 1))
        _, _, a1, b1 = norm1
        carry = (zero8(), zero8())
        if b > 0:
            for side in range(2):
                halo_sent(2 * (b - 1) + 1, 2 + b - 1, side)
        for f in order:
            alive = live(f)

            def mixing(j, carry):
                q = f * QUADS + j
                z = z1[b, pl.ds(q * GROUP, GROUP)].reshape(WIDE, 256)
                act = (gelu_fwd(z * a1 + b1) * (pad_mask * alive)).astype(BF16)
                m = dot(act, mix[b])
                z2[b, f, pl.ds(1 + j * GROUP, GROUP)] = m.reshape(GROUP, WP, 256)
                if f in (0, last):
                    halo_send[0 if f == 0 else 1, pl.ds(j * GROUP, GROUP)] = m.astype(BF16).reshape(GROUP, WP, 256)
                return (carry[0] + fold(m), carry[1] + fold(m * m))

            carry = lax.fori_loop(0, QUADS, mixing, carry)
            if f in (0, last):
                halo_start(2 * b, b, 0 if f == 0 else 1)

        def emit_conv(f):
            pad = pad_mask[:WP, :128] * live(f)

            def emit(row, half, cols, c, carry):
                c = c * pad
                conv[b, f * HH + row, :, cols] = c
                if f in (0, last):
                    halo_send[0 if f == 0 else 1, row, :, cols] = c.astype(BF16)
                e = edge[b, f + 1, row_class(row), :, cols]
                s0, s1, s2 = carry
                return (s0 + fold(c), s1 + fold(c * c), s2 + fold(c * e))

            return emit

        def fill(side):
            present = lane > 0 if side == 0 else lane < lanes - 1

            @pl.when(present)
            def _():
                halo_wait(2 * b, b, side)

                def widen(j, _):
                    hz[side, pl.ds(1 + j * GROUP, GROUP)] = halo_recv[b, side, pl.ds(j * GROUP, GROUP)].astype(F32)
                    return 0

                lax.fori_loop(0, QUADS, widen, 0)

            @pl.when(jnp.logical_not(present))
            def _():
                def clear(j, _):
                    hz[side, pl.ds(1 + j * GROUP, GROUP)] = jnp.zeros((GROUP, WP, 256), F32)
                    return 0

                lax.fori_loop(0, QUADS, clear, 0)

        acc = [[zero8(128), zero8(128)] for _ in range(3)]
        for f in range(1, last):
            acc = convolve(z2.at[b], f, b, False, emit_conv(f), acc)
        for side in range(2):
            fill(side)
            halo_sent(2 * b, b, side)
            f = 0 if side == 0 else last
            acc = convolve(z2.at[b], f, b, False, emit_conv(f), acc)
            halo_start(2 * b + 1, 2 + b, side)
        joined = [jnp.concatenate([flat_sum(a[0]), flat_sum(a[1])], axis=1) for a in acc]
        total_start(3 * b + 1, rows_of(flat_sum(carry[0]), flat_sum(carry[1]), *joined, *edge_sums[b]))
        got = total_finish(3 * b + 1)
        norm2 = affine(got[0:1], got[1:2], count, mid(b, 1, 0), mid(b, 1, 1))
        _, _, a2, b2 = norm2
        sc, scc, sce, se, see = [got[i : i + 1] for i in range(2, 7)]
        total3 = a2 * sc + b2 * se
        square3 = a2 * a2 * scc + 2.0 * a2 * b2 * sce + b2 * b2 * see
        norm3 = affine(total3, square3, count, mid(b, 2, 0), mid(b, 2, 1))
        _, _, a3, b3 = norm3

        def expanding(q, carry):
            f = lax.div(q, QUADS)
            j = lax.rem(q, QUADS)
            c = conv[b, pl.ds(q * GROUP, GROUP)].reshape(WIDE, 256)
            n3 = c * (a3 * a2) + (edge_rows(edge.at[b, f + 1], j) * (a3 * b2) + b3)
            act = squeeze(gelu_fwd(n3) * live(f)).astype(BF16)
            a3s[b, pl.ds(pl.multiple_of(q * FLAT, FLAT), FLAT)] = act
            z = dot(act, exp[b])
            return (carry[0] + fold(z), carry[1] + fold(z * z))

        carry = lax.fori_loop(0, frames * QUADS, expanding, (zero8(1024), zero8(1024)))
        total_start(3 * b + 2, rows_of(flat_sum(carry[0]), flat_sum(carry[1])))
        got = total_finish(3 * b + 2)
        norm4 = affine(wide_row(got, 0), wide_row(got, 4), count4, norm_out[b, 0:1], norm_out[b, 1:2])
        norms.append((norm1, norm2, norm3, norm4, (sc, scc, sce, se, see)))

        if b == 0:
            def closing(q, carry):
                f = lax.div(q, QUADS)
                rows = pl.ds(pl.multiple_of(q * FLAT, FLAT), FLAT)
                _, pre = open_block(0, q, f, rows)
                result = (gelu_fwd(pre) * live(f)).astype(BF16)
                x1[rows] = result
                z = dot(result, tbuf[...])
                z1[1, pl.ds(q * GROUP, GROUP)] = spread(z).reshape(GROUP, WP, 256)
                return (carry[0] + fold(z), carry[1] + fold(z * z))

            carry = lax.fori_loop(0, frames * QUADS, closing, (zero8(), zero8()))
            total_start(3, rows_of(flat_sum(carry[0]), flat_sum(carry[1])))
            tbuf[...] = exp[1].T
            got = total_finish(3)
            first_sums = (got[0:1], got[1:2])

    cot_load.wait()

    def ending(q, carry):
        f = lax.div(q, QUADS)
        alive = live(f)
        rows = pl.ds(pl.multiple_of(q * FLAT, FLAT), FLAT)
        z, pre = open_block(1, q, f, rows)
        yb[rows] = (gelu_fwd(pre) * alive).astype(BF16)
        s = gelu_slope(pre) * (sb[rows].astype(F32) * alive)
        sb[rows] = s.astype(BF16)
        return (carry[0] + fold(s), carry[1] + fold(s * z))

    carry = lax.fori_loop(0, frames * QUADS, ending, (zero8(1024), zero8(1024)))
    total_start(6, rows_of(flat_sum(carry[0]), flat_sum(carry[1])))
    for copy in out_store:
        copy.start()

    for b in reversed(range(BLOCKS)):
        turn = BLOCKS - 1 - b
        base = 6 + 3 * turn
        norm1, norm2, norm3, norm4, (sc, scc, sce, se, see) = norms[b]
        _, _, a1, b1 = norm1
        mean2, scale2, a2, b2 = norm2
        mean3, scale3, a3, b3 = norm3
        a4 = norm4[2]

        got = total_finish(base)
        slope4, bias4, gain_grad, shift_grad = back_affine(wide_row(got, 0), wide_row(got, 4), count4, norm4)
        out_grads[b] = (gain_grad, shift_grad)
        if turn == 0:
            for copy in out_store:
                copy.wait()
        for side in range(2):
            if turn == 0:
                halo_sent(2 * (BLOCKS - 1) + 1, 2 + BLOCKS - 1, side)
            else:
                halo_sent(2 * BLOCKS + turn - 1, b + 1, side)

        kind = 2 * BLOCKS + turn
        acc = (zero8(), zero8(), zero8())
        for f in order:
            alive = live(f)

            def shrinking(j, acc):
                q = f * QUADS + j
                rows = pl.ds(pl.multiple_of(q * FLAT, FLAT), FLAT)
                z = dot(a3s[b, rows], exp[b])
                d4 = (sb[rows].astype(F32) * a4 + (z * slope4 + bias4) * alive).astype(BF16)
                yb[rows] = d4
                c = conv[b, pl.ds(q * GROUP, GROUP)].reshape(WIDE, 256)
                e = edge_rows(edge.at[b, f + 1], j)
                n3 = c * (a3 * a2) + (e * (a3 * b2) + b3)
                e3 = spread(dot(d4, tbuf[...])) * gelu_slope(n3)
                dz[f, pl.ds(1 + j * GROUP, GROUP)] = e3.reshape(GROUP, WP, 256)
                if f in (0, last):
                    halo_send[0 if f == 0 else 1, pl.ds(j * GROUP, GROUP)] = e3.astype(BF16).reshape(GROUP, WP, 256)
                return (acc[0] + fold(e3), acc[1] + fold(e3 * c), acc[2] + fold(e3 * e))

            acc = lax.fori_loop(0, QUADS, shrinking, acc)
            if f in (0, last):
                halo_start(kind, b, 0 if f == 0 else 1)
        total_start(base + 1, rows_of(*[flat_sum(a) for a in acc]))

        if turn > 0:
            early.to_all(b + 1)
            final.to_rows(b + 1)
            early.clear()

        def expand_grad(i, _):
            cols = pl.ds(pl.multiple_of(i * 256, 256), 256)
            g = dot_rows(a3s[b], yb[:, cols])
            for who in range(lanes):
                for h in range(2):
                    early.put(who, 2 * i + h, 0, g[share * who : share * (who + 1), 128 * h : 128 * (h + 1)])
            return 0

        lax.fori_loop(0, 4, expand_grad, 0)
        if b > 0:
            tbuf[...] = exp[b - 1].T

        got = total_finish(base + 1)
        e3_sum, e3_conv, e3_edge = got[0:1], got[1:2], got[2:3]
        e3_third = a2 * e3_conv + b2 * e3_edge
        slope3, bias3, gain3, shift3 = back_affine(e3_sum, e3_third, count, norm3)
        third_conv = a2 * scc + b2 * sce
        third_edge = a2 * sce + b2 * see
        d3_conv = a3 * e3_conv + bias3 * sc + slope3 * third_conv
        d3_edge = a3 * e3_edge + bias3 * se + slope3 * third_edge
        slope2, bias2, gain2, shift2 = back_affine(d3_edge, d3_conv, count, norm2)

        for f in range(-1, frames + 1):
            live_pad = pad_mask[:WP] * live(f)
            for cls in range(3):
                pat[f + 1, cls] = bias3 * live_pad + (slope3 * b2) * edge[b, f + 1, cls]
        slope_c = slope3 * a2

        def to_d3(q, _):
            f = lax.div(q, QUADS)
            j = lax.rem(q, QUADS)
            rows = pl.ds(1 + j * GROUP, GROUP)
            c = conv[b, pl.ds(q * GROUP, GROUP)].reshape(WIDE, 256)
            e3 = dz[f, rows].reshape(WIDE, 256)
            d3 = e3 * a3 + c * slope_c + edge_rows(pat.at[f + 1], j)
            dz[f, rows] = d3.reshape(GROUP, WP, 256)
            return 0

        lax.fori_loop(0, frames * QUADS, to_d3, 0)

        def fill_back(side):
            present = lane > 0 if side == 0 else lane < lanes - 1
            f = -1 if side == 0 else frames

            @pl.when(present)
            def _():
                halo_wait(2 * b + 1, 2 + b, side)
                halo_wait(kind, b, side)

                def widen(j, _):
                    rows = pl.ds(j * GROUP, GROUP)
                    c = halo_recv[2 + b, side, rows].astype(F32).reshape(WIDE, 256)
                    e3 = halo_recv[b, side, rows].astype(F32).reshape(WIDE, 256)
                    d3 = e3 * a3 + c * slope_c + edge_rows(pat.at[f + 1], j)
                    hz[side, pl.ds(1 + j * GROUP, GROUP)] = d3.reshape(GROUP, WP, 256)
                    return 0

                lax.fori_loop(0, QUADS, widen, 0)

            @pl.when(jnp.logical_not(present))
            def _():
                def clear(j, _):
                    hz[side, pl.ds(1 + j * GROUP, GROUP)] = jnp.zeros((GROUP, WP, 256), F32)
                    return 0

                lax.fori_loop(0, QUADS, clear, 0)

        for side in range(2):
            fill_back(side)

        def emit_back(f):
            pad = pad_mask[:WP, :128] * live(f)

            def emit(row, half, cols, e2, carry):
                z = z2[b, f, row + 1, :, cols]
                d2 = (e2 * a2[:, cols] + (z * slope2[:, cols] + bias2[:, cols])) * pad
                d2s[f * HH + row, :, cols] = d2.astype(BF16)
                return carry

            return emit

        for f in range(frames):
            convolve(dz, f, b, True, emit_back(f), [])

        def unmixing(q, acc):
            rows = pl.ds(q * GROUP, GROUP)
            e = dot(d2s[rows].reshape(WIDE, 256), mix_t[b])
            z = z1[b, rows].reshape(WIDE, 256)
            n1 = z * a1 + b1
            a1s[rows] = (gelu_fwd(n1) * (pad_mask * live(lax.div(q, QUADS)))).astype(BF16).reshape(GROUP, WP, 256)
            e1 = e * gelu_slope(n1)
            conv[b, rows] = e1.reshape(GROUP, WP, 256)
            return (acc[0] + fold(e1), acc[1] + fold(e1 * z))

        acc = lax.fori_loop(0, frames * QUADS, unmixing, (zero8(), zero8()))
        total_start(base + 2, rows_of(*[flat_sum(a) for a in acc]))

        for half in range(2):
            cols = slice(128 * half, 128 * (half + 1))
            taps_grad = tuple(zero8(128) for _ in range(KVOL))
            for f in range(frames):
                planes = []
                for dt in range(3):
                    g = f - (dt - 1)
                    planes.append(hz.at[0] if g < 0 else hz.at[1] if g > last else dz.at[g])
                shift_rows = b2[:, cols] * (pad_mask[:WP, :128] * live(f))

                def tap_rows(h, taps_grad):
                    a = z2[b, f, h + 1, :, cols] * a2[:, cols] + shift_rows
                    moved = [pltpu.roll(a, 1, 0), a, pltpu.roll(a, WP - 1, 0)]
                    new = list(taps_grad)
                    for dt in range(3):
                        for dh in range(3):
                            d = planes[dt][h + 1 - (dh - 1), :, cols]
                            for dw in range(3):
                                k = dt * 9 + dh * 3 + dw
                                new[k] = new[k] + fold(d * moved[dw])
                    return tuple(new)

                taps_grad = lax.fori_loop(0, HH, tap_rows, taps_grad)
            lines = jnp.concatenate(
                [flat_sum(t) for t in taps_grad] + [jnp.zeros((WP - KVOL, 128), F32)], axis=0
            )
            for r in range(4):
                part = jnp.concatenate([lines[8 * r : 8 * r + 8], zero8(128)], axis=0)
                for who in range(lanes):
                    early.put(who, 2 * r + half, 80, part)
        g = dot_rows(d2s[...].reshape(frames * HH * WP, 256), a1s[...].reshape(frames * HH * WP, 256))
        for who in range(lanes):
            for r in range(4):
                for h in range(2):
                    first = share * who + 16 * r
                    early.put(who, 2 * r + h, 64, g[first : first + 16, 128 * h : 128 * (h + 1)])
        if turn > 0:
            early.finish(b + 1)
            final.to_all(b + 1)
        early.to_chan(b)

        got = total_finish(base + 2)
        slope1, bias1, gain1, shift1 = back_affine(got[0:1], got[1:2], count, norm1)
        mid_grads[b] = ((gain1, shift1), (gain2, shift2), (gain3, shift3))

        def first_grad(q):
            f = lax.div(q, QUADS)
            rows = pl.ds(pl.multiple_of(q * FLAT, FLAT), FLAT)
            wide = pl.ds(q * GROUP, GROUP)
            e1 = conv[b, wide].reshape(WIDE, 256)
            z = z1[b, wide].reshape(WIDE, 256)
            d1 = squeeze((e1 * a1 + (z * slope1 + bias1)) * live(f)).astype(BF16)
            a3s[b, rows] = d1
            return f, rows, d1

        def reduce_grad(i, _):
            cols = pl.ds(pl.multiple_of(i * 256, 256), 256)
            g = dot_rows(a3s[b], xs[b][:, cols])
            for who in range(lanes):
                for h in range(2):
                    final.put(who, 2 * i + h, 0, g[share * who : share * (who + 1), 128 * h : 128 * (h + 1)])
            return 0

        if b > 0:

            def passing(q, carry):
                f, rows, d1 = first_grad(q)
                g = dot(d1, red_t[b]) + sb[rows].astype(F32)
                z, pre = open_block(b - 1, q, f, rows)
                s = gelu_slope(pre) * (g * live(f))
                sb[rows] = s.astype(BF16)
                return (carry[0] + fold(s), carry[1] + fold(s * z))

            carry = lax.fori_loop(0, frames * QUADS, passing, (zero8(1024), zero8(1024)))
            total_start(base + 3, rows_of(flat_sum(carry[0]), flat_sum(carry[1])))
            lax.fori_loop(0, 4, reduce_grad, 0)
            final.to_chan(b)
            early.to_rows(b)
        else:

            def only_d1(q, _):
                first_grad(q)
                return 0

            lax.fori_loop(0, frames * QUADS, only_d1, 0)
            final.clear()
            lax.fori_loop(0, 4, reduce_grad, 0)
            final.to_chan(b)
            final.finish(b + 1)
            early.to_rows(b)

            def closing_grad(q, _):
                rows = pl.ds(pl.multiple_of(q * FLAT, FLAT), FLAT)
                yb[rows] = (dot(a3s[b, rows], red_t[b]) + sb[rows].astype(F32)).astype(BF16)
                return 0

            gtok_store = [frame_copy(yb, gtok_hbm, f, store_sem.at[f]) for f in range(frames)]
            for f in range(frames):
                lax.fori_loop(f * QUADS, (f + 1) * QUADS, closing_grad, 0)
                gtok_store[f].start()
            final.to_rows(b)
            early.to_all(b)
            final.to_all(b)
            early.finish(b)
            final.finish(b)

    for b in range(BLOCKS):
        for k in range(3):
            for w in range(2):
                r = (b * 3 + k) * 2 + w
                gmid_out[r : r + 1] = mid_grads[b][k][w]
        for w in range(2):
            gout_out[2 * b + w : 2 * b + w + 1] = out_grads[b][w]

    for copy in gtok_store:
        copy.wait()
    early.clear()
    final.clear()
    for copy in late:
        copy.wait_send()
    for side in range(2):
        halo_sent(2 * BLOCKS + BLOCKS - 1, 0, side)


def whole_call(groups, lanes, counts, tokens, cotangent, reduce_loc, mix_loc, expand_loc, small_loc, norm_out):
    rows = tokens.shape[0]
    frames = rows // (HH * WW)
    whole = pl.BlockSpec(memory_space=pltpu.VMEM)
    hbm = pl.BlockSpec(memory_space=pl.ANY)
    dma = pltpu.SemaphoreType.DMA
    low, high = stages(groups)
    far = low * (lanes // 2)
    lines = frames * HH
    sums = 6 * BLOCKS
    kinds = 3 * BLOCKS
    shape = jax.ShapeDtypeStruct
    return pl.pallas_call(
        functools.partial(whole_kernel, groups, lanes),
        out_shape=(
            shape((rows, 1024), BF16),
            shape((rows, 1024), BF16),
            shape((BLOCKS, 160, 1024), F32),
            shape((BLOCKS * 6, 256), F32),
            shape((BLOCKS * 2, 1024), F32),
        ),
        in_specs=[pl.BlockSpec(memory_space=pltpu.SMEM), hbm, hbm] + [whole] * 5,
        out_specs=[hbm] * 2 + [whole] * 3,
        scratch_shapes=[
            pltpu.VMEM((rows, 1024), BF16),
            pltpu.VMEM((rows, 1024), BF16),
            pltpu.VMEM((rows, 1024), BF16),
            pltpu.VMEM((rows, 1024), BF16),
            pltpu.VMEM((BLOCKS, 256, 1024), BF16),
            pltpu.VMEM((BLOCKS, 256, 1024), BF16),
            pltpu.VMEM((1024, 256), BF16),
            pltpu.VMEM((BLOCKS, 256, 256), BF16),
            pltpu.VMEM((BLOCKS, 256, 256), BF16),
            pltpu.VMEM((lanes,) + small_loc.shape, F32),
            pltpu.VMEM((BLOCKS, lines, WP, 256), F32),
            pltpu.VMEM((lines, WP, 256), BF16),
            pltpu.VMEM((BLOCKS, frames, HH + 2, WP, 256), F32),
            pltpu.VMEM((frames, HH + 2, WP, 256), F32),
            pltpu.VMEM((2, HH + 2, WP, 256), F32),
            pltpu.VMEM((BLOCKS, lines, WP, 256), F32),
            pltpu.VMEM((BLOCKS, rows, 256), BF16),
            pltpu.VMEM((BLOCKS, frames + 2, 3, WP, 256), F32),
            pltpu.VMEM((frames + 2, 3, WP, 256), F32),
            pltpu.VMEM((lines, WP, 256), BF16),
            pltpu.VMEM((2, HH, WP, 256), BF16),
            pltpu.VMEM((2 * BLOCKS, 2, HH, WP, 256), BF16),
            pltpu.VMEM((lanes, PIECES, 160, 128), BF16),
            pltpu.VMEM((lanes, PIECES, 160, 128), BF16),
            pltpu.VMEM((PIECES, 160, 128), BF16),
            pltpu.VMEM((low, PIECES // low, 160, 128), BF16),
            pltpu.VMEM((PIECES, 160, 128), BF16),
            pltpu.VMEM((BLOCKS, high, PIECES // low, 160 if high > 1 else 16, 128), BF16),
            pltpu.VMEM((sums, 2, 8, 256), F32),
            pltpu.VMEM((sums, far, 8, 256), F32),
            pltpu.VMEM((sums, high, 8, 256), F32),
            dma((sums,)),
            dma((sums,)),
            dma((sums, far)),
            dma((sums, far)),
            dma((sums, high)),
            dma((sums, high)),
            dma((7, lanes)),
            dma((7, lanes)),
            dma((kinds, 2)),
            dma((kinds, 2)),
            dma((frames + 1,)),
            dma((frames,)),
            dma((2 * BLOCKS, lanes)),
            dma((2 * BLOCKS, lanes)),
            dma((2 * BLOCKS, low)),
            dma((2 * BLOCKS, low)),
            dma((2 * BLOCKS, low)),
            dma((2 * BLOCKS, low)),
            dma((2 * BLOCKS, high)),
            dma((2 * BLOCKS, high)),
        ],
        compiler_params=pltpu.CompilerParams(
            collective_id=1, has_side_effects=True, vmem_limit_bytes=63 * 2**20
        ),
    )(counts, tokens, cotangent, reduce_loc, mix_loc, expand_loc, small_loc, norm_out)


def descend(weight, moment, grad):
    moment_new = MOMENTUM * moment + grad + DECAY * weight
    return (weight - LEARN_RATE * moment_new, moment_new)


def shards(
    tokens,
    frame_counts,
    cotangent,
    w_reduce,
    w_mix,
    w_depth,
    w_expand,
    norm_mid,
    norm_out,
    moment_reduce,
    moment_mix,
    moment_depth,
    moment_expand,
    moment_mid,
    moment_out,
):
    lane = lax.axis_index("chan")
    lanes = lax.axis_size("chan")
    narrow = w_reduce.shape[2]
    small = jnp.concatenate([w_depth.reshape(-1, narrow), norm_mid.reshape(-1, narrow)], axis=0)
    small = jnp.pad(small, ((0, -small.shape[0] % 8), (0, 0)))
    small = lax.dynamic_update_slice(jnp.zeros((small.shape[0], narrow * lanes), F32), small, (0, lane * narrow))
    output, grad_tokens, reduced, gmid, gout = whole_call(
        lax.axis_size("dp"),
        lanes,
        frame_counts,
        tokens,
        cotangent,
        jnp.swapaxes(w_reduce, 1, 2).astype(BF16),
        jnp.swapaxes(w_mix, 1, 2).astype(BF16),
        w_expand.astype(BF16),
        small,
        norm_out,
    )
    gmix = reduced[:, 64:80].reshape(BLOCKS, 16, 4, 256).swapaxes(1, 2).reshape(BLOCKS, narrow, 256)
    gdep = reduced[:, 80:88].reshape(BLOCKS, 8, 4, 256).swapaxes(1, 2).reshape(BLOCKS, WP, 256)[:, :KVOL]
    grads = (
        jnp.swapaxes(reduced[:, 96:], 1, 2),
        jnp.swapaxes(gmix, 1, 2),
        lax.dynamic_slice_in_dim(gdep, lane * narrow, narrow, 2),
        reduced[:, :64],
        lax.dynamic_slice_in_dim(gmid.reshape(BLOCKS, 3, 2, -1), lane * narrow, narrow, 3),
        gout.reshape(BLOCKS, 2, -1),
    )
    params = (w_reduce, w_mix, w_depth, w_expand, norm_mid, norm_out)
    moments = (moment_reduce, moment_mix, moment_depth, moment_expand, moment_mid, moment_out)
    updated = [descend(w, m, g) for w, m, g in zip(params, moments, grads)]
    return (output, grad_tokens) + grads + tuple(u[0] for u in updated) + tuple(u[1] for u in updated)


def solution(mesh):
    rows = P(("dp", "chan"), None)
    weights = (
        P(None, None, "chan"),
        P(None, None, "chan"),
        P(None, None, "chan"),
        P(None, "chan", None),
        P(None, None, None, "chan"),
        P(),
    )
    return jax.shard_map(
        shards,
        mesh=mesh,
        in_specs=(rows, P("dp"), rows) + weights + weights,
        out_specs=(rows, rows) + weights + weights + weights,
        check_vma=False,
    )
```

```python
import functools

import jax
import jax.numpy as jnp
from jax import lax
from jax.experimental import pallas as pl
from jax.experimental.pallas import tpu as pltpu
from jax.sharding import PartitionSpec as P

FRAMES = 12
HH = 28
WW = 28
WP = 32
KVOL = 27
BLOCKS = 2
GROUP = 4
QUADS = HH // GROUP
FLAT = GROUP * WW
WIDE = GROUP * WP
PIECES = 8
TRIO = 3

EPS = 1e-05
LEARN_RATE = 0.001
MOMENTUM = 0.9
DECAY = 0.0001
MESH = pl.DeviceIdType.MESH
F32 = jnp.float32
BF16 = jnp.bfloat16
ROOT = 0.7978845608028654
CUBE = 0.044715


def gelu_core(v):
    square = v * v
    return square, jnp.tanh(v * (ROOT + (ROOT * CUBE) * square))


def gelu_value(v, t, half):
    h = half * v
    return h * t + h


def gelu_slope(v, square, t, half):
    r = v * (half * ROOT + (half * (3.0 * ROOT * CUBE)) * square)
    return (half * t + half) + (r - r * (t * t))


def dot_rows(left, right):
    return lax.dot_general(left, right, (((0,), (0,)), ((), ())), preferred_element_type=F32)


def dot(left, right):
    return jnp.dot(left, right, preferred_element_type=F32)


def fold(v):
    return jnp.sum(v.reshape(v.shape[0] // 8, 8, v.shape[1]), axis=0)


def spread(v):
    gap = jnp.zeros((WP - WW, v.shape[1]), v.dtype)
    parts = []
    for h in range(v.shape[0] // WW):
        parts += [v[WW * h : WW * (h + 1)], gap]
    return jnp.concatenate(parts, axis=0)


def squeeze(v):
    return jnp.concatenate([v[WP * h : WP * h + WW] for h in range(v.shape[0] // WP)], axis=0)


def pieces(v, rows):
    return [v[rows * k : rows * (k + 1)] for k in range(v.shape[0] // rows)]


def rows_of(*vectors):
    parts = []
    for v in vectors:
        parts += pieces_of(v)
    n = 4 if len(parts) <= 4 else 8
    out = []
    for side in range(2):
        out += [v[:, 128 * side : 128 * (side + 1)] for v in parts]
        if len(parts) < n:
            out.append(jnp.zeros((n - len(parts), 128), F32))
    return jnp.concatenate(out, axis=0)


def pieces_of(v):
    return [v[:, 256 * i : 256 * (i + 1)] for i in range(v.shape[1] // 256)]


def flat_sum(v):
    return jnp.sum(v, axis=0, keepdims=True)


def wide_row(v, first):
    return jnp.concatenate([v[first + i : first + i + 1] for i in range(4)], axis=1)


class Net:
    def __init__(self, groups, lanes):
        self.lanes = lanes
        self.low, self.high = stages(groups)
        self.row = lax.axis_index("dp")
        self.lane = lax.axis_index("chan")
        self.core = lax.rem(self.lane, 2)
        self.side = lax.div(self.lane, 2)
        self.half = lanes // 2
        self.row_low = lax.rem(self.row, self.low)
        self.row_high = lax.div(self.row, self.low)

    def near(self):
        return [(1 - self.core, (self.row, self.side * 2 + 1 - self.core))]

    def far(self):
        out = []
        for o in range(self.low):
            for p in range(self.half):
                if o or p:
                    row = lax.rem(self.row_low + o, self.low)
                    side = lax.rem(self.side + p, self.half)
                    out.append((row * self.half + side, (self.row_high * self.low + row, side * 2 + self.core)))
        return out

    def far_slot(self):
        return self.row_low * self.half + self.side

    def top(self):
        rows = [lax.rem(self.row_high + o, self.high) for o in range(1, self.high)]
        return [(row, (row * self.low + self.row_low, self.lane)) for row in rows]

    def pair(self):
        lane = self.side * 2 + 1 - self.core
        return lane, (self.row, lane)

    def across(self):
        lane = (1 - self.side) * 2 + self.core
        return lane, (self.row, lane)

    def corner(self):
        return (1 - self.side) * 2 + 1 - self.core


def stages(groups):
    low = min(groups, 8)
    return low, groups // low


def push(src, dst, send, recv, device):
    copy = pltpu.make_async_remote_copy(
        src_ref=src, dst_ref=dst, send_sem=send, recv_sem=recv, device_id=device, device_id_type=MESH
    )
    return copy


def whole_kernel(
    groups,
    lanes,
    counts,
    tokens,
    cotangent,
    reduce_loc,
    mix_loc,
    expand_loc,
    small_loc,
    norm_out,
    out_hbm,
    gtok_hbm,
    grads_out,
    gmid_out,
    gout_out,
    x0,
    x1,
    yb,
    sb,
    red_t,
    exp,
    tbuf,
    mix_t,
    mix,
    small_in,
    small,
    z1,
    a1s,
    z2,
    dz,
    hz,
    conv,
    a3s,
    edge,
    pat,
    d2s,
    halo_send,
    halo_recv,
    grad_a,
    grad_ra,
    grad_b,
    grad_rb,
    grad_all,
    grad_top,
    near,
    far,
    top,
    near_send,
    near_recv,
    far_send,
    far_recv,
    top_send,
    top_recv,
    gather_send,
    gather_recv,
    halo_ssem,
    halo_rsem,
    load_sem,
    store_sem,
    grad_sa,
    grad_qa,
    grad_sb,
    grad_qb,
    grad_sc,
    grad_qc,
    grad_st,
    grad_qt,
):
    net = Net(groups, lanes)
    lane = net.lane
    frames = tokens.shape[0] // (HH * WW)
    frame_rows = HH * WW
    last = frames - 1
    count_here = counts[0]
    xs = (x0, x1)

    def live(frame):
        position = lane * frames + frame
        return jnp.where((position >= 0) & (position < count_here), 1.0, 0.0)

    def frame_copy(src, dst, f, sem):
        rows = pl.ds(f * frame_rows, frame_rows)
        return pltpu.make_async_copy(src.at[rows], dst.at[rows], sem)

    loads = [frame_copy(tokens, x0, f, load_sem.at[f]) for f in range(frames)]
    cot_load = pltpu.make_async_copy(cotangent, sb, load_sem.at[frames])
    for copy in loads:
        copy.start()
    cot_load.start()

    barrier = pltpu.get_barrier_semaphore()
    friends = [d for peers in (net.near(), net.far(), net.top()) for _, d in peers] + [(net.row, net.corner())]
    for device in friends:
        pl.semaphore_signal(barrier, inc=1, device_id=device, device_id_type=MESH)
    pl.semaphore_wait(barrier, len(friends))

    own = net.lane
    share = red_t.shape[1] // lanes
    late = []

    def gather(slot, src, dst_of):
        for step, (_, device) in enumerate((net.pair(), net.across())):
            copy = push(src, dst_of(own), gather_send.at[slot, step], gather_recv.at[slot, own], device)
            copy.start()
            late.append(copy)
        pltpu.make_async_copy(src, dst_of(own), gather_send.at[slot, 3]).start()

    def gather_on(slot, src, dst_of):
        who, device = net.across()
        piece = dst_of(who)
        push(src, piece, gather_send.at[slot, 1], gather_recv.at[slot, who], device).wait_recv()
        copy = push(piece, piece, gather_send.at[slot, 2], gather_recv.at[slot, who], net.pair()[1])
        copy.start()
        late.append(copy)

    def gather_wait(slot, src, dst_of):
        pltpu.make_async_copy(src, dst_of(own), gather_send.at[slot, 3]).wait()
        for who in (net.pair()[0], net.corner()):
            push(src, dst_of(who), gather_send.at[slot, 0], gather_recv.at[slot, who], net.pair()[1]).wait_recv()

    def block_rows(ref, b):
        return lambda who: ref.at[b, pl.ds(pl.multiple_of(who * share, share), share)]

    plan = {
        ("red", 0): (0, reduce_loc.at[0], block_rows(red_t, 0)),
        ("mix", 0): (1, mix_loc.at[0], block_rows(mix_t, 0)),
        ("small", 0): (2, small_loc, lambda who: small_in.at[who]),
        ("exp", 0): (3, expand_loc.at[0], block_rows(exp, 0)),
        ("red", 1): (4, reduce_loc.at[1], block_rows(red_t, 1)),
        ("mix", 1): (5, mix_loc.at[1], block_rows(mix_t, 1)),
        ("exp", 1): (6, expand_loc.at[1], block_rows(exp, 1)),
    }
    for name in (("red", 0), ("mix", 0), ("small", 0)):
        gather(*plan[name])

    used = {}

    def total_start(i, value):
        size = value.shape[0]
        used[i] = size
        near[i, net.core, :size] = value
        for who, device in net.near():
            mine = near.at[i, net.core, pl.ds(0, size)]
            copy = push(mine, mine, near_send.at[i], near_recv.at[i], device)
            copy.start()
            late.append(copy)
            copy.wait_recv()
        far[i, net.far_slot(), :size] = near[i, 0, :size] + near[i, 1, :size]
        for step, (who, device) in enumerate(net.far()):
            mine = far.at[i, net.far_slot(), pl.ds(0, size)]
            copy = push(mine, mine, far_send.at[i, step], far_recv.at[i, net.far_slot()], device)
            copy.start()
            late.append(copy)

    def total_finish(i):
        size = used[i]
        for step, (who, device) in enumerate(net.far()):
            there = far.at[i, who, pl.ds(0, size)]
            push(there, there, far_send.at[i, step], far_recv.at[i, who], device).wait_recv()
        total = far[i, 0, :size]
        for j in range(1, net.low * net.half):
            total = total + far[i, j, :size]
        if net.high > 1:
            mine = top.at[i, net.row_high, pl.ds(0, size)]
            top[i, net.row_high, :size] = total
            for step, (who, device) in enumerate(net.top()):
                copy = push(mine, mine, top_send.at[i, step], top_recv.at[i, net.row_high], device)
                copy.start()
                late.append(copy)
            for step, (who, device) in enumerate(net.top()):
                there = top.at[i, who, pl.ds(0, size)]
                push(there, there, top_send.at[i, step], top_recv.at[i, who], device).wait_recv()
            total = top[i, 0, :size]
            for j in range(1, net.high):
                total = total + top[i, j, :size]
        return jnp.concatenate([total[: size // 2], total[size // 2 :]], axis=1)

    def halo_copy(kind, slot, side):
        step = -1 if side == 0 else 1
        return push(
            halo_send.at[side],
            halo_recv.at[slot, 1 - side],
            halo_ssem.at[kind, side],
            halo_rsem.at[kind, 1 - side],
            (net.row, lane + step),
        )

    def sends_to(side):
        return lane > 0 if side == 0 else lane < lanes - 1

    def halo_start(kind, slot, side):
        @pl.when(sends_to(side))
        def _():
            halo_copy(kind, slot, side).start()

    def halo_sent(kind, slot, side):
        @pl.when(sends_to(side))
        def _():
            halo_copy(kind, slot, side).wait_send()

    def halo_wait(kind, slot, side):
        step = -1 if side == 0 else 1
        push(
            halo_send.at[1 - side],
            halo_recv.at[slot, side],
            halo_ssem.at[kind, 1 - side],
            halo_rsem.at[kind, side],
            (net.row, lane + step),
        ).wait_recv()

    column = lax.broadcasted_iota(jnp.int32, (WIDE, 256), 0) % WP
    pad_mask = (column < WW).astype(F32)

    def half_mask(alive, lines):
        return jnp.concatenate([pad_mask[:WP] * (0.5 * alive)] * lines, axis=0)

    def affine(total, square, count, gain, shift):
        mean = total / count
        var = square / count - mean * mean
        scale = lax.rsqrt(var + EPS)
        return mean, scale, gain * scale, shift - mean * (gain * scale)

    def back_affine(e_sum, ez_sum, count, norm):
        mean, scale, a, _ = norm
        gain_grad = scale * (ez_sum - mean * e_sum)
        slope = -a * scale * gain_grad / count
        bias = -a * e_sum / count - slope * mean
        return slope, bias, gain_grad, e_sum

    def zero8(n=256):
        return jnp.zeros((8, n), F32)

    blank = jnp.zeros((WP, 256), F32)
    for f in range(frames):
        for b in range(BLOCKS):
            z2[b, f, 0] = blank
            z2[b, f, HH + 1] = blank
        dz[f, 0] = blank
        dz[f, HH + 1] = blank
    for side in range(2):
        hz[side, 0] = blank
        hz[side, HH + 1] = blank

    for name in (("red", 0), ("mix", 0), ("small", 0)):
        gather_on(*plan[name])
    gather_wait(*plan["red", 0])
    tbuf[...] = red_t[0].T

    carry = (zero8(), zero8())
    for f in range(frames):
        loads[f].wait()
        alive = live(f)

        z = dot(x0[f * frame_rows : (f + 1) * frame_rows], tbuf[...])
        z1[0, f * HH : (f + 1) * HH] = spread(z).reshape(HH, WP, 256)
        carry = (carry[0] + fold(z) * alive, carry[1] + fold(z * z) * alive)

    alive_all = sum(live(f) for f in range(frames)) * (HH * WW)
    here_count = jnp.full((1, 256), 1.0, F32) * alive_all
    total_start(0, rows_of(flat_sum(carry[0]), flat_sum(carry[1]), here_count))

    gather_wait(*plan["small", 0])
    half_rows = small_loc.shape[0]
    for side in range(2):
        here = [small_in[who, :, 64 * side : 64 * (side + 1)] for who in range(lanes)]
        small[half_rows * side : half_rows * (side + 1)] = jnp.concatenate(here, axis=1)

    def mid(b, norm, which):
        r = BLOCKS * KVOL + (b * 3 + norm) * 2 + which
        return small[r : r + 1]

    edge_sums = []
    pattern_col = lax.broadcasted_iota(jnp.int32, (WP, 256), 0)
    for b in range(BLOCKS):
        taps_b = [[small[b * KVOL + dt * 9 + k : b * KVOL + dt * 9 + k + 1] for k in range(9)] for dt in range(3)]
        se = jnp.zeros((1, 256), F32)
        see = jnp.zeros((1, 256), F32)
        for f in range(-1, frames + 1):
            here = live(f)
            t = [
                here * (live(f - 1) * taps_b[0][k] + here * taps_b[1][k] + live(f + 1) * taps_b[2][k])
                for k in range(9)
            ]
            for cls in range(3):
                use = [dh for dh in range(3) if not (cls == 0 and dh == 0) and not (cls == 2 and dh == 2)]
                col = []
                for dw in range(3):
                    v = t[use[0] * 3 + dw]
                    for dh in use[1:]:
                        v = v + t[dh * 3 + dw]
                    col.append(v)
                inner = col[0] + col[1] + col[2]
                left, right = col[1] + col[2], col[0] + col[1]
                edge[b, f + 1, cls] = jnp.where(
                    pattern_col == 0,
                    left,
                    jnp.where(pattern_col == WW - 1, right, jnp.where(pattern_col < WW - 1, inner, 0.0)),
                )
                if 0 <= f < frames:
                    times = 1.0 if cls != 1 else HH - 2.0
                    se = se + times * (left + right + (WW - 2.0) * inner)
                    see = see + times * (left * left + right * right + (WW - 2.0) * (inner * inner))
        edge_sums.append((se, see))

    gather_wait(*plan["mix", 0])
    mix[...] = mix_t[0].T

    got = total_finish(0)
    count = got[2:3]
    count4 = jnp.concatenate([count] * 4, axis=1)
    first_sums = (got[0:1], got[1:2])

    def edge_rows(ref, j):
        top = jnp.where(j == 0, 0, 1)
        bottom = jnp.where(j == QUADS - 1, 2, 1)
        middle = ref[1]
        return jnp.concatenate([ref[top], middle, middle, ref[bottom]], axis=0)

    def trio(i):
        rows = pl.ds(pl.multiple_of(i * (TRIO * FLAT), TRIO * FLAT), TRIO * FLAT)
        lines = pl.ds(i * (TRIO * GROUP), TRIO * GROUP)
        where = []
        for k in range(TRIO):
            q = TRIO * i + k
            where.append((lax.div(q, QUADS), lax.rem(q, QUADS)))
        return rows, lines, where

    trios = frames * QUADS // TRIO

    def norm3_pattern(b, a3, b2, b3):
        for f in range(frames):
            for cls in range(3):
                pat[f + 1, cls] = edge[b, f + 1, cls] * (a3 * b2) + b3

    def row_class(h):
        return jnp.where(h == 0, 0, jnp.where(h == HH - 1, 2, 1))

    def convolve(local, f, b, flip, emit, acc):
        done = []
        for half in range(2):
            cols = slice(128 * half, 128 * (half + 1))
            kern = [small[b * KVOL + k : b * KVOL + k + 1, cols] for k in range(KVOL)]
            if flip:
                kern = kern[::-1]
            planes = []
            for dt in range(3):
                g = f + dt - 1
                planes.append(hz.at[0] if g < 0 else hz.at[1] if g > last else local.at[g])

            def two_rows(i, carry):
                h = 2 * i
                part = [[None] * 3 for _ in range(2)]
                for dt in range(3):
                    for rr in range(4):
                        v = planes[dt][h + rr, :, cols]
                        for o in range(2):
                            dh = rr - o
                            if 0 <= dh < 3:
                                for dw in range(3):
                                    term = kern[dt * 9 + dh * 3 + dw] * v
                                    part[o][dw] = term if part[o][dw] is None else part[o][dw] + term
                for o in range(2):
                    p = part[o]
                    c = p[1] + pltpu.roll(p[0], 1, 0) + pltpu.roll(p[2], WP - 1, 0)
                    carry = emit(h + o, half, cols, c, carry)
                return carry

            done.append(lax.fori_loop(0, HH // 2, two_rows, tuple(a[half] for a in acc)))
        return [[done[0][k], done[1][k]] for k in range(len(acc))]

    class Reduction:
        def __init__(self, first, size, out_row):
            self.lines = pl.ds(first, size)
            self.size, self.out_row = size, out_row
            self.which = 0 if first == 0 else 1
            self.open = {"a": [], "b": [], "all": []}

        def put(self, who, piece, first, value):
            grad_a[who, piece, pl.ds(self.lines.start + first, value.shape[0])] = value.astype(BF16)

        def clear(self, *names):
            for name in names:
                for copy in self.open[name]:
                    copy.wait_send()
                self.open[name] = []

        def move(self, name, copy):
            copy.start()
            self.open[name].append(copy)

        def pair_copy(self, b, side):
            i = 2 * b + self.which
            src, dst = grad_a.at[2 * side + 1 - net.core, :, self.lines], grad_ra.at[side, :, self.lines]
            return push(src, dst, grad_sa.at[i, side], grad_qa.at[i, side], net.pair()[1])

        def to_pair(self, b):
            for side in range(2):
                self.move("a", self.pair_copy(b, side))

        def across_copy(self, b):
            i = 2 * b + self.which
            src, dst = grad_a.at[net.across()[0], :, self.lines], grad_ra.at[2, :, self.lines]
            return push(src, dst, grad_sa.at[i, 2], grad_qa.at[i, 2], net.across()[1])

        def to_side(self, b):
            for side in range(2):
                self.pair_copy(b, side).wait_recv()
            other = net.across()[0]

            def add(piece, _):
                mine, theirs = grad_a[other, piece, self.lines], grad_ra[1 - net.side, piece, self.lines]
                grad_a[other, piece, self.lines] = (mine.astype(F32) + theirs.astype(F32)).astype(BF16)
                return 0

            lax.fori_loop(0, PIECES, add, 0)
            self.move("a", self.across_copy(b))

        def low_peers(self):
            rows = [lax.rem(net.row_low + o, net.low) for o in range(1, net.low)]
            return [(row, (net.row_high * net.low + row, lane)) for row in rows]

        def to_rows(self, b):
            i = 2 * b + self.which
            self.across_copy(b).wait_recv()
            self.clear("b")

            def add(piece, _):
                total = grad_a[own, piece, self.lines].astype(F32) + grad_ra[net.side, piece, self.lines].astype(F32)
                grad_b[piece, self.lines] = (total + grad_ra[2, piece, self.lines].astype(F32)).astype(BF16)
                return 0

            lax.fori_loop(0, PIECES, add, 0)
            each = PIECES // net.low
            for step, (who, device) in enumerate(self.low_peers()):
                src = grad_b.at[pl.ds(who * each, each), self.lines]
                dst = grad_rb.at[net.row_low, :, self.lines]
                self.move("b", push(src, dst, grad_sb.at[i, step], grad_qb.at[i, net.row_low], device))

        def to_all(self, b):
            i = 2 * b + self.which
            each = PIECES // net.low
            mine = pl.ds(net.row_low * each, each)
            for step, (who, device) in enumerate(self.low_peers()):
                src, dst = grad_b.at[mine, self.lines], grad_rb.at[who, :, self.lines]
                push(src, dst, grad_sb.at[i, step], grad_qb.at[i, who], device).wait_recv()
            total = grad_b[mine, self.lines].astype(F32)
            for who, _device in self.low_peers():
                total = total + grad_rb[who, :, self.lines].astype(F32)
            if net.high > 1:
                grad_top[b, net.row_high, :, self.lines] = total.astype(BF16)
                for step, (who, device) in enumerate(net.top()):
                    here = grad_top.at[b, net.row_high, :, self.lines]
                    self.move("all", push(here, here, grad_st.at[i, step], grad_qt.at[i, net.row_high], device))
                for step, (who, device) in enumerate(net.top()):
                    there = grad_top.at[b, who, :, self.lines]
                    push(there, there, grad_st.at[i, step], grad_qt.at[i, who], device).wait_recv()
                self.clear("all")
                total = grad_top[b, 0, :, self.lines].astype(F32)
                for j in range(1, net.high):
                    total = total + grad_top[b, j, :, self.lines].astype(F32)
            self.clear("all")
            grad_all[mine, self.lines] = total.astype(BF16)
            for step, (who, device) in enumerate(self.low_peers()):
                here = grad_all.at[mine, self.lines]
                self.move("all", push(here, here, grad_sc.at[i, step], grad_qc.at[i, net.row_low], device))

        def finish(self, b):
            i = 2 * b + self.which
            each = PIECES // net.low
            for step, (who, device) in enumerate(self.low_peers()):
                there = grad_all.at[pl.ds(who * each, each), self.lines]
                push(there, there, grad_sc.at[i, step], grad_qc.at[i, who], device).wait_recv()
            for piece in range(PIECES):
                cols = slice(128 * piece, 128 * (piece + 1))
                grads_out[b, self.out_row : self.out_row + self.size, cols] = grad_all[piece, self.lines].astype(F32)

    early = Reduction(0, 96, 0)
    final = Reduction(96, 64, 96)

    order = (0, last) + tuple(range(1, last))
    norms = []
    mid_grads = {}
    out_grads = {}

    def open_block(b, rows):
        z = dot(a3s[b, rows], exp[b])
        a4, b4 = norms[b][3][2], norms[b][3][3]
        return z, (z * a4 + b4) + xs[b][rows].astype(F32)

    out_store = [frame_copy(yb, out_hbm, f, store_sem.at[f]) for f in range(frames)]

    for b in range(BLOCKS):
        norm1 = affine(first_sums[0], first_sums[1], count, mid(b, 0, 0), mid(b, 0, 1))
        if b == 0:
            gather(*plan["exp", 0])
        _, _, a1, b1 = norm1
        carry = (zero8(), zero8())
        if b > 0:
            for side in range(2):
                halo_sent(2 * (b - 1) + 1, 2 + b - 1, side)
        for f in order:
            alive = live(f)

            v = z1[b, f * HH : (f + 1) * HH].reshape(HH * WP, 256) * a1 + b1
            _, t = gelu_core(v)
            m = dot(gelu_value(v, t, half_mask(alive, HH)).astype(BF16), mix[...])
            z2[b, f, 1 : 1 + HH] = m.reshape(HH, WP, 256)
            if f in (0, last):
                halo_send[0 if f == 0 else 1] = m.astype(BF16).reshape(HH, WP, 256)
            carry = (carry[0] + fold(m), carry[1] + fold(m * m))
            if f in (0, last):
                halo_start(2 * b, b, 0 if f == 0 else 1)

        def emit_conv(f):
            pad = pad_mask[:WP, :128] * live(f)

            def emit(row, half, cols, c, carry):
                c = c * pad
                conv[b, f * HH + row, :, cols] = c
                if f in (0, last):
                    halo_send[0 if f == 0 else 1, row, :, cols] = c.astype(BF16)
                e = edge[b, f + 1, row_class(row), :, cols]
                s0, s1, s2 = carry
                return (s0 + fold(c), s1 + fold(c * c), s2 + fold(c * e))

            return emit

        def fill(side):
            present = lane > 0 if side == 0 else lane < lanes - 1

            @pl.when(present)
            def _():
                halo_wait(2 * b, b, side)

                def widen(j, _):
                    hz[side, pl.ds(1 + j * GROUP, GROUP)] = halo_recv[b, side, pl.ds(j * GROUP, GROUP)].astype(F32)
                    return 0

                lax.fori_loop(0, QUADS, widen, 0)

            @pl.when(jnp.logical_not(present))
            def _():
                def clear(j, _):
                    hz[side, pl.ds(1 + j * GROUP, GROUP)] = jnp.zeros((GROUP, WP, 256), F32)
                    return 0

                lax.fori_loop(0, QUADS, clear, 0)

        acc = [[zero8(128), zero8(128)] for _ in range(3)]
        for f in range(1, last):
            acc = convolve(z2.at[b], f, b, False, emit_conv(f), acc)
        if b == 0:
            gather_on(*plan["exp", 0])
        for side in range(2):
            fill(side)
            halo_sent(2 * b, b, side)
            f = 0 if side == 0 else last
            acc = convolve(z2.at[b], f, b, False, emit_conv(f), acc)
            halo_start(2 * b + 1, 2 + b, side)
        joined = [jnp.concatenate([flat_sum(a[0]), flat_sum(a[1])], axis=1) for a in acc]
        total_start(3 * b + 1, rows_of(flat_sum(carry[0]), flat_sum(carry[1]), *joined, *edge_sums[b]))
        if b == 0:
            gather_wait(*plan["exp", 0])
        else:
            gather_wait(*plan["exp", 1])
            tbuf[...] = exp[1].T
        got = total_finish(3 * b + 1)
        norm2 = affine(got[0:1], got[1:2], count, mid(b, 1, 0), mid(b, 1, 1))
        _, _, a2, b2 = norm2
        sc, scc, sce, se, see = [got[i : i + 1] for i in range(2, 7)]
        total3 = a2 * sc + b2 * se
        square3 = a2 * a2 * scc + 2.0 * a2 * b2 * sce + b2 * b2 * see
        norm3 = affine(total3, square3, count, mid(b, 2, 0), mid(b, 2, 1))
        _, _, a3, b3 = norm3

        norm3_pattern(b, a3, b2, b3)
        if b == 0:
            gather(*plan["red", 1])
            gather(*plan["mix", 1])

        def activate(i, _):
            rows, lines, where = trio(i)
            c = conv[b, lines].reshape(TRIO * WIDE, 256)
            acts = []
            for k, (f, j) in enumerate(where):
                v = c[WIDE * k : WIDE * (k + 1)] * (a3 * a2) + edge_rows(pat.at[f + 1], j)
                _, t = gelu_core(v)
                acts.append(squeeze(gelu_value(v, t, 0.5 * live(f))))
            a3s[b, rows] = jnp.concatenate(acts, axis=0).astype(BF16)
            return 0

        lax.fori_loop(0, trios, activate, 0)
        gram = dot_rows(a3s[b], a3s[b])
        line = dot(jnp.ones((16, frames * frame_rows), BF16), a3s[b])
        high = jnp.concatenate([gram, line], axis=0)
        split = high.astype(BF16)
        grown = dot(split, exp[b]) + dot((high - split.astype(F32)).astype(BF16), exp[b])
        squares = flat_sum(fold(grown[:256] * exp[b].astype(F32)))
        if b == 0:
            gather_on(*plan["red", 1])
            gather_on(*plan["mix", 1])
        total_start(3 * b + 2, rows_of(grown[256:257], squares))
        if b == 0:
            gather_wait(*plan["red", 1])
            tbuf[...] = red_t[1].T
        got = total_finish(3 * b + 2)
        norm4 = affine(wide_row(got, 0), wide_row(got, 4), count4, norm_out[b, 0:1], norm_out[b, 1:2])
        norms.append((norm1, norm2, norm3, norm4, (sc, scc, sce, se, see)))

        if b == 0:
            gather(*plan["exp", 1])

            def closing(i, carry):
                rows, lines, where = trio(i)
                _, pre = open_block(0, rows)
                results = []
                for (f, j), v in zip(where, pieces(pre, FLAT)):
                    _, t = gelu_core(v)
                    results.append(gelu_value(v, t, 0.5 * live(f)).astype(BF16))
                result = jnp.concatenate(results, axis=0)
                x1[rows] = result
                z = dot(result, tbuf[...])
                z1[1, lines] = spread(z).reshape(TRIO * GROUP, WP, 256)
                return (carry[0] + fold(z), carry[1] + fold(z * z))

            carry = lax.fori_loop(0, trios, closing, (zero8(), zero8()))
            gather_on(*plan["exp", 1])
            total_start(3, rows_of(flat_sum(carry[0]), flat_sum(carry[1])))
            gather_wait(*plan["mix", 1])
            mix[...] = mix_t[1].T
            got = total_finish(3)
            first_sums = (got[0:1], got[1:2])

    cot_load.wait()

    def ending(i, carry):
        rows, lines, where = trio(i)
        z, pre = open_block(1, rows)
        g = sb[rows]
        s0, s1 = carry
        for k, (f, j) in enumerate(where):
            here = slice(FLAT * k, FLAT * (k + 1))
            v, half = pre[here], 0.5 * live(f)
            square, t = gelu_core(v)
            part = pl.ds(pl.multiple_of((TRIO * i + k) * FLAT, FLAT), FLAT)
            yb[part] = gelu_value(v, t, half).astype(BF16)
            s = gelu_slope(v, square, t, half) * g[here].astype(F32)
            sb[part] = s.astype(BF16)
            s0, s1 = s0 + fold(s), s1 + fold(s * z[here])
        return s0, s1

    carry = lax.fori_loop(0, trios, ending, (zero8(1024), zero8(1024)))
    total_start(6, rows_of(flat_sum(carry[0]), flat_sum(carry[1])))
    for copy in out_store:
        copy.start()

    for b in reversed(range(BLOCKS)):
        turn = BLOCKS - 1 - b
        base = 6 + 3 * turn
        norm1, norm2, norm3, norm4, (sc, scc, sce, se, see) = norms[b]
        _, _, a1, b1 = norm1
        mean2, scale2, a2, b2 = norm2
        mean3, scale3, a3, b3 = norm3
        a4 = norm4[2]

        got = total_finish(base)
        slope4, bias4, gain_grad, shift_grad = back_affine(wide_row(got, 0), wide_row(got, 4), count4, norm4)
        out_grads[b] = (gain_grad, shift_grad)
        if turn == 0:
            for copy in out_store:
                copy.wait()
        for side in range(2):
            if turn == 0:
                halo_sent(2 * (BLOCKS - 1) + 1, 2 + BLOCKS - 1, side)
            else:
                halo_sent(2 * BLOCKS + turn - 1, b + 1, side)

        if turn > 0:
            early.to_rows(b + 1)
            final.to_side(b + 1)
        kind = 2 * BLOCKS + turn
        norm3_pattern(b, a3, b2, b3)
        acc = (zero8(), zero8(), zero8())
        for f in order:
            alive = live(f)

            rows = slice(f * frame_rows, (f + 1) * frame_rows)
            z = dot(a3s[b, rows], exp[b])
            d4 = (sb[rows].astype(F32) * a4 + (z * slope4 + bias4 * alive)).astype(BF16)
            yb[rows] = d4
            back = spread(dot(d4, tbuf[...]))
            for j in range(QUADS):
                c = conv[b, f * HH + GROUP * j : f * HH + GROUP * (j + 1)].reshape(WIDE, 256)
                v = c * (a3 * a2) + edge_rows(pat.at[f + 1], j)
                square, t = gelu_core(v)
                e3 = back[WIDE * j : WIDE * (j + 1)] * gelu_slope(v, square, t, 0.5)
                dz[f, 1 + GROUP * j : 1 + GROUP * (j + 1)] = e3.reshape(GROUP, WP, 256)
                if f in (0, last):
                    halo_send[0 if f == 0 else 1, GROUP * j : GROUP * (j + 1)] = e3.astype(BF16).reshape(GROUP, WP, 256)
                e = edge_rows(edge.at[b, f + 1], j)
                acc = (acc[0] + fold(e3), acc[1] + fold(e3 * c), acc[2] + fold(e3 * e))
            if f in (0, last):
                halo_start(kind, b, 0 if f == 0 else 1)
        total_start(base + 1, rows_of(*[flat_sum(a) for a in acc]))

        if turn > 0:
            early.clear("a")

        def expand_grad(i, _):
            cols = pl.ds(pl.multiple_of(i * 256, 256), 256)
            g = dot_rows(a3s[b], yb[:, cols])
            for who in range(lanes):
                for h in range(2):
                    early.put(who, 2 * i + h, 0, g[share * who : share * (who + 1), 128 * h : 128 * (h + 1)])
            return 0

        lax.fori_loop(0, 4, expand_grad, 0)
        if b > 0:
            tbuf[...] = exp[b - 1].T

        got = total_finish(base + 1)
        e3_sum, e3_conv, e3_edge = got[0:1], got[1:2], got[2:3]
        e3_third = a2 * e3_conv + b2 * e3_edge
        slope3, bias3, gain3, shift3 = back_affine(e3_sum, e3_third, count, norm3)
        third_conv = a2 * scc + b2 * sce
        third_edge = a2 * sce + b2 * see
        d3_conv = a3 * e3_conv + bias3 * sc + slope3 * third_conv
        d3_edge = a3 * e3_edge + bias3 * se + slope3 * third_edge
        slope2, bias2, gain2, shift2 = back_affine(d3_edge, d3_conv, count, norm2)

        if turn > 0:
            early.to_all(b + 1)
            final.to_rows(b + 1)
        for f in range(-1, frames + 1):
            live_pad = pad_mask[:WP] * live(f)
            for cls in range(3):
                pat[f + 1, cls] = bias3 * live_pad + (slope3 * b2) * edge[b, f + 1, cls]
        slope_c = slope3 * a2

        def to_d3(q, _):
            f = lax.div(q, QUADS)
            j = lax.rem(q, QUADS)
            rows = pl.ds(1 + j * GROUP, GROUP)
            c = conv[b, pl.ds(q * GROUP, GROUP)].reshape(WIDE, 256)
            e3 = dz[f, rows].reshape(WIDE, 256)
            d3 = e3 * a3 + c * slope_c + edge_rows(pat.at[f + 1], j)
            dz[f, rows] = d3.reshape(GROUP, WP, 256)
            return 0

        lax.fori_loop(0, frames * QUADS, to_d3, 0)

        def fill_back(side):
            present = lane > 0 if side == 0 else lane < lanes - 1
            f = -1 if side == 0 else frames

            @pl.when(present)
            def _():
                halo_wait(2 * b + 1, 2 + b, side)
                halo_wait(kind, b, side)

                def widen(j, _):
                    rows = pl.ds(j * GROUP, GROUP)
                    c = halo_recv[2 + b, side, rows].astype(F32).reshape(WIDE, 256)
                    e3 = halo_recv[b, side, rows].astype(F32).reshape(WIDE, 256)
                    d3 = e3 * a3 + c * slope_c + edge_rows(pat.at[f + 1], j)
                    hz[side, pl.ds(1 + j * GROUP, GROUP)] = d3.reshape(GROUP, WP, 256)
                    return 0

                lax.fori_loop(0, QUADS, widen, 0)

            @pl.when(jnp.logical_not(present))
            def _():
                def clear(j, _):
                    hz[side, pl.ds(1 + j * GROUP, GROUP)] = jnp.zeros((GROUP, WP, 256), F32)
                    return 0

                lax.fori_loop(0, QUADS, clear, 0)

        for side in range(2):
            fill_back(side)

        def emit_back(f):
            pad = pad_mask[:WP, :128] * live(f)

            def emit(row, half, cols, e2, carry):
                z = z2[b, f, row + 1, :, cols]
                d2 = (e2 * a2[:, cols] + (z * slope2[:, cols] + bias2[:, cols])) * pad
                d2s[f * HH + row, :, cols] = d2.astype(BF16)
                return carry

            return emit

        for f in range(frames):
            convolve(dz, f, b, True, emit_back(f), [])

        def unmixing(i, acc):
            _, lines, where = trio(i)
            e = dot(d2s[lines].reshape(TRIO * WIDE, 256), mix_t[b])
            z = z1[b, lines].reshape(TRIO * WIDE, 256)
            for k, (f, j) in enumerate(where):
                here = slice(WIDE * k, WIDE * (k + 1))
                v = z[here] * a1 + b1
                square, t = gelu_core(v)
                part = pl.ds((TRIO * i + k) * GROUP, GROUP)
                a1s[part] = gelu_value(v, t, half_mask(live(f), GROUP)).astype(BF16).reshape(GROUP, WP, 256)
                e1 = e[here] * gelu_slope(v, square, t, 0.5)
                conv[b, part] = e1.reshape(GROUP, WP, 256)
                acc = (acc[0] + fold(e1), acc[1] + fold(e1 * z[here]))
            return acc

        acc = lax.fori_loop(0, trios, unmixing, (zero8(), zero8()))
        if turn > 0:
            early.finish(b + 1)
        total_start(base + 2, rows_of(*[flat_sum(a) for a in acc]))

        for half in range(2):
            cols = slice(128 * half, 128 * (half + 1))
            taps_grad = tuple(zero8(128) for _ in range(KVOL))
            for f in range(frames):
                planes = []
                for dt in range(3):
                    g = f - (dt - 1)
                    planes.append(hz.at[0] if g < 0 else hz.at[1] if g > last else dz.at[g])
                shift_rows = b2[:, cols] * (pad_mask[:WP, :128] * live(f))

                def tap_rows(h, taps_grad):
                    a = z2[b, f, h + 1, :, cols] * a2[:, cols] + shift_rows
                    moved = [pltpu.roll(a, 1, 0), a, pltpu.roll(a, WP - 1, 0)]
                    new = list(taps_grad)
                    for dt in range(3):
                        for dh in range(3):
                            d = planes[dt][h + 1 - (dh - 1), :, cols]
                            for dw in range(3):
                                k = dt * 9 + dh * 3 + dw
                                new[k] = new[k] + fold(d * moved[dw])
                    return tuple(new)

                taps_grad = lax.fori_loop(0, HH, tap_rows, taps_grad)
            lines = jnp.concatenate(
                [flat_sum(t) for t in taps_grad] + [jnp.zeros((WP - KVOL, 128), F32)], axis=0
            )
            for r in range(4):
                part = jnp.concatenate([lines[8 * r : 8 * r + 8], zero8(128)], axis=0)
                for who in range(lanes):
                    early.put(who, 2 * r + half, 80, part)
        g = dot_rows(d2s[...].reshape(frames * HH * WP, 256), a1s[...].reshape(frames * HH * WP, 256))
        for who in range(lanes):
            for r in range(4):
                for h in range(2):
                    first = share * who + 16 * r
                    early.put(who, 2 * r + h, 64, g[first : first + 16, 128 * h : 128 * (h + 1)])
        early.to_pair(b)

        got = total_finish(base + 2)
        slope1, bias1, gain1, shift1 = back_affine(got[0:1], got[1:2], count, norm1)
        mid_grads[b] = ((gain1, shift1), (gain2, shift2), (gain3, shift3))

        early.to_side(b)
        def first_grad(i):
            rows, lines, where = trio(i)
            e1 = conv[b, lines].reshape(TRIO * WIDE, 256)
            z = z1[b, lines].reshape(TRIO * WIDE, 256)
            parts = []
            for k, (f, j) in enumerate(where):
                here = slice(WIDE * k, WIDE * (k + 1))
                alive = live(f)
                parts.append(squeeze(e1[here] * a1 + (z[here] * (slope1 * alive) + bias1 * alive)))
            d1 = jnp.concatenate(parts, axis=0).astype(BF16)
            a3s[b, rows] = d1
            return rows, where, d1

        def reduce_grad(i, _):
            cols = pl.ds(pl.multiple_of(i * 256, 256), 256)
            g = dot_rows(a3s[b], xs[b][:, cols])
            for who in range(lanes):
                for h in range(2):
                    final.put(who, 2 * i + h, 0, g[share * who : share * (who + 1), 128 * h : 128 * (h + 1)])
            return 0

        if b > 0:

            def passing(i, carry):
                rows, where, d1 = first_grad(i)
                g = dot(d1, red_t[b]) + sb[rows].astype(F32)
                z, pre = open_block(b - 1, rows)
                s0, s1 = carry
                for k, (f, j) in enumerate(where):
                    here = slice(FLAT * k, FLAT * (k + 1))
                    v = pre[here]
                    square, t = gelu_core(v)
                    s = gelu_slope(v, square, t, 0.5 * live(f)) * g[here]
                    sb[pl.ds(pl.multiple_of((TRIO * i + k) * FLAT, FLAT), FLAT)] = s.astype(BF16)
                    s0, s1 = s0 + fold(s), s1 + fold(s * z[here])
                return s0, s1

            carry = lax.fori_loop(0, trios, passing, (zero8(1024), zero8(1024)))
            total_start(base + 3, rows_of(flat_sum(carry[0]), flat_sum(carry[1])))
            lax.fori_loop(0, 4, reduce_grad, 0)
            final.to_pair(b)
        else:
            final.to_all(b + 1)

            def only_d1(i, _):
                first_grad(i)
                return 0

            lax.fori_loop(0, trios, only_d1, 0)
            final.clear("a")
            lax.fori_loop(0, 4, reduce_grad, 0)
            final.to_pair(b)
            early.to_rows(b)
            steps = (lambda: final.to_side(b), lambda: early.to_all(b), lambda: None)
            gtok_store = [frame_copy(yb, gtok_hbm, f, store_sem.at[f]) for f in range(frames)]
            for f in range(frames):
                rows = slice(f * frame_rows, (f + 1) * frame_rows)
                yb[rows] = (dot(a3s[b, rows], red_t[b]) + sb[rows].astype(F32)).astype(BF16)
                gtok_store[f].start()
                if f < len(steps):
                    steps[f]()
            final.finish(b + 1)
            final.to_rows(b)
            early.finish(b)
            final.to_all(b)
            final.finish(b)

    for b in range(BLOCKS):
        for k in range(3):
            for w in range(2):
                r = (b * 3 + k) * 2 + w
                gmid_out[r : r + 1] = mid_grads[b][k][w]
        for w in range(2):
            gout_out[2 * b + w : 2 * b + w + 1] = out_grads[b][w]

    for copy in gtok_store:
        copy.wait()
    early.clear("a", "b", "all")
    final.clear("a", "b", "all")
    for copy in late:
        copy.wait_send()
    for side in range(2):
        halo_sent(2 * BLOCKS + BLOCKS - 1, 0, side)


def whole_call(groups, lanes, counts, tokens, cotangent, reduce_loc, mix_loc, expand_loc, small_loc, norm_out):
    rows = tokens.shape[0]
    frames = rows // (HH * WW)
    whole = pl.BlockSpec(memory_space=pltpu.VMEM)
    hbm = pl.BlockSpec(memory_space=pl.ANY)
    dma = pltpu.SemaphoreType.DMA
    low, high = stages(groups)
    far = low * (lanes // 2)
    lines = frames * HH
    sums = 6 * BLOCKS
    kinds = 3 * BLOCKS
    shape = jax.ShapeDtypeStruct
    return pl.pallas_call(
        functools.partial(whole_kernel, groups, lanes),
        out_shape=(
            shape((rows, 1024), BF16),
            shape((rows, 1024), BF16),
            shape((BLOCKS, 160, 1024), F32),
            shape((BLOCKS * 6, 256), F32),
            shape((BLOCKS * 2, 1024), F32),
        ),
        in_specs=[pl.BlockSpec(memory_space=pltpu.SMEM)] + [hbm] * 6 + [whole],
        out_specs=[hbm] * 2 + [whole] * 3,
        scratch_shapes=[
            pltpu.VMEM((rows, 1024), BF16),
            pltpu.VMEM((rows, 1024), BF16),
            pltpu.VMEM((rows, 1024), BF16),
            pltpu.VMEM((rows, 1024), BF16),
            pltpu.VMEM((BLOCKS, 256, 1024), BF16),
            pltpu.VMEM((BLOCKS, 256, 1024), BF16),
            pltpu.VMEM((1024, 256), BF16),
            pltpu.VMEM((BLOCKS, 256, 256), BF16),
            pltpu.VMEM((256, 256), BF16),
            pltpu.VMEM((lanes,) + small_loc.shape, F32),
            pltpu.VMEM((2 * small_loc.shape[0], 256), F32),
            pltpu.VMEM((BLOCKS, lines, WP, 256), F32),
            pltpu.VMEM((lines, WP, 256), BF16),
            pltpu.VMEM((BLOCKS, frames, HH + 2, WP, 256), F32),
            pltpu.VMEM((frames, HH + 2, WP, 256), F32),
            pltpu.VMEM((2, HH + 2, WP, 256), F32),
            pltpu.VMEM((BLOCKS, lines, WP, 256), F32),
            pltpu.VMEM((BLOCKS, rows, 256), BF16),
            pltpu.VMEM((BLOCKS, frames + 2, 3, WP, 256), F32),
            pltpu.VMEM((frames + 2, 3, WP, 256), F32),
            pltpu.VMEM((lines, WP, 256), BF16),
            pltpu.VMEM((2, HH, WP, 256), BF16),
            pltpu.VMEM((2 * BLOCKS, 2, HH, WP, 256), BF16),
            pltpu.VMEM((lanes, PIECES, 160, 128), BF16),
            pltpu.VMEM((3, PIECES, 160, 128), BF16),
            pltpu.VMEM((PIECES, 160, 128), BF16),
            pltpu.VMEM((low, PIECES // low, 160, 128), BF16),
            pltpu.VMEM((PIECES, 160, 128), BF16),
            pltpu.VMEM((BLOCKS, high, PIECES // low, 160 if high > 1 else 16, 128), BF16),
            pltpu.VMEM((sums, 2, 16, 128), F32),
            pltpu.VMEM((sums, far, 16, 128), F32),
            pltpu.VMEM((sums, high, 16, 128), F32),
            dma((sums,)),
            dma((sums,)),
            dma((sums, far)),
            dma((sums, far)),
            dma((sums, high)),
            dma((sums, high)),
            dma((7, 4)),
            dma((7, lanes)),
            dma((kinds, 2)),
            dma((kinds, 2)),
            dma((frames + 1,)),
            dma((frames,)),
            dma((2 * BLOCKS, 3)),
            dma((2 * BLOCKS, 3)),
            dma((2 * BLOCKS, low)),
            dma((2 * BLOCKS, low)),
            dma((2 * BLOCKS, low)),
            dma((2 * BLOCKS, low)),
            dma((2 * BLOCKS, high)),
            dma((2 * BLOCKS, high)),
        ],
        compiler_params=pltpu.CompilerParams(
            collective_id=1, has_side_effects=True, vmem_limit_bytes=63 * 2**20
        ),
    )(counts, tokens, cotangent, reduce_loc, mix_loc, expand_loc, small_loc, norm_out)


def descend(weight, moment, grad):
    moment_new = MOMENTUM * moment + grad + DECAY * weight
    return (weight - LEARN_RATE * moment_new, moment_new)


def shards(
    tokens,
    frame_counts,
    cotangent,
    w_reduce,
    w_mix,
    w_depth,
    w_expand,
    norm_mid,
    norm_out,
    moment_reduce,
    moment_mix,
    moment_depth,
    moment_expand,
    moment_mid,
    moment_out,
):
    lane = lax.axis_index("chan")
    lanes = lax.axis_size("chan")
    narrow = w_reduce.shape[2]
    small = jnp.concatenate([w_depth.reshape(-1, narrow), norm_mid.reshape(-1, narrow)], axis=0)
    small = jnp.pad(small, ((0, -small.shape[0] % 16), (0, 0)))
    small = jnp.concatenate(jnp.split(small, 2, axis=0), axis=1)
    output, grad_tokens, reduced, gmid, gout = whole_call(
        lax.axis_size("dp"),
        lanes,
        frame_counts,
        tokens,
        cotangent,
        jnp.swapaxes(w_reduce, 1, 2).astype(BF16),
        jnp.swapaxes(w_mix, 1, 2).astype(BF16),
        w_expand.astype(BF16),
        small,
        norm_out,
    )
    gmix = reduced[:, 64:80].reshape(BLOCKS, 16, 4, 256).swapaxes(1, 2).reshape(BLOCKS, narrow, 256)
    gdep = reduced[:, 80:88].reshape(BLOCKS, 8, 4, 256).swapaxes(1, 2).reshape(BLOCKS, WP, 256)[:, :KVOL]
    grads = (
        jnp.swapaxes(reduced[:, 96:], 1, 2),
        jnp.swapaxes(gmix, 1, 2),
        lax.dynamic_slice_in_dim(gdep, lane * narrow, narrow, 2),
        reduced[:, :64],
        lax.dynamic_slice_in_dim(gmid.reshape(BLOCKS, 3, 2, -1), lane * narrow, narrow, 3),
        gout.reshape(BLOCKS, 2, -1),
    )
    params = (w_reduce, w_mix, w_depth, w_expand, norm_mid, norm_out)
    moments = (moment_reduce, moment_mix, moment_depth, moment_expand, moment_mid, moment_out)
    updated = [descend(w, m, g) for w, m, g in zip(params, moments, grads)]
    return (output, grad_tokens) + grads + tuple(u[0] for u in updated) + tuple(u[1] for u in updated)


def solution(mesh):
    rows = P(("dp", "chan"), None)
    weights = (
        P(None, None, "chan"),
        P(None, None, "chan"),
        P(None, None, "chan"),
        P(None, "chan", None),
        P(None, None, None, "chan"),
        P(),
    )
    return jax.shard_map(
        shards,
        mesh=mesh,
        in_specs=(rows, P("dp"), rows) + weights + weights,
        out_specs=(rows, rows) + weights + weights + weights,
        check_vma=False,
    )
```

```python
import functools

import jax
import jax.numpy as jnp
from jax import lax
from jax.experimental import pallas as pl
from jax.experimental.pallas import tpu as pltpu
from jax.sharding import PartitionSpec as P

FRAMES = 12
HH = 28
WW = 28
WP = 32
KVOL = 27
BLOCKS = 2
GROUP = 4
QUADS = HH // GROUP
FLAT = GROUP * WW
WIDE = GROUP * WP
PIECES = 8
TRIO = 3

EPS = 1e-05
LEARN_RATE = 0.001
MOMENTUM = 0.9
DECAY = 0.0001
MESH = pl.DeviceIdType.MESH
F32 = jnp.float32
BF16 = jnp.bfloat16
ROOT = 0.7978845608028654
CUBE = 0.044715


def gelu_core(v):
    square = v * v
    return square, jnp.tanh(v * (ROOT + (ROOT * CUBE) * square))


def gelu_value(v, t, half):
    h = half * v
    return h * t + h


def gelu_slope(v, square, t, half):
    r = v * (half * ROOT + (half * (3.0 * ROOT * CUBE)) * square)
    return (half * t + half) + (r - r * (t * t))


def dot_rows(left, right):
    return lax.dot_general(left, right, (((0,), (0,)), ((), ())), preferred_element_type=F32)


def dot(left, right):
    return jnp.dot(left, right, preferred_element_type=F32)


def fold(v):
    return jnp.sum(v.reshape(v.shape[0] // 8, 8, v.shape[1]), axis=0)


def spread(v):
    gap = jnp.zeros((WP - WW, v.shape[1]), v.dtype)
    parts = []
    for h in range(v.shape[0] // WW):
        parts += [v[WW * h : WW * (h + 1)], gap]
    return jnp.concatenate(parts, axis=0)


def squeeze(v):
    return jnp.concatenate([v[WP * h : WP * h + WW] for h in range(v.shape[0] // WP)], axis=0)


def pieces(v, rows):
    return [v[rows * k : rows * (k + 1)] for k in range(v.shape[0] // rows)]


def rows_of(*vectors):
    parts = []
    for v in vectors:
        parts += pieces_of(v)
    n = 4 if len(parts) <= 4 else 8
    out = []
    for side in range(2):
        out += [v[:, 128 * side : 128 * (side + 1)] for v in parts]
        if len(parts) < n:
            out.append(jnp.zeros((n - len(parts), 128), F32))
    return jnp.concatenate(out, axis=0)


def pieces_of(v):
    return [v[:, 256 * i : 256 * (i + 1)] for i in range(v.shape[1] // 256)]


def flat_sum(v):
    return jnp.sum(v, axis=0, keepdims=True)


def wide_row(v, first):
    return jnp.concatenate([v[first + i : first + i + 1] for i in range(4)], axis=1)


class Net:
    def __init__(self, groups, lanes):
        self.lanes = lanes
        self.low, self.high = stages(groups)
        self.row = lax.axis_index("dp")
        self.lane = lax.axis_index("chan")
        self.core = lax.rem(self.lane, 2)
        self.side = lax.div(self.lane, 2)
        self.half = lanes // 2
        self.row_low = lax.rem(self.row, self.low)
        self.row_high = lax.div(self.row, self.low)

    def near(self):
        return [(1 - self.core, (self.row, self.side * 2 + 1 - self.core))]

    def far(self):
        out = []
        for o in sorted(range(self.low), key=lambda o: abs(2 * o - self.low - 1)):
            for p in range(self.half):
                if o or p:
                    row = lax.rem(self.row_low + o, self.low)
                    side = lax.rem(self.side + p, self.half)
                    out.append((row * self.half + side, (self.row_high * self.low + row, side * 2 + self.core)))
        return out

    def far_slot(self):
        return self.row_low * self.half + self.side

    def top(self):
        rows = [lax.rem(self.row_high + o, self.high) for o in range(1, self.high)]
        return [(row, (row * self.low + self.row_low, self.lane)) for row in rows]

    def pair(self):
        lane = self.side * 2 + 1 - self.core
        return lane, (self.row, lane)

    def across(self):
        lane = (1 - self.side) * 2 + self.core
        return lane, (self.row, lane)

    def corner(self):
        return (1 - self.side) * 2 + 1 - self.core


def stages(groups):
    low = min(groups, 8)
    return low, groups // low


def push(src, dst, send, recv, device):
    copy = pltpu.make_async_remote_copy(
        src_ref=src, dst_ref=dst, send_sem=send, recv_sem=recv, device_id=device, device_id_type=MESH
    )
    return copy


def whole_kernel(
    groups,
    lanes,
    counts,
    tokens,
    cotangent,
    reduce_loc,
    mix_loc,
    expand_loc,
    small_loc,
    norm_out,
    out_hbm,
    gtok_hbm,
    grads_out,
    gmid_out,
    gout_out,
    x0,
    x1,
    yb,
    sb,
    red_t,
    exp,
    tbuf,
    mix_t,
    mix,
    small_in,
    small,
    z1,
    a1s,
    z2,
    dz,
    hz,
    conv,
    a3s,
    edge,
    pat,
    d2s,
    halo_send,
    halo_recv,
    grad_a,
    grad_ra,
    grad_b,
    grad_rb,
    grad_all,
    grad_top,
    near,
    far,
    top,
    near_send,
    near_recv,
    far_send,
    far_recv,
    top_send,
    top_recv,
    gather_send,
    gather_recv,
    halo_ssem,
    halo_rsem,
    load_sem,
    store_sem,
    grad_sa,
    grad_qa,
    grad_sb,
    grad_qb,
    grad_sc,
    grad_qc,
    grad_st,
    grad_qt,
    weight_sem,
):
    net = Net(groups, lanes)
    lane = net.lane
    frames = tokens.shape[0] // (HH * WW)
    frame_rows = HH * WW
    last = frames - 1
    count_here = counts[0]
    xs = (x0, x1)

    def live(frame):
        position = lane * frames + frame
        return jnp.where((position >= 0) & (position < count_here), 1.0, 0.0)

    def frame_copy(src, dst, f, sem):
        rows = pl.ds(f * frame_rows, frame_rows)
        return pltpu.make_async_copy(src.at[rows], dst.at[rows], sem)

    loads = [frame_copy(tokens, x0, f, load_sem.at[f]) for f in range(frames)]
    cot_load = pltpu.make_async_copy(cotangent, sb, load_sem.at[frames])
    for copy in loads:
        copy.start()
    cot_load.start()
    weight_loads = {}
    for b in range(BLOCKS):
        places = [
            ("red", reduce_loc.at[b], grads_out.at[b, pl.ds(0, 64)]),
            ("exp", expand_loc.at[b], grads_out.at[b, pl.ds(64, 64)]),
            ("mix", mix_loc.at[b, pl.ds(0, 32)], grads_out.at[b, pl.ds(128, 32), pl.ds(0, 256)]),
            ("mix", mix_loc.at[b, pl.ds(32, 32)], grads_out.at[b, pl.ds(128, 32), pl.ds(256, 256)]),
        ]
        for k, (name, src, dst) in enumerate(places):
            copy = pltpu.make_async_copy(src, dst, weight_sem.at[b, k])
            copy.start()
            weight_loads.setdefault((name, b), []).append(copy)

    barrier = pltpu.get_barrier_semaphore()
    friends = [d for peers in (net.near(), net.far(), net.top()) for _, d in peers] + [(net.row, net.corner())]
    for device in friends:
        pl.semaphore_signal(barrier, inc=1, device_id=device, device_id_type=MESH)
    pl.semaphore_wait(barrier, len(friends))

    own = net.lane
    share = red_t.shape[1] // lanes
    late = []

    def gather(name, b):
        slot, dst_of = plan[name, b]
        mine = dst_of(own)
        for copy in weight_loads.get((name, b), []):
            copy.wait()
        if name == "red":
            mine[...] = grads_out[b, :64].astype(BF16)
        elif name == "exp":
            mine[...] = grads_out[b, 64:128].astype(BF16)
        elif name == "mix":
            parts = [grads_out[b, 128:160, :256], grads_out[b, 128:160, 256:512]]
            mine[...] = jnp.concatenate(parts, axis=0).astype(BF16)
        else:
            mine[...] = small_loc[...]
        for step, (_, device) in enumerate((net.pair(), net.across())):
            copy = push(mine, mine, gather_send.at[slot, step], gather_recv.at[slot, own], device)
            copy.start()
            late.append(copy)

    def gather_on(name, b):
        slot, dst_of = plan[name, b]
        who, device = net.across()
        piece = dst_of(who)
        push(piece, piece, gather_send.at[slot, 1], gather_recv.at[slot, who], device).wait_recv()
        copy = push(piece, piece, gather_send.at[slot, 2], gather_recv.at[slot, who], net.pair()[1])
        copy.start()
        late.append(copy)

    def gather_wait(name, b):
        slot, dst_of = plan[name, b]
        for who in (net.pair()[0], net.corner()):
            push(dst_of(who), dst_of(who), gather_send.at[slot, 0], gather_recv.at[slot, who], net.pair()[1]).wait_recv()

    def block_rows(ref, b):
        return lambda who: ref.at[b, pl.ds(pl.multiple_of(who * share, share), share)]

    plan = {
        ("red", 0): (0, block_rows(red_t, 0)),
        ("mix", 0): (1, block_rows(mix_t, 0)),
        ("small", 0): (2, lambda who: small_in.at[who]),
        ("exp", 0): (3, block_rows(exp, 0)),
        ("red", 1): (4, block_rows(red_t, 1)),
        ("mix", 1): (5, block_rows(mix_t, 1)),
        ("exp", 1): (6, block_rows(exp, 1)),
    }
    for name in (("red", 0), ("mix", 0), ("small", 0)):
        gather(*name)

    used = {}
    travelling = []

    def total_start(i, value):
        size = value.shape[0]
        used[i] = size
        turn = i % 2
        gone, travelling[:] = list(travelling), []
        near[turn, net.core, :size] = value
        for who, device in net.near():
            mine = near.at[turn, net.core, pl.ds(0, size)]
            copy = push(mine, mine, near_send.at[i], near_recv.at[i], device)
            copy.start()
            travelling.append(copy)
            copy.wait_recv()
        far[turn, net.far_slot(), :size] = near[turn, 0, :size] + near[turn, 1, :size]
        for step, (who, device) in enumerate(net.far()):
            mine = far.at[turn, net.far_slot(), pl.ds(0, size)]
            copy = push(mine, mine, far_send.at[i, step], far_recv.at[i, net.far_slot()], device)
            copy.start()
            travelling.append(copy)
        for copy in gone:
            copy.wait_send()

    def total_finish(i):
        size = used[i]
        turn = i % 2
        for step, (who, device) in enumerate(net.far()):
            there = far.at[turn, who, pl.ds(0, size)]
            push(there, there, far_send.at[i, step], far_recv.at[i, who], device).wait_recv()
        total = far[turn, 0, :size]
        for j in range(1, net.low * net.half):
            total = total + far[turn, j, :size]
        if net.high > 1:
            mine = top.at[turn, net.row_high, pl.ds(0, size)]
            top[turn, net.row_high, :size] = total
            for step, (who, device) in enumerate(net.top()):
                copy = push(mine, mine, top_send.at[i, step], top_recv.at[i, net.row_high], device)
                copy.start()
                travelling.append(copy)
            for step, (who, device) in enumerate(net.top()):
                there = top.at[turn, who, pl.ds(0, size)]
                push(there, there, top_send.at[i, step], top_recv.at[i, who], device).wait_recv()
            total = top[turn, 0, :size]
            for j in range(1, net.high):
                total = total + top[turn, j, :size]
        return jnp.concatenate([total[: size // 2], total[size // 2 :]], axis=1)

    def halo_copy(kind, slot, side):
        step = -1 if side == 0 else 1
        return push(
            halo_send.at[side],
            halo_recv.at[slot, 1 - side],
            halo_ssem.at[kind, side],
            halo_rsem.at[kind, 1 - side],
            (net.row, lane + step),
        )

    def sends_to(side):
        return lane > 0 if side == 0 else lane < lanes - 1

    def halo_start(kind, slot, side):
        @pl.when(sends_to(side))
        def _():
            halo_copy(kind, slot, side).start()

    def halo_sent(kind, slot, side):
        @pl.when(sends_to(side))
        def _():
            halo_copy(kind, slot, side).wait_send()

    def halo_wait(kind, slot, side):
        step = -1 if side == 0 else 1
        push(
            halo_send.at[1 - side],
            halo_recv.at[slot, side],
            halo_ssem.at[kind, 1 - side],
            halo_rsem.at[kind, side],
            (net.row, lane + step),
        ).wait_recv()

    column = lax.broadcasted_iota(jnp.int32, (WIDE, 256), 0) % WP
    pad_mask = (column < WW).astype(F32)

    def half_mask(alive, lines):
        return jnp.concatenate([pad_mask[:WP] * (0.5 * alive)] * lines, axis=0)

    def affine(total, square, count, gain, shift):
        mean = total / count
        var = square / count - mean * mean
        scale = lax.rsqrt(var + EPS)
        return mean, scale, gain * scale, shift - mean * (gain * scale)

    def back_affine(e_sum, ez_sum, count, norm):
        mean, scale, a, _ = norm
        gain_grad = scale * (ez_sum - mean * e_sum)
        slope = -a * scale * gain_grad / count
        bias = -a * e_sum / count - slope * mean
        return slope, bias, gain_grad, e_sum

    def zero8(n=256):
        return jnp.zeros((8, n), F32)

    blank = jnp.zeros((WP, 256), F32)
    for f in range(frames):
        for b in range(BLOCKS):
            z2[b, f, 0] = blank
            z2[b, f, HH + 1] = blank
        dz[f, 0] = blank
        dz[f, HH + 1] = blank
    for side in range(2):
        hz[side, 0] = blank
        hz[side, HH + 1] = blank

    for name in (("red", 0), ("mix", 0), ("small", 0)):
        gather_on(*name)
    gather_wait("red", 0)
    tbuf[...] = red_t[0].T

    carry = (zero8(), zero8())
    for f in range(frames):
        loads[f].wait()
        alive = live(f)

        z = dot(x0[f * frame_rows : (f + 1) * frame_rows], tbuf[...])
        z1[0, f * HH : (f + 1) * HH] = spread(z).reshape(HH, WP, 256)
        carry = (carry[0] + fold(z) * alive, carry[1] + fold(z * z) * alive)

    alive_all = sum(live(f) for f in range(frames)) * (HH * WW)
    here_count = jnp.full((1, 256), 1.0, F32) * alive_all
    total_start(0, rows_of(flat_sum(carry[0]), flat_sum(carry[1]), here_count))

    gather_wait("small", 0)
    half_rows = small_loc.shape[0]
    for side in range(2):
        here = [small_in[who, :, 64 * side : 64 * (side + 1)] for who in range(lanes)]
        small[half_rows * side : half_rows * (side + 1)] = jnp.concatenate(here, axis=1)

    def mid(b, norm, which):
        r = BLOCKS * KVOL + (b * 3 + norm) * 2 + which
        return small[r : r + 1]

    edge_sums = []
    pattern_col = lax.broadcasted_iota(jnp.int32, (WP, 256), 0)
    for b in range(BLOCKS):
        taps_b = [[small[b * KVOL + dt * 9 + k : b * KVOL + dt * 9 + k + 1] for k in range(9)] for dt in range(3)]
        se = jnp.zeros((1, 256), F32)
        see = jnp.zeros((1, 256), F32)
        for f in range(-1, frames + 1):
            here = live(f)
            t = [
                here * (live(f - 1) * taps_b[0][k] + here * taps_b[1][k] + live(f + 1) * taps_b[2][k])
                for k in range(9)
            ]
            for cls in range(3):
                use = [dh for dh in range(3) if not (cls == 0 and dh == 0) and not (cls == 2 and dh == 2)]
                col = []
                for dw in range(3):
                    v = t[use[0] * 3 + dw]
                    for dh in use[1:]:
                        v = v + t[dh * 3 + dw]
                    col.append(v)
                inner = col[0] + col[1] + col[2]
                left, right = col[1] + col[2], col[0] + col[1]
                edge[b, f + 1, cls] = jnp.where(
                    pattern_col == 0,
                    left,
                    jnp.where(pattern_col == WW - 1, right, jnp.where(pattern_col < WW - 1, inner, 0.0)),
                )
                if 0 <= f < frames:
                    times = 1.0 if cls != 1 else HH - 2.0
                    se = se + times * (left + right + (WW - 2.0) * inner)
                    see = see + times * (left * left + right * right + (WW - 2.0) * (inner * inner))
        edge_sums.append((se, see))

    gather_wait("mix", 0)
    mix[...] = mix_t[0].T

    got = total_finish(0)
    count = got[2:3]
    count4 = jnp.concatenate([count] * 4, axis=1)
    first_sums = (got[0:1], got[1:2])

    def edge_rows(ref, j):
        top = jnp.where(j == 0, 0, 1)
        bottom = jnp.where(j == QUADS - 1, 2, 1)
        middle = ref[1]
        return jnp.concatenate([ref[top], middle, middle, ref[bottom]], axis=0)

    def trio(i):
        rows = pl.ds(pl.multiple_of(i * (TRIO * FLAT), TRIO * FLAT), TRIO * FLAT)
        lines = pl.ds(i * (TRIO * GROUP), TRIO * GROUP)
        where = []
        for k in range(TRIO):
            q = TRIO * i + k
            where.append((lax.div(q, QUADS), lax.rem(q, QUADS)))
        return rows, lines, where

    trios = frames * QUADS // TRIO

    def norm3_pattern(b, a3, b2, b3):
        for f in range(frames):
            for cls in range(3):
                pat[f + 1, cls] = edge[b, f + 1, cls] * (a3 * b2) + b3

    def row_class(h):
        return jnp.where(h == 0, 0, jnp.where(h == HH - 1, 2, 1))

    def convolve(local, f, b, flip, emit, acc):
        done = []
        for half in range(2):
            cols = slice(128 * half, 128 * (half + 1))
            kern = [small[b * KVOL + k : b * KVOL + k + 1, cols] for k in range(KVOL)]
            if flip:
                kern = kern[::-1]
            planes = []
            for dt in range(3):
                g = f + dt - 1
                planes.append(hz.at[0] if g < 0 else hz.at[1] if g > last else local.at[g])

            def two_rows(i, carry):
                h = 2 * i
                part = [[None] * 3 for _ in range(2)]
                for dt in range(3):
                    for rr in range(4):
                        v = planes[dt][h + rr, :, cols]
                        for o in range(2):
                            dh = rr - o
                            if 0 <= dh < 3:
                                for dw in range(3):
                                    term = kern[dt * 9 + dh * 3 + dw] * v
                                    part[o][dw] = term if part[o][dw] is None else part[o][dw] + term
                for o in range(2):
                    p = part[o]
                    c = p[1] + pltpu.roll(p[0], 1, 0) + pltpu.roll(p[2], WP - 1, 0)
                    carry = emit(h + o, half, cols, c, carry)
                return carry

            done.append(lax.fori_loop(0, HH // 2, two_rows, tuple(a[half] for a in acc)))
        return [[done[0][k], done[1][k]] for k in range(len(acc))]

    class Reduction:
        def __init__(self, first, size):
            self.lines = pl.ds(first, size)
            self.first, self.size = first, size
            self.which = 0 if first == 0 else 1
            self.open = {"a": [], "b": [], "all": []}

        def put(self, who, piece, first, value):
            grad_a[who, piece, pl.ds(self.lines.start + first, value.shape[0])] = value.astype(BF16)

        def clear(self, *names):
            for name in names:
                for copy in self.open[name]:
                    copy.wait_send()
                self.open[name] = []

        def move(self, name, copy):
            copy.start()
            self.open[name].append(copy)

        def pair_copy(self, b, side):
            i = 2 * b + self.which
            src, dst = grad_a.at[2 * side + 1 - net.core, :, self.lines], grad_ra.at[side, :, self.lines]
            return push(src, dst, grad_sa.at[i, side], grad_qa.at[i, side], net.pair()[1])

        def to_pair(self, b):
            for side in range(2):
                self.move("a", self.pair_copy(b, side))

        def across_copy(self, b):
            i = 2 * b + self.which
            src, dst = grad_a.at[net.across()[0], :, self.lines], grad_ra.at[2, :, self.lines]
            return push(src, dst, grad_sa.at[i, 2], grad_qa.at[i, 2], net.across()[1])

        def to_side(self, b):
            for side in range(2):
                self.pair_copy(b, side).wait_recv()
            other = net.across()[0]

            def add(piece, _):
                mine, theirs = grad_a[other, piece, self.lines], grad_ra[1 - net.side, piece, self.lines]
                grad_a[other, piece, self.lines] = (mine.astype(F32) + theirs.astype(F32)).astype(BF16)
                return 0

            lax.fori_loop(0, PIECES, add, 0)
            self.move("a", self.across_copy(b))

        def low_peers(self):
            rows = [lax.rem(net.row_low + o, net.low) for o in range(1, net.low)]
            return [(row, (net.row_high * net.low + row, lane)) for row in rows]

        def to_rows(self, b):
            i = 2 * b + self.which
            self.across_copy(b).wait_recv()
            self.clear("b")

            def add(piece, _):
                total = grad_a[own, piece, self.lines].astype(F32) + grad_ra[net.side, piece, self.lines].astype(F32)
                grad_b[piece, self.lines] = (total + grad_ra[2, piece, self.lines].astype(F32)).astype(BF16)
                return 0

            lax.fori_loop(0, PIECES, add, 0)
            each = PIECES // net.low
            for step, (who, device) in enumerate(self.low_peers()):
                src = grad_b.at[pl.ds(who * each, each), self.lines]
                dst = grad_rb.at[net.row_low, :, self.lines]
                self.move("b", push(src, dst, grad_sb.at[i, step], grad_qb.at[i, net.row_low], device))

        def to_all(self, b):
            i = 2 * b + self.which
            each = PIECES // net.low
            mine = pl.ds(net.row_low * each, each)
            for step, (who, device) in enumerate(self.low_peers()):
                src, dst = grad_b.at[mine, self.lines], grad_rb.at[who, :, self.lines]
                push(src, dst, grad_sb.at[i, step], grad_qb.at[i, who], device).wait_recv()
            total = grad_b[mine, self.lines].astype(F32)
            for who, _device in self.low_peers():
                total = total + grad_rb[who, :, self.lines].astype(F32)
            if net.high > 1:
                grad_top[b, net.row_high, :, self.lines] = total.astype(BF16)
                for step, (who, device) in enumerate(net.top()):
                    here = grad_top.at[b, net.row_high, :, self.lines]
                    self.move("all", push(here, here, grad_st.at[i, step], grad_qt.at[i, net.row_high], device))
                for step, (who, device) in enumerate(net.top()):
                    there = grad_top.at[b, who, :, self.lines]
                    push(there, there, grad_st.at[i, step], grad_qt.at[i, who], device).wait_recv()
                self.clear("all")
                total = grad_top[b, 0, :, self.lines].astype(F32)
                for j in range(1, net.high):
                    total = total + grad_top[b, j, :, self.lines].astype(F32)
            self.clear("all")
            grad_all[mine, self.lines] = total.astype(BF16)
            for step, (who, device) in enumerate(self.low_peers()):
                here = grad_all.at[mine, self.lines]
                self.move("all", push(here, here, grad_sc.at[i, step], grad_qc.at[i, net.row_low], device))

        def finish(self, b):
            i = 2 * b + self.which
            each = PIECES // net.low
            for step, (who, device) in enumerate(self.low_peers()):
                there = grad_all.at[pl.ds(who * each, each), self.lines]
                push(there, there, grad_sc.at[i, step], grad_qc.at[i, who], device).wait_recv()
            for piece in range(PIECES):
                cols = slice(128 * piece, 128 * (piece + 1))
                grads_out[b, self.first : self.first + self.size, cols] = grad_all[piece, self.lines].astype(F32)

    early = [Reduction(0, 96 if b == 0 else 80) for b in range(BLOCKS)]
    final = [Reduction(96, 64 if b == 0 else 80) for b in range(BLOCKS)]

    order = (0, last) + tuple(range(1, last))
    norms = []
    mid_grads = {}
    out_grads = {}

    def open_block(b, rows):
        z = dot(a3s[b, rows], exp[b])
        a4, b4 = norms[b][3][2], norms[b][3][3]
        return z, (z * a4 + b4) + xs[b][rows].astype(F32)

    out_store = [frame_copy(yb, out_hbm, f, store_sem.at[f]) for f in range(frames)]

    for b in range(BLOCKS):
        norm1 = affine(first_sums[0], first_sums[1], count, mid(b, 0, 0), mid(b, 0, 1))
        if b == 0:
            gather("exp", 0)
        _, _, a1, b1 = norm1
        carry = (zero8(), zero8())
        if b > 0:
            for side in range(2):
                halo_sent(2 * (b - 1) + 1, 2 + b - 1, side)
        for f in order:
            alive = live(f)

            v = z1[b, f * HH : (f + 1) * HH].reshape(HH * WP, 256) * a1 + b1
            _, t = gelu_core(v)
            m = dot(gelu_value(v, t, half_mask(alive, HH)).astype(BF16), mix[...])
            z2[b, f, 1 : 1 + HH] = m.reshape(HH, WP, 256)
            if f in (0, last):
                halo_send[0 if f == 0 else 1] = m.astype(BF16).reshape(HH, WP, 256)
            carry = (carry[0] + fold(m), carry[1] + fold(m * m))
            if f in (0, last):
                halo_start(2 * b, b, 0 if f == 0 else 1)

        def emit_conv(f):
            pad = pad_mask[:WP, :128] * live(f)

            def emit(row, half, cols, c, carry):
                c = c * pad
                conv[b, f * HH + row, :, cols] = c
                if f in (0, last):
                    halo_send[0 if f == 0 else 1, row, :, cols] = c.astype(BF16)
                e = edge[b, f + 1, row_class(row), :, cols]
                s0, s1, s2 = carry
                return (s0 + fold(c), s1 + fold(c * c), s2 + fold(c * e))

            return emit

        def fill(side):
            present = lane > 0 if side == 0 else lane < lanes - 1

            @pl.when(present)
            def _():
                halo_wait(2 * b, b, side)

                def widen(j, _):
                    hz[side, pl.ds(1 + j * GROUP, GROUP)] = halo_recv[b, side, pl.ds(j * GROUP, GROUP)].astype(F32)
                    return 0

                lax.fori_loop(0, QUADS, widen, 0)

            @pl.when(jnp.logical_not(present))
            def _():
                def clear(j, _):
                    hz[side, pl.ds(1 + j * GROUP, GROUP)] = jnp.zeros((GROUP, WP, 256), F32)
                    return 0

                lax.fori_loop(0, QUADS, clear, 0)

        acc = [[zero8(128), zero8(128)] for _ in range(3)]
        for f in range(1, last):
            acc = convolve(z2.at[b], f, b, False, emit_conv(f), acc)
        if b == 0:
            gather_on("exp", 0)
        for side in range(2):
            fill(side)
            halo_sent(2 * b, b, side)
            f = 0 if side == 0 else last
            acc = convolve(z2.at[b], f, b, False, emit_conv(f), acc)
            halo_start(2 * b + 1, 2 + b, side)
        joined = [jnp.concatenate([flat_sum(a[0]), flat_sum(a[1])], axis=1) for a in acc]
        total_start(3 * b + 1, rows_of(flat_sum(carry[0]), flat_sum(carry[1]), *joined, *edge_sums[b]))
        if b == 0:
            gather_wait("exp", 0)
        else:
            gather_wait("exp", 1)
            tbuf[...] = exp[1].T
        got = total_finish(3 * b + 1)
        norm2 = affine(got[0:1], got[1:2], count, mid(b, 1, 0), mid(b, 1, 1))
        _, _, a2, b2 = norm2
        sc, scc, sce, se, see = [got[i : i + 1] for i in range(2, 7)]
        total3 = a2 * sc + b2 * se
        square3 = a2 * a2 * scc + 2.0 * a2 * b2 * sce + b2 * b2 * see
        norm3 = affine(total3, square3, count, mid(b, 2, 0), mid(b, 2, 1))
        _, _, a3, b3 = norm3

        norm3_pattern(b, a3, b2, b3)
        if b == 0:
            gather("red", 1)
            gather("mix", 1)

        def activate(i, _):
            rows, lines, where = trio(i)
            c = conv[b, lines].reshape(TRIO * WIDE, 256)
            acts = []
            for k, (f, j) in enumerate(where):
                v = c[WIDE * k : WIDE * (k + 1)] * (a3 * a2) + edge_rows(pat.at[f + 1], j)
                _, t = gelu_core(v)
                acts.append(squeeze(gelu_value(v, t, 0.5 * live(f))))
            a3s[b, rows] = jnp.concatenate(acts, axis=0).astype(BF16)
            return 0

        lax.fori_loop(0, trios, activate, 0)
        gram = dot_rows(a3s[b], a3s[b])
        line = dot(jnp.ones((16, frames * frame_rows), BF16), a3s[b])
        high = jnp.concatenate([gram, line], axis=0)
        split = high.astype(BF16)
        grown = dot(split, exp[b]) + dot((high - split.astype(F32)).astype(BF16), exp[b])
        squares = flat_sum(fold(grown[:256] * exp[b].astype(F32)))
        if b == 0:
            gather_on("red", 1)
            gather_on("mix", 1)
        total_start(3 * b + 2, rows_of(grown[256:257], squares))
        if b == 0:
            gather_wait("red", 1)
            tbuf[...] = red_t[1].T
        got = total_finish(3 * b + 2)
        norm4 = affine(wide_row(got, 0), wide_row(got, 4), count4, norm_out[b, 0:1], norm_out[b, 1:2])
        norms.append((norm1, norm2, norm3, norm4, (sc, scc, sce, se, see)))

        if b == 0:
            gather("exp", 1)

            def closing(i, carry):
                rows, lines, where = trio(i)
                _, pre = open_block(0, rows)
                results = []
                for (f, j), v in zip(where, pieces(pre, FLAT)):
                    _, t = gelu_core(v)
                    results.append(gelu_value(v, t, 0.5 * live(f)).astype(BF16))
                result = jnp.concatenate(results, axis=0)
                x1[rows] = result
                z = dot(result, tbuf[...])
                z1[1, lines] = spread(z).reshape(TRIO * GROUP, WP, 256)
                return (carry[0] + fold(z), carry[1] + fold(z * z))

            carry = lax.fori_loop(0, trios, closing, (zero8(), zero8()))
            gather_on("exp", 1)
            total_start(3, rows_of(flat_sum(carry[0]), flat_sum(carry[1])))
            gather_wait("mix", 1)
            mix[...] = mix_t[1].T
            got = total_finish(3)
            first_sums = (got[0:1], got[1:2])

    cot_load.wait()

    def ending(i, carry):
        rows, lines, where = trio(i)
        z, pre = open_block(1, rows)
        g = sb[rows]
        s0, s1 = carry
        for k, (f, j) in enumerate(where):
            here = slice(FLAT * k, FLAT * (k + 1))
            v, half = pre[here], 0.5 * live(f)
            square, t = gelu_core(v)
            part = pl.ds(pl.multiple_of((TRIO * i + k) * FLAT, FLAT), FLAT)
            yb[part] = gelu_value(v, t, half).astype(BF16)
            s = gelu_slope(v, square, t, half) * g[here].astype(F32)
            sb[part] = s.astype(BF16)
            s0, s1 = s0 + fold(s), s1 + fold(s * z[here])
        return s0, s1

    carry = lax.fori_loop(0, trios, ending, (zero8(1024), zero8(1024)))
    total_start(6, rows_of(flat_sum(carry[0]), flat_sum(carry[1])))
    for copy in out_store:
        copy.start()

    for b in reversed(range(BLOCKS)):
        turn = BLOCKS - 1 - b
        base = 6 + 3 * turn
        norm1, norm2, norm3, norm4, (sc, scc, sce, se, see) = norms[b]
        _, _, a1, b1 = norm1
        mean2, scale2, a2, b2 = norm2
        mean3, scale3, a3, b3 = norm3
        a4 = norm4[2]

        got = total_finish(base)
        slope4, bias4, gain_grad, shift_grad = back_affine(wide_row(got, 0), wide_row(got, 4), count4, norm4)
        out_grads[b] = (gain_grad, shift_grad)
        if turn == 0:
            for copy in out_store:
                copy.wait()
        for side in range(2):
            if turn == 0:
                halo_sent(2 * (BLOCKS - 1) + 1, 2 + BLOCKS - 1, side)
            else:
                halo_sent(2 * BLOCKS + turn - 1, b + 1, side)

        if turn > 0:
            early[b + 1].to_rows(b + 1)
            final[b + 1].to_side(b + 1)
        kind = 2 * BLOCKS + turn
        norm3_pattern(b, a3, b2, b3)
        acc = (zero8(), zero8(), zero8())
        for f in order:
            alive = live(f)

            rows = slice(f * frame_rows, (f + 1) * frame_rows)
            z = dot(a3s[b, rows], exp[b])
            d4 = (sb[rows].astype(F32) * a4 + (z * slope4 + bias4 * alive)).astype(BF16)
            yb[rows] = d4
            back = spread(dot(d4, tbuf[...]))
            for j in range(QUADS):
                c = conv[b, f * HH + GROUP * j : f * HH + GROUP * (j + 1)].reshape(WIDE, 256)
                v = c * (a3 * a2) + edge_rows(pat.at[f + 1], j)
                square, t = gelu_core(v)
                e3 = back[WIDE * j : WIDE * (j + 1)] * gelu_slope(v, square, t, 0.5)
                dz[f, 1 + GROUP * j : 1 + GROUP * (j + 1)] = e3.reshape(GROUP, WP, 256)
                if f in (0, last):
                    halo_send[0 if f == 0 else 1, GROUP * j : GROUP * (j + 1)] = e3.astype(BF16).reshape(GROUP, WP, 256)
                e = edge_rows(edge.at[b, f + 1], j)
                acc = (acc[0] + fold(e3), acc[1] + fold(e3 * c), acc[2] + fold(e3 * e))
            if f in (0, last):
                halo_start(kind, b, 0 if f == 0 else 1)
        total_start(base + 1, rows_of(*[flat_sum(a) for a in acc]))

        if turn > 0:
            early[b + 1].clear("a")

        def expand_grad(i, _):
            cols = pl.ds(pl.multiple_of(i * 256, 256), 256)
            g = dot_rows(a3s[b], yb[:, cols])
            for who in range(lanes):
                for h in range(2):
                    early[b].put(who, 2 * i + h, 0, g[share * who : share * (who + 1), 128 * h : 128 * (h + 1)])
            return 0

        lax.fori_loop(0, 4, expand_grad, 0)
        if b > 0:
            tbuf[...] = exp[b - 1].T

        got = total_finish(base + 1)
        e3_sum, e3_conv, e3_edge = got[0:1], got[1:2], got[2:3]
        e3_third = a2 * e3_conv + b2 * e3_edge
        slope3, bias3, gain3, shift3 = back_affine(e3_sum, e3_third, count, norm3)
        third_conv = a2 * scc + b2 * sce
        third_edge = a2 * sce + b2 * see
        d3_conv = a3 * e3_conv + bias3 * sc + slope3 * third_conv
        d3_edge = a3 * e3_edge + bias3 * se + slope3 * third_edge
        slope2, bias2, gain2, shift2 = back_affine(d3_edge, d3_conv, count, norm2)

        if turn > 0:
            early[b + 1].to_all(b + 1)
            final[b + 1].to_rows(b + 1)
        for f in range(-1, frames + 1):
            live_pad = pad_mask[:WP] * live(f)
            for cls in range(3):
                pat[f + 1, cls] = bias3 * live_pad + (slope3 * b2) * edge[b, f + 1, cls]
        slope_c = slope3 * a2

        def to_d3(q, _):
            f = lax.div(q, QUADS)
            j = lax.rem(q, QUADS)
            rows = pl.ds(1 + j * GROUP, GROUP)
            c = conv[b, pl.ds(q * GROUP, GROUP)].reshape(WIDE, 256)
            e3 = dz[f, rows].reshape(WIDE, 256)
            d3 = e3 * a3 + c * slope_c + edge_rows(pat.at[f + 1], j)
            dz[f, rows] = d3.reshape(GROUP, WP, 256)
            return 0

        lax.fori_loop(0, frames * QUADS, to_d3, 0)

        def fill_back(side):
            present = lane > 0 if side == 0 else lane < lanes - 1
            f = -1 if side == 0 else frames

            @pl.when(present)
            def _():
                halo_wait(2 * b + 1, 2 + b, side)
                halo_wait(kind, b, side)

                def widen(j, _):
                    rows = pl.ds(j * GROUP, GROUP)
                    c = halo_recv[2 + b, side, rows].astype(F32).reshape(WIDE, 256)
                    e3 = halo_recv[b, side, rows].astype(F32).reshape(WIDE, 256)
                    d3 = e3 * a3 + c * slope_c + edge_rows(pat.at[f + 1], j)
                    hz[side, pl.ds(1 + j * GROUP, GROUP)] = d3.reshape(GROUP, WP, 256)
                    return 0

                lax.fori_loop(0, QUADS, widen, 0)

            @pl.when(jnp.logical_not(present))
            def _():
                def clear(j, _):
                    hz[side, pl.ds(1 + j * GROUP, GROUP)] = jnp.zeros((GROUP, WP, 256), F32)
                    return 0

                lax.fori_loop(0, QUADS, clear, 0)

        for side in range(2):
            fill_back(side)

        def emit_back(f):
            pad = pad_mask[:WP, :128] * live(f)

            def emit(row, half, cols, e2, carry):
                z = z2[b, f, row + 1, :, cols]
                d2 = (e2 * a2[:, cols] + (z * slope2[:, cols] + bias2[:, cols])) * pad
                d2s[f * HH + row, :, cols] = d2.astype(BF16)
                return carry

            return emit

        for f in range(frames):
            convolve(dz, f, b, True, emit_back(f), [])

        def unmixing(i, acc):
            _, lines, where = trio(i)
            e = dot(d2s[lines].reshape(TRIO * WIDE, 256), mix_t[b])
            z = z1[b, lines].reshape(TRIO * WIDE, 256)
            for k, (f, j) in enumerate(where):
                here = slice(WIDE * k, WIDE * (k + 1))
                v = z[here] * a1 + b1
                square, t = gelu_core(v)
                part = pl.ds((TRIO * i + k) * GROUP, GROUP)
                a1s[part] = gelu_value(v, t, half_mask(live(f), GROUP)).astype(BF16).reshape(GROUP, WP, 256)
                e1 = e[here] * gelu_slope(v, square, t, 0.5)
                conv[b, part] = e1.reshape(GROUP, WP, 256)
                acc = (acc[0] + fold(e1), acc[1] + fold(e1 * z[here]))
            return acc

        acc = lax.fori_loop(0, trios, unmixing, (zero8(), zero8()))
        if turn > 0:
            early[b + 1].finish(b + 1)
        total_start(base + 2, rows_of(*[flat_sum(a) for a in acc]))

        def depth_grad(half, b=b, a2=a2, b2=b2):
            place, at = (early[b], 80) if b == 0 else (final[b], 64)
            cols = slice(128 * half, 128 * (half + 1))
            taps_grad = tuple(zero8(128) for _ in range(KVOL))
            for f in range(frames):
                planes = []
                for dt in range(3):
                    g = f - (dt - 1)
                    planes.append(hz.at[0] if g < 0 else hz.at[1] if g > last else dz.at[g])
                shift_rows = b2[:, cols] * (pad_mask[:WP, :128] * live(f))

                def tap_rows(h, taps_grad):
                    a = z2[b, f, h + 1, :, cols] * a2[:, cols] + shift_rows
                    moved = [pltpu.roll(a, 1, 0), a, pltpu.roll(a, WP - 1, 0)]
                    new = list(taps_grad)
                    for dt in range(3):
                        for dh in range(3):
                            d = planes[dt][h + 1 - (dh - 1), :, cols]
                            for dw in range(3):
                                k = dt * 9 + dh * 3 + dw
                                new[k] = new[k] + fold(d * moved[dw])
                    return tuple(new)

                taps_grad = lax.fori_loop(0, HH, tap_rows, taps_grad)
            lines = jnp.concatenate(
                [flat_sum(t) for t in taps_grad] + [jnp.zeros((WP - KVOL, 128), F32)], axis=0
            )
            for r in range(4):
                part = jnp.concatenate([lines[8 * r : 8 * r + 8], zero8(128)], axis=0)
                for who in range(lanes):
                    place.put(who, 2 * r + half, at, part)

        depth_grad(0)
        if b == 0:
            depth_grad(1)
        g = dot_rows(d2s[...].reshape(frames * HH * WP, 256), a1s[...].reshape(frames * HH * WP, 256))
        for who in range(lanes):
            for r in range(4):
                for h in range(2):
                    first = share * who + 16 * r
                    early[b].put(who, 2 * r + h, 64, g[first : first + 16, 128 * h : 128 * (h + 1)])
        early[b].to_pair(b)

        got = total_finish(base + 2)
        slope1, bias1, gain1, shift1 = back_affine(got[0:1], got[1:2], count, norm1)
        mid_grads[b] = ((gain1, shift1), (gain2, shift2), (gain3, shift3))

        early[b].to_side(b)
        def first_grad(i):
            rows, lines, where = trio(i)
            e1 = conv[b, lines].reshape(TRIO * WIDE, 256)
            z = z1[b, lines].reshape(TRIO * WIDE, 256)
            parts = []
            for k, (f, j) in enumerate(where):
                here = slice(WIDE * k, WIDE * (k + 1))
                alive = live(f)
                parts.append(squeeze(e1[here] * a1 + (z[here] * (slope1 * alive) + bias1 * alive)))
            d1 = jnp.concatenate(parts, axis=0).astype(BF16)
            a3s[b, rows] = d1
            return rows, where, d1

        def reduce_grad(i, _):
            cols = pl.ds(pl.multiple_of(i * 256, 256), 256)
            g = dot_rows(a3s[b], xs[b][:, cols])
            for who in range(lanes):
                for h in range(2):
                    final[b].put(who, 2 * i + h, 0, g[share * who : share * (who + 1), 128 * h : 128 * (h + 1)])
            return 0

        if b > 0:

            def passing(i, carry):
                rows, where, d1 = first_grad(i)
                g = dot(d1, red_t[b]) + sb[rows].astype(F32)
                z, pre = open_block(b - 1, rows)
                s0, s1 = carry
                for k, (f, j) in enumerate(where):
                    here = slice(FLAT * k, FLAT * (k + 1))
                    v = pre[here]
                    square, t = gelu_core(v)
                    s = gelu_slope(v, square, t, 0.5 * live(f)) * g[here]
                    sb[pl.ds(pl.multiple_of((TRIO * i + k) * FLAT, FLAT), FLAT)] = s.astype(BF16)
                    s0, s1 = s0 + fold(s), s1 + fold(s * z[here])
                return s0, s1

            carry = lax.fori_loop(0, trios, passing, (zero8(1024), zero8(1024)))
            total_start(base + 3, rows_of(flat_sum(carry[0]), flat_sum(carry[1])))
            depth_grad(1)
            lax.fori_loop(0, 4, reduce_grad, 0)
            final[b].to_pair(b)
        else:
            final[b + 1].to_all(b + 1)

            def only_d1(i, _):
                first_grad(i)
                return 0

            lax.fori_loop(0, trios, only_d1, 0)
            final[b + 1].clear("a")
            lax.fori_loop(0, 4, reduce_grad, 0)
            final[b].to_pair(b)
            early[b + 1].clear("b", "all")
            early[b].to_rows(b)
            steps = (lambda: final[b].to_side(b), lambda: early[b].to_all(b))
            gtok_store = [frame_copy(yb, gtok_hbm, f, store_sem.at[f]) for f in range(frames)]
            for f in range(frames):
                rows = slice(f * frame_rows, (f + 1) * frame_rows)
                yb[rows] = (dot(a3s[b, rows], red_t[b]) + sb[rows].astype(F32)).astype(BF16)
                gtok_store[f].start()
                if f < len(steps):
                    steps[f]()
            final[b + 1].finish(b + 1)
            final[b + 1].clear("b", "all")
            final[b].to_rows(b)
            early[b].finish(b)
            final[b].to_all(b)
            final[b].finish(b)

    for b in range(BLOCKS):
        for k in range(3):
            for w in range(2):
                r = (b * 3 + k) * 2 + w
                gmid_out[r : r + 1] = mid_grads[b][k][w]
        for w in range(2):
            gout_out[2 * b + w : 2 * b + w + 1] = out_grads[b][w]

    for copy in gtok_store:
        copy.wait()
    early[0].clear("a", "b", "all")
    final[0].clear("a", "b", "all")
    for copy in late + travelling:
        copy.wait_send()
    for side in range(2):
        halo_sent(2 * BLOCKS + BLOCKS - 1, 0, side)


def whole_call(groups, lanes, counts, tokens, cotangent, reduce_loc, mix_loc, expand_loc, small_loc, norm_out):
    rows = tokens.shape[0]
    frames = rows // (HH * WW)
    whole = pl.BlockSpec(memory_space=pltpu.VMEM)
    hbm = pl.BlockSpec(memory_space=pl.ANY)
    dma = pltpu.SemaphoreType.DMA
    low, high = stages(groups)
    far = low * (lanes // 2)
    lines = frames * HH
    sums = 6 * BLOCKS
    kinds = 3 * BLOCKS
    shape = jax.ShapeDtypeStruct
    return pl.pallas_call(
        functools.partial(whole_kernel, groups, lanes),
        out_shape=(
            shape((rows, 1024), BF16),
            shape((rows, 1024), BF16),
            shape((BLOCKS, 176, 1024), F32),
            shape((BLOCKS * 6, 256), F32),
            shape((BLOCKS * 2, 1024), F32),
        ),
        in_specs=[pl.BlockSpec(memory_space=pltpu.SMEM)] + [hbm] * 5 + [whole] * 2,
        out_specs=[hbm] * 2 + [whole] * 3,
        scratch_shapes=[
            pltpu.VMEM((rows, 1024), BF16),
            pltpu.VMEM((rows, 1024), BF16),
            pltpu.VMEM((rows, 1024), BF16),
            pltpu.VMEM((rows, 1024), BF16),
            pltpu.VMEM((BLOCKS, 256, 1024), BF16),
            pltpu.VMEM((BLOCKS, 256, 1024), BF16),
            pltpu.VMEM((1024, 256), BF16),
            pltpu.VMEM((BLOCKS, 256, 256), BF16),
            pltpu.VMEM((256, 256), BF16),
            pltpu.VMEM((lanes,) + small_loc.shape, F32),
            pltpu.VMEM((2 * small_loc.shape[0], 256), F32),
            pltpu.VMEM((BLOCKS, lines, WP, 256), F32),
            pltpu.VMEM((lines, WP, 256), BF16),
            pltpu.VMEM((BLOCKS, frames, HH + 2, WP, 256), F32),
            pltpu.VMEM((frames, HH + 2, WP, 256), F32),
            pltpu.VMEM((2, HH + 2, WP, 256), F32),
            pltpu.VMEM((BLOCKS, lines, WP, 256), F32),
            pltpu.VMEM((BLOCKS, rows, 256), BF16),
            pltpu.VMEM((BLOCKS, frames + 2, 3, WP, 256), F32),
            pltpu.VMEM((frames + 2, 3, WP, 256), F32),
            pltpu.VMEM((lines, WP, 256), BF16),
            pltpu.VMEM((2, HH, WP, 256), BF16),
            pltpu.VMEM((2 * BLOCKS, 2, HH, WP, 256), BF16),
            pltpu.VMEM((lanes, PIECES, 176, 128), BF16),
            pltpu.VMEM((3, PIECES, 176, 128), BF16),
            pltpu.VMEM((PIECES, 176, 128), BF16),
            pltpu.VMEM((low, PIECES // low, 176, 128), BF16),
            pltpu.VMEM((PIECES, 176, 128), BF16),
            pltpu.VMEM((BLOCKS, high, PIECES // low, 176 if high > 1 else 16, 128), BF16),
            pltpu.VMEM((2, 2, 16, 128), F32),
            pltpu.VMEM((2, far, 16, 128), F32),
            pltpu.VMEM((2, high, 16, 128), F32),
            dma((sums,)),
            dma((sums,)),
            dma((sums, far)),
            dma((sums, far)),
            dma((sums, high)),
            dma((sums, high)),
            dma((7, 3)),
            dma((7, lanes)),
            dma((kinds, 2)),
            dma((kinds, 2)),
            dma((frames + 1,)),
            dma((frames,)),
            dma((2 * BLOCKS, 3)),
            dma((2 * BLOCKS, 3)),
            dma((2 * BLOCKS, low)),
            dma((2 * BLOCKS, low)),
            dma((2 * BLOCKS, low)),
            dma((2 * BLOCKS, low)),
            dma((2 * BLOCKS, high)),
            dma((2 * BLOCKS, high)),
            dma((BLOCKS, 4)),
        ],
        compiler_params=pltpu.CompilerParams(
            collective_id=1, has_side_effects=True, vmem_limit_bytes=63 * 2**20
        ),
    )(counts, tokens, cotangent, reduce_loc, mix_loc, expand_loc, small_loc, norm_out)


def descend(weight, moment, grad):
    moment_new = MOMENTUM * moment + grad + DECAY * weight
    return (weight - LEARN_RATE * moment_new, moment_new)


def update_kernel(lanes, *refs):
    out_raw, gtok_raw, reduced, gmid, gout = refs[:5]
    weights, moments = refs[5:11], refs[11:17]
    out, gtok = refs[17:19]
    grads, new_weights, new_moments = refs[19:25], refs[25:31], refs[31:37]
    held, sems, store_sems = refs[37:]
    rows = out.shape[0] // 3
    copies, stores = [], []
    for k in range(3):
        for which, (src, dst) in enumerate(((out_raw, out), (gtok_raw, gtok))):
            here = pl.ds(k * rows, rows)
            copies.append(pltpu.make_async_copy(src.at[here], held.at[which, here], sems.at[which, k]))
            stores.append(pltpu.make_async_copy(held.at[which, here], dst.at[here], store_sems.at[which, k]))
    for copy in copies:
        copy.start()
    lane = lax.axis_index("chan")
    narrow = 256 // lanes

    def mine(v):
        out = v[:, :narrow]
        for who in range(1, lanes):
            out = jnp.where(lane == who, v[:, narrow * who : narrow * (who + 1)], out)
        return out

    def step(slot, at, grad):
        weight, moment = descend(weights[slot][at], moments[slot][at], grad)
        grads[slot][at] = grad
        new_weights[slot][at] = weight
        new_moments[slot][at] = moment

    depths = []
    for b in range(BLOCKS):
        step(0, (b,), reduced[b, 96:160])
        mix = reduced[b, 64:80]
        step(1, (b,), jnp.concatenate([mix[:, 256 * r : 256 * (r + 1)] for r in range(4)], axis=0))
        depth = reduced[b, 80:88] if b == 0 else reduced[b, 160:168]
        depths.append(mine(jnp.concatenate([depth[:, 256 * r : 256 * (r + 1)] for r in range(4)], axis=0)))
        step(3, (b,), reduced[b, 0:64])
        step(5, (b,), gout[2 * b : 2 * b + 2])
    for k in range(KVOL):
        step(2, (k,), jnp.concatenate([depth[k : k + 1] for depth in depths], axis=0))
    middle = mine(gmid[...])
    for k in range(BLOCKS * 3):
        step(4, (k,), middle[2 * k : 2 * k + 2])
    for copy, store in zip(copies, stores):
        copy.wait()
        store.start()
    for store in stores:
        store.wait()


def update_call(lanes, *args):
    whole = pl.BlockSpec(memory_space=pltpu.VMEM)
    hbm = pl.BlockSpec(memory_space=pl.ANY)
    like = [jax.ShapeDtypeStruct(v.shape, v.dtype) for v in args]
    return pl.pallas_call(
        functools.partial(update_kernel, lanes),
        out_shape=tuple(like[:2] + like[5:11] * 3),
        in_specs=[hbm] * 2 + [whole] * 15,
        out_specs=[hbm] * 2 + [whole] * 18,
        scratch_shapes=[
            pltpu.VMEM((2,) + args[0].shape, args[0].dtype),
            pltpu.SemaphoreType.DMA((2, 3)),
            pltpu.SemaphoreType.DMA((2, 3)),
        ],
        compiler_params=pltpu.CompilerParams(vmem_limit_bytes=60 * 2**20),
    )(*args)


def shards(
    tokens,
    frame_counts,
    cotangent,
    w_reduce,
    w_mix,
    w_depth,
    w_expand,
    norm_mid,
    norm_out,
    moment_reduce,
    moment_mix,
    moment_depth,
    moment_expand,
    moment_mid,
    moment_out,
):
    lane = lax.axis_index("chan")
    lanes = lax.axis_size("chan")
    narrow = w_reduce.shape[2]
    small = jnp.concatenate([w_depth.reshape(-1, narrow), norm_mid.reshape(-1, narrow)], axis=0)
    small = jnp.pad(small, ((0, -small.shape[0] % 16), (0, 0)))
    small = jnp.concatenate(jnp.split(small, 2, axis=0), axis=1)
    turned = lambda v: jnp.swapaxes(v, 1, 2)
    raw = whole_call(
        lax.axis_size("dp"),
        lanes,
        frame_counts,
        tokens,
        cotangent,
        turned(w_reduce),
        turned(w_mix),
        w_expand,
        small,
        norm_out,
    )
    swap = lambda v: jnp.swapaxes(v, 0, 1)
    flat = lambda v: v.reshape((-1,) + v.shape[2:])
    inside = lambda r, m, d, e, mid, out: (turned(r), turned(m), swap(d), e, flat(mid), out)
    outside = lambda r, m, d, e, mid, out: (turned(r), turned(m), swap(d), e, mid.reshape(norm_mid.shape), out)
    done = update_call(
        lanes,
        *raw,
        *inside(w_reduce, w_mix, w_depth, w_expand, norm_mid, norm_out),
        *inside(moment_reduce, moment_mix, moment_depth, moment_expand, moment_mid, moment_out),
    )
    return done[:2] + outside(*done[2:8]) + outside(*done[8:14]) + outside(*done[14:20])


def solution(mesh):
    rows = P(("dp", "chan"), None)
    weights = (
        P(None, None, "chan"),
        P(None, None, "chan"),
        P(None, None, "chan"),
        P(None, "chan", None),
        P(None, None, None, "chan"),
        P(),
    )
    return jax.shard_map(
        shards,
        mesh=mesh,
        in_specs=(rows, P("dp"), rows) + weights + weights,
        out_specs=(rows, rows) + weights + weights + weights,
        check_vma=False,
    )
```

```python
import functools

import jax
import jax.numpy as jnp
from jax import lax
from jax.experimental import pallas as pl
from jax.experimental.pallas import tpu as pltpu
from jax.sharding import PartitionSpec as P

FRAMES = 12
HH = 28
WW = 28
WP = 32
KVOL = 27
BLOCKS = 2
GROUP = 4
QUADS = HH // GROUP
FLAT = GROUP * WW
WIDE = GROUP * WP
PIECES = 8
TRIO = 3

EPS = 1e-05
LEARN_RATE = 0.001
MOMENTUM = 0.9
DECAY = 0.0001
MESH = pl.DeviceIdType.MESH
F32 = jnp.float32
BF16 = jnp.bfloat16
ROOT = 0.7978845608028654
CUBE = 0.044715


def gelu_core(v):
    square = v * v
    return square, jnp.tanh(v * (ROOT + (ROOT * CUBE) * square))


def gelu_value(v, t, half):
    h = half * v
    return h * t + h


def gelu_slope(v, square, t, half):
    r = v * (half * ROOT + (half * (3.0 * ROOT * CUBE)) * square)
    return (half * t + half) + (r - r * (t * t))


def dot_rows(left, right):
    return lax.dot_general(left, right, (((0,), (0,)), ((), ())), preferred_element_type=F32)


def dot(left, right):
    return jnp.dot(left, right, preferred_element_type=F32)


def fold(v):
    return jnp.sum(v.reshape(v.shape[0] // 8, 8, v.shape[1]), axis=0)


def spread(v):
    gap = jnp.zeros((WP - WW, v.shape[1]), v.dtype)
    parts = []
    for h in range(v.shape[0] // WW):
        parts += [v[WW * h : WW * (h + 1)], gap]
    return jnp.concatenate(parts, axis=0)


def squeeze(v):
    return jnp.concatenate([v[WP * h : WP * h + WW] for h in range(v.shape[0] // WP)], axis=0)


def pieces(v, rows):
    return [v[rows * k : rows * (k + 1)] for k in range(v.shape[0] // rows)]


def rows_of(*vectors):
    parts = []
    for v in vectors:
        parts += pieces_of(v)
    n = 4 if len(parts) <= 4 else 8
    out = []
    for side in range(2):
        out += [v[:, 128 * side : 128 * (side + 1)] for v in parts]
        if len(parts) < n:
            out.append(jnp.zeros((n - len(parts), 128), F32))
    return jnp.concatenate(out, axis=0)


def pieces_of(v):
    return [v[:, 256 * i : 256 * (i + 1)] for i in range(v.shape[1] // 256)]


def flat_sum(v):
    return jnp.sum(v, axis=0, keepdims=True)


def wide_row(v, first):
    return jnp.concatenate([v[first + i : first + i + 1] for i in range(4)], axis=1)


class Net:
    def __init__(self, groups, lanes):
        self.lanes = lanes
        self.low, self.high = stages(groups)
        self.row = lax.axis_index("dp")
        self.lane = lax.axis_index("chan")
        self.core = lax.rem(self.lane, 2)
        self.side = lax.div(self.lane, 2)
        self.half = lanes // 2
        self.row_low = lax.rem(self.row, self.low)
        self.row_high = lax.div(self.row, self.low)

    def near(self):
        return [(1 - self.core, (self.row, self.side * 2 + 1 - self.core))]

    def far(self):
        out = []
        for o in sorted(range(self.low), key=lambda o: abs(2 * o - self.low - 1)):
            for p in range(self.half):
                if o or p:
                    row = lax.rem(self.row_low + o, self.low)
                    side = lax.rem(self.side + p, self.half)
                    out.append((row * self.half + side, (self.row_high * self.low + row, side * 2 + self.core)))
        return out

    def far_slot(self):
        return self.row_low * self.half + self.side

    def top(self):
        rows = [lax.rem(self.row_high + o, self.high) for o in range(1, self.high)]
        return [(row, (row * self.low + self.row_low, self.lane)) for row in rows]

    def pair(self):
        lane = self.side * 2 + 1 - self.core
        return lane, (self.row, lane)

    def across(self):
        lane = (1 - self.side) * 2 + self.core
        return lane, (self.row, lane)

    def corner(self):
        return (1 - self.side) * 2 + 1 - self.core


def stages(groups):
    low = min(groups, 8)
    return low, groups // low


def push(src, dst, send, recv, device):
    copy = pltpu.make_async_remote_copy(
        src_ref=src, dst_ref=dst, send_sem=send, recv_sem=recv, device_id=device, device_id_type=MESH
    )
    return copy


def whole_kernel(
    groups,
    lanes,
    counts,
    tokens,
    cotangent,
    reduce_loc,
    mix_loc,
    expand_loc,
    small_loc,
    norm_out,
    out_hbm,
    gtok_hbm,
    grads_out,
    gmid_out,
    gout_out,
    keep_big,
    keep_mid,
    x0,
    x1,
    yb,
    sb,
    red_t,
    exp,
    tbuf,
    mix_t,
    mix,
    small_in,
    small,
    z1,
    a1s,
    z2,
    dz,
    hz,
    conv,
    a3s,
    edge,
    pat,
    d2s,
    d1s,
    halo_send,
    halo_recv,
    grad_a,
    grad_ra,
    grad_b,
    grad_rb,
    grad_all,
    grad_top,
    near,
    far,
    top,
    near_send,
    near_recv,
    far_send,
    far_recv,
    top_send,
    top_recv,
    gather_send,
    gather_recv,
    halo_ssem,
    halo_rsem,
    load_sem,
    store_sem,
    grad_sa,
    grad_qa,
    grad_sb,
    grad_qb,
    grad_sc,
    grad_qc,
    grad_st,
    grad_qt,
    weight_sem,
    keep_sem,
    back_sem,
):
    net = Net(groups, lanes)
    lane = net.lane
    frames = tokens.shape[0] // (HH * WW)
    frame_rows = HH * WW
    last = frames - 1
    count_here = counts[0]
    xs = (x0, x1)

    def live(frame):
        position = lane * frames + frame
        return jnp.where((position >= 0) & (position < count_here), 1.0, 0.0)

    def frame_copy(src, dst, f, sem):
        rows = pl.ds(f * frame_rows, frame_rows)
        return pltpu.make_async_copy(src.at[rows], dst.at[rows], sem)

    loads = [frame_copy(tokens, x0, f, load_sem.at[f]) for f in range(frames)]
    cot_load = pltpu.make_async_copy(cotangent, sb, load_sem.at[frames])
    for copy in loads:
        copy.start()
    cot_load.start()
    weight_loads = {}
    for b in range(BLOCKS):
        places = [
            ("red", reduce_loc.at[b], grads_out.at[b, pl.ds(0, 64)]),
            ("exp", expand_loc.at[b], grads_out.at[b, pl.ds(64, 64)]),
            ("mix", mix_loc.at[b, pl.ds(0, 32)], grads_out.at[b, pl.ds(128, 32), pl.ds(0, 256)]),
            ("mix", mix_loc.at[b, pl.ds(32, 32)], grads_out.at[b, pl.ds(128, 32), pl.ds(256, 256)]),
        ]
        for k, (name, src, dst) in enumerate(places):
            copy = pltpu.make_async_copy(src, dst, weight_sem.at[b, k])
            copy.start()
            weight_loads.setdefault((name, b), []).append(copy)

    barrier = pltpu.get_barrier_semaphore()
    friends = [d for peers in (net.near(), net.far(), net.top()) for _, d in peers] + [(net.row, net.corner())]
    for device in friends:
        pl.semaphore_signal(barrier, inc=1, device_id=device, device_id_type=MESH)
    pl.semaphore_wait(barrier, len(friends))

    own = net.lane
    share = red_t.shape[1] // lanes
    late = []

    def gather(name, b):
        slot, dst_of = plan[name, b]
        mine = dst_of(own)
        for copy in weight_loads.get((name, b), []):
            copy.wait()
        if name == "red":
            mine[...] = grads_out[b, :64].astype(BF16)
        elif name == "exp":
            mine[...] = grads_out[b, 64:128].astype(BF16)
        elif name == "mix":
            parts = [grads_out[b, 128:160, :256], grads_out[b, 128:160, 256:512]]
            mine[...] = jnp.concatenate(parts, axis=0).astype(BF16)
        else:
            mine[...] = small_loc[...]
        for step, (_, device) in enumerate((net.pair(), net.across())):
            copy = push(mine, mine, gather_send.at[slot, step], gather_recv.at[slot, own], device)
            copy.start()
            late.append(copy)

    def gather_on(name, b):
        slot, dst_of = plan[name, b]
        who, device = net.across()
        piece = dst_of(who)
        push(piece, piece, gather_send.at[slot, 1], gather_recv.at[slot, who], device).wait_recv()
        copy = push(piece, piece, gather_send.at[slot, 2], gather_recv.at[slot, who], net.pair()[1])
        copy.start()
        late.append(copy)

    def gather_wait(name, b):
        slot, dst_of = plan[name, b]
        for who in (net.pair()[0], net.corner()):
            push(dst_of(who), dst_of(who), gather_send.at[slot, 0], gather_recv.at[slot, who], net.pair()[1]).wait_recv()

    def block_rows(ref, b):
        return lambda who: ref.at[b, pl.ds(pl.multiple_of(who * share, share), share)]

    plan = {
        ("red", 0): (0, block_rows(red_t, 0)),
        ("mix", 0): (1, block_rows(mix_t, 0)),
        ("small", 0): (2, lambda who: small_in.at[who]),
        ("exp", 0): (3, block_rows(exp, 0)),
        ("red", 1): (4, block_rows(red_t, 1)),
        ("mix", 1): (5, block_rows(mix_t, 1)),
        ("exp", 1): (6, block_rows(exp, 1)),
    }
    for name in (("red", 0), ("mix", 0), ("small", 0)):
        gather(*name)

    used = {}
    travelling = []

    def total_start(i, value):
        size = value.shape[0]
        used[i] = size
        turn = i % 2
        gone, travelling[:] = list(travelling), []
        near[turn, net.core, :size] = value
        for who, device in net.near():
            mine = near.at[turn, net.core, pl.ds(0, size)]
            copy = push(mine, mine, near_send.at[i], near_recv.at[i], device)
            copy.start()
            travelling.append(copy)
            copy.wait_recv()
        far[turn, net.far_slot(), :size] = near[turn, 0, :size] + near[turn, 1, :size]
        for step, (who, device) in enumerate(net.far()):
            mine = far.at[turn, net.far_slot(), pl.ds(0, size)]
            copy = push(mine, mine, far_send.at[i, step], far_recv.at[i, net.far_slot()], device)
            copy.start()
            travelling.append(copy)
        for copy in gone:
            copy.wait_send()

    def total_finish(i):
        size = used[i]
        turn = i % 2
        for step, (who, device) in enumerate(net.far()):
            there = far.at[turn, who, pl.ds(0, size)]
            push(there, there, far_send.at[i, step], far_recv.at[i, who], device).wait_recv()
        total = far[turn, 0, :size]
        for j in range(1, net.low * net.half):
            total = total + far[turn, j, :size]
        if net.high > 1:
            mine = top.at[turn, net.row_high, pl.ds(0, size)]
            top[turn, net.row_high, :size] = total
            for step, (who, device) in enumerate(net.top()):
                copy = push(mine, mine, top_send.at[i, step], top_recv.at[i, net.row_high], device)
                copy.start()
                travelling.append(copy)
            for step, (who, device) in enumerate(net.top()):
                there = top.at[turn, who, pl.ds(0, size)]
                push(there, there, top_send.at[i, step], top_recv.at[i, who], device).wait_recv()
            total = top[turn, 0, :size]
            for j in range(1, net.high):
                total = total + top[turn, j, :size]
        return jnp.concatenate([total[: size // 2], total[size // 2 :]], axis=1)

    def halo_copy(kind, slot, side):
        step = -1 if side == 0 else 1
        return push(
            halo_send.at[side],
            halo_recv.at[slot, 1 - side],
            halo_ssem.at[kind, side],
            halo_rsem.at[kind, 1 - side],
            (net.row, lane + step),
        )

    def sends_to(side):
        return lane > 0 if side == 0 else lane < lanes - 1

    def halo_start(kind, slot, side):
        @pl.when(sends_to(side))
        def _():
            halo_copy(kind, slot, side).start()

    def halo_sent(kind, slot, side):
        @pl.when(sends_to(side))
        def _():
            halo_copy(kind, slot, side).wait_send()

    def halo_wait(kind, slot, side):
        step = -1 if side == 0 else 1
        push(
            halo_send.at[1 - side],
            halo_recv.at[slot, side],
            halo_ssem.at[kind, 1 - side],
            halo_rsem.at[kind, side],
            (net.row, lane + step),
        ).wait_recv()

    column = lax.broadcasted_iota(jnp.int32, (WIDE, 256), 0) % WP
    pad_mask = (column < WW).astype(F32)

    def half_mask(alive, lines):
        return jnp.concatenate([pad_mask[:WP] * (0.5 * alive)] * lines, axis=0)

    def affine(total, square, count, gain, shift):
        mean = total / count
        var = square / count - mean * mean
        scale = lax.rsqrt(var + EPS)
        return mean, scale, gain * scale, shift - mean * (gain * scale)

    def back_affine(e_sum, ez_sum, count, norm):
        mean, scale, a, _ = norm
        gain_grad = scale * (ez_sum - mean * e_sum)
        slope = -a * scale * gain_grad / count
        bias = -a * e_sum / count - slope * mean
        return slope, bias, gain_grad, e_sum

    def zero8(n=256):
        return jnp.zeros((8, n), F32)

    blank = jnp.zeros((WP, 256), F32)
    for f in range(frames):
        for b in range(BLOCKS):
            z2[b, f, 0] = blank
            z2[b, f, HH + 1] = blank
        dz[f, 0] = blank
        dz[f, HH + 1] = blank
    for side in range(2):
        hz[side, 0] = blank
        hz[side, HH + 1] = blank

    for name in (("red", 0), ("mix", 0), ("small", 0)):
        gather_on(*name)
    gather_wait("red", 0)
    tbuf[...] = red_t[0].T

    carry = (zero8(), zero8())
    for f in range(frames):
        loads[f].wait()
        alive = live(f)

        z = dot(x0[f * frame_rows : (f + 1) * frame_rows], tbuf[...])
        z1[0, f * HH : (f + 1) * HH] = spread(z).reshape(HH, WP, 256)
        carry = (carry[0] + fold(z) * alive, carry[1] + fold(z * z) * alive)

    alive_all = sum(live(f) for f in range(frames)) * (HH * WW)
    here_count = jnp.full((1, 256), 1.0, F32) * alive_all
    total_start(0, rows_of(flat_sum(carry[0]), flat_sum(carry[1]), here_count))

    gather_wait("small", 0)
    half_rows = small_loc.shape[0]
    for side in range(2):
        here = [small_in[who, :, 64 * side : 64 * (side + 1)] for who in range(lanes)]
        small[half_rows * side : half_rows * (side + 1)] = jnp.concatenate(here, axis=1)

    def mid(b, norm, which):
        r = BLOCKS * KVOL + (b * 3 + norm) * 2 + which
        return small[r : r + 1]

    edge_sums = []
    pattern_col = lax.broadcasted_iota(jnp.int32, (WP, 256), 0)
    for b in range(BLOCKS):
        taps_b = [[small[b * KVOL + dt * 9 + k : b * KVOL + dt * 9 + k + 1] for k in range(9)] for dt in range(3)]
        se = jnp.zeros((1, 256), F32)
        see = jnp.zeros((1, 256), F32)
        for f in range(-1, frames + 1):
            here = live(f)
            t = [
                here * (live(f - 1) * taps_b[0][k] + here * taps_b[1][k] + live(f + 1) * taps_b[2][k])
                for k in range(9)
            ]
            for cls in range(3):
                use = [dh for dh in range(3) if not (cls == 0 and dh == 0) and not (cls == 2 and dh == 2)]
                col = []
                for dw in range(3):
                    v = t[use[0] * 3 + dw]
                    for dh in use[1:]:
                        v = v + t[dh * 3 + dw]
                    col.append(v)
                inner = col[0] + col[1] + col[2]
                left, right = col[1] + col[2], col[0] + col[1]
                edge[b, f + 1, cls] = jnp.where(
                    pattern_col == 0,
                    left,
                    jnp.where(pattern_col == WW - 1, right, jnp.where(pattern_col < WW - 1, inner, 0.0)),
                )
                if 0 <= f < frames:
                    times = 1.0 if cls != 1 else HH - 2.0
                    se = se + times * (left + right + (WW - 2.0) * inner)
                    see = see + times * (left * left + right * right + (WW - 2.0) * (inner * inner))
        edge_sums.append((se, see))

    gather_wait("mix", 0)
    mix[...] = mix_t[0].T

    got = total_finish(0)
    count = got[2:3]
    count4 = jnp.concatenate([count] * 4, axis=1)
    first_sums = (got[0:1], got[1:2])

    def edge_rows(ref, j):
        top = jnp.where(j == 0, 0, 1)
        bottom = jnp.where(j == QUADS - 1, 2, 1)
        middle = ref[1]
        return jnp.concatenate([ref[top], middle, middle, ref[bottom]], axis=0)

    def trio(i):
        rows = pl.ds(pl.multiple_of(i * (TRIO * FLAT), TRIO * FLAT), TRIO * FLAT)
        lines = pl.ds(i * (TRIO * GROUP), TRIO * GROUP)
        where = []
        for k in range(TRIO):
            q = TRIO * i + k
            where.append((lax.div(q, QUADS), lax.rem(q, QUADS)))
        return rows, lines, where

    trios = frames * QUADS // TRIO

    def norm3_pattern(b, a3, b2, b3):
        for f in range(frames):
            for cls in range(3):
                pat[f + 1, cls] = edge[b, f + 1, cls] * (a3 * b2) + b3

    def row_class(h):
        return jnp.where(h == 0, 0, jnp.where(h == HH - 1, 2, 1))

    def convolve(local, f, b, flip, emit, acc):
        done = []
        for half in range(2):
            cols = slice(128 * half, 128 * (half + 1))
            kern = [small[b * KVOL + k : b * KVOL + k + 1, cols] for k in range(KVOL)]
            if flip:
                kern = kern[::-1]
            planes = []
            for dt in range(3):
                g = f + dt - 1
                planes.append(hz.at[0] if g < 0 else hz.at[1] if g > last else local.at[g])

            def two_rows(i, carry):
                h = 2 * i
                part = [[None] * 3 for _ in range(2)]
                for dt in range(3):
                    for rr in range(4):
                        v = planes[dt][h + rr, :, cols]
                        for o in range(2):
                            dh = rr - o
                            if 0 <= dh < 3:
                                for dw in range(3):
                                    term = kern[dt * 9 + dh * 3 + dw] * v
                                    part[o][dw] = term if part[o][dw] is None else part[o][dw] + term
                for o in range(2):
                    p = part[o]
                    c = p[1] + pltpu.roll(p[0], 1, 0) + pltpu.roll(p[2], WP - 1, 0)
                    carry = emit(h + o, half, cols, c, carry)
                return carry

            done.append(lax.fori_loop(0, HH // 2, two_rows, tuple(a[half] for a in acc)))
        return [[done[0][k], done[1][k]] for k in range(len(acc))]

    class Reduction:
        def __init__(self, first, size):
            self.lines = pl.ds(first, size)
            self.first, self.size = first, size
            self.which = 0 if first == 0 else 1
            self.open = {"a": [], "b": [], "all": []}

        def put(self, who, piece, first, value):
            grad_a[who, piece, pl.ds(self.lines.start + first, value.shape[0])] = value.astype(BF16)

        def clear(self, *names):
            for name in names:
                for copy in self.open[name]:
                    copy.wait_send()
                self.open[name] = []

        def move(self, name, copy):
            copy.start()
            self.open[name].append(copy)

        def pair_copy(self, b, side):
            i = 2 * b + self.which
            src, dst = grad_a.at[2 * side + 1 - net.core, :, self.lines], grad_ra.at[side, :, self.lines]
            return push(src, dst, grad_sa.at[i, side], grad_qa.at[i, side], net.pair()[1])

        def to_pair(self, b):
            for side in range(2):
                self.move("a", self.pair_copy(b, side))

        def across_copy(self, b):
            i = 2 * b + self.which
            src, dst = grad_a.at[net.across()[0], :, self.lines], grad_ra.at[2, :, self.lines]
            return push(src, dst, grad_sa.at[i, 2], grad_qa.at[i, 2], net.across()[1])

        def to_side(self, b):
            for side in range(2):
                self.pair_copy(b, side).wait_recv()
            other = net.across()[0]

            def add(piece, _):
                mine, theirs = grad_a[other, piece, self.lines], grad_ra[1 - net.side, piece, self.lines]
                grad_a[other, piece, self.lines] = (mine.astype(F32) + theirs.astype(F32)).astype(BF16)
                return 0

            lax.fori_loop(0, PIECES, add, 0)
            self.move("a", self.across_copy(b))

        def low_peers(self):
            rows = [lax.rem(net.row_low + o, net.low) for o in range(1, net.low)]
            return [(row, (net.row_high * net.low + row, lane)) for row in rows]

        def to_rows(self, b):
            i = 2 * b + self.which
            self.across_copy(b).wait_recv()
            self.clear("b")

            def add(piece, _):
                total = grad_a[own, piece, self.lines].astype(F32) + grad_ra[net.side, piece, self.lines].astype(F32)
                grad_b[piece, self.lines] = (total + grad_ra[2, piece, self.lines].astype(F32)).astype(BF16)
                return 0

            lax.fori_loop(0, PIECES, add, 0)
            each = PIECES // net.low
            for step, (who, device) in enumerate(self.low_peers()):
                src = grad_b.at[pl.ds(who * each, each), self.lines]
                dst = grad_rb.at[net.row_low, :, self.lines]
                self.move("b", push(src, dst, grad_sb.at[i, step], grad_qb.at[i, net.row_low], device))

        def to_all(self, b):
            i = 2 * b + self.which
            each = PIECES // net.low
            mine = pl.ds(net.row_low * each, each)
            for step, (who, device) in enumerate(self.low_peers()):
                src, dst = grad_b.at[mine, self.lines], grad_rb.at[who, :, self.lines]
                push(src, dst, grad_sb.at[i, step], grad_qb.at[i, who], device).wait_recv()
            total = grad_b[mine, self.lines].astype(F32)
            for who, _device in self.low_peers():
                total = total + grad_rb[who, :, self.lines].astype(F32)
            if net.high > 1:
                grad_top[b, net.row_high, :, self.lines] = total.astype(BF16)
                for step, (who, device) in enumerate(net.top()):
                    here = grad_top.at[b, net.row_high, :, self.lines]
                    self.move("all", push(here, here, grad_st.at[i, step], grad_qt.at[i, net.row_high], device))
                for step, (who, device) in enumerate(net.top()):
                    there = grad_top.at[b, who, :, self.lines]
                    push(there, there, grad_st.at[i, step], grad_qt.at[i, who], device).wait_recv()
                self.clear("all")
                total = grad_top[b, 0, :, self.lines].astype(F32)
                for j in range(1, net.high):
                    total = total + grad_top[b, j, :, self.lines].astype(F32)
            self.clear("all")
            grad_all[mine, self.lines] = total.astype(BF16)
            for step, (who, device) in enumerate(self.low_peers()):
                here = grad_all.at[mine, self.lines]
                self.move("all", push(here, here, grad_sc.at[i, step], grad_qc.at[i, net.row_low], device))

        def finish(self, b):
            i = 2 * b + self.which
            each = PIECES // net.low
            for step, (who, device) in enumerate(self.low_peers()):
                there = grad_all.at[pl.ds(who * each, each), self.lines]
                push(there, there, grad_sc.at[i, step], grad_qc.at[i, who], device).wait_recv()
            for piece in range(PIECES):
                cols = slice(128 * piece, 128 * (piece + 1))
                grads_out[b, self.first : self.first + self.size, cols] = grad_all[piece, self.lines].astype(F32)

    early = [Reduction(0, 96 if b == 0 else 80) for b in range(BLOCKS)]
    final = [Reduction(96, 64 if b == 0 else 80) for b in range(BLOCKS)]

    order = (0, last) + tuple(range(1, last))
    norms = []
    mid_grads = {}
    out_grads = {}

    def open_block(b, rows):
        z = dot(a3s[b, rows], exp[b])
        a4, b4 = norms[b][3][2], norms[b][3][3]
        return z, (z * a4 + b4) + xs[b][rows].astype(F32)

    kept = [(a1s, keep_mid.at[0]), (d1s, keep_mid.at[1]), (d2s, keep_mid.at[2]), (yb, keep_big)]
    keeps = [pltpu.make_async_copy(held, far_away, keep_sem.at[k]) for k, (held, far_away) in enumerate(kept)]
    backs = [pltpu.make_async_copy(far_away, held, back_sem.at[k]) for k, (held, far_away) in enumerate(kept)]

    def slope_rows(i, _):
        rows, lines, where = trio(i)
        _, pre = open_block(0, rows)
        for k, (f, j) in enumerate(where):
            v = pre[FLAT * k : FLAT * (k + 1)]
            square, t = gelu_core(v)
            part = pl.ds(pl.multiple_of((TRIO * i + k) * FLAT, FLAT), FLAT)
            yb[part] = gelu_slope(v, square, t, 0.5 * live(f)).astype(BF16)
        return 0

    out_store = [frame_copy(yb, out_hbm, f, store_sem.at[f]) for f in range(frames)]

    for b in range(BLOCKS):
        norm1 = affine(first_sums[0], first_sums[1], count, mid(b, 0, 0), mid(b, 0, 1))
        if b == 0:
            gather("exp", 0)
        _, _, a1, b1 = norm1
        carry = (zero8(), zero8())
        if b > 0:
            keeps[0].wait()
            for side in range(2):
                halo_sent(2 * (b - 1) + 1, 2 + b - 1, side)
        for f in order:
            alive = live(f)

            v = z1[b, f * HH : (f + 1) * HH].reshape(HH * WP, 256) * a1 + b1
            _, t = gelu_core(v)
            act = gelu_value(v, t, half_mask(alive, HH)).astype(BF16)
            a1s[f * HH : (f + 1) * HH] = act.reshape(HH, WP, 256)
            m = dot(act, mix[...])
            z2[b, f, 1 : 1 + HH] = m.reshape(HH, WP, 256)
            if f in (0, last):
                halo_send[0 if f == 0 else 1] = m.astype(BF16).reshape(HH, WP, 256)
            carry = (carry[0] + fold(m), carry[1] + fold(m * m))
            if f in (0, last):
                halo_start(2 * b, b, 0 if f == 0 else 1)

        if b == 0:
            keeps[0].start()

        def emit_conv(f):
            pad = pad_mask[:WP, :128] * live(f)

            def emit(row, half, cols, c, carry):
                c = c * pad
                conv[b, f * HH + row, :, cols] = c
                if f in (0, last):
                    halo_send[0 if f == 0 else 1, row, :, cols] = c.astype(BF16)
                e = edge[b, f + 1, row_class(row), :, cols]
                s0, s1, s2 = carry
                return (s0 + fold(c), s1 + fold(c * c), s2 + fold(c * e))

            return emit

        def fill(side):
            present = lane > 0 if side == 0 else lane < lanes - 1

            @pl.when(present)
            def _():
                halo_wait(2 * b, b, side)

                def widen(j, _):
                    hz[side, pl.ds(1 + j * GROUP, GROUP)] = halo_recv[b, side, pl.ds(j * GROUP, GROUP)].astype(F32)
                    return 0

                lax.fori_loop(0, QUADS, widen, 0)

            @pl.when(jnp.logical_not(present))
            def _():
                def clear(j, _):
                    hz[side, pl.ds(1 + j * GROUP, GROUP)] = jnp.zeros((GROUP, WP, 256), F32)
                    return 0

                lax.fori_loop(0, QUADS, clear, 0)

        acc = [[zero8(128), zero8(128)] for _ in range(3)]
        for f in range(1, last):
            acc = convolve(z2.at[b], f, b, False, emit_conv(f), acc)
        if b == 0:
            gather_on("exp", 0)
        for side in range(2):
            fill(side)
            halo_sent(2 * b, b, side)
            f = 0 if side == 0 else last
            acc = convolve(z2.at[b], f, b, False, emit_conv(f), acc)
            halo_start(2 * b + 1, 2 + b, side)
        joined = [jnp.concatenate([flat_sum(a[0]), flat_sum(a[1])], axis=1) for a in acc]
        total_start(3 * b + 1, rows_of(flat_sum(carry[0]), flat_sum(carry[1]), *joined, *edge_sums[b]))
        if b == 0:
            gather_wait("exp", 0)
        else:
            gather_wait("exp", 1)
            tbuf[...] = exp[1].T
            keeps[1].wait()

        def slope1(i, _):
            _, lines, where = trio(i)
            v = z1[b, lines].reshape(TRIO * WIDE, 256) * a1 + b1
            square, t = gelu_core(v)
            d1s[lines] = gelu_slope(v, square, t, 0.5).astype(BF16).reshape(TRIO * GROUP, WP, 256)
            return 0

        lax.fori_loop(0, trios, slope1, 0)
        if b == 0:
            keeps[1].start()
        else:
            lax.fori_loop(trios - 2, trios, slope_rows, 0)
            keeps[3].start()
        got = total_finish(3 * b + 1)
        norm2 = affine(got[0:1], got[1:2], count, mid(b, 1, 0), mid(b, 1, 1))
        _, _, a2, b2 = norm2
        sc, scc, sce, se, see = [got[i : i + 1] for i in range(2, 7)]
        total3 = a2 * sc + b2 * se
        square3 = a2 * a2 * scc + 2.0 * a2 * b2 * sce + b2 * b2 * see
        norm3 = affine(total3, square3, count, mid(b, 2, 0), mid(b, 2, 1))
        _, _, a3, b3 = norm3

        norm3_pattern(b, a3, b2, b3)
        if b == 0:
            gather("red", 1)
            gather("mix", 1)

        def activate(i, _):
            rows, lines, where = trio(i)
            c = conv[b, lines].reshape(TRIO * WIDE, 256)
            acts = []
            for k, (f, j) in enumerate(where):
                v = c[WIDE * k : WIDE * (k + 1)] * (a3 * a2) + edge_rows(pat.at[f + 1], j)
                _, t = gelu_core(v)
                acts.append(squeeze(gelu_value(v, t, 0.5 * live(f))))
            a3s[b, rows] = jnp.concatenate(acts, axis=0).astype(BF16)
            return 0

        lax.fori_loop(0, trios, activate, 0)
        gram = dot_rows(a3s[b], a3s[b])
        line = dot(jnp.ones((16, frames * frame_rows), BF16), a3s[b])
        high = jnp.concatenate([gram, line], axis=0)
        split = high.astype(BF16)
        grown = dot(split, exp[b]) + dot((high - split.astype(F32)).astype(BF16), exp[b])
        squares = flat_sum(fold(grown[:256] * exp[b].astype(F32)))
        if b == 0:
            gather_on("red", 1)
            gather_on("mix", 1)
        total_start(3 * b + 2, rows_of(grown[256:257], squares))
        if b == 0:
            gather_wait("red", 1)
            tbuf[...] = red_t[1].T
        else:
            keeps[2].wait()

        def slope3(i, _):
            _, lines, where = trio(i)
            c = conv[b, lines].reshape(TRIO * WIDE, 256)
            out = []
            for k, (f, j) in enumerate(where):
                v = c[WIDE * k : WIDE * (k + 1)] * (a3 * a2) + edge_rows(pat.at[f + 1], j)
                square, t = gelu_core(v)
                out.append(gelu_slope(v, square, t, 0.5).astype(BF16))
            d2s[lines] = jnp.concatenate(out, axis=0).reshape(TRIO * GROUP, WP, 256)
            return 0

        lax.fori_loop(0, trios, slope3, 0)
        if b == 0:
            keeps[2].start()
        got = total_finish(3 * b + 2)
        norm4 = affine(wide_row(got, 0), wide_row(got, 4), count4, norm_out[b, 0:1], norm_out[b, 1:2])
        norms.append((norm1, norm2, norm3, norm4, (sc, scc, sce, se, see)))

        if b == 0:
            gather("exp", 1)

            def closing(i, carry):
                rows, lines, where = trio(i)
                _, pre = open_block(0, rows)
                results = []
                for (f, j), v in zip(where, pieces(pre, FLAT)):
                    _, t = gelu_core(v)
                    results.append(gelu_value(v, t, 0.5 * live(f)).astype(BF16))
                result = jnp.concatenate(results, axis=0)
                x1[rows] = result
                z = dot(result, tbuf[...])
                z1[1, lines] = spread(z).reshape(TRIO * GROUP, WP, 256)
                return (carry[0] + fold(z), carry[1] + fold(z * z))

            carry = lax.fori_loop(0, trios, closing, (zero8(), zero8()))
            gather_on("exp", 1)
            total_start(3, rows_of(flat_sum(carry[0]), flat_sum(carry[1])))
            gather_wait("mix", 1)
            mix[...] = mix_t[1].T
            lax.fori_loop(0, trios - 2, slope_rows, 0)
            got = total_finish(3)
            first_sums = (got[0:1], got[1:2])

    cot_load.wait()
    keeps[3].wait()

    def ending(i, carry):
        rows, lines, where = trio(i)
        z, pre = open_block(1, rows)
        g = sb[rows]
        s0, s1 = carry
        for k, (f, j) in enumerate(where):
            here = slice(FLAT * k, FLAT * (k + 1))
            v, half = pre[here], 0.5 * live(f)
            square, t = gelu_core(v)
            part = pl.ds(pl.multiple_of((TRIO * i + k) * FLAT, FLAT), FLAT)
            yb[part] = gelu_value(v, t, half).astype(BF16)
            s = gelu_slope(v, square, t, half) * g[here].astype(F32)
            sb[part] = s.astype(BF16)
            s0, s1 = s0 + fold(s), s1 + fold(s * z[here])
        return s0, s1

    carry = lax.fori_loop(0, trios, ending, (zero8(1024), zero8(1024)))
    total_start(6, rows_of(flat_sum(carry[0]), flat_sum(carry[1])))
    for copy in out_store:
        copy.start()

    for b in reversed(range(BLOCKS)):
        turn = BLOCKS - 1 - b
        base = 6 + 3 * turn
        norm1, norm2, norm3, norm4, (sc, scc, sce, se, see) = norms[b]
        _, _, a1, b1 = norm1
        mean2, scale2, a2, b2 = norm2
        mean3, scale3, a3, b3 = norm3
        a4 = norm4[2]

        got = total_finish(base)
        slope4, bias4, gain_grad, shift_grad = back_affine(wide_row(got, 0), wide_row(got, 4), count4, norm4)
        out_grads[b] = (gain_grad, shift_grad)
        if turn == 0:
            for copy in out_store:
                copy.wait()
        for side in range(2):
            if turn == 0:
                halo_sent(2 * (BLOCKS - 1) + 1, 2 + BLOCKS - 1, side)
            else:
                halo_sent(2 * BLOCKS + turn - 1, b + 1, side)

        if turn > 0:
            early[b + 1].to_rows(b + 1)
            final[b + 1].to_side(b + 1)
        kind = 2 * BLOCKS + turn
        if turn > 0:
            backs[2].wait()
        acc = (zero8(), zero8(), zero8())
        for f in order:
            alive = live(f)

            rows = slice(f * frame_rows, (f + 1) * frame_rows)
            z = dot(a3s[b, rows], exp[b])
            d4 = (sb[rows].astype(F32) * a4 + (z * slope4 + bias4 * alive)).astype(BF16)
            yb[rows] = d4
            back = spread(dot(d4, tbuf[...]))
            for j in range(QUADS):
                c = conv[b, f * HH + GROUP * j : f * HH + GROUP * (j + 1)].reshape(WIDE, 256)
                slope = d2s[f * HH + GROUP * j : f * HH + GROUP * (j + 1)].reshape(WIDE, 256)
                e3 = back[WIDE * j : WIDE * (j + 1)] * slope.astype(F32)
                dz[f, 1 + GROUP * j : 1 + GROUP * (j + 1)] = e3.reshape(GROUP, WP, 256)
                if f in (0, last):
                    halo_send[0 if f == 0 else 1, GROUP * j : GROUP * (j + 1)] = e3.astype(BF16).reshape(GROUP, WP, 256)
                e = edge_rows(edge.at[b, f + 1], j)
                acc = (acc[0] + fold(e3), acc[1] + fold(e3 * c), acc[2] + fold(e3 * e))
            if f in (0, last):
                halo_start(kind, b, 0 if f == 0 else 1)
        total_start(base + 1, rows_of(*[flat_sum(a) for a in acc]))

        if turn > 0:
            early[b + 1].clear("a")

        def expand_grad(i, _):
            cols = pl.ds(pl.multiple_of(i * 256, 256), 256)
            g = dot_rows(a3s[b], yb[:, cols])
            for who in range(lanes):
                for h in range(2):
                    early[b].put(who, 2 * i + h, 0, g[share * who : share * (who + 1), 128 * h : 128 * (h + 1)])
            return 0

        lax.fori_loop(0, 4, expand_grad, 0)
        if b > 0:
            tbuf[...] = exp[b - 1].T
            backs[3].start()

        got = total_finish(base + 1)
        e3_sum, e3_conv, e3_edge = got[0:1], got[1:2], got[2:3]
        e3_third = a2 * e3_conv + b2 * e3_edge
        slope3, bias3, gain3, shift3 = back_affine(e3_sum, e3_third, count, norm3)
        third_conv = a2 * scc + b2 * sce
        third_edge = a2 * sce + b2 * see
        d3_conv = a3 * e3_conv + bias3 * sc + slope3 * third_conv
        d3_edge = a3 * e3_edge + bias3 * se + slope3 * third_edge
        slope2, bias2, gain2, shift2 = back_affine(d3_edge, d3_conv, count, norm2)

        if turn > 0:
            early[b + 1].to_all(b + 1)
            final[b + 1].to_rows(b + 1)
        for f in range(-1, frames + 1):
            live_pad = pad_mask[:WP] * live(f)
            for cls in range(3):
                pat[f + 1, cls] = bias3 * live_pad + (slope3 * b2) * edge[b, f + 1, cls]
        slope_c = slope3 * a2

        def to_d3(q, _):
            f = lax.div(q, QUADS)
            j = lax.rem(q, QUADS)
            rows = pl.ds(1 + j * GROUP, GROUP)
            c = conv[b, pl.ds(q * GROUP, GROUP)].reshape(WIDE, 256)
            e3 = dz[f, rows].reshape(WIDE, 256)
            d3 = e3 * a3 + c * slope_c + edge_rows(pat.at[f + 1], j)
            dz[f, rows] = d3.reshape(GROUP, WP, 256)
            return 0

        lax.fori_loop(0, frames * QUADS, to_d3, 0)

        def fill_back(side):
            present = lane > 0 if side == 0 else lane < lanes - 1
            f = -1 if side == 0 else frames

            @pl.when(present)
            def _():
                halo_wait(2 * b + 1, 2 + b, side)
                halo_wait(kind, b, side)

                def widen(j, _):
                    rows = pl.ds(j * GROUP, GROUP)
                    c = halo_recv[2 + b, side, rows].astype(F32).reshape(WIDE, 256)
                    e3 = halo_recv[b, side, rows].astype(F32).reshape(WIDE, 256)
                    d3 = e3 * a3 + c * slope_c + edge_rows(pat.at[f + 1], j)
                    hz[side, pl.ds(1 + j * GROUP, GROUP)] = d3.reshape(GROUP, WP, 256)
                    return 0

                lax.fori_loop(0, QUADS, widen, 0)

            @pl.when(jnp.logical_not(present))
            def _():
                def clear(j, _):
                    hz[side, pl.ds(1 + j * GROUP, GROUP)] = jnp.zeros((GROUP, WP, 256), F32)
                    return 0

                lax.fori_loop(0, QUADS, clear, 0)

        for side in range(2):
            fill_back(side)

        def emit_back(f):
            pad = pad_mask[:WP, :128] * live(f)

            def emit(row, half, cols, e2, carry):
                z = z2[b, f, row + 1, :, cols]
                d2 = (e2 * a2[:, cols] + (z * slope2[:, cols] + bias2[:, cols])) * pad
                d2s[f * HH + row, :, cols] = d2.astype(BF16)
                return carry

            return emit

        for f in range(frames):
            convolve(dz, f, b, True, emit_back(f), [])

        if turn > 0:
            backs[0].wait()
            backs[1].wait()

        def unmixing(i, acc):
            _, lines, where = trio(i)
            e = dot(d2s[lines].reshape(TRIO * WIDE, 256), mix_t[b])
            z = z1[b, lines].reshape(TRIO * WIDE, 256)
            for k, (f, j) in enumerate(where):
                here = slice(WIDE * k, WIDE * (k + 1))
                part = pl.ds((TRIO * i + k) * GROUP, GROUP)
                e1 = e[here] * d1s[part].reshape(WIDE, 256).astype(F32)
                conv[b, part] = e1.reshape(GROUP, WP, 256)
                acc = (acc[0] + fold(e1), acc[1] + fold(e1 * z[here]))
            return acc

        acc = lax.fori_loop(0, trios, unmixing, (zero8(), zero8()))
        if turn > 0:
            early[b + 1].finish(b + 1)
        total_start(base + 2, rows_of(*[flat_sum(a) for a in acc]))

        def depth_grad(half, b=b, a2=a2, b2=b2):
            place, at = (early[b], 80) if b == 0 else (final[b], 64)
            cols = slice(128 * half, 128 * (half + 1))
            taps_grad = tuple(zero8(128) for _ in range(KVOL))
            for f in range(frames):
                planes = []
                for dt in range(3):
                    g = f - (dt - 1)
                    planes.append(hz.at[0] if g < 0 else hz.at[1] if g > last else dz.at[g])
                shift_rows = b2[:, cols] * (pad_mask[:WP, :128] * live(f))

                def tap_rows(h, taps_grad):
                    a = z2[b, f, h + 1, :, cols] * a2[:, cols] + shift_rows
                    moved = [pltpu.roll(a, 1, 0), a, pltpu.roll(a, WP - 1, 0)]
                    new = list(taps_grad)
                    for dt in range(3):
                        for dh in range(3):
                            d = planes[dt][h + 1 - (dh - 1), :, cols]
                            for dw in range(3):
                                k = dt * 9 + dh * 3 + dw
                                new[k] = new[k] + fold(d * moved[dw])
                    return tuple(new)

                taps_grad = lax.fori_loop(0, HH, tap_rows, taps_grad)
            lines = jnp.concatenate(
                [flat_sum(t) for t in taps_grad] + [jnp.zeros((WP - KVOL, 128), F32)], axis=0
            )
            for r in range(4):
                part = jnp.concatenate([lines[8 * r : 8 * r + 8], zero8(128)], axis=0)
                for who in range(lanes):
                    place.put(who, 2 * r + half, at, part)

        depth_grad(0)
        if b == 0:
            depth_grad(1)
        g = dot_rows(d2s[...].reshape(frames * HH * WP, 256), a1s[...].reshape(frames * HH * WP, 256))
        for who in range(lanes):
            for r in range(4):
                for h in range(2):
                    first = share * who + 16 * r
                    early[b].put(who, 2 * r + h, 64, g[first : first + 16, 128 * h : 128 * (h + 1)])
        early[b].to_pair(b)
        if b > 0:
            for k in range(3):
                backs[k].start()

        got = total_finish(base + 2)
        slope1, bias1, gain1, shift1 = back_affine(got[0:1], got[1:2], count, norm1)
        mid_grads[b] = ((gain1, shift1), (gain2, shift2), (gain3, shift3))

        early[b].to_side(b)
        def first_grad(i):
            rows, lines, where = trio(i)
            e1 = conv[b, lines].reshape(TRIO * WIDE, 256)
            z = z1[b, lines].reshape(TRIO * WIDE, 256)
            parts = []
            for k, (f, j) in enumerate(where):
                here = slice(WIDE * k, WIDE * (k + 1))
                alive = live(f)
                parts.append(squeeze(e1[here] * a1 + (z[here] * (slope1 * alive) + bias1 * alive)))
            d1 = jnp.concatenate(parts, axis=0).astype(BF16)
            a3s[b, rows] = d1
            return rows, where, d1

        def reduce_grad(i, _):
            cols = pl.ds(pl.multiple_of(i * 256, 256), 256)
            g = dot_rows(a3s[b], xs[b][:, cols])
            for who in range(lanes):
                for h in range(2):
                    final[b].put(who, 2 * i + h, 0, g[share * who : share * (who + 1), 128 * h : 128 * (h + 1)])
            return 0

        if b > 0:

            backs[3].wait()

            def passing(i, carry):
                rows, where, d1 = first_grad(i)
                g = dot(d1, red_t[b]) + sb[rows].astype(F32)
                z = dot(a3s[b - 1, rows], exp[b - 1])
                slope = yb[rows]
                s0, s1 = carry
                for k, (f, j) in enumerate(where):
                    here = slice(FLAT * k, FLAT * (k + 1))
                    s = slope[here].astype(F32) * g[here]
                    sb[pl.ds(pl.multiple_of((TRIO * i + k) * FLAT, FLAT), FLAT)] = s.astype(BF16)
                    s0, s1 = s0 + fold(s), s1 + fold(s * z[here])
                return s0, s1

            carry = lax.fori_loop(0, trios, passing, (zero8(1024), zero8(1024)))
            total_start(base + 3, rows_of(flat_sum(carry[0]), flat_sum(carry[1])))
            depth_grad(1)
            lax.fori_loop(0, 4, reduce_grad, 0)
            final[b].to_pair(b)
        else:
            final[b + 1].to_all(b + 1)

            def only_d1(i, _):
                first_grad(i)
                return 0

            lax.fori_loop(0, trios, only_d1, 0)
            final[b + 1].clear("a")
            lax.fori_loop(0, 4, reduce_grad, 0)
            final[b].to_pair(b)
            early[b + 1].clear("b", "all")
            early[b].to_rows(b)
            steps = (lambda: final[b].to_side(b), lambda: early[b].to_all(b))
            gtok_store = [frame_copy(yb, gtok_hbm, f, store_sem.at[f]) for f in range(frames)]
            for f in range(frames):
                rows = slice(f * frame_rows, (f + 1) * frame_rows)
                yb[rows] = (dot(a3s[b, rows], red_t[b]) + sb[rows].astype(F32)).astype(BF16)
                gtok_store[f].start()
                if f < len(steps):
                    steps[f]()
            final[b + 1].finish(b + 1)
            final[b + 1].clear("b", "all")
            final[b].to_rows(b)
            early[b].finish(b)
            final[b].to_all(b)
            final[b].finish(b)

    for b in range(BLOCKS):
        for k in range(3):
            for w in range(2):
                r = (b * 3 + k) * 2 + w
                gmid_out[r : r + 1] = mid_grads[b][k][w]
        for w in range(2):
            gout_out[2 * b + w : 2 * b + w + 1] = out_grads[b][w]

    for copy in gtok_store:
        copy.wait()
    early[0].clear("a", "b", "all")
    final[0].clear("a", "b", "all")
    for copy in late + travelling:
        copy.wait_send()
    for side in range(2):
        halo_sent(2 * BLOCKS + BLOCKS - 1, 0, side)


def whole_call(groups, lanes, counts, tokens, cotangent, reduce_loc, mix_loc, expand_loc, small_loc, norm_out):
    rows = tokens.shape[0]
    frames = rows // (HH * WW)
    whole = pl.BlockSpec(memory_space=pltpu.VMEM)
    hbm = pl.BlockSpec(memory_space=pl.ANY)
    dma = pltpu.SemaphoreType.DMA
    low, high = stages(groups)
    far = low * (lanes // 2)
    lines = frames * HH
    sums = 6 * BLOCKS
    kinds = 3 * BLOCKS
    shape = jax.ShapeDtypeStruct
    return pl.pallas_call(
        functools.partial(whole_kernel, groups, lanes),
        out_shape=(
            shape((rows, 1024), BF16),
            shape((rows, 1024), BF16),
            shape((BLOCKS, 176, 1024), F32),
            shape((BLOCKS * 6, 256), F32),
            shape((BLOCKS * 2, 1024), F32),
            shape((rows, 1024), BF16),
            shape((3, lines, WP, 256), BF16),
        ),
        in_specs=[pl.BlockSpec(memory_space=pltpu.SMEM)] + [hbm] * 5 + [whole] * 2,
        out_specs=[hbm] * 2 + [whole] * 3 + [hbm] * 2,
        scratch_shapes=[
            pltpu.VMEM((rows, 1024), BF16),
            pltpu.VMEM((rows, 1024), BF16),
            pltpu.VMEM((rows, 1024), BF16),
            pltpu.VMEM((rows, 1024), BF16),
            pltpu.VMEM((BLOCKS, 256, 1024), BF16),
            pltpu.VMEM((BLOCKS, 256, 1024), BF16),
            pltpu.VMEM((1024, 256), BF16),
            pltpu.VMEM((BLOCKS, 256, 256), BF16),
            pltpu.VMEM((256, 256), BF16),
            pltpu.VMEM((lanes,) + small_loc.shape, F32),
            pltpu.VMEM((2 * small_loc.shape[0], 256), F32),
            pltpu.VMEM((BLOCKS, lines, WP, 256), F32),
            pltpu.VMEM((lines, WP, 256), BF16),
            pltpu.VMEM((BLOCKS, frames, HH + 2, WP, 256), F32),
            pltpu.VMEM((frames, HH + 2, WP, 256), F32),
            pltpu.VMEM((2, HH + 2, WP, 256), F32),
            pltpu.VMEM((BLOCKS, lines, WP, 256), F32),
            pltpu.VMEM((BLOCKS, rows, 256), BF16),
            pltpu.VMEM((BLOCKS, frames + 2, 3, WP, 256), F32),
            pltpu.VMEM((frames + 2, 3, WP, 256), F32),
            pltpu.VMEM((lines, WP, 256), BF16),
            pltpu.VMEM((lines, WP, 256), BF16),
            pltpu.VMEM((2, HH, WP, 256), BF16),
            pltpu.VMEM((2 * BLOCKS, 2, HH, WP, 256), BF16),
            pltpu.VMEM((lanes, PIECES, 176, 128), BF16),
            pltpu.VMEM((3, PIECES, 176, 128), BF16),
            pltpu.VMEM((PIECES, 176, 128), BF16),
            pltpu.VMEM((low, PIECES // low, 176, 128), BF16),
            pltpu.VMEM((PIECES, 176, 128), BF16),
            pltpu.VMEM((BLOCKS, high, PIECES // low, 176 if high > 1 else 16, 128), BF16),
            pltpu.VMEM((2, 2, 16, 128), F32),
            pltpu.VMEM((2, far, 16, 128), F32),
            pltpu.VMEM((2, high, 16, 128), F32),
            dma((sums,)),
            dma((sums,)),
            dma((sums, far)),
            dma((sums, far)),
            dma((sums, high)),
            dma((sums, high)),
            dma((7, 3)),
            dma((7, lanes)),
            dma((kinds, 2)),
            dma((kinds, 2)),
            dma((frames + 1,)),
            dma((frames,)),
            dma((2 * BLOCKS, 3)),
            dma((2 * BLOCKS, 3)),
            dma((2 * BLOCKS, low)),
            dma((2 * BLOCKS, low)),
            dma((2 * BLOCKS, low)),
            dma((2 * BLOCKS, low)),
            dma((2 * BLOCKS, high)),
            dma((2 * BLOCKS, high)),
            dma((BLOCKS, 4)),
            dma((4,)),
            dma((4,)),
        ],
        compiler_params=pltpu.CompilerParams(
            collective_id=1, has_side_effects=True, vmem_limit_bytes=63 * 2**20
        ),
    )(counts, tokens, cotangent, reduce_loc, mix_loc, expand_loc, small_loc, norm_out)


def descend(weight, moment, grad):
    moment_new = MOMENTUM * moment + grad + DECAY * weight
    return (weight - LEARN_RATE * moment_new, moment_new)


def update_kernel(lanes, *refs):
    out_raw, gtok_raw = refs[:2]
    out, gtok = refs[17:19]
    held = refs[37:70]
    big, sems, store_sems, small_sems, small_stores = refs[70:]
    smalls = [pltpu.make_async_copy(refs[2 + k], held[k], small_sems.at[k]) for k in range(15)]
    results = [pltpu.make_async_copy(held[15 + k], refs[19 + k], small_stores.at[k]) for k in range(18)]
    reduced, gmid, gout = held[:3]
    weights, moments = held[3:9], held[9:15]
    grads, new_weights, new_moments = held[15:21], held[21:27], held[27:33]
    chunks = sems.shape[1]
    rows = out.shape[0] // chunks
    copies, stores = [], []
    for k in range(chunks):
        for which, (src, dst) in enumerate(((out_raw, out), (gtok_raw, gtok))):
            here = pl.ds(k * rows, rows)
            copies.append(pltpu.make_async_copy(src.at[here], big.at[which, here], sems.at[which, k]))
            stores.append(pltpu.make_async_copy(big.at[which, here], dst.at[here], store_sems.at[which, k]))
    for copy in smalls + copies:
        copy.start()
    for copy in smalls:
        copy.wait()
    lane = lax.axis_index("chan")
    narrow = 256 // lanes

    def mine(v):
        out = v[:, :narrow]
        for who in range(1, lanes):
            out = jnp.where(lane == who, v[:, narrow * who : narrow * (who + 1)], out)
        return out

    def step(slot, at, grad):
        weight, moment = descend(weights[slot][at], moments[slot][at], grad)
        grads[slot][at] = grad
        new_weights[slot][at] = weight
        new_moments[slot][at] = moment

    depths = []
    for b in range(BLOCKS):
        step(0, (b,), reduced[b, 96:160])
        mix = reduced[b, 64:80]
        step(1, (b,), jnp.concatenate([mix[:, 256 * r : 256 * (r + 1)] for r in range(4)], axis=0))
        depth = reduced[b, 80:88] if b == 0 else reduced[b, 160:168]
        depths.append(mine(jnp.concatenate([depth[:, 256 * r : 256 * (r + 1)] for r in range(4)], axis=0)))
        step(3, (b,), reduced[b, 0:64])
        step(5, (b,), gout[2 * b : 2 * b + 2])
    for k in range(KVOL):
        step(2, (k,), jnp.concatenate([depth[k : k + 1] for depth in depths], axis=0))
    middle = mine(gmid[...])
    for k in range(BLOCKS * 3):
        step(4, (k,), middle[2 * k : 2 * k + 2])
    for copy in results:
        copy.start()
    for copy, store in zip(copies, stores):
        copy.wait()
        store.start()
    for store in stores + results:
        store.wait()


def update_call(lanes, *args):
    hbm = pl.BlockSpec(memory_space=pl.ANY)
    like = [jax.ShapeDtypeStruct(v.shape, v.dtype) for v in args]
    return pl.pallas_call(
        functools.partial(update_kernel, lanes),
        out_shape=tuple(like[:2] + like[5:11] * 3),
        in_specs=[hbm] * 17,
        out_specs=[hbm] * 20,
        scratch_shapes=[pltpu.VMEM(v.shape, v.dtype) for v in like[2:] + like[5:11] * 3]
        + [
            pltpu.VMEM((2,) + args[0].shape, args[0].dtype),
            pltpu.SemaphoreType.DMA((2, 7)),
            pltpu.SemaphoreType.DMA((2, 7)),
            pltpu.SemaphoreType.DMA((15,)),
            pltpu.SemaphoreType.DMA((18,)),
        ],
        compiler_params=pltpu.CompilerParams(vmem_limit_bytes=60 * 2**20),
    )(*args)


def shards(
    tokens,
    frame_counts,
    cotangent,
    w_reduce,
    w_mix,
    w_depth,
    w_expand,
    norm_mid,
    norm_out,
    moment_reduce,
    moment_mix,
    moment_depth,
    moment_expand,
    moment_mid,
    moment_out,
):
    lane = lax.axis_index("chan")
    lanes = lax.axis_size("chan")
    narrow = w_reduce.shape[2]
    small = jnp.concatenate([w_depth.reshape(-1, narrow), norm_mid.reshape(-1, narrow)], axis=0)
    small = jnp.pad(small, ((0, -small.shape[0] % 16), (0, 0)))
    small = jnp.concatenate(jnp.split(small, 2, axis=0), axis=1)
    turned = lambda v: jnp.swapaxes(v, 1, 2)
    raw = whole_call(
        lax.axis_size("dp"),
        lanes,
        frame_counts,
        tokens,
        cotangent,
        turned(w_reduce),
        turned(w_mix),
        w_expand,
        small,
        norm_out,
    )
    swap = lambda v: jnp.swapaxes(v, 0, 1)
    flat = lambda v: v.reshape((-1,) + v.shape[2:])
    inside = lambda r, m, d, e, mid, out: (turned(r), turned(m), swap(d), e, flat(mid), out)
    outside = lambda r, m, d, e, mid, out: (turned(r), turned(m), swap(d), e, mid.reshape(norm_mid.shape), out)
    done = update_call(
        lanes,
        *raw[:5],
        *inside(w_reduce, w_mix, w_depth, w_expand, norm_mid, norm_out),
        *inside(moment_reduce, moment_mix, moment_depth, moment_expand, moment_mid, moment_out),
    )
    return done[:2] + outside(*done[2:8]) + outside(*done[8:14]) + outside(*done[14:20])


def solution(mesh):
    rows = P(("dp", "chan"), None)
    weights = (
        P(None, None, "chan"),
        P(None, None, "chan"),
        P(None, None, "chan"),
        P(None, "chan", None),
        P(None, None, None, "chan"),
        P(),
    )
    return jax.shard_map(
        shards,
        mesh=mesh,
        in_specs=(rows, P("dp"), rows) + weights + weights,
        out_specs=(rows, rows) + weights + weights + weights,
        check_vma=False,
    )
```

```python
import functools

import jax
import jax.numpy as jnp
from jax import lax
from jax.experimental import pallas as pl
from jax.experimental.pallas import tpu as pltpu
from jax.sharding import PartitionSpec as P

FRAMES = 12
HH = 28
WW = 28
WP = 32
KVOL = 27
BLOCKS = 2
GROUP = 4
QUADS = HH // GROUP
FLAT = GROUP * WW
WIDE = GROUP * WP
PIECES = 8
TRIO = 3

EPS = 1e-05
LEARN_RATE = 0.001
MOMENTUM = 0.9
DECAY = 0.0001
MESH = pl.DeviceIdType.MESH
F32 = jnp.float32
BF16 = jnp.bfloat16
ROOT = 0.7978845608028654
CUBE = 0.044715


def gelu_core(v):
    square = v * v
    return square, jnp.tanh(v * (ROOT + (ROOT * CUBE) * square))


def gelu_value(v, t, half):
    h = half * v
    return h * t + h


def gelu_slope(v, square, t, half):
    r = v * (half * ROOT + (half * (3.0 * ROOT * CUBE)) * square)
    return (half * t + half) + (r - r * (t * t))


def dot_rows(left, right):
    return lax.dot_general(left, right, (((0,), (0,)), ((), ())), preferred_element_type=F32)


def dot(left, right):
    return jnp.dot(left, right, preferred_element_type=F32)


def fold(v):
    return jnp.sum(v.reshape(v.shape[0] // 8, 8, v.shape[1]), axis=0)


def spread(v):
    gap = jnp.zeros((WP - WW, v.shape[1]), v.dtype)
    parts = []
    for h in range(v.shape[0] // WW):
        parts += [v[WW * h : WW * (h + 1)], gap]
    return jnp.concatenate(parts, axis=0)


def squeeze(v):
    return jnp.concatenate([v[WP * h : WP * h + WW] for h in range(v.shape[0] // WP)], axis=0)


def pieces(v, rows):
    return [v[rows * k : rows * (k + 1)] for k in range(v.shape[0] // rows)]


def rows_of(*vectors):
    parts = []
    for v in vectors:
        parts += pieces_of(v)
    n = 4 if len(parts) <= 4 else 8
    out = []
    for side in range(2):
        out += [v[:, 128 * side : 128 * (side + 1)] for v in parts]
        if len(parts) < n:
            out.append(jnp.zeros((n - len(parts), 128), F32))
    return jnp.concatenate(out, axis=0)


def pieces_of(v):
    return [v[:, 256 * i : 256 * (i + 1)] for i in range(v.shape[1] // 256)]


def flat_sum(v):
    return jnp.sum(v, axis=0, keepdims=True)


def wide_row(v, first):
    return jnp.concatenate([v[first + i : first + i + 1] for i in range(4)], axis=1)


class Net:
    def __init__(self, groups, lanes):
        self.lanes = lanes
        self.low, self.high = stages(groups)
        self.row = lax.axis_index("dp")
        self.lane = lax.axis_index("chan")
        self.core = lax.rem(self.lane, 2)
        self.side = lax.div(self.lane, 2)
        self.half = lanes // 2
        self.row_low = lax.rem(self.row, self.low)
        self.row_high = lax.div(self.row, self.low)

    def near(self):
        return [(1 - self.core, (self.row, self.side * 2 + 1 - self.core))]

    def far(self):
        out = []
        for o in sorted(range(self.low), key=lambda o: abs(2 * o - self.low - 1)):
            for p in range(self.half):
                if o or p:
                    row = lax.rem(self.row_low + o, self.low)
                    side = lax.rem(self.side + p, self.half)
                    out.append((row * self.half + side, (self.row_high * self.low + row, side * 2 + self.core)))
        return out

    def far_slot(self):
        return self.row_low * self.half + self.side

    def top(self):
        rows = [lax.rem(self.row_high + o, self.high) for o in range(1, self.high)]
        return [(row, (row * self.low + self.row_low, self.lane)) for row in rows]

    def pair(self):
        lane = self.side * 2 + 1 - self.core
        return lane, (self.row, lane)

    def across(self):
        lane = (1 - self.side) * 2 + self.core
        return lane, (self.row, lane)

    def corner(self):
        return (1 - self.side) * 2 + 1 - self.core


def stages(groups):
    low = min(groups, 8)
    return low, groups // low


def push(src, dst, send, recv, device):
    copy = pltpu.make_async_remote_copy(
        src_ref=src, dst_ref=dst, send_sem=send, recv_sem=recv, device_id=device, device_id_type=MESH
    )
    return copy


def whole_kernel(
    groups,
    lanes,
    counts,
    tokens,
    cotangent,
    reduce_loc,
    mix_loc,
    expand_loc,
    depth_loc,
    mid_loc,
    norm_out,
    out_hbm,
    gtok_hbm,
    grads_out,
    gmid_out,
    gout_out,
    keep_big,
    keep_mid,
    x0,
    x1,
    yb,
    sb,
    red_t,
    exp,
    tbuf,
    mix_t,
    mix,
    small_in,
    small,
    z1,
    a1s,
    z2,
    dz,
    hz,
    conv,
    a3s,
    edge,
    pat,
    d2s,
    d1s,
    halo_send,
    halo_recv,
    grad_a,
    grad_ra,
    grad_b,
    grad_rb,
    grad_all,
    grad_top,
    near,
    far,
    top,
    near_send,
    near_recv,
    far_send,
    far_recv,
    top_send,
    top_recv,
    gather_send,
    gather_recv,
    halo_ssem,
    halo_rsem,
    load_sem,
    store_sem,
    grad_sa,
    grad_qa,
    grad_sb,
    grad_qb,
    grad_sc,
    grad_qc,
    grad_st,
    grad_qt,
    weight_sem,
    keep_sem,
    back_sem,
):
    net = Net(groups, lanes)
    lane = net.lane
    frames = tokens.shape[0] // (HH * WW)
    frame_rows = HH * WW
    last = frames - 1
    count_here = counts[0]
    xs = (x0, x1)

    def live(frame):
        position = lane * frames + frame
        return jnp.where((position >= 0) & (position < count_here), 1.0, 0.0)

    def frame_copy(src, dst, f, sem):
        rows = pl.ds(f * frame_rows, frame_rows)
        return pltpu.make_async_copy(src.at[rows], dst.at[rows], sem)

    loads = [frame_copy(tokens, x0, f, load_sem.at[f]) for f in range(frames)]
    cot_load = pltpu.make_async_copy(cotangent, sb, load_sem.at[frames])
    for copy in loads:
        copy.start()
    cot_load.start()
    weight_loads = {}
    for b in range(BLOCKS):
        places = [
            ("red", reduce_loc.at[b], grads_out.at[b, pl.ds(0, 64)]),
            ("exp", expand_loc.at[b], grads_out.at[b, pl.ds(64, 64)]),
            ("mix", mix_loc.at[b, pl.ds(0, 32)], grads_out.at[b, pl.ds(128, 32), pl.ds(0, 256)]),
            ("mix", mix_loc.at[b, pl.ds(32, 32)], grads_out.at[b, pl.ds(128, 32), pl.ds(256, 256)]),
        ]
        for k, (name, src, dst) in enumerate(places):
            copy = pltpu.make_async_copy(src, dst, weight_sem.at[b, k])
            copy.start()
            weight_loads.setdefault((name, b), []).append(copy)

    barrier = pltpu.get_barrier_semaphore()
    friends = [d for peers in (net.near(), net.far(), net.top()) for _, d in peers] + [(net.row, net.corner())]
    for device in friends:
        pl.semaphore_signal(barrier, inc=1, device_id=device, device_id_type=MESH)
    pl.semaphore_wait(barrier, len(friends))

    own = net.lane
    share = red_t.shape[1] // lanes
    late = []

    def gather(name, b):
        slot, dst_of = plan[name, b]
        mine = dst_of(own)
        for copy in weight_loads.get((name, b), []):
            copy.wait()
        if name == "red":
            mine[...] = grads_out[b, :64].astype(BF16)
        elif name == "exp":
            mine[...] = grads_out[b, 64:128].astype(BF16)
        elif name == "mix":
            parts = [grads_out[b, 128:160, :256], grads_out[b, 128:160, 256:512]]
            mine[...] = jnp.concatenate(parts, axis=0).astype(BF16)
        else:
            half_rows = small.shape[0] // 2
            lines = [depth_loc[k, b : b + 1] for b in range(BLOCKS) for k in range(KVOL)]
            lines += [mid_loc[k, w : w + 1] for k in range(3 * BLOCKS) for w in range(2)]
            for r, line in enumerate(lines):
                side = r // half_rows
                mine[r - side * half_rows : r - side * half_rows + 1, 64 * side : 64 * (side + 1)] = line
        for step, (_, device) in enumerate((net.pair(), net.across())):
            copy = push(mine, mine, gather_send.at[slot, step], gather_recv.at[slot, own], device)
            copy.start()
            late.append(copy)

    def gather_on(name, b):
        slot, dst_of = plan[name, b]
        who, device = net.across()
        piece = dst_of(who)
        push(piece, piece, gather_send.at[slot, 1], gather_recv.at[slot, who], device).wait_recv()
        copy = push(piece, piece, gather_send.at[slot, 2], gather_recv.at[slot, who], net.pair()[1])
        copy.start()
        late.append(copy)

    def gather_wait(name, b):
        slot, dst_of = plan[name, b]
        for who in (net.pair()[0], net.corner()):
            push(dst_of(who), dst_of(who), gather_send.at[slot, 0], gather_recv.at[slot, who], net.pair()[1]).wait_recv()

    def block_rows(ref, b):
        return lambda who: ref.at[b, pl.ds(pl.multiple_of(who * share, share), share)]

    plan = {
        ("red", 0): (0, block_rows(red_t, 0)),
        ("mix", 0): (1, block_rows(mix_t, 0)),
        ("small", 0): (2, lambda who: small_in.at[who]),
        ("exp", 0): (3, block_rows(exp, 0)),
        ("red", 1): (4, block_rows(red_t, 1)),
        ("mix", 1): (5, block_rows(mix_t, 1)),
        ("exp", 1): (6, block_rows(exp, 1)),
    }
    for name in (("red", 0), ("mix", 0), ("small", 0)):
        gather(*name)

    used = {}
    travelling = []

    def total_start(i, value):
        size = value.shape[0]
        used[i] = size
        turn = i % 2
        gone, travelling[:] = list(travelling), []
        near[turn, net.core, :size] = value
        for who, device in net.near():
            mine = near.at[turn, net.core, pl.ds(0, size)]
            copy = push(mine, mine, near_send.at[i], near_recv.at[i], device)
            copy.start()
            travelling.append(copy)
            copy.wait_recv()
        far[turn, net.far_slot(), :size] = near[turn, 0, :size] + near[turn, 1, :size]
        for step, (who, device) in enumerate(net.far()):
            mine = far.at[turn, net.far_slot(), pl.ds(0, size)]
            copy = push(mine, mine, far_send.at[i, step], far_recv.at[i, net.far_slot()], device)
            copy.start()
            travelling.append(copy)
        for copy in gone:
            copy.wait_send()

    def total_finish(i):
        size = used[i]
        turn = i % 2
        for step, (who, device) in enumerate(net.far()):
            there = far.at[turn, who, pl.ds(0, size)]
            push(there, there, far_send.at[i, step], far_recv.at[i, who], device).wait_recv()
        total = far[turn, 0, :size]
        for j in range(1, net.low * net.half):
            total = total + far[turn, j, :size]
        if net.high > 1:
            mine = top.at[turn, net.row_high, pl.ds(0, size)]
            top[turn, net.row_high, :size] = total
            for step, (who, device) in enumerate(net.top()):
                copy = push(mine, mine, top_send.at[i, step], top_recv.at[i, net.row_high], device)
                copy.start()
                travelling.append(copy)
            for step, (who, device) in enumerate(net.top()):
                there = top.at[turn, who, pl.ds(0, size)]
                push(there, there, top_send.at[i, step], top_recv.at[i, who], device).wait_recv()
            total = top[turn, 0, :size]
            for j in range(1, net.high):
                total = total + top[turn, j, :size]
        return jnp.concatenate([total[: size // 2], total[size // 2 :]], axis=1)

    def halo_copy(kind, slot, side):
        step = -1 if side == 0 else 1
        return push(
            halo_send.at[side],
            halo_recv.at[slot, 1 - side],
            halo_ssem.at[kind, side],
            halo_rsem.at[kind, 1 - side],
            (net.row, lane + step),
        )

    def sends_to(side):
        return lane > 0 if side == 0 else lane < lanes - 1

    def halo_start(kind, slot, side):
        @pl.when(sends_to(side))
        def _():
            halo_copy(kind, slot, side).start()

    def halo_sent(kind, slot, side):
        @pl.when(sends_to(side))
        def _():
            halo_copy(kind, slot, side).wait_send()

    def halo_wait(kind, slot, side):
        step = -1 if side == 0 else 1
        push(
            halo_send.at[1 - side],
            halo_recv.at[slot, side],
            halo_ssem.at[kind, 1 - side],
            halo_rsem.at[kind, side],
            (net.row, lane + step),
        ).wait_recv()

    column = lax.broadcasted_iota(jnp.int32, (WIDE, 256), 0) % WP
    pad_mask = (column < WW).astype(F32)

    def half_mask(alive, lines):
        return jnp.concatenate([pad_mask[:WP] * (0.5 * alive)] * lines, axis=0)

    def affine(total, square, count, gain, shift):
        mean = total / count
        var = square / count - mean * mean
        scale = lax.rsqrt(var + EPS)
        return mean, scale, gain * scale, shift - mean * (gain * scale)

    def back_affine(e_sum, ez_sum, count, norm):
        mean, scale, a, _ = norm
        gain_grad = scale * (ez_sum - mean * e_sum)
        slope = -a * scale * gain_grad / count
        bias = -a * e_sum / count - slope * mean
        return slope, bias, gain_grad, e_sum

    def zero8(n=256):
        return jnp.zeros((8, n), F32)

    blank = jnp.zeros((WP, 256), F32)
    for f in range(frames):
        for b in range(BLOCKS):
            z2[b, f, 0] = blank
            z2[b, f, HH + 1] = blank
        dz[f, 0] = blank
        dz[f, HH + 1] = blank
    for side in range(2):
        hz[side, 0] = blank
        hz[side, HH + 1] = blank

    for name in (("red", 0), ("mix", 0), ("small", 0)):
        gather_on(*name)
    gather_wait("red", 0)
    tbuf[...] = red_t[0].T

    carry = (zero8(), zero8())
    for f in range(frames):
        loads[f].wait()
        alive = live(f)

        z = dot(x0[f * frame_rows : (f + 1) * frame_rows], tbuf[...])
        z1[0, f * HH : (f + 1) * HH] = spread(z).reshape(HH, WP, 256)
        carry = (carry[0] + fold(z) * alive, carry[1] + fold(z * z) * alive)

    alive_all = sum(live(f) for f in range(frames)) * (HH * WW)
    here_count = jnp.full((1, 256), 1.0, F32) * alive_all
    total_start(0, rows_of(flat_sum(carry[0]), flat_sum(carry[1]), here_count))

    gather_wait("small", 0)
    half_rows = small.shape[0] // 2
    for side in range(2):
        here = [small_in[who, :, 64 * side : 64 * (side + 1)] for who in range(lanes)]
        small[half_rows * side : half_rows * (side + 1)] = jnp.concatenate(here, axis=1)

    def mid(b, norm, which):
        r = BLOCKS * KVOL + (b * 3 + norm) * 2 + which
        return small[r : r + 1]

    edge_sums = []
    pattern_col = lax.broadcasted_iota(jnp.int32, (WP, 256), 0)
    for b in range(BLOCKS):
        taps_b = [[small[b * KVOL + dt * 9 + k : b * KVOL + dt * 9 + k + 1] for k in range(9)] for dt in range(3)]
        se = jnp.zeros((1, 256), F32)
        see = jnp.zeros((1, 256), F32)
        for f in range(-1, frames + 1):
            here = live(f)
            t = [
                here * (live(f - 1) * taps_b[0][k] + here * taps_b[1][k] + live(f + 1) * taps_b[2][k])
                for k in range(9)
            ]
            for cls in range(3):
                use = [dh for dh in range(3) if not (cls == 0 and dh == 0) and not (cls == 2 and dh == 2)]
                col = []
                for dw in range(3):
                    v = t[use[0] * 3 + dw]
                    for dh in use[1:]:
                        v = v + t[dh * 3 + dw]
                    col.append(v)
                inner = col[0] + col[1] + col[2]
                left, right = col[1] + col[2], col[0] + col[1]
                edge[b, f + 1, cls] = jnp.where(
                    pattern_col == 0,
                    left,
                    jnp.where(pattern_col == WW - 1, right, jnp.where(pattern_col < WW - 1, inner, 0.0)),
                )
                if 0 <= f < frames:
                    times = 1.0 if cls != 1 else HH - 2.0
                    se = se + times * (left + right + (WW - 2.0) * inner)
                    see = see + times * (left * left + right * right + (WW - 2.0) * (inner * inner))
        edge_sums.append((se, see))

    gather_wait("mix", 0)
    mix[...] = mix_t[0].T

    got = total_finish(0)
    count = got[2:3]
    count4 = jnp.concatenate([count] * 4, axis=1)
    first_sums = (got[0:1], got[1:2])

    def edge_rows(ref, j):
        top = jnp.where(j == 0, 0, 1)
        bottom = jnp.where(j == QUADS - 1, 2, 1)
        middle = ref[1]
        return jnp.concatenate([ref[top], middle, middle, ref[bottom]], axis=0)

    def trio(i):
        rows = pl.ds(pl.multiple_of(i * (TRIO * FLAT), TRIO * FLAT), TRIO * FLAT)
        lines = pl.ds(i * (TRIO * GROUP), TRIO * GROUP)
        where = []
        for k in range(TRIO):
            q = TRIO * i + k
            where.append((lax.div(q, QUADS), lax.rem(q, QUADS)))
        return rows, lines, where

    trios = frames * QUADS // TRIO

    def norm3_pattern(b, a3, b2, b3):
        for f in range(frames):
            for cls in range(3):
                pat[f + 1, cls] = edge[b, f + 1, cls] * (a3 * b2) + b3

    def row_class(h):
        return jnp.where(h == 0, 0, jnp.where(h == HH - 1, 2, 1))

    def convolve(local, f, b, flip, emit, acc):
        done = []
        for half in range(2):
            cols = slice(128 * half, 128 * (half + 1))
            kern = [small[b * KVOL + k : b * KVOL + k + 1, cols] for k in range(KVOL)]
            if flip:
                kern = kern[::-1]
            planes = []
            for dt in range(3):
                g = f + dt - 1
                planes.append(hz.at[0] if g < 0 else hz.at[1] if g > last else local.at[g])

            def two_rows(i, carry):
                h = 2 * i
                part = [[None] * 3 for _ in range(2)]
                for dt in range(3):
                    for rr in range(4):
                        v = planes[dt][h + rr, :, cols]
                        for o in range(2):
                            dh = rr - o
                            if 0 <= dh < 3:
                                for dw in range(3):
                                    term = kern[dt * 9 + dh * 3 + dw] * v
                                    part[o][dw] = term if part[o][dw] is None else part[o][dw] + term
                for o in range(2):
                    p = part[o]
                    c = p[1] + pltpu.roll(p[0], 1, 0) + pltpu.roll(p[2], WP - 1, 0)
                    carry = emit(h + o, half, cols, c, carry)
                return carry

            done.append(lax.fori_loop(0, HH // 2, two_rows, tuple(a[half] for a in acc)))
        return [[done[0][k], done[1][k]] for k in range(len(acc))]

    class Reduction:
        def __init__(self, first, size):
            self.lines = pl.ds(first, size)
            self.first, self.size = first, size
            self.which = 0 if first == 0 else 1
            self.open = {"a": [], "b": [], "all": []}

        def put(self, who, piece, first, value):
            grad_a[who, piece, pl.ds(self.lines.start + first, value.shape[0])] = value.astype(BF16)

        def clear(self, *names):
            for name in names:
                for copy in self.open[name]:
                    copy.wait_send()
                self.open[name] = []

        def move(self, name, copy):
            copy.start()
            self.open[name].append(copy)

        def pair_copy(self, b, side):
            i = 2 * b + self.which
            src, dst = grad_a.at[2 * side + 1 - net.core, :, self.lines], grad_ra.at[side, :, self.lines]
            return push(src, dst, grad_sa.at[i, side], grad_qa.at[i, side], net.pair()[1])

        def to_pair(self, b):
            for side in range(2):
                self.move("a", self.pair_copy(b, side))

        def across_copy(self, b):
            i = 2 * b + self.which
            src, dst = grad_a.at[net.across()[0], :, self.lines], grad_ra.at[2, :, self.lines]
            return push(src, dst, grad_sa.at[i, 2], grad_qa.at[i, 2], net.across()[1])

        def to_side(self, b):
            for side in range(2):
                self.pair_copy(b, side).wait_recv()
            other = net.across()[0]

            def add(piece, _):
                mine, theirs = grad_a[other, piece, self.lines], grad_ra[1 - net.side, piece, self.lines]
                grad_a[other, piece, self.lines] = (mine.astype(F32) + theirs.astype(F32)).astype(BF16)
                return 0

            lax.fori_loop(0, PIECES, add, 0)
            self.move("a", self.across_copy(b))

        def low_peers(self):
            rows = [lax.rem(net.row_low + o, net.low) for o in range(1, net.low)]
            return [(row, (net.row_high * net.low + row, lane)) for row in rows]

        def to_rows(self, b):
            i = 2 * b + self.which
            self.across_copy(b).wait_recv()
            self.clear("b")

            def add(piece):
                total = grad_a[own, piece, self.lines].astype(F32) + grad_ra[net.side, piece, self.lines].astype(F32)
                grad_b[piece, self.lines] = (total + grad_ra[2, piece, self.lines].astype(F32)).astype(BF16)

            each = PIECES // net.low
            for step, (who, device) in enumerate(self.low_peers()):
                for k in range(each):
                    add(who * each + k)
                src = grad_b.at[pl.ds(who * each, each), self.lines]
                dst = grad_rb.at[net.row_low, :, self.lines]
                self.move("b", push(src, dst, grad_sb.at[i, step], grad_qb.at[i, net.row_low], device))
            for k in range(each):
                add(net.row_low * each + k)

        def to_all(self, b):
            i = 2 * b + self.which
            each = PIECES // net.low
            mine = pl.ds(net.row_low * each, each)
            for step, (who, device) in enumerate(self.low_peers()):
                src, dst = grad_b.at[mine, self.lines], grad_rb.at[who, :, self.lines]
                push(src, dst, grad_sb.at[i, step], grad_qb.at[i, who], device).wait_recv()
            total = grad_b[mine, self.lines].astype(F32)
            for who, _device in self.low_peers():
                total = total + grad_rb[who, :, self.lines].astype(F32)
            if net.high > 1:
                grad_top[b, net.row_high, :, self.lines] = total.astype(BF16)
                for step, (who, device) in enumerate(net.top()):
                    here = grad_top.at[b, net.row_high, :, self.lines]
                    self.move("all", push(here, here, grad_st.at[i, step], grad_qt.at[i, net.row_high], device))
                for step, (who, device) in enumerate(net.top()):
                    there = grad_top.at[b, who, :, self.lines]
                    push(there, there, grad_st.at[i, step], grad_qt.at[i, who], device).wait_recv()
                self.clear("all")
                total = grad_top[b, 0, :, self.lines].astype(F32)
                for j in range(1, net.high):
                    total = total + grad_top[b, j, :, self.lines].astype(F32)
            self.clear("all")
            grad_all[mine, self.lines] = total.astype(BF16)
            for step, (who, device) in enumerate(self.low_peers()):
                here = grad_all.at[mine, self.lines]
                self.move("all", push(here, here, grad_sc.at[i, step], grad_qc.at[i, net.row_low], device))

        def finish(self, b):
            i = 2 * b + self.which
            each = PIECES // net.low
            for step, (who, device) in enumerate(self.low_peers()):
                there = grad_all.at[pl.ds(who * each, each), self.lines]
                push(there, there, grad_sc.at[i, step], grad_qc.at[i, who], device).wait_recv()
            for piece in range(PIECES):
                cols = slice(128 * piece, 128 * (piece + 1))
                grads_out[b, self.first : self.first + self.size, cols] = grad_all[piece, self.lines].astype(F32)

    early = [Reduction(0, 96 if b == 0 else 80) for b in range(BLOCKS)]
    final = [Reduction(96, 64 if b == 0 else 80) for b in range(BLOCKS)]

    order = (0, last) + tuple(range(1, last))
    norms = []
    mid_grads = {}
    out_grads = {}

    def open_block(b, rows):
        z = dot(a3s[b, rows], exp[b])
        a4, b4 = norms[b][3][2], norms[b][3][3]
        return z, (z * a4 + b4) + xs[b][rows].astype(F32)

    kept = [(a1s, keep_mid.at[0]), (d1s, keep_mid.at[1]), (d2s, keep_mid.at[2]), (yb, keep_big)]
    keeps = [pltpu.make_async_copy(held, far_away, keep_sem.at[k]) for k, (held, far_away) in enumerate(kept)]
    backs = [pltpu.make_async_copy(far_away, held, back_sem.at[k]) for k, (held, far_away) in enumerate(kept)]

    def slope_rows(i, _):
        rows, lines, where = trio(i)
        _, pre = open_block(0, rows)
        for k, (f, j) in enumerate(where):
            v = pre[FLAT * k : FLAT * (k + 1)]
            square, t = gelu_core(v)
            part = pl.ds(pl.multiple_of((TRIO * i + k) * FLAT, FLAT), FLAT)
            yb[part] = gelu_slope(v, square, t, 0.5 * live(f)).astype(BF16)
        return 0

    out_store = [frame_copy(yb, out_hbm, f, store_sem.at[f]) for f in range(frames)]

    for b in range(BLOCKS):
        norm1 = affine(first_sums[0], first_sums[1], count, mid(b, 0, 0), mid(b, 0, 1))
        if b == 0:
            gather("exp", 0)
        _, _, a1, b1 = norm1
        carry = (zero8(), zero8())
        if b > 0:
            keeps[0].wait()
            for side in range(2):
                halo_sent(2 * (b - 1) + 1, 2 + b - 1, side)
        for f in order:
            alive = live(f)

            v = z1[b, f * HH : (f + 1) * HH].reshape(HH * WP, 256) * a1 + b1
            _, t = gelu_core(v)
            act = gelu_value(v, t, half_mask(alive, HH)).astype(BF16)
            a1s[f * HH : (f + 1) * HH] = act.reshape(HH, WP, 256)
            m = dot(act, mix[...])
            z2[b, f, 1 : 1 + HH] = m.reshape(HH, WP, 256)
            if f in (0, last):
                halo_send[0 if f == 0 else 1] = m.astype(BF16).reshape(HH, WP, 256)
            carry = (carry[0] + fold(m), carry[1] + fold(m * m))
            if f in (0, last):
                halo_start(2 * b, b, 0 if f == 0 else 1)

        if b == 0:
            keeps[0].start()

        def emit_conv(f):
            pad = pad_mask[:WP, :128] * live(f)

            def emit(row, half, cols, c, carry):
                c = c * pad
                conv[b, f * HH + row, :, cols] = c
                if f in (0, last):
                    halo_send[0 if f == 0 else 1, row, :, cols] = c.astype(BF16)
                e = edge[b, f + 1, row_class(row), :, cols]
                s0, s1, s2 = carry
                return (s0 + fold(c), s1 + fold(c * c), s2 + fold(c * e))

            return emit

        def fill(side):
            present = lane > 0 if side == 0 else lane < lanes - 1

            @pl.when(present)
            def _():
                halo_wait(2 * b, b, side)

                def widen(j, _):
                    hz[side, pl.ds(1 + j * GROUP, GROUP)] = halo_recv[b, side, pl.ds(j * GROUP, GROUP)].astype(F32)
                    return 0

                lax.fori_loop(0, QUADS, widen, 0)

            @pl.when(jnp.logical_not(present))
            def _():
                def clear(j, _):
                    hz[side, pl.ds(1 + j * GROUP, GROUP)] = jnp.zeros((GROUP, WP, 256), F32)
                    return 0

                lax.fori_loop(0, QUADS, clear, 0)

        acc = [[zero8(128), zero8(128)] for _ in range(3)]
        for f in range(1, last):
            acc = convolve(z2.at[b], f, b, False, emit_conv(f), acc)
        if b == 0:
            gather_on("exp", 0)
        for side in range(2):
            fill(side)
            halo_sent(2 * b, b, side)
            f = 0 if side == 0 else last
            acc = convolve(z2.at[b], f, b, False, emit_conv(f), acc)
            halo_start(2 * b + 1, 2 + b, side)
        joined = [jnp.concatenate([flat_sum(a[0]), flat_sum(a[1])], axis=1) for a in acc]
        total_start(3 * b + 1, rows_of(flat_sum(carry[0]), flat_sum(carry[1]), *joined, *edge_sums[b]))
        if b == 0:
            gather_wait("exp", 0)
        else:
            gather_wait("exp", 1)
            tbuf[...] = exp[1].T
            keeps[1].wait()

        def slope1(i, _):
            _, lines, where = trio(i)
            v = z1[b, lines].reshape(TRIO * WIDE, 256) * a1 + b1
            square, t = gelu_core(v)
            d1s[lines] = gelu_slope(v, square, t, 0.5).astype(BF16).reshape(TRIO * GROUP, WP, 256)
            return 0

        lax.fori_loop(0, trios, slope1, 0)
        if b == 0:
            keeps[1].start()
        else:
            lax.fori_loop(trios - 2, trios, slope_rows, 0)
            keeps[3].start()
        got = total_finish(3 * b + 1)
        norm2 = affine(got[0:1], got[1:2], count, mid(b, 1, 0), mid(b, 1, 1))
        _, _, a2, b2 = norm2
        sc, scc, sce, se, see = [got[i : i + 1] for i in range(2, 7)]
        total3 = a2 * sc + b2 * se
        square3 = a2 * a2 * scc + 2.0 * a2 * b2 * sce + b2 * b2 * see
        norm3 = affine(total3, square3, count, mid(b, 2, 0), mid(b, 2, 1))
        _, _, a3, b3 = norm3

        norm3_pattern(b, a3, b2, b3)
        if b == 0:
            gather("red", 1)
            gather("mix", 1)

        def activate(i, _):
            rows, lines, where = trio(i)
            c = conv[b, lines].reshape(TRIO * WIDE, 256)
            acts = []
            for k, (f, j) in enumerate(where):
                v = c[WIDE * k : WIDE * (k + 1)] * (a3 * a2) + edge_rows(pat.at[f + 1], j)
                _, t = gelu_core(v)
                acts.append(squeeze(gelu_value(v, t, 0.5 * live(f))))
            a3s[b, rows] = jnp.concatenate(acts, axis=0).astype(BF16)
            return 0

        lax.fori_loop(0, trios, activate, 0)
        gram = dot_rows(a3s[b], a3s[b])
        line = dot(jnp.ones((16, frames * frame_rows), BF16), a3s[b])
        high = jnp.concatenate([gram, line], axis=0)
        split = high.astype(BF16)
        grown = dot(split, exp[b]) + dot((high - split.astype(F32)).astype(BF16), exp[b])
        squares = flat_sum(fold(grown[:256] * exp[b].astype(F32)))
        if b == 0:
            gather_on("red", 1)
            gather_on("mix", 1)
        total_start(3 * b + 2, rows_of(grown[256:257], squares))
        if b == 0:
            gather_wait("red", 1)
            tbuf[...] = red_t[1].T
        else:
            keeps[2].wait()

        def slope3(i, _):
            _, lines, where = trio(i)
            c = conv[b, lines].reshape(TRIO * WIDE, 256)
            out = []
            for k, (f, j) in enumerate(where):
                v = c[WIDE * k : WIDE * (k + 1)] * (a3 * a2) + edge_rows(pat.at[f + 1], j)
                square, t = gelu_core(v)
                out.append(gelu_slope(v, square, t, 0.5).astype(BF16))
            d2s[lines] = jnp.concatenate(out, axis=0).reshape(TRIO * GROUP, WP, 256)
            return 0

        lax.fori_loop(0, trios, slope3, 0)
        if b == 0:
            keeps[2].start()
        got = total_finish(3 * b + 2)
        norm4 = affine(wide_row(got, 0), wide_row(got, 4), count4, norm_out[b, 0:1], norm_out[b, 1:2])
        norms.append((norm1, norm2, norm3, norm4, (sc, scc, sce, se, see)))

        if b == 0:
            gather("exp", 1)

            def closing(i, carry):
                rows, lines, where = trio(i)
                _, pre = open_block(0, rows)
                results = []
                for (f, j), v in zip(where, pieces(pre, FLAT)):
                    half = jnp.full((1, 1024), 0.5 * live(f), F32).astype(BF16)
                    v = v.astype(BF16)
                    _, t = gelu_core(v)
                    results.append(gelu_value(v, t, half))
                result = jnp.concatenate(results, axis=0)
                x1[rows] = result
                z = dot(result, tbuf[...])
                z1[1, lines] = spread(z).reshape(TRIO * GROUP, WP, 256)
                return (carry[0] + fold(z), carry[1] + fold(z * z))

            carry = lax.fori_loop(0, trios, closing, (zero8(), zero8()))
            gather_on("exp", 1)
            total_start(3, rows_of(flat_sum(carry[0]), flat_sum(carry[1])))
            gather_wait("mix", 1)
            mix[...] = mix_t[1].T
            lax.fori_loop(0, trios - 2, slope_rows, 0)
            got = total_finish(3)
            first_sums = (got[0:1], got[1:2])

    cot_load.wait()
    keeps[3].wait()

    def ending(i, carry):
        rows, lines, where = trio(i)
        z, pre = open_block(1, rows)
        g = sb[rows]
        s0, s1 = carry
        for k, (f, j) in enumerate(where):
            here = slice(FLAT * k, FLAT * (k + 1))
            v, half = pre[here].astype(BF16), jnp.full((1, 1024), 0.5 * live(f), F32).astype(BF16)
            square, t = gelu_core(v)
            part = pl.ds(pl.multiple_of((TRIO * i + k) * FLAT, FLAT), FLAT)
            yb[part] = gelu_value(v, t, half)
            low = gelu_slope(v, square, t, half) * g[here]
            sb[part] = low
            s = low.astype(F32)
            s0, s1 = s0 + fold(s), s1 + fold(s * z[here])
        return s0, s1

    carry = lax.fori_loop(0, trios, ending, (zero8(1024), zero8(1024)))
    total_start(6, rows_of(flat_sum(carry[0]), flat_sum(carry[1])))
    for copy in out_store:
        copy.start()

    for b in reversed(range(BLOCKS)):
        turn = BLOCKS - 1 - b
        base = 6 + 3 * turn
        norm1, norm2, norm3, norm4, (sc, scc, sce, se, see) = norms[b]
        _, _, a1, b1 = norm1
        mean2, scale2, a2, b2 = norm2
        mean3, scale3, a3, b3 = norm3
        a4 = norm4[2]

        got = total_finish(base)
        slope4, bias4, gain_grad, shift_grad = back_affine(wide_row(got, 0), wide_row(got, 4), count4, norm4)
        out_grads[b] = (gain_grad, shift_grad)
        if turn == 0:
            for copy in out_store:
                copy.wait()
        for side in range(2):
            if turn == 0:
                halo_sent(2 * (BLOCKS - 1) + 1, 2 + BLOCKS - 1, side)
            else:
                halo_sent(2 * BLOCKS + turn - 1, b + 1, side)

        if turn > 0:
            early[b + 1].to_rows(b + 1)
            final[b + 1].to_side(b + 1)
        kind = 2 * BLOCKS + turn
        if turn > 0:
            backs[2].wait()
        acc = (zero8(), zero8(), zero8())
        for f in order:
            alive = live(f)

            rows = slice(f * frame_rows, (f + 1) * frame_rows)
            z = dot(a3s[b, rows], exp[b])
            d4 = (sb[rows].astype(F32) * a4 + (z * slope4 + bias4 * alive)).astype(BF16)
            yb[rows] = d4
            back = spread(dot(d4, tbuf[...]))
            for j in range(QUADS):
                c = conv[b, f * HH + GROUP * j : f * HH + GROUP * (j + 1)].reshape(WIDE, 256)
                slope = d2s[f * HH + GROUP * j : f * HH + GROUP * (j + 1)].reshape(WIDE, 256)
                e3 = back[WIDE * j : WIDE * (j + 1)] * slope.astype(F32)
                dz[f, 1 + GROUP * j : 1 + GROUP * (j + 1)] = e3.reshape(GROUP, WP, 256)
                if f in (0, last):
                    halo_send[0 if f == 0 else 1, GROUP * j : GROUP * (j + 1)] = e3.astype(BF16).reshape(GROUP, WP, 256)
                e = edge_rows(edge.at[b, f + 1], j)
                acc = (acc[0] + fold(e3), acc[1] + fold(e3 * c), acc[2] + fold(e3 * e))
            if f in (0, last):
                halo_start(kind, b, 0 if f == 0 else 1)
        total_start(base + 1, rows_of(*[flat_sum(a) for a in acc]))

        if turn > 0:
            early[b + 1].clear("a")

        def expand_grad(i, _):
            cols = pl.ds(pl.multiple_of(i * 256, 256), 256)
            g = dot_rows(a3s[b], yb[:, cols])
            for who in range(lanes):
                for h in range(2):
                    early[b].put(who, 2 * i + h, 0, g[share * who : share * (who + 1), 128 * h : 128 * (h + 1)])
            return 0

        lax.fori_loop(0, 4, expand_grad, 0)
        if b > 0:
            tbuf[...] = exp[b - 1].T
            backs[3].start()

        got = total_finish(base + 1)
        e3_sum, e3_conv, e3_edge = got[0:1], got[1:2], got[2:3]
        e3_third = a2 * e3_conv + b2 * e3_edge
        slope3, bias3, gain3, shift3 = back_affine(e3_sum, e3_third, count, norm3)
        third_conv = a2 * scc + b2 * sce
        third_edge = a2 * sce + b2 * see
        d3_conv = a3 * e3_conv + bias3 * sc + slope3 * third_conv
        d3_edge = a3 * e3_edge + bias3 * se + slope3 * third_edge
        slope2, bias2, gain2, shift2 = back_affine(d3_edge, d3_conv, count, norm2)

        if turn > 0:
            early[b + 1].to_all(b + 1)
            final[b + 1].to_rows(b + 1)
        for f in range(-1, frames + 1):
            live_pad = pad_mask[:WP] * live(f)
            for cls in range(3):
                pat[f + 1, cls] = bias3 * live_pad + (slope3 * b2) * edge[b, f + 1, cls]
        slope_c = slope3 * a2

        def to_d3(q, _):
            f = lax.div(q, QUADS)
            j = lax.rem(q, QUADS)
            rows = pl.ds(1 + j * GROUP, GROUP)
            c = conv[b, pl.ds(q * GROUP, GROUP)].reshape(WIDE, 256)
            e3 = dz[f, rows].reshape(WIDE, 256)
            d3 = e3 * a3 + c * slope_c + edge_rows(pat.at[f + 1], j)
            dz[f, rows] = d3.reshape(GROUP, WP, 256)
            return 0

        lax.fori_loop(0, frames * QUADS, to_d3, 0)

        def fill_back(side):
            present = lane > 0 if side == 0 else lane < lanes - 1
            f = -1 if side == 0 else frames

            @pl.when(present)
            def _():
                halo_wait(2 * b + 1, 2 + b, side)
                halo_wait(kind, b, side)

                def widen(j, _):
                    rows = pl.ds(j * GROUP, GROUP)
                    c = halo_recv[2 + b, side, rows].astype(F32).reshape(WIDE, 256)
                    e3 = halo_recv[b, side, rows].astype(F32).reshape(WIDE, 256)
                    d3 = e3 * a3 + c * slope_c + edge_rows(pat.at[f + 1], j)
                    hz[side, pl.ds(1 + j * GROUP, GROUP)] = d3.reshape(GROUP, WP, 256)
                    return 0

                lax.fori_loop(0, QUADS, widen, 0)

            @pl.when(jnp.logical_not(present))
            def _():
                def clear(j, _):
                    hz[side, pl.ds(1 + j * GROUP, GROUP)] = jnp.zeros((GROUP, WP, 256), F32)
                    return 0

                lax.fori_loop(0, QUADS, clear, 0)

        for side in range(2):
            fill_back(side)

        def emit_back(f):
            pad = pad_mask[:WP, :128] * live(f)

            def emit(row, half, cols, e2, carry):
                z = z2[b, f, row + 1, :, cols]
                d2 = (e2 * a2[:, cols] + (z * slope2[:, cols] + bias2[:, cols])) * pad
                d2s[f * HH + row, :, cols] = d2.astype(BF16)
                return carry

            return emit

        for f in range(frames):
            convolve(dz, f, b, True, emit_back(f), [])

        if turn > 0:
            backs[0].wait()
            backs[1].wait()

        def unmixing(i, acc):
            _, lines, where = trio(i)
            e = dot(d2s[lines].reshape(TRIO * WIDE, 256), mix_t[b])
            z = z1[b, lines].reshape(TRIO * WIDE, 256)
            for k, (f, j) in enumerate(where):
                here = slice(WIDE * k, WIDE * (k + 1))
                part = pl.ds((TRIO * i + k) * GROUP, GROUP)
                e1 = e[here] * d1s[part].reshape(WIDE, 256).astype(F32)
                conv[b, part] = e1.reshape(GROUP, WP, 256)
                acc = (acc[0] + fold(e1), acc[1] + fold(e1 * z[here]))
            return acc

        acc = lax.fori_loop(0, trios, unmixing, (zero8(), zero8()))
        if turn > 0:
            early[b + 1].finish(b + 1)
        total_start(base + 2, rows_of(*[flat_sum(a) for a in acc]))

        def depth_grad(half, b=b, a2=a2, b2=b2):
            place, at = (early[b], 80) if b == 0 else (final[b], 64)
            cols = slice(128 * half, 128 * (half + 1))
            taps_grad = tuple(zero8(128) for _ in range(KVOL))
            for f in range(frames):
                planes = []
                for dt in range(3):
                    g = f - (dt - 1)
                    planes.append(hz.at[0] if g < 0 else hz.at[1] if g > last else dz.at[g])
                shift_rows = b2[:, cols] * (pad_mask[:WP, :128] * live(f))

                def tap_rows(h, taps_grad):
                    a = z2[b, f, h + 1, :, cols] * a2[:, cols] + shift_rows
                    moved = [pltpu.roll(a, 1, 0), a, pltpu.roll(a, WP - 1, 0)]
                    new = list(taps_grad)
                    for dt in range(3):
                        for dh in range(3):
                            d = planes[dt][h + 1 - (dh - 1), :, cols]
                            for dw in range(3):
                                k = dt * 9 + dh * 3 + dw
                                new[k] = new[k] + fold(d * moved[dw])
                    return tuple(new)

                taps_grad = lax.fori_loop(0, HH, tap_rows, taps_grad)
            lines = jnp.concatenate(
                [flat_sum(t) for t in taps_grad] + [jnp.zeros((WP - KVOL, 128), F32)], axis=0
            )
            for r in range(4):
                part = jnp.concatenate([lines[8 * r : 8 * r + 8], zero8(128)], axis=0)
                for who in range(lanes):
                    place.put(who, 2 * r + half, at, part)

        depth_grad(0)
        if b == 0:
            depth_grad(1)
        g = dot_rows(d2s[...].reshape(frames * HH * WP, 256), a1s[...].reshape(frames * HH * WP, 256))
        for who in range(lanes):
            for r in range(4):
                for h in range(2):
                    first = share * who + 16 * r
                    early[b].put(who, 2 * r + h, 64, g[first : first + 16, 128 * h : 128 * (h + 1)])
        early[b].to_pair(b)
        if b > 0:
            for k in range(3):
                backs[k].start()

        got = total_finish(base + 2)
        slope1, bias1, gain1, shift1 = back_affine(got[0:1], got[1:2], count, norm1)
        mid_grads[b] = ((gain1, shift1), (gain2, shift2), (gain3, shift3))

        early[b].to_side(b)
        def first_grad(i):
            rows, lines, where = trio(i)
            e1 = conv[b, lines].reshape(TRIO * WIDE, 256)
            z = z1[b, lines].reshape(TRIO * WIDE, 256)
            parts = []
            for k, (f, j) in enumerate(where):
                here = slice(WIDE * k, WIDE * (k + 1))
                alive = live(f)
                parts.append(squeeze(e1[here] * a1 + (z[here] * (slope1 * alive) + bias1 * alive)))
            d1 = jnp.concatenate(parts, axis=0).astype(BF16)
            a3s[b, rows] = d1
            return rows, where, d1

        def reduce_grad(i, _):
            cols = pl.ds(pl.multiple_of(i * 256, 256), 256)
            g = dot_rows(a3s[b], xs[b][:, cols])
            for who in range(lanes):
                for h in range(2):
                    final[b].put(who, 2 * i + h, 0, g[share * who : share * (who + 1), 128 * h : 128 * (h + 1)])
            return 0

        if b > 0:

            backs[3].wait()

            def passing(i, carry):
                rows, where, d1 = first_grad(i)
                g = dot(d1, red_t[b]) + sb[rows].astype(F32)
                z = dot(a3s[b - 1, rows], exp[b - 1])
                slope = yb[rows]
                s0, s1 = carry
                for k, (f, j) in enumerate(where):
                    here = slice(FLAT * k, FLAT * (k + 1))
                    s = slope[here].astype(F32) * g[here]
                    sb[pl.ds(pl.multiple_of((TRIO * i + k) * FLAT, FLAT), FLAT)] = s.astype(BF16)
                    s0, s1 = s0 + fold(s), s1 + fold(s * z[here])
                return s0, s1

            carry = lax.fori_loop(0, trios, passing, (zero8(1024), zero8(1024)))
            total_start(base + 3, rows_of(flat_sum(carry[0]), flat_sum(carry[1])))
            depth_grad(1)
            lax.fori_loop(0, 4, reduce_grad, 0)
            final[b].to_pair(b)
        else:
            final[b + 1].to_all(b + 1)

            def only_d1(i, _):
                first_grad(i)
                return 0

            lax.fori_loop(0, trios, only_d1, 0)
            final[b + 1].clear("a")
            lax.fori_loop(0, 4, reduce_grad, 0)
            final[b].to_pair(b)
            early[b + 1].clear("b", "all")
            early[b].to_rows(b)
            steps = (lambda: final[b].to_side(b), lambda: early[b].to_all(b))
            gtok_store = [frame_copy(yb, gtok_hbm, f, store_sem.at[f]) for f in range(frames)]
            for f in range(frames):
                rows = slice(f * frame_rows, (f + 1) * frame_rows)
                yb[rows] = (dot(a3s[b, rows], red_t[b]) + sb[rows].astype(F32)).astype(BF16)
                gtok_store[f].start()
                if f < len(steps):
                    steps[f]()
            final[b + 1].finish(b + 1)
            final[b + 1].clear("b", "all")
            final[b].to_rows(b)
            early[b].finish(b)
            final[b].to_all(b)
            final[b].finish(b)

    for b in range(BLOCKS):
        for k in range(3):
            for w in range(2):
                r = (b * 3 + k) * 2 + w
                gmid_out[r : r + 1] = mid_grads[b][k][w]
        for w in range(2):
            gout_out[2 * b + w : 2 * b + w + 1] = out_grads[b][w]

    for copy in gtok_store:
        copy.wait()
    early[0].clear("a", "b", "all")
    final[0].clear("a", "b", "all")
    for copy in late + travelling:
        copy.wait_send()
    for side in range(2):
        halo_sent(2 * BLOCKS + BLOCKS - 1, 0, side)


def whole_call(groups, lanes, counts, tokens, cotangent, reduce_loc, mix_loc, expand_loc, depth_loc, mid_loc, norm_out):
    rows = tokens.shape[0]
    frames = rows // (HH * WW)
    whole = pl.BlockSpec(memory_space=pltpu.VMEM)
    hbm = pl.BlockSpec(memory_space=pl.ANY)
    dma = pltpu.SemaphoreType.DMA
    low, high = stages(groups)
    far = low * (lanes // 2)
    lines = frames * HH
    sums = 6 * BLOCKS
    kinds = 3 * BLOCKS
    shape = jax.ShapeDtypeStruct
    return pl.pallas_call(
        functools.partial(whole_kernel, groups, lanes),
        out_shape=(
            shape((rows, 1024), BF16),
            shape((rows, 1024), BF16),
            shape((BLOCKS, 176, 1024), F32),
            shape((BLOCKS * 6, 256), F32),
            shape((BLOCKS * 2, 1024), F32),
            shape((rows, 1024), BF16),
            shape((3, lines, WP, 256), BF16),
        ),
        in_specs=[pl.BlockSpec(memory_space=pltpu.SMEM)] + [hbm] * 5 + [whole] * 3,
        out_specs=[hbm] * 2 + [whole] * 3 + [hbm] * 2,
        scratch_shapes=[
            pltpu.VMEM((rows, 1024), BF16),
            pltpu.VMEM((rows, 1024), BF16),
            pltpu.VMEM((rows, 1024), BF16),
            pltpu.VMEM((rows, 1024), BF16),
            pltpu.VMEM((BLOCKS, 256, 1024), BF16),
            pltpu.VMEM((BLOCKS, 256, 1024), BF16),
            pltpu.VMEM((1024, 256), BF16),
            pltpu.VMEM((BLOCKS, 256, 256), BF16),
            pltpu.VMEM((256, 256), BF16),
            pltpu.VMEM((lanes, 40, 128), F32),
            pltpu.VMEM((80, 256), F32),
            pltpu.VMEM((BLOCKS, lines, WP, 256), F32),
            pltpu.VMEM((lines, WP, 256), BF16),
            pltpu.VMEM((BLOCKS, frames, HH + 2, WP, 256), F32),
            pltpu.VMEM((frames, HH + 2, WP, 256), F32),
            pltpu.VMEM((2, HH + 2, WP, 256), F32),
            pltpu.VMEM((BLOCKS, lines, WP, 256), F32),
            pltpu.VMEM((BLOCKS, rows, 256), BF16),
            pltpu.VMEM((BLOCKS, frames + 2, 3, WP, 256), F32),
            pltpu.VMEM((frames + 2, 3, WP, 256), F32),
            pltpu.VMEM((lines, WP, 256), BF16),
            pltpu.VMEM((lines, WP, 256), BF16),
            pltpu.VMEM((2, HH, WP, 256), BF16),
            pltpu.VMEM((2 * BLOCKS, 2, HH, WP, 256), BF16),
            pltpu.VMEM((lanes, PIECES, 176, 128), BF16),
            pltpu.VMEM((3, PIECES, 176, 128), BF16),
            pltpu.VMEM((PIECES, 176, 128), BF16),
            pltpu.VMEM((low, PIECES // low, 176, 128), BF16),
            pltpu.VMEM((PIECES, 176, 128), BF16),
            pltpu.VMEM((BLOCKS, high, PIECES // low, 176 if high > 1 else 16, 128), BF16),
            pltpu.VMEM((2, 2, 16, 128), F32),
            pltpu.VMEM((2, far, 16, 128), F32),
            pltpu.VMEM((2, high, 16, 128), F32),
            dma((sums,)),
            dma((sums,)),
            dma((sums, far)),
            dma((sums, far)),
            dma((sums, high)),
            dma((sums, high)),
            dma((7, 3)),
            dma((7, lanes)),
            dma((kinds, 2)),
            dma((kinds, 2)),
            dma((frames + 1,)),
            dma((frames,)),
            dma((2 * BLOCKS, 3)),
            dma((2 * BLOCKS, 3)),
            dma((2 * BLOCKS, low)),
            dma((2 * BLOCKS, low)),
            dma((2 * BLOCKS, low)),
            dma((2 * BLOCKS, low)),
            dma((2 * BLOCKS, high)),
            dma((2 * BLOCKS, high)),
            dma((BLOCKS, 4)),
            dma((4,)),
            dma((4,)),
        ],
        compiler_params=pltpu.CompilerParams(
            collective_id=1, has_side_effects=True, vmem_limit_bytes=63 * 2**20
        ),
    )(counts, tokens, cotangent, reduce_loc, mix_loc, expand_loc, depth_loc, mid_loc, norm_out)


def descend(weight, moment, grad):
    moment_new = MOMENTUM * moment + grad + DECAY * weight
    return (weight - LEARN_RATE * moment_new, moment_new)


def update_kernel(lanes, *refs):
    out_raw, gtok_raw = refs[:2]
    out, gtok = refs[17:19]
    held = refs[37:70]
    big, sems, store_sems, small_sems, small_stores = refs[70:]
    smalls = [pltpu.make_async_copy(refs[2 + k], held[k], small_sems.at[k]) for k in range(15)]
    results = [pltpu.make_async_copy(held[15 + k], refs[19 + k], small_stores.at[k]) for k in range(18)]
    reduced, gmid, gout = held[:3]
    weights, moments = held[3:9], held[9:15]
    grads, new_weights, new_moments = held[15:21], held[21:27], held[27:33]
    chunks = sems.shape[1]
    rows = out.shape[0] // chunks
    copies, stores = [], []
    for k in range(chunks):
        for which, (src, dst) in enumerate(((out_raw, out), (gtok_raw, gtok))):
            here = pl.ds(k * rows, rows)
            copies.append(pltpu.make_async_copy(src.at[here], big.at[which, here], sems.at[which, k]))
            stores.append(pltpu.make_async_copy(big.at[which, here], dst.at[here], store_sems.at[which, k]))
    for copy in smalls + copies:
        copy.start()
    for copy in smalls:
        copy.wait()
    lane = lax.axis_index("chan")
    narrow = 256 // lanes

    def mine(v):
        out = v[:, :narrow]
        for who in range(1, lanes):
            out = jnp.where(lane == who, v[:, narrow * who : narrow * (who + 1)], out)
        return out

    def step(slot, at, grad):
        weight, moment = descend(weights[slot][at], moments[slot][at], grad)
        grads[slot][at] = grad
        new_weights[slot][at] = weight
        new_moments[slot][at] = moment

    depths = []
    for b in range(BLOCKS):
        step(0, (b,), reduced[b, 96:160])
        mix = reduced[b, 64:80]
        step(1, (b,), jnp.concatenate([mix[:, 256 * r : 256 * (r + 1)] for r in range(4)], axis=0))
        depth = reduced[b, 80:88] if b == 0 else reduced[b, 160:168]
        depths.append(mine(jnp.concatenate([depth[:, 256 * r : 256 * (r + 1)] for r in range(4)], axis=0)))
        step(3, (b,), reduced[b, 0:64])
        step(5, (b,), gout[2 * b : 2 * b + 2])
    for k in range(KVOL):
        step(2, (k,), jnp.concatenate([depth[k : k + 1] for depth in depths], axis=0))
    middle = mine(gmid[...])
    for k in range(BLOCKS * 3):
        step(4, (k,), middle[2 * k : 2 * k + 2])
    for copy in results:
        copy.start()
    for copy, store in zip(copies, stores):
        copy.wait()
        store.start()
    for store in stores + results:
        store.wait()


def update_call(lanes, *args):
    hbm = pl.BlockSpec(memory_space=pl.ANY)
    like = [jax.ShapeDtypeStruct(v.shape, v.dtype) for v in args]
    return pl.pallas_call(
        functools.partial(update_kernel, lanes),
        out_shape=tuple(like[:2] + like[5:11] * 3),
        in_specs=[hbm] * 17,
        out_specs=[hbm] * 20,
        scratch_shapes=[pltpu.VMEM(v.shape, v.dtype) for v in like[2:] + like[5:11] * 3]
        + [
            pltpu.VMEM((2,) + args[0].shape, args[0].dtype),
            pltpu.SemaphoreType.DMA((2, 7)),
            pltpu.SemaphoreType.DMA((2, 7)),
            pltpu.SemaphoreType.DMA((15,)),
            pltpu.SemaphoreType.DMA((18,)),
        ],
        compiler_params=pltpu.CompilerParams(vmem_limit_bytes=60 * 2**20),
    )(*args)


def shards(
    tokens,
    frame_counts,
    cotangent,
    w_reduce,
    w_mix,
    w_depth,
    w_expand,
    norm_mid,
    norm_out,
    moment_reduce,
    moment_mix,
    moment_depth,
    moment_expand,
    moment_mid,
    moment_out,
):
    lanes = lax.axis_size("chan")
    turned = lambda v: jnp.swapaxes(v, 1, 2)
    swap = lambda v: jnp.swapaxes(v, 0, 1)
    flat = lambda v: v.reshape((-1,) + v.shape[2:])
    raw = whole_call(
        lax.axis_size("dp"),
        lanes,
        frame_counts,
        tokens,
        cotangent,
        turned(w_reduce),
        turned(w_mix),
        w_expand,
        swap(w_depth),
        flat(norm_mid),
        norm_out,
    )
    inside = lambda r, m, d, e, mid, out: (turned(r), turned(m), swap(d), e, flat(mid), out)
    outside = lambda r, m, d, e, mid, out: (turned(r), turned(m), swap(d), e, mid.reshape(norm_mid.shape), out)
    done = update_call(
        lanes,
        *raw[:5],
        *inside(w_reduce, w_mix, w_depth, w_expand, norm_mid, norm_out),
        *inside(moment_reduce, moment_mix, moment_depth, moment_expand, moment_mid, moment_out),
    )
    return done[:2] + outside(*done[2:8]) + outside(*done[8:14]) + outside(*done[14:20])


def solution(mesh):
    rows = P(("dp", "chan"), None)
    weights = (
        P(None, None, "chan"),
        P(None, None, "chan"),
        P(None, None, "chan"),
        P(None, "chan", None),
        P(None, None, None, "chan"),
        P(),
    )
    return jax.shard_map(
        shards,
        mesh=mesh,
        in_specs=(rows, P("dp"), rows) + weights + weights,
        out_specs=(rows, rows) + weights + weights + weights,
        check_vma=False,
    )
```

```python
import functools

import jax
import jax.numpy as jnp
from jax import lax
from jax.experimental import pallas as pl
from jax.experimental.pallas import tpu as pltpu
from jax.sharding import PartitionSpec as P

FRAMES = 12
HH = 28
WW = 28
WP = 32
KVOL = 27
BLOCKS = 2
GROUP = 4
QUADS = HH // GROUP
FLAT = GROUP * WW
WIDE = GROUP * WP
PIECES = 8
TRIO = 3

EPS = 1e-05
LEARN_RATE = 0.001
MOMENTUM = 0.9
DECAY = 0.0001
MESH = pl.DeviceIdType.MESH
F32 = jnp.float32
BF16 = jnp.bfloat16
ROOT = 0.7978845608028654
CUBE = 0.044715


def gelu_core(v):
    square = v * v
    return square, jnp.tanh(v * (ROOT + (ROOT * CUBE) * square))


def gelu_value(v, t, half):
    h = half * v
    return h * t + h


def gelu_slope(v, square, t, half):
    r = v * (half * ROOT + (half * (3.0 * ROOT * CUBE)) * square)
    return (half * t + half) + (r - r * (t * t))


def dot_rows(left, right):
    return lax.dot_general(left, right, (((0,), (0,)), ((), ())), preferred_element_type=F32)


def dot(left, right):
    return jnp.dot(left, right, preferred_element_type=F32)


def fold(v):
    return jnp.sum(v.reshape(v.shape[0] // 8, 8, v.shape[1]), axis=0)


def spread(v):
    gap = jnp.zeros((WP - WW, v.shape[1]), v.dtype)
    parts = []
    for h in range(v.shape[0] // WW):
        parts += [v[WW * h : WW * (h + 1)], gap]
    return jnp.concatenate(parts, axis=0)


def squeeze(v):
    return jnp.concatenate([v[WP * h : WP * h + WW] for h in range(v.shape[0] // WP)], axis=0)


def pieces(v, rows):
    return [v[rows * k : rows * (k + 1)] for k in range(v.shape[0] // rows)]


def rows_of(*vectors):
    parts = []
    for v in vectors:
        parts += pieces_of(v)
    n = 4 if len(parts) <= 4 else 8
    out = []
    for side in range(2):
        out += [v[:, 128 * side : 128 * (side + 1)] for v in parts]
        if len(parts) < n:
            out.append(jnp.zeros((n - len(parts), 128), F32))
    return jnp.concatenate(out, axis=0)


def pieces_of(v):
    return [v[:, 256 * i : 256 * (i + 1)] for i in range(v.shape[1] // 256)]


def flat_sum(v):
    return jnp.sum(v, axis=0, keepdims=True)


def wide_row(v, first):
    return jnp.concatenate([v[first + i : first + i + 1] for i in range(4)], axis=1)


class Net:
    def __init__(self, groups, lanes):
        self.lanes = lanes
        self.low, self.high = stages(groups)
        self.row = lax.axis_index("dp")
        self.lane = lax.axis_index("chan")
        self.core = lax.rem(self.lane, 2)
        self.side = lax.div(self.lane, 2)
        self.half = lanes // 2
        self.row_low = lax.rem(self.row, self.low)
        self.row_high = lax.div(self.row, self.low)

    def near(self):
        return [(1 - self.core, (self.row, self.side * 2 + 1 - self.core))]

    def far(self):
        out = []
        for o in sorted(range(self.low), key=lambda o: abs(2 * o - self.low - 1)):
            for p in range(self.half):
                if o or p:
                    row = lax.rem(self.row_low + o, self.low)
                    side = lax.rem(self.side + p, self.half)
                    out.append((row * self.half + side, (self.row_high * self.low + row, side * 2 + self.core)))
        return out

    def far_slot(self):
        return self.row_low * self.half + self.side

    def top(self):
        rows = [lax.rem(self.row_high + o, self.high) for o in range(1, self.high)]
        return [(row, (row * self.low + self.row_low, self.lane)) for row in rows]

    def pair(self):
        lane = self.side * 2 + 1 - self.core
        return lane, (self.row, lane)

    def across(self):
        lane = (1 - self.side) * 2 + self.core
        return lane, (self.row, lane)

    def corner(self):
        return (1 - self.side) * 2 + 1 - self.core


def stages(groups):
    low = min(groups, 8)
    return low, groups // low


def push(src, dst, send, recv, device):
    copy = pltpu.make_async_remote_copy(
        src_ref=src, dst_ref=dst, send_sem=send, recv_sem=recv, device_id=device, device_id_type=MESH
    )
    return copy


def whole_kernel(
    groups,
    lanes,
    counts,
    tokens,
    cotangent,
    reduce_loc,
    mix_loc,
    expand_loc,
    depth_loc,
    mid_loc,
    norm_out,
    out_hbm,
    gtok_hbm,
    grads_out,
    gmid_out,
    gout_out,
    keep_big,
    keep_mid,
    x0,
    x1,
    yb,
    sb,
    red_t,
    exp,
    tbuf,
    mix_t,
    mix,
    small_in,
    small,
    z1,
    a1s,
    z2,
    dz,
    hz,
    conv,
    a3s,
    edge,
    pat,
    d2s,
    d1s,
    halo_send,
    halo_recv,
    grad_a,
    grad_ra,
    grad_b,
    grad_rb,
    grad_all,
    grad_top,
    near,
    far,
    top,
    near_send,
    near_recv,
    far_send,
    far_recv,
    top_send,
    top_recv,
    gather_send,
    gather_recv,
    halo_ssem,
    halo_rsem,
    load_sem,
    store_sem,
    grad_sa,
    grad_qa,
    grad_sb,
    grad_qb,
    grad_sc,
    grad_qc,
    grad_st,
    grad_qt,
    weight_sem,
    keep_sem,
    back_sem,
):
    net = Net(groups, lanes)
    lane = net.lane
    frames = tokens.shape[0] // (HH * WW)
    frame_rows = HH * WW
    last = frames - 1
    count_here = counts[0]
    xs = (x0, x1)

    def live(frame):
        position = lane * frames + frame
        return jnp.where((position >= 0) & (position < count_here), 1.0, 0.0)

    def frame_copy(src, dst, f, sem):
        rows = pl.ds(f * frame_rows, frame_rows)
        return pltpu.make_async_copy(src.at[rows], dst.at[rows], sem)

    loads = [frame_copy(tokens, x0, f, load_sem.at[f]) for f in range(frames)]
    cot_load = pltpu.make_async_copy(cotangent, sb, load_sem.at[frames])
    for copy in loads:
        copy.start()
    cot_load.start()
    weight_loads = {}
    for b in range(BLOCKS):
        places = [
            ("red", reduce_loc.at[b], grads_out.at[b, pl.ds(0, 64)]),
            ("exp", expand_loc.at[b], grads_out.at[b, pl.ds(64, 64)]),
            ("mix", mix_loc.at[b, pl.ds(0, 32)], grads_out.at[b, pl.ds(128, 32), pl.ds(0, 256)]),
            ("mix", mix_loc.at[b, pl.ds(32, 32)], grads_out.at[b, pl.ds(128, 32), pl.ds(256, 256)]),
        ]
        for k, (name, src, dst) in enumerate(places):
            copy = pltpu.make_async_copy(src, dst, weight_sem.at[b, k])
            copy.start()
            weight_loads.setdefault((name, b), []).append(copy)

    barrier = pltpu.get_barrier_semaphore()
    friends = [d for peers in (net.near(), net.far(), net.top()) for _, d in peers] + [(net.row, net.corner())]
    for device in friends:
        pl.semaphore_signal(barrier, inc=1, device_id=device, device_id_type=MESH)
    pl.semaphore_wait(barrier, len(friends))

    own = net.lane
    share = red_t.shape[1] // lanes
    late = []

    def gather(name, b):
        slot, dst_of = plan[name, b]
        mine = dst_of(own)
        for copy in weight_loads.get((name, b), []):
            copy.wait()
        if name == "red":
            mine[...] = grads_out[b, :64].astype(BF16)
        elif name == "exp":
            mine[...] = grads_out[b, 64:128].astype(BF16)
        elif name == "mix":
            parts = [grads_out[b, 128:160, :256], grads_out[b, 128:160, 256:512]]
            mine[...] = jnp.concatenate(parts, axis=0).astype(BF16)
        else:
            half_rows = small.shape[0] // 2
            lines = [depth_loc[k, b : b + 1] for b in range(BLOCKS) for k in range(KVOL)]
            lines += [mid_loc[k, w : w + 1] for k in range(3 * BLOCKS) for w in range(2)]
            for r, line in enumerate(lines):
                side = r // half_rows
                mine[r - side * half_rows : r - side * half_rows + 1, 64 * side : 64 * (side + 1)] = line
        for step, (_, device) in enumerate((net.pair(), net.across())):
            copy = push(mine, mine, gather_send.at[slot, step], gather_recv.at[slot, own], device)
            copy.start()
            late.append(copy)

    def gather_on(name, b):
        slot, dst_of = plan[name, b]
        who, device = net.across()
        piece = dst_of(who)
        push(piece, piece, gather_send.at[slot, 1], gather_recv.at[slot, who], device).wait_recv()
        copy = push(piece, piece, gather_send.at[slot, 2], gather_recv.at[slot, who], net.pair()[1])
        copy.start()
        late.append(copy)

    def gather_wait(name, b):
        slot, dst_of = plan[name, b]
        for who in (net.pair()[0], net.corner()):
            push(dst_of(who), dst_of(who), gather_send.at[slot, 0], gather_recv.at[slot, who], net.pair()[1]).wait_recv()

    def block_rows(ref, b):
        return lambda who: ref.at[b, pl.ds(pl.multiple_of(who * share, share), share)]

    plan = {
        ("red", 0): (0, block_rows(red_t, 0)),
        ("mix", 0): (1, block_rows(mix_t, 0)),
        ("small", 0): (2, lambda who: small_in.at[who]),
        ("exp", 0): (3, block_rows(exp, 0)),
        ("red", 1): (4, block_rows(red_t, 1)),
        ("mix", 1): (5, block_rows(mix_t, 1)),
        ("exp", 1): (6, block_rows(exp, 1)),
    }
    for name in (("red", 0), ("mix", 0), ("small", 0)):
        gather(*name)

    used = {}
    travelling = []

    def total_start(i, value):
        size = value.shape[0]
        used[i] = size
        turn = i % 2
        gone, travelling[:] = list(travelling), []
        near[turn, net.core, :size] = value
        for who, device in net.near():
            mine = near.at[turn, net.core, pl.ds(0, size)]
            copy = push(mine, mine, near_send.at[i], near_recv.at[i], device)
            copy.start()
            travelling.append(copy)
            copy.wait_recv()
        far[turn, net.far_slot(), :size] = near[turn, 0, :size] + near[turn, 1, :size]
        for step, (who, device) in enumerate(net.far()):
            mine = far.at[turn, net.far_slot(), pl.ds(0, size)]
            copy = push(mine, mine, far_send.at[i, step], far_recv.at[i, net.far_slot()], device)
            copy.start()
            travelling.append(copy)
        for copy in gone:
            copy.wait_send()

    def total_finish(i):
        size = used[i]
        turn = i % 2
        for step, (who, device) in enumerate(net.far()):
            there = far.at[turn, who, pl.ds(0, size)]
            push(there, there, far_send.at[i, step], far_recv.at[i, who], device).wait_recv()
        total = far[turn, 0, :size]
        for j in range(1, net.low * net.half):
            total = total + far[turn, j, :size]
        if net.high > 1:
            mine = top.at[turn, net.row_high, pl.ds(0, size)]
            top[turn, net.row_high, :size] = total
            for step, (who, device) in enumerate(net.top()):
                copy = push(mine, mine, top_send.at[i, step], top_recv.at[i, net.row_high], device)
                copy.start()
                travelling.append(copy)
            for step, (who, device) in enumerate(net.top()):
                there = top.at[turn, who, pl.ds(0, size)]
                push(there, there, top_send.at[i, step], top_recv.at[i, who], device).wait_recv()
            total = top[turn, 0, :size]
            for j in range(1, net.high):
                total = total + top[turn, j, :size]
        return jnp.concatenate([total[: size // 2], total[size // 2 :]], axis=1)

    def halo_copy(kind, slot, side):
        step = -1 if side == 0 else 1
        return push(
            halo_send.at[side],
            halo_recv.at[slot, 1 - side],
            halo_ssem.at[kind, side],
            halo_rsem.at[kind, 1 - side],
            (net.row, lane + step),
        )

    def sends_to(side):
        return lane > 0 if side == 0 else lane < lanes - 1

    def halo_start(kind, slot, side):
        @pl.when(sends_to(side))
        def _():
            halo_copy(kind, slot, side).start()

    def halo_sent(kind, slot, side):
        @pl.when(sends_to(side))
        def _():
            halo_copy(kind, slot, side).wait_send()

    def halo_wait(kind, slot, side):
        step = -1 if side == 0 else 1
        push(
            halo_send.at[1 - side],
            halo_recv.at[slot, side],
            halo_ssem.at[kind, 1 - side],
            halo_rsem.at[kind, side],
            (net.row, lane + step),
        ).wait_recv()

    column = lax.broadcasted_iota(jnp.int32, (WIDE, 256), 0) % WP
    pad_mask = (column < WW).astype(F32)

    def half_mask(alive, lines):
        return jnp.concatenate([pad_mask[:WP] * (0.5 * alive)] * lines, axis=0)

    def affine(total, square, count, gain, shift):
        mean = total / count
        var = square / count - mean * mean
        scale = lax.rsqrt(var + EPS)
        return mean, scale, gain * scale, shift - mean * (gain * scale)

    def back_affine(e_sum, ez_sum, count, norm):
        mean, scale, a, _ = norm
        gain_grad = scale * (ez_sum - mean * e_sum)
        slope = -a * scale * gain_grad / count
        bias = -a * e_sum / count - slope * mean
        return slope, bias, gain_grad, e_sum

    def zero8(n=256):
        return jnp.zeros((8, n), F32)

    blank = jnp.zeros((WP, 256), F32)
    for f in range(frames):
        for b in range(BLOCKS):
            z2[b, f, 0] = blank
            z2[b, f, HH + 1] = blank
        dz[f, 0] = blank
        dz[f, HH + 1] = blank
    for side in range(2):
        hz[side, 0] = blank
        hz[side, HH + 1] = blank

    for name in (("red", 0), ("mix", 0), ("small", 0)):
        gather_on(*name)
    gather_wait("red", 0)
    tbuf[...] = red_t[0].T

    carry = (zero8(), zero8())
    for f in range(frames):
        loads[f].wait()
        alive = live(f)

        z = dot(x0[f * frame_rows : (f + 1) * frame_rows], tbuf[...])
        z1[0, f * HH : (f + 1) * HH] = spread(z).reshape(HH, WP, 256)
        carry = (carry[0] + fold(z) * alive, carry[1] + fold(z * z) * alive)

    alive_all = sum(live(f) for f in range(frames)) * (HH * WW)
    here_count = jnp.full((1, 256), 1.0, F32) * alive_all
    total_start(0, rows_of(flat_sum(carry[0]), flat_sum(carry[1]), here_count))

    gather_wait("small", 0)
    half_rows = small.shape[0] // 2
    for side in range(2):
        here = [small_in[who, :, 64 * side : 64 * (side + 1)] for who in range(lanes)]
        small[half_rows * side : half_rows * (side + 1)] = jnp.concatenate(here, axis=1)

    def mid(b, norm, which):
        r = BLOCKS * KVOL + (b * 3 + norm) * 2 + which
        return small[r : r + 1]

    edge_sums = []
    pattern_col = lax.broadcasted_iota(jnp.int32, (WP, 256), 0)
    for b in range(BLOCKS):
        taps_b = [[small[b * KVOL + dt * 9 + k : b * KVOL + dt * 9 + k + 1] for k in range(9)] for dt in range(3)]
        se = jnp.zeros((1, 256), F32)
        see = jnp.zeros((1, 256), F32)
        for f in range(-1, frames + 1):
            here = live(f)
            t = [
                here * (live(f - 1) * taps_b[0][k] + here * taps_b[1][k] + live(f + 1) * taps_b[2][k])
                for k in range(9)
            ]
            for cls in range(3):
                use = [dh for dh in range(3) if not (cls == 0 and dh == 0) and not (cls == 2 and dh == 2)]
                col = []
                for dw in range(3):
                    v = t[use[0] * 3 + dw]
                    for dh in use[1:]:
                        v = v + t[dh * 3 + dw]
                    col.append(v)
                inner = col[0] + col[1] + col[2]
                left, right = col[1] + col[2], col[0] + col[1]
                edge[b, f + 1, cls] = jnp.where(
                    pattern_col == 0,
                    left,
                    jnp.where(pattern_col == WW - 1, right, jnp.where(pattern_col < WW - 1, inner, 0.0)),
                )
                if 0 <= f < frames:
                    times = 1.0 if cls != 1 else HH - 2.0
                    se = se + times * (left + right + (WW - 2.0) * inner)
                    see = see + times * (left * left + right * right + (WW - 2.0) * (inner * inner))
        edge_sums.append((se, see))

    gather_wait("mix", 0)
    mix[...] = mix_t[0].T

    got = total_finish(0)
    count = got[2:3]
    count4 = jnp.concatenate([count] * 4, axis=1)
    first_sums = (got[0:1], got[1:2])

    def edge_rows(ref, j):
        top = jnp.where(j == 0, 0, 1)
        bottom = jnp.where(j == QUADS - 1, 2, 1)
        middle = ref[1]
        return jnp.concatenate([ref[top], middle, middle, ref[bottom]], axis=0)

    def trio(i):
        rows = pl.ds(pl.multiple_of(i * (TRIO * FLAT), TRIO * FLAT), TRIO * FLAT)
        lines = pl.ds(i * (TRIO * GROUP), TRIO * GROUP)
        where = []
        for k in range(TRIO):
            q = TRIO * i + k
            where.append((lax.div(q, QUADS), lax.rem(q, QUADS)))
        return rows, lines, where

    trios = frames * QUADS // TRIO

    def norm3_pattern(b, a3, b2, b3):
        for f in range(frames):
            for cls in range(3):
                pat[f + 1, cls] = edge[b, f + 1, cls] * (a3 * b2) + b3

    def row_class(h):
        return jnp.where(h == 0, 0, jnp.where(h == HH - 1, 2, 1))

    def convolve(local, f, b, flip, emit, acc):
        done = []
        for half in range(2):
            cols = slice(128 * half, 128 * (half + 1))
            kern = [small[b * KVOL + k : b * KVOL + k + 1, cols] for k in range(KVOL)]
            if flip:
                kern = kern[::-1]
            planes = []
            for dt in range(3):
                g = f + dt - 1
                planes.append(hz.at[0] if g < 0 else hz.at[1] if g > last else local.at[g])

            def two_rows(i, carry):
                h = 2 * i
                part = [[None] * 3 for _ in range(2)]
                for dt in range(3):
                    for rr in range(4):
                        v = planes[dt][h + rr, :, cols]
                        for o in range(2):
                            dh = rr - o
                            if 0 <= dh < 3:
                                for dw in range(3):
                                    term = kern[dt * 9 + dh * 3 + dw] * v
                                    part[o][dw] = term if part[o][dw] is None else part[o][dw] + term
                for o in range(2):
                    p = part[o]
                    c = p[1] + pltpu.roll(p[0], 1, 0) + pltpu.roll(p[2], WP - 1, 0)
                    carry = emit(h + o, half, cols, c, carry)
                return carry

            done.append(lax.fori_loop(0, HH // 2, two_rows, tuple(a[half] for a in acc)))
        return [[done[0][k], done[1][k]] for k in range(len(acc))]

    class Reduction:
        def __init__(self, first, size):
            self.lines = pl.ds(first, size)
            self.first, self.size = first, size
            self.which = 0 if first == 0 else 1
            self.open = {"a": [], "b": [], "all": []}

        def put(self, who, piece, first, value):
            grad_a[who, piece, pl.ds(self.lines.start + first, value.shape[0])] = value.astype(BF16)

        def clear(self, *names):
            for name in names:
                for copy in self.open[name]:
                    copy.wait_send()
                self.open[name] = []

        def move(self, name, copy):
            copy.start()
            self.open[name].append(copy)

        def pair_copy(self, b, side):
            i = 2 * b + self.which
            src, dst = grad_a.at[2 * side + 1 - net.core, :, self.lines], grad_ra.at[side, :, self.lines]
            return push(src, dst, grad_sa.at[i, side], grad_qa.at[i, side], net.pair()[1])

        def to_pair(self, b):
            for side in range(2):
                self.move("a", self.pair_copy(b, side))

        def across_copy(self, b):
            i = 2 * b + self.which
            src, dst = grad_a.at[net.across()[0], :, self.lines], grad_ra.at[2, :, self.lines]
            return push(src, dst, grad_sa.at[i, 2], grad_qa.at[i, 2], net.across()[1])

        def to_side(self, b):
            for side in range(2):
                self.pair_copy(b, side).wait_recv()
            other = net.across()[0]

            def add(piece, _):
                mine, theirs = grad_a[other, piece, self.lines], grad_ra[1 - net.side, piece, self.lines]
                grad_a[other, piece, self.lines] = (mine.astype(F32) + theirs.astype(F32)).astype(BF16)
                return 0

            lax.fori_loop(0, PIECES, add, 0)
            self.move("a", self.across_copy(b))

        def low_peers(self):
            rows = [lax.rem(net.row_low + o, net.low) for o in range(1, net.low)]
            return [(row, (net.row_high * net.low + row, lane)) for row in rows]

        def to_rows(self, b):
            i = 2 * b + self.which
            self.across_copy(b).wait_recv()
            self.clear("b")

            def add(piece):
                total = grad_a[own, piece, self.lines].astype(F32) + grad_ra[net.side, piece, self.lines].astype(F32)
                grad_b[piece, self.lines] = (total + grad_ra[2, piece, self.lines].astype(F32)).astype(BF16)

            each = PIECES // net.low
            for step, (who, device) in enumerate(self.low_peers()):
                for k in range(each):
                    add(who * each + k)
                src = grad_b.at[pl.ds(who * each, each), self.lines]
                dst = grad_rb.at[net.row_low, :, self.lines]
                self.move("b", push(src, dst, grad_sb.at[i, step], grad_qb.at[i, net.row_low], device))
            for k in range(each):
                add(net.row_low * each + k)

        def to_all(self, b):
            i = 2 * b + self.which
            each = PIECES // net.low
            mine = pl.ds(net.row_low * each, each)
            for step, (who, device) in enumerate(self.low_peers()):
                src, dst = grad_b.at[mine, self.lines], grad_rb.at[who, :, self.lines]
                push(src, dst, grad_sb.at[i, step], grad_qb.at[i, who], device).wait_recv()
            total = grad_b[mine, self.lines].astype(F32)
            for who, _device in self.low_peers():
                total = total + grad_rb[who, :, self.lines].astype(F32)
            if net.high > 1:
                grad_top[b, net.row_high, :, self.lines] = total.astype(BF16)
                for step, (who, device) in enumerate(net.top()):
                    here = grad_top.at[b, net.row_high, :, self.lines]
                    self.move("all", push(here, here, grad_st.at[i, step], grad_qt.at[i, net.row_high], device))
                for step, (who, device) in enumerate(net.top()):
                    there = grad_top.at[b, who, :, self.lines]
                    push(there, there, grad_st.at[i, step], grad_qt.at[i, who], device).wait_recv()
                self.clear("all")
                total = grad_top[b, 0, :, self.lines].astype(F32)
                for j in range(1, net.high):
                    total = total + grad_top[b, j, :, self.lines].astype(F32)
            self.clear("all")
            grad_all[mine, self.lines] = total.astype(BF16)
            for step, (who, device) in enumerate(self.low_peers()):
                here = grad_all.at[mine, self.lines]
                self.move("all", push(here, here, grad_sc.at[i, step], grad_qc.at[i, net.row_low], device))

        def finish(self, b):
            i = 2 * b + self.which
            each = PIECES // net.low
            for step, (who, device) in enumerate(self.low_peers()):
                there = grad_all.at[pl.ds(who * each, each), self.lines]
                push(there, there, grad_sc.at[i, step], grad_qc.at[i, who], device).wait_recv()
            for piece in range(PIECES):
                cols = slice(128 * piece, 128 * (piece + 1))
                grads_out[b, self.first : self.first + self.size, cols] = grad_all[piece, self.lines].astype(F32)

    early = [Reduction(0, 96 if b == 0 else 80) for b in range(BLOCKS)]
    final = [Reduction(96, 64 if b == 0 else 80) for b in range(BLOCKS)]

    order = (0, last) + tuple(range(1, last))
    norms = []
    mid_grads = {}
    out_grads = {}

    def open_block(b, rows):
        z = dot(a3s[b, rows], exp[b])
        a4, b4 = norms[b][3][2], norms[b][3][3]
        return z, (z * a4 + b4) + xs[b][rows].astype(F32)

    kept = [(a1s, keep_mid.at[0]), (d1s, keep_mid.at[1]), (d2s, keep_mid.at[2]), (yb, keep_big)]
    keeps = [pltpu.make_async_copy(held, far_away, keep_sem.at[k]) for k, (held, far_away) in enumerate(kept)]
    backs = [pltpu.make_async_copy(far_away, held, back_sem.at[k]) for k, (held, far_away) in enumerate(kept)]

    def slope_rows(i, _):
        rows, lines, where = trio(i)
        _, pre = open_block(0, rows)
        for k, (f, j) in enumerate(where):
            v = pre[FLAT * k : FLAT * (k + 1)]
            square, t = gelu_core(v)
            part = pl.ds(pl.multiple_of((TRIO * i + k) * FLAT, FLAT), FLAT)
            yb[part] = gelu_slope(v, square, t, 0.5 * live(f)).astype(BF16)
        return 0

    out_store = [frame_copy(yb, out_hbm, f, store_sem.at[f]) for f in range(frames)]

    for b in range(BLOCKS):
        norm1 = affine(first_sums[0], first_sums[1], count, mid(b, 0, 0), mid(b, 0, 1))
        if b == 0:
            gather("exp", 0)
        _, _, a1, b1 = norm1
        carry = (zero8(), zero8())
        if b > 0:
            keeps[0].wait()
            for side in range(2):
                halo_sent(2 * (b - 1) + 1, 2 + b - 1, side)
        for f in order:
            alive = live(f)

            v = (z1[b, f * HH : (f + 1) * HH].reshape(HH * WP, 256) * a1 + b1).astype(BF16)
            _, t = gelu_core(v)
            act = gelu_value(v, t, half_mask(alive, HH).astype(BF16))
            a1s[f * HH : (f + 1) * HH] = act.reshape(HH, WP, 256)
            m = dot(act, mix[...])
            z2[b, f, 1 : 1 + HH] = m.reshape(HH, WP, 256)
            if f in (0, last):
                halo_send[0 if f == 0 else 1] = m.astype(BF16).reshape(HH, WP, 256)
            carry = (carry[0] + fold(m), carry[1] + fold(m * m))
            if f in (0, last):
                halo_start(2 * b, b, 0 if f == 0 else 1)

        if b == 0:
            keeps[0].start()

        def emit_conv(f):
            pad = pad_mask[:WP, :128] * live(f)

            def emit(row, half, cols, c, carry):
                c = c * pad
                conv[b, f * HH + row, :, cols] = c
                if f in (0, last):
                    halo_send[0 if f == 0 else 1, row, :, cols] = c.astype(BF16)
                e = edge[b, f + 1, row_class(row), :, cols]
                s0, s1, s2 = carry
                return (s0 + fold(c), s1 + fold(c * c), s2 + fold(c * e))

            return emit

        def fill(side):
            present = lane > 0 if side == 0 else lane < lanes - 1

            @pl.when(present)
            def _():
                halo_wait(2 * b, b, side)

                def widen(j, _):
                    hz[side, pl.ds(1 + j * GROUP, GROUP)] = halo_recv[b, side, pl.ds(j * GROUP, GROUP)].astype(F32)
                    return 0

                lax.fori_loop(0, QUADS, widen, 0)

            @pl.when(jnp.logical_not(present))
            def _():
                def clear(j, _):
                    hz[side, pl.ds(1 + j * GROUP, GROUP)] = jnp.zeros((GROUP, WP, 256), F32)
                    return 0

                lax.fori_loop(0, QUADS, clear, 0)

        acc = [[zero8(128), zero8(128)] for _ in range(3)]
        for f in range(1, last):
            acc = convolve(z2.at[b], f, b, False, emit_conv(f), acc)
        if b == 0:
            gather_on("exp", 0)
        for side in range(2):
            fill(side)
            halo_sent(2 * b, b, side)
            f = 0 if side == 0 else last
            acc = convolve(z2.at[b], f, b, False, emit_conv(f), acc)
            halo_start(2 * b + 1, 2 + b, side)
        joined = [jnp.concatenate([flat_sum(a[0]), flat_sum(a[1])], axis=1) for a in acc]
        total_start(3 * b + 1, rows_of(flat_sum(carry[0]), flat_sum(carry[1]), *joined, *edge_sums[b]))
        if b == 0:
            gather_wait("exp", 0)
        else:
            gather_wait("exp", 1)
            tbuf[...] = exp[1].T
            keeps[1].wait()

        def slope1(i, _):
            _, lines, where = trio(i)
            v = z1[b, lines].reshape(TRIO * WIDE, 256) * a1 + b1
            square, t = gelu_core(v)
            d1s[lines] = gelu_slope(v, square, t, 0.5).astype(BF16).reshape(TRIO * GROUP, WP, 256)
            return 0

        lax.fori_loop(0, trios, slope1, 0)
        if b == 0:
            keeps[1].start()
        else:
            lax.fori_loop(trios - 2, trios, slope_rows, 0)
            keeps[3].start()
        got = total_finish(3 * b + 1)
        norm2 = affine(got[0:1], got[1:2], count, mid(b, 1, 0), mid(b, 1, 1))
        _, _, a2, b2 = norm2
        sc, scc, sce, se, see = [got[i : i + 1] for i in range(2, 7)]
        total3 = a2 * sc + b2 * se
        square3 = a2 * a2 * scc + 2.0 * a2 * b2 * sce + b2 * b2 * see
        norm3 = affine(total3, square3, count, mid(b, 2, 0), mid(b, 2, 1))
        _, _, a3, b3 = norm3

        norm3_pattern(b, a3, b2, b3)
        if b == 0:
            gather("red", 1)
            gather("mix", 1)

        def activate(i, _):
            rows, lines, where = trio(i)
            c = conv[b, lines].reshape(TRIO * WIDE, 256)
            acts = []
            for k, (f, j) in enumerate(where):
                v = c[WIDE * k : WIDE * (k + 1)] * (a3 * a2) + edge_rows(pat.at[f + 1], j)
                _, t = gelu_core(v)
                acts.append(squeeze(gelu_value(v, t, 0.5 * live(f))))
            a3s[b, rows] = jnp.concatenate(acts, axis=0).astype(BF16)
            return 0

        lax.fori_loop(0, trios, activate, 0)
        gram = dot_rows(a3s[b], a3s[b])
        line = dot(jnp.ones((16, frames * frame_rows), BF16), a3s[b])
        high = jnp.concatenate([gram, line], axis=0)
        split = high.astype(BF16)
        grown = dot(split, exp[b]) + dot((high - split.astype(F32)).astype(BF16), exp[b])
        squares = flat_sum(fold(grown[:256] * exp[b].astype(F32)))
        if b == 0:
            gather_on("red", 1)
            gather_on("mix", 1)
        total_start(3 * b + 2, rows_of(grown[256:257], squares))
        if b == 0:
            gather_wait("red", 1)
            tbuf[...] = red_t[1].T
        else:
            keeps[2].wait()

        def slope3(i, _):
            _, lines, where = trio(i)
            c = conv[b, lines].reshape(TRIO * WIDE, 256)
            out = []
            for k, (f, j) in enumerate(where):
                v = c[WIDE * k : WIDE * (k + 1)] * (a3 * a2) + edge_rows(pat.at[f + 1], j)
                square, t = gelu_core(v)
                out.append(gelu_slope(v, square, t, 0.5).astype(BF16))
            d2s[lines] = jnp.concatenate(out, axis=0).reshape(TRIO * GROUP, WP, 256)
            return 0

        lax.fori_loop(0, trios, slope3, 0)
        if b == 0:
            keeps[2].start()
        got = total_finish(3 * b + 2)
        norm4 = affine(wide_row(got, 0), wide_row(got, 4), count4, norm_out[b, 0:1], norm_out[b, 1:2])
        norms.append((norm1, norm2, norm3, norm4, (sc, scc, sce, se, see)))

        if b == 0:
            gather("exp", 1)

            def closing(i, carry):
                rows, lines, where = trio(i)
                _, pre = open_block(0, rows)
                results = []
                for (f, j), v in zip(where, pieces(pre, FLAT)):
                    half = jnp.full((1, 1024), 0.5 * live(f), F32).astype(BF16)
                    v = v.astype(BF16)
                    _, t = gelu_core(v)
                    results.append(gelu_value(v, t, half))
                result = jnp.concatenate(results, axis=0)
                x1[rows] = result
                z = dot(result, tbuf[...])
                z1[1, lines] = spread(z).reshape(TRIO * GROUP, WP, 256)
                return (carry[0] + fold(z), carry[1] + fold(z * z))

            carry = lax.fori_loop(0, trios, closing, (zero8(), zero8()))
            gather_on("exp", 1)
            total_start(3, rows_of(flat_sum(carry[0]), flat_sum(carry[1])))
            gather_wait("mix", 1)
            mix[...] = mix_t[1].T
            lax.fori_loop(0, trios - 2, slope_rows, 0)
            got = total_finish(3)
            first_sums = (got[0:1], got[1:2])

    cot_load.wait()
    keeps[3].wait()

    def ending(i, carry):
        rows, lines, where = trio(i)
        z, pre = open_block(1, rows)
        g = sb[rows]
        s0, s1 = carry
        for k, (f, j) in enumerate(where):
            here = slice(FLAT * k, FLAT * (k + 1))
            v, half = pre[here].astype(BF16), jnp.full((1, 1024), 0.5 * live(f), F32).astype(BF16)
            square, t = gelu_core(v)
            part = pl.ds(pl.multiple_of((TRIO * i + k) * FLAT, FLAT), FLAT)
            yb[part] = gelu_value(v, t, half)
            low = gelu_slope(v, square, t, half) * g[here]
            sb[part] = low
            s = low.astype(F32)
            s0, s1 = s0 + fold(s), s1 + fold(s * z[here])
        return s0, s1

    carry = lax.fori_loop(0, trios, ending, (zero8(1024), zero8(1024)))
    total_start(6, rows_of(flat_sum(carry[0]), flat_sum(carry[1])))
    for copy in out_store:
        copy.start()

    for b in reversed(range(BLOCKS)):
        turn = BLOCKS - 1 - b
        base = 6 + 3 * turn
        norm1, norm2, norm3, norm4, (sc, scc, sce, se, see) = norms[b]
        _, _, a1, b1 = norm1
        mean2, scale2, a2, b2 = norm2
        mean3, scale3, a3, b3 = norm3
        a4 = norm4[2]

        got = total_finish(base)
        slope4, bias4, gain_grad, shift_grad = back_affine(wide_row(got, 0), wide_row(got, 4), count4, norm4)
        out_grads[b] = (gain_grad, shift_grad)
        if turn == 0:
            for copy in out_store:
                copy.wait()
        for side in range(2):
            if turn == 0:
                halo_sent(2 * (BLOCKS - 1) + 1, 2 + BLOCKS - 1, side)
            else:
                halo_sent(2 * BLOCKS + turn - 1, b + 1, side)

        if turn > 0:
            early[b + 1].to_rows(b + 1)
            final[b + 1].to_side(b + 1)
        kind = 2 * BLOCKS + turn
        if turn > 0:
            backs[2].wait()
        acc = (zero8(), zero8(), zero8())
        for f in order:
            alive = live(f)

            rows = slice(f * frame_rows, (f + 1) * frame_rows)
            z = dot(a3s[b, rows], exp[b])
            d4 = (sb[rows].astype(F32) * a4 + (z * slope4 + bias4 * alive)).astype(BF16)
            yb[rows] = d4
            back = spread(dot(d4, tbuf[...]))
            for j in range(QUADS):
                c = conv[b, f * HH + GROUP * j : f * HH + GROUP * (j + 1)].reshape(WIDE, 256)
                slope = d2s[f * HH + GROUP * j : f * HH + GROUP * (j + 1)].reshape(WIDE, 256)
                e3 = back[WIDE * j : WIDE * (j + 1)] * slope.astype(F32)
                dz[f, 1 + GROUP * j : 1 + GROUP * (j + 1)] = e3.reshape(GROUP, WP, 256)
                if f in (0, last):
                    halo_send[0 if f == 0 else 1, GROUP * j : GROUP * (j + 1)] = e3.astype(BF16).reshape(GROUP, WP, 256)
                e = edge_rows(edge.at[b, f + 1], j)
                acc = (acc[0] + fold(e3), acc[1] + fold(e3 * c), acc[2] + fold(e3 * e))
            if f in (0, last):
                halo_start(kind, b, 0 if f == 0 else 1)
        total_start(base + 1, rows_of(*[flat_sum(a) for a in acc]))

        if turn > 0:
            early[b + 1].clear("a")

        def expand_grad(i, _):
            cols = pl.ds(pl.multiple_of(i * 256, 256), 256)
            g = dot_rows(a3s[b], yb[:, cols])
            for who in range(lanes):
                for h in range(2):
                    early[b].put(who, 2 * i + h, 0, g[share * who : share * (who + 1), 128 * h : 128 * (h + 1)])
            return 0

        lax.fori_loop(0, 4, expand_grad, 0)
        if b > 0:
            tbuf[...] = exp[b - 1].T
            backs[3].start()

        got = total_finish(base + 1)
        e3_sum, e3_conv, e3_edge = got[0:1], got[1:2], got[2:3]
        e3_third = a2 * e3_conv + b2 * e3_edge
        slope3, bias3, gain3, shift3 = back_affine(e3_sum, e3_third, count, norm3)
        third_conv = a2 * scc + b2 * sce
        third_edge = a2 * sce + b2 * see
        d3_conv = a3 * e3_conv + bias3 * sc + slope3 * third_conv
        d3_edge = a3 * e3_edge + bias3 * se + slope3 * third_edge
        slope2, bias2, gain2, shift2 = back_affine(d3_edge, d3_conv, count, norm2)

        if turn > 0:
            early[b + 1].to_all(b + 1)
            final[b + 1].to_rows(b + 1)
        for f in range(-1, frames + 1):
            live_pad = pad_mask[:WP] * live(f)
            for cls in range(3):
                pat[f + 1, cls] = bias3 * live_pad + (slope3 * b2) * edge[b, f + 1, cls]
        slope_c = slope3 * a2

        def to_d3(q, _):
            f = lax.div(q, QUADS)
            j = lax.rem(q, QUADS)
            rows = pl.ds(1 + j * GROUP, GROUP)
            c = conv[b, pl.ds(q * GROUP, GROUP)].reshape(WIDE, 256)
            e3 = dz[f, rows].reshape(WIDE, 256)
            d3 = e3 * a3 + c * slope_c + edge_rows(pat.at[f + 1], j)
            dz[f, rows] = d3.reshape(GROUP, WP, 256)
            return 0

        lax.fori_loop(0, frames * QUADS, to_d3, 0)

        def fill_back(side):
            present = lane > 0 if side == 0 else lane < lanes - 1
            f = -1 if side == 0 else frames

            @pl.when(present)
            def _():
                halo_wait(2 * b + 1, 2 + b, side)
                halo_wait(kind, b, side)

                def widen(j, _):
                    rows = pl.ds(j * GROUP, GROUP)
                    c = halo_recv[2 + b, side, rows].astype(F32).reshape(WIDE, 256)
                    e3 = halo_recv[b, side, rows].astype(F32).reshape(WIDE, 256)
                    d3 = e3 * a3 + c * slope_c + edge_rows(pat.at[f + 1], j)
                    hz[side, pl.ds(1 + j * GROUP, GROUP)] = d3.reshape(GROUP, WP, 256)
                    return 0

                lax.fori_loop(0, QUADS, widen, 0)

            @pl.when(jnp.logical_not(present))
            def _():
                def clear(j, _):
                    hz[side, pl.ds(1 + j * GROUP, GROUP)] = jnp.zeros((GROUP, WP, 256), F32)
                    return 0

                lax.fori_loop(0, QUADS, clear, 0)

        for side in range(2):
            fill_back(side)

        def emit_back(f):
            pad = pad_mask[:WP, :128] * live(f)

            def emit(row, half, cols, e2, carry):
                z = z2[b, f, row + 1, :, cols]
                d2 = (e2 * a2[:, cols] + (z * slope2[:, cols] + bias2[:, cols])) * pad
                d2s[f * HH + row, :, cols] = d2.astype(BF16)
                return carry

            return emit

        for f in range(frames):
            convolve(dz, f, b, True, emit_back(f), [])

        if turn > 0:
            backs[0].wait()
            backs[1].wait()

        def unmixing(i, acc):
            _, lines, where = trio(i)
            e = dot(d2s[lines].reshape(TRIO * WIDE, 256), mix_t[b])
            z = z1[b, lines].reshape(TRIO * WIDE, 256)
            for k, (f, j) in enumerate(where):
                here = slice(WIDE * k, WIDE * (k + 1))
                part = pl.ds((TRIO * i + k) * GROUP, GROUP)
                e1 = e[here] * d1s[part].reshape(WIDE, 256).astype(F32)
                conv[b, part] = e1.reshape(GROUP, WP, 256)
                acc = (acc[0] + fold(e1), acc[1] + fold(e1 * z[here]))
            return acc

        acc = lax.fori_loop(0, trios, unmixing, (zero8(), zero8()))
        if turn > 0:
            early[b + 1].finish(b + 1)
        total_start(base + 2, rows_of(*[flat_sum(a) for a in acc]))

        def depth_grad(half, b=b, a2=a2, b2=b2):
            place, at = (early[b], 80) if b == 0 else (final[b], 64)
            cols = slice(128 * half, 128 * (half + 1))
            taps_grad = tuple(zero8(128) for _ in range(KVOL))
            for f in range(frames):
                planes = []
                for dt in range(3):
                    g = f - (dt - 1)
                    planes.append(hz.at[0] if g < 0 else hz.at[1] if g > last else dz.at[g])
                shift_rows = b2[:, cols] * (pad_mask[:WP, :128] * live(f))

                def tap_rows(h, taps_grad):
                    a = z2[b, f, h + 1, :, cols] * a2[:, cols] + shift_rows
                    moved = [pltpu.roll(a, 1, 0), a, pltpu.roll(a, WP - 1, 0)]
                    new = list(taps_grad)
                    for dt in range(3):
                        for dh in range(3):
                            d = planes[dt][h + 1 - (dh - 1), :, cols]
                            for dw in range(3):
                                k = dt * 9 + dh * 3 + dw
                                new[k] = new[k] + fold(d * moved[dw])
                    return tuple(new)

                taps_grad = lax.fori_loop(0, HH, tap_rows, taps_grad)
            lines = jnp.concatenate(
                [flat_sum(t) for t in taps_grad] + [jnp.zeros((WP - KVOL, 128), F32)], axis=0
            )
            for r in range(4):
                part = jnp.concatenate([lines[8 * r : 8 * r + 8], zero8(128)], axis=0)
                for who in range(lanes):
                    place.put(who, 2 * r + half, at, part)

        depth_grad(0)
        if b == 0:
            depth_grad(1)
        g = dot_rows(d2s[...].reshape(frames * HH * WP, 256), a1s[...].reshape(frames * HH * WP, 256))
        for who in range(lanes):
            for r in range(4):
                for h in range(2):
                    first = share * who + 16 * r
                    early[b].put(who, 2 * r + h, 64, g[first : first + 16, 128 * h : 128 * (h + 1)])
        early[b].to_pair(b)
        if b > 0:
            for k in range(3):
                backs[k].start()

        got = total_finish(base + 2)
        slope1, bias1, gain1, shift1 = back_affine(got[0:1], got[1:2], count, norm1)
        mid_grads[b] = ((gain1, shift1), (gain2, shift2), (gain3, shift3))

        early[b].to_side(b)
        def first_grad(i):
            rows, lines, where = trio(i)
            e1 = conv[b, lines].reshape(TRIO * WIDE, 256)
            z = z1[b, lines].reshape(TRIO * WIDE, 256)
            parts = []
            for k, (f, j) in enumerate(where):
                here = slice(WIDE * k, WIDE * (k + 1))
                alive = live(f)
                parts.append(squeeze(e1[here] * a1 + (z[here] * (slope1 * alive) + bias1 * alive)))
            d1 = jnp.concatenate(parts, axis=0).astype(BF16)
            a3s[b, rows] = d1
            return rows, where, d1

        def reduce_grad(i, _):
            cols = pl.ds(pl.multiple_of(i * 256, 256), 256)
            g = dot_rows(a3s[b], xs[b][:, cols])
            for who in range(lanes):
                for h in range(2):
                    final[b].put(who, 2 * i + h, 0, g[share * who : share * (who + 1), 128 * h : 128 * (h + 1)])
            return 0

        if b > 0:

            backs[3].wait()

            def passing(i, carry):
                rows, where, d1 = first_grad(i)
                g = dot(d1, red_t[b]) + sb[rows].astype(F32)
                z = dot(a3s[b - 1, rows], exp[b - 1])
                slope = yb[rows]
                s0, s1 = carry
                for k, (f, j) in enumerate(where):
                    here = slice(FLAT * k, FLAT * (k + 1))
                    s = slope[here].astype(F32) * g[here]
                    sb[pl.ds(pl.multiple_of((TRIO * i + k) * FLAT, FLAT), FLAT)] = s.astype(BF16)
                    s0, s1 = s0 + fold(s), s1 + fold(s * z[here])
                return s0, s1

            carry = lax.fori_loop(0, trios, passing, (zero8(1024), zero8(1024)))
            total_start(base + 3, rows_of(flat_sum(carry[0]), flat_sum(carry[1])))
            depth_grad(1)
            lax.fori_loop(0, 4, reduce_grad, 0)
            final[b].to_pair(b)
        else:
            final[b + 1].to_all(b + 1)

            def only_d1(i, _):
                first_grad(i)
                return 0

            lax.fori_loop(0, trios, only_d1, 0)
            final[b + 1].clear("a")
            lax.fori_loop(0, 4, reduce_grad, 0)
            final[b].to_pair(b)
            early[b + 1].clear("b", "all")
            early[b].to_rows(b)
            steps = (lambda: final[b].to_side(b), lambda: early[b].to_all(b))
            gtok_store = [frame_copy(yb, gtok_hbm, f, store_sem.at[f]) for f in range(frames)]
            for f in range(frames):
                rows = slice(f * frame_rows, (f + 1) * frame_rows)
                yb[rows] = (dot(a3s[b, rows], red_t[b]) + sb[rows].astype(F32)).astype(BF16)
                gtok_store[f].start()
                if f < len(steps):
                    steps[f]()
            final[b + 1].finish(b + 1)
            final[b + 1].clear("b", "all")
            final[b].to_rows(b)
            early[b].finish(b)
            final[b].to_all(b)
            final[b].finish(b)

    for b in range(BLOCKS):
        for k in range(3):
            for w in range(2):
                r = (b * 3 + k) * 2 + w
                gmid_out[r : r + 1] = mid_grads[b][k][w]
        for w in range(2):
            gout_out[2 * b + w : 2 * b + w + 1] = out_grads[b][w]

    for copy in gtok_store:
        copy.wait()
    early[0].clear("a", "b", "all")
    final[0].clear("a", "b", "all")
    for copy in late + travelling:
        copy.wait_send()
    for side in range(2):
        halo_sent(2 * BLOCKS + BLOCKS - 1, 0, side)


def whole_call(groups, lanes, counts, tokens, cotangent, reduce_loc, mix_loc, expand_loc, depth_loc, mid_loc, norm_out):
    rows = tokens.shape[0]
    frames = rows // (HH * WW)
    whole = pl.BlockSpec(memory_space=pltpu.VMEM)
    hbm = pl.BlockSpec(memory_space=pl.ANY)
    dma = pltpu.SemaphoreType.DMA
    low, high = stages(groups)
    far = low * (lanes // 2)
    lines = frames * HH
    sums = 6 * BLOCKS
    kinds = 3 * BLOCKS
    shape = jax.ShapeDtypeStruct
    return pl.pallas_call(
        functools.partial(whole_kernel, groups, lanes),
        out_shape=(
            shape((rows, 1024), BF16),
            shape((rows, 1024), BF16),
            shape((BLOCKS, 176, 1024), F32),
            shape((BLOCKS * 6, 256), F32),
            shape((BLOCKS * 2, 1024), F32),
            shape((rows, 1024), BF16),
            shape((3, lines, WP, 256), BF16),
        ),
        in_specs=[pl.BlockSpec(memory_space=pltpu.SMEM)] + [hbm] * 5 + [whole] * 3,
        out_specs=[hbm] * 2 + [whole] * 3 + [hbm] * 2,
        scratch_shapes=[
            pltpu.VMEM((rows, 1024), BF16),
            pltpu.VMEM((rows, 1024), BF16),
            pltpu.VMEM((rows, 1024), BF16),
            pltpu.VMEM((rows, 1024), BF16),
            pltpu.VMEM((BLOCKS, 256, 1024), BF16),
            pltpu.VMEM((BLOCKS, 256, 1024), BF16),
            pltpu.VMEM((1024, 256), BF16),
            pltpu.VMEM((BLOCKS, 256, 256), BF16),
            pltpu.VMEM((256, 256), BF16),
            pltpu.VMEM((lanes, 40, 128), F32),
            pltpu.VMEM((80, 256), F32),
            pltpu.VMEM((BLOCKS, lines, WP, 256), F32),
            pltpu.VMEM((lines, WP, 256), BF16),
            pltpu.VMEM((BLOCKS, frames, HH + 2, WP, 256), F32),
            pltpu.VMEM((frames, HH + 2, WP, 256), F32),
            pltpu.VMEM((2, HH + 2, WP, 256), F32),
            pltpu.VMEM((BLOCKS, lines, WP, 256), F32),
            pltpu.VMEM((BLOCKS, rows, 256), BF16),
            pltpu.VMEM((BLOCKS, frames + 2, 3, WP, 256), F32),
            pltpu.VMEM((frames + 2, 3, WP, 256), F32),
            pltpu.VMEM((lines, WP, 256), BF16),
            pltpu.VMEM((lines, WP, 256), BF16),
            pltpu.VMEM((2, HH, WP, 256), BF16),
            pltpu.VMEM((2 * BLOCKS, 2, HH, WP, 256), BF16),
            pltpu.VMEM((lanes, PIECES, 176, 128), BF16),
            pltpu.VMEM((3, PIECES, 176, 128), BF16),
            pltpu.VMEM((PIECES, 176, 128), BF16),
            pltpu.VMEM((low, PIECES // low, 176, 128), BF16),
            pltpu.VMEM((PIECES, 176, 128), BF16),
            pltpu.VMEM((BLOCKS, high, PIECES // low, 176 if high > 1 else 16, 128), BF16),
            pltpu.VMEM((2, 2, 16, 128), F32),
            pltpu.VMEM((2, far, 16, 128), F32),
            pltpu.VMEM((2, high, 16, 128), F32),
            dma((sums,)),
            dma((sums,)),
            dma((sums, far)),
            dma((sums, far)),
            dma((sums, high)),
            dma((sums, high)),
            dma((7, 3)),
            dma((7, lanes)),
            dma((kinds, 2)),
            dma((kinds, 2)),
            dma((frames + 1,)),
            dma((frames,)),
            dma((2 * BLOCKS, 3)),
            dma((2 * BLOCKS, 3)),
            dma((2 * BLOCKS, low)),
            dma((2 * BLOCKS, low)),
            dma((2 * BLOCKS, low)),
            dma((2 * BLOCKS, low)),
            dma((2 * BLOCKS, high)),
            dma((2 * BLOCKS, high)),
            dma((BLOCKS, 4)),
            dma((4,)),
            dma((4,)),
        ],
        compiler_params=pltpu.CompilerParams(
            collective_id=1, has_side_effects=True, vmem_limit_bytes=63 * 2**20
        ),
    )(counts, tokens, cotangent, reduce_loc, mix_loc, expand_loc, depth_loc, mid_loc, norm_out)


def descend(weight, moment, grad):
    moment_new = MOMENTUM * moment + grad + DECAY * weight
    return (weight - LEARN_RATE * moment_new, moment_new)


def update_kernel(lanes, *refs):
    out_raw, gtok_raw = refs[:2]
    out, gtok = refs[17:19]
    held = refs[37:70]
    big, sems, store_sems, small_sems, small_stores = refs[70:]
    smalls = [pltpu.make_async_copy(refs[2 + k], held[k], small_sems.at[k]) for k in range(15)]
    results = [pltpu.make_async_copy(held[15 + k], refs[19 + k], small_stores.at[k]) for k in range(18)]
    reduced, gmid, gout = held[:3]
    weights, moments = held[3:9], held[9:15]
    grads, new_weights, new_moments = held[15:21], held[21:27], held[27:33]
    chunks = sems.shape[1]
    rows = out.shape[0] // chunks
    copies, stores = [], []
    for k in range(chunks):
        for which, (src, dst) in enumerate(((out_raw, out), (gtok_raw, gtok))):
            here = pl.ds(k * rows, rows)
            copies.append(pltpu.make_async_copy(src.at[here], big.at[which, here], sems.at[which, k]))
            stores.append(pltpu.make_async_copy(big.at[which, here], dst.at[here], store_sems.at[which, k]))
    for copy in smalls + copies:
        copy.start()
    for copy in smalls:
        copy.wait()
    lane = lax.axis_index("chan")
    narrow = 256 // lanes

    def mine(v):
        out = v[:, :narrow]
        for who in range(1, lanes):
            out = jnp.where(lane == who, v[:, narrow * who : narrow * (who + 1)], out)
        return out

    def step(slot, at, grad):
        weight, moment = descend(weights[slot][at], moments[slot][at], grad)
        grads[slot][at] = grad
        new_weights[slot][at] = weight
        new_moments[slot][at] = moment

    depths = []
    for b in range(BLOCKS):
        step(0, (b,), reduced[b, 96:160])
        mix = reduced[b, 64:80]
        step(1, (b,), jnp.concatenate([mix[:, 256 * r : 256 * (r + 1)] for r in range(4)], axis=0))
        depth = reduced[b, 80:88] if b == 0 else reduced[b, 160:168]
        depths.append(mine(jnp.concatenate([depth[:, 256 * r : 256 * (r + 1)] for r in range(4)], axis=0)))
        step(3, (b,), reduced[b, 0:64])
        step(5, (b,), gout[2 * b : 2 * b + 2])
    for k in range(KVOL):
        step(2, (k,), jnp.concatenate([depth[k : k + 1] for depth in depths], axis=0))
    middle = mine(gmid[...])
    for k in range(BLOCKS * 3):
        step(4, (k,), middle[2 * k : 2 * k + 2])
    for copy in results:
        copy.start()
    for copy, store in zip(copies, stores):
        copy.wait()
        store.start()
    for store in stores + results:
        store.wait()


def update_call(lanes, *args):
    hbm = pl.BlockSpec(memory_space=pl.ANY)
    like = [jax.ShapeDtypeStruct(v.shape, v.dtype) for v in args]
    return pl.pallas_call(
        functools.partial(update_kernel, lanes),
        out_shape=tuple(like[:2] + like[5:11] * 3),
        in_specs=[hbm] * 17,
        out_specs=[hbm] * 20,
        scratch_shapes=[pltpu.VMEM(v.shape, v.dtype) for v in like[2:] + like[5:11] * 3]
        + [
            pltpu.VMEM((2,) + args[0].shape, args[0].dtype),
            pltpu.SemaphoreType.DMA((2, 7)),
            pltpu.SemaphoreType.DMA((2, 7)),
            pltpu.SemaphoreType.DMA((15,)),
            pltpu.SemaphoreType.DMA((18,)),
        ],
        compiler_params=pltpu.CompilerParams(vmem_limit_bytes=60 * 2**20),
    )(*args)


def shards(
    tokens,
    frame_counts,
    cotangent,
    w_reduce,
    w_mix,
    w_depth,
    w_expand,
    norm_mid,
    norm_out,
    moment_reduce,
    moment_mix,
    moment_depth,
    moment_expand,
    moment_mid,
    moment_out,
):
    lanes = lax.axis_size("chan")
    turned = lambda v: jnp.swapaxes(v, 1, 2)
    swap = lambda v: jnp.swapaxes(v, 0, 1)
    flat = lambda v: v.reshape((-1,) + v.shape[2:])
    raw = whole_call(
        lax.axis_size("dp"),
        lanes,
        frame_counts,
        tokens,
        cotangent,
        turned(w_reduce),
        turned(w_mix),
        w_expand,
        swap(w_depth),
        flat(norm_mid),
        norm_out,
    )
    inside = lambda r, m, d, e, mid, out: (turned(r), turned(m), swap(d), e, flat(mid), out)
    outside = lambda r, m, d, e, mid, out: (turned(r), turned(m), swap(d), e, mid.reshape(norm_mid.shape), out)
    done = update_call(
        lanes,
        *raw[:5],
        *inside(w_reduce, w_mix, w_depth, w_expand, norm_mid, norm_out),
        *inside(moment_reduce, moment_mix, moment_depth, moment_expand, moment_mid, moment_out),
    )
    return done[:2] + outside(*done[2:8]) + outside(*done[8:14]) + outside(*done[14:20])


def solution(mesh):
    rows = P(("dp", "chan"), None)
    weights = (
        P(None, None, "chan"),
        P(None, None, "chan"),
        P(None, None, "chan"),
        P(None, "chan", None),
        P(None, None, None, "chan"),
        P(),
    )
    return jax.shard_map(
        shards,
        mesh=mesh,
        in_specs=(rows, P("dp"), rows) + weights + weights,
        out_specs=(rows, rows) + weights + weights + weights,
        check_vma=False,
    )
```
